32 devices in a mesh: dp: 4 (over z), seq: 8 (over y, x, core).
Axes of the slice: x: 2, y: 2, z: 4, core: 2. Of those that a mesh axis runs over, the one named last changes fastest.
Arguments:
- inputs: bfloat16 [2, 4, 1024, 2048], P(None, 'dp', 'seq'), may hold values from -6 to 6
- lengths: int32 [2, 4], P(None, 'dp'), may hold values from 256 to 1024, as said below
- first_gain: float32 [2048], replicated, may hold values from 0.5 to 1.5
- input_weight: bfloat16 [2048, 8192], P(('dp', 'seq')), may hold values from -0.125 to 0.125
- decay_weight: bfloat16 [2048, 32], replicated, may hold values from -0.125 to 0.125
- conv_weight: float32 [4, 6144], replicated, may hold values from -3 to 3
- decay_log: float32 [16], replicated, may hold values from -12 to -2
- decay_bias: float32 [16], replicated, may hold values from -1.5 to 1
- head_gain: float32 [128], replicated, may hold values from 0.5 to 1.5
- output_weight: bfloat16 [2048, 2048], P(('dp', 'seq')), may hold values from -0.1875 to 0.1875
- second_gain: float32 [2048], replicated, may hold values from 0.5 to 1.5
- gate_up_weight: bfloat16 [2048, 11264], P(('dp', 'seq')), may hold values from -0.125 to 0.125
- down_weight: bfloat16 [5632, 2048], P(('dp', 'seq')), may hold values from -0.15625 to 0.15625
- cotangent: bfloat16 [2, 4, 1024, 2048], P(None, 'dp', 'seq'), may hold values from -6 to 6
Outputs:
- result: float32 [2, 4, 1024, 2048], P(None, 'dp', 'seq')
- inputs_grad: float32 [2, 4, 1024, 2048], P(None, 'dp', 'seq')
- first_gain_grad: float32 [2048], replicated
- input_weight_grad: float32 [2048, 8192], P(('dp', 'seq'))
- decay_weight_grad: float32 [2048, 32], replicated
- conv_weight_grad: float32 [4, 6144], replicated
- decay_log_grad: float32 [16], replicated
- decay_bias_grad: float32 [16], replicated
- head_gain_grad: float32 [128], replicated
- output_weight_grad: float32 [2048, 2048], P(('dp', 'seq'))
- second_gain_grad: float32 [2048], replicated
- gate_up_grad: float32 [2048, 11264], P(('dp', 'seq'))
- down_grad: float32 [5632, 2048], P(('dp', 'seq'))
The draws below stay inside these ranges and needn't reach their ends.
Inputs may be any that keep to these rules, and one draw needn't show every extreme that they name: `lengths`: in each aligned group of 1 column, one entry over both micro-batches equals 1024.
All inputs are finite; a program needn't handle non-finite values.
Results may differ from the reference program's by a relative error of at most 0.015.
Values may be sent and summed in bfloat16 or wider, within the bound.
A program may use at most 512 MiB of HBM per device.

```python
import math
import jax
import jax.numpy as jnp
from jax import lax

D = 2048
H = 16
DK = 128
FF = 5632
KD = 2048
CONV = 4
SPAN = 64
MICRO = 2
SEQ_DEV = 1
SEQS = 4
LENGTH = 1024


def draw_lengths(key, part):
    key = jax.random.fold_in(key, 5)
    first_key, second_key = jax.random.split(key)
    drawn = jax.random.randint(first_key, (MICRO, SEQS), LENGTH // 4, LENGTH + 1)
    picked = jax.random.randint(second_key, (SEQS // SEQ_DEV,), 0, MICRO * SEQ_DEV)
    micro_index = lax.broadcasted_iota(jnp.int32, (MICRO, SEQS), 0)
    column = lax.broadcasted_iota(jnp.int32, (MICRO, SEQS), 1)
    flat_index = micro_index * SEQ_DEV + column % SEQ_DEV
    chosen = picked[column // SEQ_DEV]
    return jnp.where(flat_index == chosen, LENGTH, drawn).astype(jnp.int32)


def draw_decay_log(key, part):
    key = jax.random.fold_in(key, 11)
    rates = jax.random.uniform(key, (H,), jnp.float32, math.log(0.5 / LENGTH), math.log(1.0 / 16.0))
    return rates.astype(jnp.float32)


def block_scale(key, shape, cuts, smallest, top_value):
    def one(position, shards_of):
        heights = jax.random.uniform(jax.random.fold_in(jax.random.fold_in(key, 6), position), (shards_of,), jnp.float32, smallest / len(cuts), top_value / len(cuts))
        return jnp.repeat(jnp.exp(heights), shape[position] // shards_of).reshape((-1,) + (1,) * (len(shape) - position - 1))

    level = one(*cuts[0])
    for cut in cuts[1:]:
        level = level * one(*cut)
    return level


def bell_draw(key, dims, spread, most, shards=(), held_as=jnp.bfloat16):
    level = block_scale(key, dims, shards, -0.22, 0.18) if shards else 1.0
    result = jax.random.normal(key, dims, jnp.float32) * spread * level
    return jnp.minimum(jnp.maximum(result, -most), most).astype(held_as)


def setup_inputs(seed: int = 0) -> dict:
    seeds = jax.random.split(jax.random.key(seed), 15)
    return {
        "inputs": bell_draw(seeds[0], (MICRO, SEQS, LENGTH, D), 1.0, 6.0, ((1, 4), (2, 8))),
        "lengths": draw_lengths(jax.random.fold_in(seeds[14], 71), 0),
        "first_gain": jnp.clip(1.0 + 0.1 * jax.random.normal(seeds[2], (D,), jnp.float32), 0.5, 1.5),
        "input_weight": bell_draw(seeds[3], (D, 4 * KD), D ** -0.5, 0.125, ((0, 32),)),
        "decay_weight": bell_draw(seeds[4], (D, 2 * H), D ** -0.5, 0.125),
        "conv_weight": bell_draw(seeds[5], (CONV, 3 * KD), CONV ** -0.5, 3.0, (), jnp.float32),
        "decay_log": draw_decay_log(jax.random.fold_in(seeds[14], 71), 0),
        "decay_bias": jnp.clip(jax.random.uniform(seeds[7], (H,), jnp.float32, -1.5, 1.0), -1.5, 1.0),
        "head_gain": jnp.clip(1.0 + 0.1 * jax.random.normal(seeds[8], (DK,), jnp.float32), 0.5, 1.5),
        "output_weight": bell_draw(seeds[9], (KD, D), (KD // 2) ** -0.5, 0.1875, ((0, 32),)),
        "second_gain": jnp.clip(1.0 + 0.1 * jax.random.normal(seeds[10], (D,), jnp.float32), 0.5, 1.5),
        "gate_up_weight": bell_draw(seeds[11], (D, 2 * FF), D ** -0.5, 0.125, ((0, 32),)),
        "down_weight": bell_draw(seeds[12], (FF, D), (FF // 4) ** -0.5, 0.15625, ((0, 32),)),
        "cotangent": bell_draw(seeds[13], (MICRO, SEQS, LENGTH, D), 1.0, 6.0, ((1, 4), (2, 8))),
    }


HIGH = lax.Precision.HIGHEST

@jax.custom_vjp
def low(v):
    return lax.optimization_barrier(v.astype(jnp.bfloat16)).astype(jnp.float32)

@jax.custom_vjp
def low_back(v):
    return v

def low_keep(v):
    return (low(v), None)

def low_pass(kept, grad):
    return (grad,)

def back_keep(v):
    return (v, None)

def back_low(kept, grad):
    return (low(grad),)
low.defvjp(low_keep, low_pass)
low_back.defvjp(back_keep, back_low)

def matmul(left, right):
    return jnp.dot(left, right, precision=HIGH, preferred_element_type=jnp.float32)

def rms_norm(values, gain):
    return values * lax.rsqrt(lax.optimization_barrier(jnp.mean(values * values, -1, keepdims=True)) + 1e-05) * gain

def unit_norm(vectors):
    return vectors * lax.rsqrt(lax.optimization_barrier(jnp.sum(vectors * vectors, -1, keepdims=True)) + 1e-06)

def delta_rule(queries, probes, writes, decays, strengths):
    head_count, length, head_size = queries.shape

    def block(memory, pieces):

        def advance(inner_state, item_tuple):
            asking, probing, writing, fading, weighting = item_tuple
            inner_state = jnp.exp(fading)[:, None, None] * inner_state
            recalled = jnp.einsum('hde,hd->he', inner_state, probing, precision=HIGH)
            inner_state = inner_state + weighting[:, None, None] * probing[:, :, None] * (writing - recalled)[:, None, :]
            return (inner_state, jnp.einsum('hde,hd->he', inner_state, asking, precision=HIGH))
        return lax.scan(advance, memory, pieces)

    def arrange(tensor):
        moved_axes = jnp.moveaxis(tensor, 1, 0)
        return moved_axes.reshape((length // SPAN, SPAN) + moved_axes.shape[1:])
    pieces = (arrange(queries), arrange(probes), arrange(writes), arrange(decays), arrange(strengths))
    initial = jnp.zeros((head_count, head_size, head_size), jnp.float32)
    _, outputs = lax.scan(jax.checkpoint(block), initial, pieces)
    return jnp.moveaxis(outputs.reshape(length, head_count, head_size), 0, 1)

def layer(weight_set, tokens, valid_rows):
    first_gain, input_weight, decay_weight, conv_weight, decay_log, decay_bias, head_gain, output_weight, second_gain, gate_up_weight, down_weight = weight_set
    length = tokens.shape[0]
    head_count = decay_log.shape[0]
    key_width = output_weight.shape[0]
    head_size = key_width // head_count
    normed = low(rms_norm(tokens, first_gain))
    projected = low_back(matmul(normed, input_weight))
    mixed = low(projected[:, :3 * key_width])
    gate_raw = projected[:, 3 * key_width:]
    logits = matmul(normed, decay_weight)
    tap_count = conv_weight.shape[0]
    padded = jnp.pad(mixed, ((tap_count - 1, 0), (0, 0)))
    convolved = conv_weight[0] * padded[0:length]
    for tap_index in range(1, tap_count):
        convolved = convolved + conv_weight[tap_index] * padded[tap_index:tap_index + length]
    active = jax.nn.silu(convolved)

    def split_heads(portion):
        return jnp.transpose(portion.reshape(length, head_count, head_size), (1, 0, 2))
    queries = unit_norm(split_heads(active[:, :key_width])) * head_size ** (-0.5)
    probes = unit_norm(split_heads(active[:, key_width:2 * key_width]))
    writes = split_heads(active[:, 2 * key_width:])
    decays = jnp.transpose(-jnp.exp(decay_log) * jax.nn.softplus(logits[:, :head_count] + decay_bias))
    strengths = jnp.transpose(jax.nn.sigmoid(logits[:, head_count:]))
    mixer_out = delta_rule(queries, probes, writes, decays, strengths)
    normal_out = rms_norm(mixer_out, head_gain)
    gated_rows = low(jnp.transpose(normal_out, (1, 0, 2)).reshape(length, key_width) * jax.nn.silu(gate_raw))
    hidden = tokens + low_back(matmul(gated_rows, output_weight))
    second = low(rms_norm(hidden, second_gain))
    gate_up = low_back(matmul(second, gate_up_weight))
    ffn_width = gate_up.shape[1] // 2
    activated = low(jax.nn.silu(gate_up[:, :ffn_width]) * gate_up[:, ffn_width:])
    final_rows = hidden + low_back(matmul(activated, down_weight))
    return valid_rows[:, None] * final_rows

def reference(inputs, lengths, first_gain, input_weight, decay_weight, conv_weight, decay_log, decay_bias, head_gain, output_weight, second_gain, gate_up_weight, down_weight, cotangent):
    micro_count, seq_local, length, model_width = inputs.shape
    seq_total = micro_count * seq_local
    weight_set = (first_gain.astype(jnp.float32), input_weight.astype(jnp.float32), decay_weight.astype(jnp.float32), conv_weight.astype(jnp.float32), decay_log.astype(jnp.float32), decay_bias.astype(jnp.float32), head_gain.astype(jnp.float32), output_weight.astype(jnp.float32), second_gain.astype(jnp.float32), gate_up_weight.astype(jnp.float32), down_weight.astype(jnp.float32))
    tokens_all = inputs.reshape(seq_total, length, model_width).astype(jnp.float32)
    upstream_all = cotangent.reshape(seq_total, length, model_width).astype(jnp.float32)
    limits = lengths.reshape(seq_total).astype(jnp.int32)
    positions = jnp.arange(length, dtype=jnp.int32)

    def step(totals, item_tuple):
        token_rows, upstream, limit_len = item_tuple
        valid_rows = (positions < limit_len).astype(jnp.float32)
        finals, pullback = jax.vjp(lambda weights_now, rows_now: layer(weights_now, rows_now, valid_rows), weight_set, token_rows)
        weight_grads, token_grads = pullback(upstream)
        totals = jax.tree.map(jnp.add, totals, weight_grads)
        return (totals, (finals, token_grads))
    zero_grads = jax.tree.map(jnp.zeros_like, weight_set)
    totals, (finals, token_grads) = lax.scan(step, zero_grads, (tokens_all, upstream_all, limits))
    first_gain_grad, input_weight_grad, decay_weight_grad, conv_weight_grad, decay_log_grad, decay_bias_grad, head_gain_grad, output_weight_grad, second_gain_grad, gate_up_grad, down_grad = totals
    return (finals.reshape(inputs.shape), token_grads.reshape(inputs.shape), first_gain_grad, input_weight_grad, decay_weight_grad, conv_weight_grad, decay_log_grad, decay_bias_grad, head_gain_grad, output_weight_grad, second_gain_grad, gate_up_grad, down_grad)
```

```python
import functools

import jax
import jax.numpy as jnp
from jax import lax
from jax.experimental import pallas as pl
from jax.experimental.pallas import tpu as pltpu
from jax.sharding import PartitionSpec as P

SPAN = 64
VMEM_LIMIT = 48 * 1024 * 1024


HIGH = lax.Precision.HIGHEST


def shifted(value, axis, steps):
    count = lax.axis_size(axis)
    initial, last = (max(0, -steps), min(count, count - steps))
    return lax.ppermute(value, axis, [(source, source + steps) for source in range(initial, last)])


def rms_norm(values, gain):
    return values * lax.rsqrt(jnp.mean(values * values, -1, keepdims=True) + 1e-05) * gain


def unit_norm(vectors):
    return vectors * lax.rsqrt(jnp.sum(vectors * vectors, -1, keepdims=True) + 1e-06)


def swish_product(gate_part, up_part):
    return jax.nn.silu(gate_part) * up_part


def unit_inverse(strict_lower):
    extent = strict_lower.shape[-1]
    identity_matrix = jnp.eye(extent, dtype=jnp.float32)
    inverse = identity_matrix - strict_lower
    power_term = strict_lower
    for level_index in range(1, (extent - 1).bit_length()):
        power_term = jnp.einsum("bhij,bhjk->bhik", power_term, power_term, precision=HIGH)
        inverse = jnp.einsum(
            "bhij,bhjk->bhik", inverse, identity_matrix + power_term, precision=HIGH
        )
    return inverse


def span_step(memory, pieces):
    queries, probes, writes, decays, strengths = pieces
    extent = decays.shape[-1]
    running = jnp.cumsum(decays, axis=-1)
    spread = running[..., :, None] - running[..., None, :]
    row_index = lax.broadcasted_iota(jnp.int32, (extent, extent), 0)
    col_index = lax.broadcasted_iota(jnp.int32, (extent, extent), 1)
    faded = jnp.exp(jnp.minimum(spread, 0.0))
    inclusive = jnp.where(col_index <= row_index, faded, 0.0) * strengths[..., None, :]
    strict_mask = jnp.where(col_index < row_index, faded, 0.0) * strengths[..., None, :]
    strict_lower = strict_mask * jnp.einsum("bhtd,bhsd->bhts", probes, probes, precision=HIGH)
    scale_in = jnp.exp(running)[..., None]
    target = writes - scale_in * jnp.einsum("bhtd,bhde->bhte", probes, memory, precision=HIGH)
    fresh_values = jnp.einsum("bhts,bhse->bhte", unit_inverse(strict_lower), target, precision=HIGH)
    mixing = inclusive * jnp.einsum("bhtd,bhsd->bhts", queries, probes, precision=HIGH)
    outputs = scale_in * jnp.einsum("bhtd,bhde->bhte", queries, memory, precision=HIGH)
    outputs = outputs + jnp.einsum("bhts,bhse->bhte", mixing, fresh_values, precision=HIGH)
    remaining = jnp.exp(running[..., -1:] - running) * strengths
    memory = jnp.exp(running[..., -1])[..., None, None] * memory + jnp.einsum(
        "bhsd,bhse->bhde", probes * remaining[..., None], fresh_values, precision=HIGH
    )
    return (memory, outputs)


def delta_local(queries, probes, writes, decays, strengths, memory):
    seq_count, head_count, length, head_size = queries.shape
    blocks = length // SPAN

    def arrange(tensor):
        shaped = tensor.reshape(tensor.shape[:2] + (blocks, SPAN) + tensor.shape[3:])
        return jnp.moveaxis(shaped, 2, 0)

    pieces = (
        arrange(queries),
        arrange(probes),
        arrange(writes),
        arrange(decays),
        arrange(strengths),
    )
    memory, outputs = lax.scan(span_step, memory, pieces)
    outputs = jnp.moveaxis(outputs, 0, 2)
    return (outputs.reshape(seq_count, head_count, length, outputs.shape[-1]), memory)


def prepare(packed, logits, conv_weight, decay_log, decay_bias):
    seq_count, length, logit_width = logits.shape
    head_count = decay_log.shape[0]
    tap_count = conv_weight.shape[0]
    convolved = conv_weight[0] * packed[:, 0:length]
    for tap_index in range(1, tap_count):
        convolved = convolved + conv_weight[tap_index] * packed[:, tap_index : tap_index + length]
    active = jax.nn.silu(convolved)
    key_width = active.shape[-1] // 3
    head_size = key_width // head_count

    def split_heads(portion):
        return jnp.transpose(
            portion.reshape(seq_count, length, head_count, head_size), (0, 2, 1, 3)
        )

    queries = unit_norm(split_heads(active[..., :key_width])) * head_size ** (-0.5)
    probes = unit_norm(split_heads(active[..., key_width : 2 * key_width]))
    writes = split_heads(active[..., 2 * key_width :])
    decays = jnp.transpose(
        -jnp.exp(decay_log) * jax.nn.softplus(logits[..., :head_count] + decay_bias), (0, 2, 1)
    )
    strengths = jnp.transpose(jax.nn.sigmoid(logits[..., head_count:]), (0, 2, 1))
    return (queries, probes, writes, decays, strengths)


def mixer_core(packed, logits, conv_weight, decay_log, decay_bias, memory):
    queries, probes, writes, decays, strengths = prepare(
        packed, logits, conv_weight, decay_log, decay_bias
    )
    return delta_local(queries, probes, writes, decays, strengths, memory)


def finish(mixer_out, gate_raw, head_gain):
    seq_count, head_count, length, head_size = mixer_out.shape
    normal_out = rms_norm(mixer_out, head_gain)
    flat_rows = jnp.transpose(normal_out, (0, 2, 1, 3)).reshape(
        seq_count, length, head_count * head_size
    )
    return flat_rows * jax.nn.silu(gate_raw)


def carry_forward(transfer, offset):

    def turn_step(step_index, incoming):
        leaving = jnp.einsum("bhij,bhjk->bhik", transfer, incoming, precision=HIGH) + offset
        return shifted(leaving.astype(jnp.bfloat16), "seq", 1).astype(leaving.dtype)

    return lax.fori_loop(0, lax.axis_size("seq") - 1, turn_step, jnp.zeros_like(offset))


def carry_back(transfer, source):
    flipped = jnp.swapaxes(transfer, 2, 3)

    def turn_step(step_index, incoming):
        leaving = jnp.einsum("bhij,bhjk->bhik", flipped, incoming, precision=HIGH) + source
        return shifted(leaving.astype(jnp.bfloat16), "seq", -1).astype(leaving.dtype)

    return lax.fori_loop(0, lax.axis_size("seq") - 1, turn_step, jnp.zeros_like(source))


def per_device(
    inputs,
    lengths,
    first_gain,
    input_weight,
    decay_weight,
    conv_weight,
    decay_log,
    decay_bias,
    head_gain,
    output_weight,
    second_gain,
    gate_up_weight,
    down_weight,
    cotangent,
):
    micro_count, seq_local, length, model_width = inputs.shape
    seq_count = micro_count * seq_local
    row_count = seq_count * length
    head_count = decay_log.shape[0]
    key_width = input_weight.shape[1] // 4
    head_size = key_width // head_count
    tap_count = conv_weight.shape[0]
    tokens = inputs.reshape(row_count, model_width).astype(jnp.float32)
    positions = lax.axis_index("seq") * length + lax.broadcasted_iota(
        jnp.int32, (micro_count, seq_local, length), 2
    )
    valid_rows = (positions < lengths[:, :, None]).astype(jnp.float32).reshape(row_count, 1)
    in_full, out_full, gate_up_full, down_full = (
        lax.all_gather(input_weight, ("dp", "seq"), axis=0, tiled=True),
        lax.all_gather(output_weight, ("dp", "seq"), axis=0, tiled=True),
        lax.all_gather(gate_up_weight, ("dp", "seq"), axis=0, tiled=True),
        lax.all_gather(down_weight, ("dp", "seq"), axis=0, tiled=True),
    )
    normed, first_pullback = jax.vjp(rms_norm, tokens, first_gain)
    normed_low = normed.astype(jnp.bfloat16)
    projected = jnp.dot(normed_low, in_full, preferred_element_type=jnp.float32)
    mixed_low = (
        projected[:, : 3 * key_width].astype(jnp.bfloat16).reshape(seq_count, length, 3 * key_width)
    )
    gate_raw = projected[:, 3 * key_width :].reshape(seq_count, length, key_width)
    logits = jnp.dot(normed_low, decay_weight, preferred_element_type=jnp.float32).reshape(
        seq_count, length, 2 * head_count
    )
    left_edge = shifted(mixed_low[:, length - tap_count + 1 :], "seq", 1)
    packed = jnp.concatenate([left_edge, mixed_low], 1).astype(jnp.float32)
    queries, probes, writes, decays, strengths = prepare(
        packed, logits, conv_weight, decay_log, decay_bias
    )
    blank_state = jnp.zeros((seq_count, head_count, head_size, head_size), jnp.float32)
    identity_maps = jnp.broadcast_to(jnp.eye(head_size, dtype=jnp.float32), blank_state.shape)
    joined_writes = jnp.concatenate([writes, jnp.zeros_like(writes)], -1)
    joined_outputs, joined_end = delta_local(
        queries,
        probes,
        joined_writes,
        decays,
        strengths,
        jnp.concatenate([blank_state, identity_maps], -1),
    )
    own_out = joined_outputs[..., :head_size]
    carry_out = joined_outputs[..., head_size:]
    offset = joined_end[..., :head_size]
    transfer = joined_end[..., head_size:]
    state_in = carry_forward(transfer, offset)
    mixer_out = own_out + jnp.einsum("bhtd,bhde->bhte", carry_out, state_in, precision=HIGH)
    gated_rows, finish_pullback = jax.vjp(finish, mixer_out, gate_raw, head_gain)
    gated_low = gated_rows.reshape(row_count, key_width).astype(jnp.bfloat16)
    hidden = tokens + jnp.dot(gated_low, out_full, preferred_element_type=jnp.float32)
    second, second_pullback = jax.vjp(rms_norm, hidden, second_gain)
    second_low = second.astype(jnp.bfloat16)
    gate_up = jnp.dot(second_low, gate_up_full, preferred_element_type=jnp.float32)
    ffn_width = gate_up.shape[1] // 2
    activated, swish_pullback = jax.vjp(
        swish_product, gate_up[:, :ffn_width], gate_up[:, ffn_width:]
    )
    activated_low = activated.astype(jnp.bfloat16)
    final_rows = hidden + jnp.dot(activated_low, down_full, preferred_element_type=jnp.float32)
    result = valid_rows * final_rows
    upstream = valid_rows * cotangent.reshape(row_count, model_width).astype(jnp.float32)
    out_err = upstream.astype(jnp.bfloat16)
    down_term = jnp.einsum("nf,nd->fd", activated_low, out_err, preferred_element_type=jnp.float32)
    activated_grad = jnp.einsum("nd,fd->nf", out_err, down_full, preferred_element_type=jnp.float32)
    gate_grad, up_grad = swish_pullback(activated_grad)
    gate_up_err = jnp.concatenate([gate_grad, up_grad], 1).astype(jnp.bfloat16)
    gate_up_term = jnp.einsum(
        "nd,nf->df", second_low, gate_up_err, preferred_element_type=jnp.float32
    )
    second_grad = jnp.einsum(
        "nf,df->nd", gate_up_err, gate_up_full, preferred_element_type=jnp.float32
    )
    hidden_part, second_gain_grad = second_pullback(second_grad)
    hidden_grad = upstream + hidden_part
    gate_up_share, down_share = (
        scatter_rows(gate_up_term.astype(BF16), ("dp", "seq")).astype(F32),
        scatter_rows(down_term.astype(BF16), ("dp", "seq")).astype(F32),
    )
    branch_err = hidden_grad.astype(jnp.bfloat16)
    output_term = jnp.einsum("nk,nd->kd", gated_low, branch_err, preferred_element_type=jnp.float32)
    gated_grad = jnp.einsum("nd,kd->nk", branch_err, out_full, preferred_element_type=jnp.float32)
    mixer_grad, gate_raw_grad, head_gain_grad = finish_pullback(
        gated_grad.reshape(seq_count, length, key_width)
    )
    source = jnp.einsum("bhtd,bhte->bhde", carry_out, mixer_grad, precision=HIGH)
    state_out_grad = carry_back(transfer, source)
    _, core_pullback = jax.vjp(
        mixer_core, packed, logits, conv_weight, decay_log, decay_bias, state_in
    )
    packed_grad, logits_grad, conv_grad, decay_log_grad, decay_bias_grad, _ = core_pullback(
        (mixer_grad, state_out_grad)
    )
    edge_grad = shifted(packed_grad[:, : tap_count - 1].astype(jnp.bfloat16), "seq", -1).astype(
        jnp.float32
    )
    mixed_grad = packed_grad[:, tap_count - 1 :] + jnp.pad(
        edge_grad, ((0, 0), (length - tap_count + 1, 0), (0, 0))
    )
    in_err = jnp.concatenate(
        [mixed_grad.reshape(row_count, 3 * key_width), gate_raw_grad.reshape(row_count, key_width)],
        1,
    ).astype(jnp.bfloat16)
    input_term = jnp.einsum("nd,nk->dk", normed_low, in_err, preferred_element_type=jnp.float32)
    logits_flat = logits_grad.reshape(row_count, 2 * head_count)
    decay_weight_grad = jnp.einsum(
        "nd,nk->dk", normed_low.astype(jnp.float32), logits_flat, precision=HIGH
    )
    normed_grad = jnp.einsum("nk,dk->nd", in_err, in_full, preferred_element_type=jnp.float32)
    normed_grad = normed_grad + jnp.einsum(
        "nk,dk->nd", logits_flat, decay_weight.astype(jnp.float32), precision=HIGH
    )
    token_part, first_gain_grad = first_pullback(normed_grad)
    inputs_grad = hidden_grad + token_part
    input_share, output_share = (
        scatter_rows(input_term.astype(BF16), ("dp", "seq")).astype(F32),
        scatter_rows(output_term.astype(BF16), ("dp", "seq")).astype(F32),
    )
    small_sums = lax.psum(
        (
            first_gain_grad,
            decay_weight_grad,
            conv_grad,
            decay_log_grad,
            decay_bias_grad,
            head_gain_grad,
            second_gain_grad,
        ),
        ("dp", "seq"),
    )
    return (
        result.reshape(inputs.shape),
        inputs_grad.reshape(inputs.shape),
        small_sums[0],
        input_share,
        small_sums[1],
        small_sums[2],
        small_sums[3],
        small_sums[4],
        small_sums[5],
        output_share,
        small_sums[6],
        gate_up_share,
        down_share,
    )


F32 = jnp.float32
BF16 = jnp.bfloat16


def parts(value):
    top = value.astype(BF16)
    return (top, (value - top.astype(F32)).astype(BF16))


def contract(left, right, right_dim):
    lhs = jnp.concatenate([left[0], left[1], left[0]], 1)
    rhs = jnp.concatenate([right[0], right[0], right[1]], right_dim)
    return lax.dot_general(lhs, rhs, (((1,), (right_dim,)), ((), ())), preferred_element_type=F32)


def mm(left, right):
    return contract(left, right, 0)


def mm_nt(left, right):
    return contract(left, right, 1)


def ones_dot(ones, value):
    first = value.astype(BF16)
    rest = value - first.astype(F32)
    second = rest.astype(BF16)
    third = (rest - second.astype(F32)).astype(BF16)
    return (
        jnp.dot(ones, first, preferred_element_type=F32)
        + jnp.dot(ones, second, preferred_element_type=F32)
        + jnp.dot(ones, third, preferred_element_type=F32)
    )


def lower_inverse(strict_lower, row_index, col_index):
    extent = strict_lower.shape[0]

    def below(width):
        same = (row_index // (2 * width)) == (col_index // (2 * width))
        return same & ((row_index // width) % 2 == 1) & ((col_index // width) % 2 == 0)

    inverse = jnp.where(row_index == col_index, 1.0, 0.0) - jnp.where(below(1), strict_lower, 0.0)
    width = 2
    while width < extent:
        block = jnp.where(below(width), strict_lower, 0.0)
        split = parts(inverse)
        inverse = inverse - mm(parts(mm(split, parts(block))), split)
        width *= 2
    return inverse


def active_rows(before, rows, taps):
    extended = jnp.concatenate([before, rows], 0)
    count = rows.shape[0]
    tap_count = taps.shape[0]
    start = before.shape[0] - tap_count + 1
    shifts = [extended[start + j : start + j + count] for j in range(tap_count)]
    total = taps[0:1] * shifts[0]
    for j in range(1, tap_count):
        total = total + taps[j : j + 1] * shifts[j]
    return (total, shifts)


def soft_plus(value):
    return jnp.maximum(value, 0.0) + jnp.log(1.0 + jnp.exp(-jnp.abs(value)))


def sigmoid(value):
    return 1.0 / (1.0 + jnp.exp(-value))


def unit(vectors):
    scale = lax.rsqrt(jnp.sum(vectors * vectors, -1, keepdims=True) + 1e-06)
    return (vectors * scale, scale)


def unit_back(vectors, scale, grad):
    inner = jnp.sum(vectors * grad, -1, keepdims=True)
    return scale * grad - vectors * (scale * scale * scale * inner)


def decay_terms(logit, param_ref, heads, ones):
    shifted_logit = logit + param_ref[1:2, :]
    lane = lax.broadcasted_iota(jnp.int32, logit.shape, 1)
    decays = jnp.where(lane < heads, -jnp.exp(param_ref[0:1, :]) * soft_plus(shifted_logit), 0.0)
    strengths = sigmoid(logit)
    running = ones_dot(ones, decays)
    return (shifted_logit, decays, strengths, running)


def mixer_forward(
    mixed_ref,
    gate_ref,
    logit_ref,
    taps_ref,
    param_ref,
    gain_ref,
    gated_ref,
    memory_ref,
    inverse_ref,
    fresh_ref,
    out_ref,
    state_ref,
    halo_ref,
):
    seqs, span, _ = mixed_ref.shape
    heads, head_size = memory_ref.shape[1], memory_ref.shape[2]

    @pl.when(pl.program_id(0) == 0)
    def _():
        state_ref[...] = jnp.zeros_like(state_ref)
        halo_ref[...] = jnp.zeros_like(halo_ref)

    row_index = lax.broadcasted_iota(jnp.int32, (span, span), 0)
    col_index = lax.broadcasted_iota(jnp.int32, (span, span), 1)
    ones = jnp.where(col_index <= row_index, 1.0, 0.0).astype(BF16)
    taps = taps_ref[...]
    width = heads * head_size
    for m in range(seqs):
        rows = mixed_ref[m].astype(F32)
        convolved, _ = active_rows(halo_ref[m], rows, taps)
        halo_ref[m] = rows[span - 8 :]
        active = convolved * sigmoid(convolved)
        _, decays, strengths, running = decay_terms(logit_ref[m], param_ref, heads, ones)
        running_rows = jnp.transpose(running)
        strength_rows = jnp.transpose(strengths)
        for h in range(heads):
            own = slice(h * head_size, (h + 1) * head_size)
            queries = unit(active[:, own])[0] * head_size ** (-0.5)
            probes = unit(active[:, width + h * head_size : width + (h + 1) * head_size])[0]
            writes = active[:, 2 * width + h * head_size : 2 * width + (h + 1) * head_size]
            run = running[:, h : h + 1]
            last = running[span - 1 : span, h : h + 1]
            weight_row = strength_rows[heads + h : heads + h + 1, :]
            weight_col = strengths[:, heads + h : heads + h + 1]
            faded = jnp.exp(jnp.minimum(run - running_rows[h : h + 1, :], 0.0)) * weight_row
            probe_parts = parts(probes)
            query_parts = parts(queries)
            strict = jnp.where(col_index < row_index, faded * mm_nt(probe_parts, probe_parts), 0.0)
            mixing = jnp.where(col_index <= row_index, faded * mm_nt(query_parts, probe_parts), 0.0)
            inverse = lower_inverse(strict, row_index, col_index)
            scale_in = jnp.exp(run)
            both = mm(
                parts(inverse), parts(jnp.concatenate([writes, scale_in * probes], 1))
            )
            memory = state_ref[m, h]
            memory_parts = parts(memory)
            reads = mm(
                parts(jnp.concatenate([both[:, head_size:], scale_in * queries], 0)), memory_parts
            )
            fresh = both[:, :head_size] - reads[:span]
            fresh_parts = parts(fresh)
            mixer_out = reads[span:] + mm(parts(mixing), fresh_parts)
            kept = jnp.transpose(jnp.exp(last - run) * weight_col * probes)
            state_ref[m, h] = jnp.exp(last) * memory + mm(parts(kept), fresh_parts)
            memory_ref[m, h] = memory
            inverse_ref[m, h] = inverse
            fresh_ref[m, :, own] = fresh
            out_ref[m, :, own] = mixer_out
            scale = lax.rsqrt(jnp.mean(mixer_out * mixer_out, -1, keepdims=True) + 1e-05)
            gate = gate_ref[m, :, own]
            gated_ref[m, :, own] = (
                mixer_out * scale * gain_ref[...] * (gate * sigmoid(gate))
            ).astype(BF16)


def mixer_backward(
    mixed_ref,
    before_ref,
    gate_ref,
    logit_ref,
    taps_ref,
    param_ref,
    gain_ref,
    memory_ref,
    inverse_ref,
    fresh_ref,
    out_ref,
    grad_ref,
    error_ref,
    logit_grad_ref,
    taps_grad_ref,
    param_grad_ref,
    gain_grad_ref,
    state_ref,
    halo_ref,
):
    seqs, span, _ = mixed_ref.shape
    heads, head_size = memory_ref.shape[1], memory_ref.shape[2]
    step = pl.program_id(0)

    @pl.when(step == 0)
    def _():
        state_ref[...] = jnp.zeros_like(state_ref)
        halo_ref[...] = jnp.zeros_like(halo_ref)
        taps_grad_ref[...] = jnp.zeros_like(taps_grad_ref)
        param_grad_ref[...] = jnp.zeros_like(param_grad_ref)
        gain_grad_ref[...] = jnp.zeros_like(gain_grad_ref)

    first = step == pl.num_programs(0) - 1
    row_index = lax.broadcasted_iota(jnp.int32, (span, span), 0)
    col_index = lax.broadcasted_iota(jnp.int32, (span, span), 1)
    ones = jnp.where(col_index <= row_index, 1.0, 0.0).astype(BF16)
    ones_back = jnp.where(col_index >= row_index, 1.0, 0.0).astype(BF16)
    taps = taps_ref[...]
    tap_count = taps.shape[0]
    width = heads * head_size
    gain = gain_ref[...]
    edge = before_ref.shape[1]
    for m in range(seqs):
        rows = mixed_ref[m].astype(F32)
        before = jnp.where(first, 0.0, before_ref[m].astype(F32))[edge - 8 :]
        convolved, shifts = active_rows(before, rows, taps)
        opening = sigmoid(convolved)
        active = convolved * opening
        logit = logit_ref[m]
        shifted_logit, decays, strengths, running = decay_terms(logit, param_ref, heads, ones)
        running_rows = jnp.transpose(running)
        strength_rows = jnp.transpose(strengths)
        active_grads = [None] * (3 * heads)
        gate_grads = [None] * heads
        col_terms = jnp.zeros((span, span), F32)
        row_terms = jnp.zeros((span, span), F32)
        for h in range(heads):
            own = slice(h * head_size, (h + 1) * head_size)
            raw_queries = active[:, own]
            raw_probes = active[:, width + h * head_size : width + (h + 1) * head_size]
            queries, query_scale = unit(raw_queries)
            queries = queries * head_size ** (-0.5)
            probes, probe_scale = unit(raw_probes)
            mixer_out = out_ref[m, :, own]
            gate = gate_ref[m, :, own]
            gated_grad = grad_ref[m, :, own].astype(F32)
            scale = lax.rsqrt(jnp.mean(mixer_out * mixer_out, -1, keepdims=True) + 1e-05)
            gate_open = sigmoid(gate)
            normal = mixer_out * scale
            gate_grads[h] = gated_grad * normal * gain * (gate_open * (1.0 + gate * (1.0 - gate_open)))
            normal_grad = gated_grad * (gate * gate_open)
            gain_grad_ref[0:1, :] += jnp.sum(normal_grad * normal, 0, keepdims=True)
            weighted = normal_grad * gain
            out_grad = scale * (
                weighted - normal * jnp.mean(weighted * normal, -1, keepdims=True)
            )

            run = running[:, h : h + 1]
            last = running[span - 1 : span, h : h + 1]
            weight_row = strength_rows[heads + h : heads + h + 1, :]
            weight_col = strengths[:, heads + h : heads + h + 1]
            faded = jnp.exp(jnp.minimum(run - running_rows[h : h + 1, :], 0.0))
            scale_in = jnp.exp(run)
            end_scale = jnp.exp(last)
            remaining = jnp.exp(last - run)
            kept = remaining * weight_col

            memory = memory_ref[m, h]
            fresh = fresh_ref[m, :, own]
            state_grad = state_ref[m, h]
            probe_parts = parts(probes)
            query_parts = parts(queries)
            fresh_parts = parts(fresh)
            memory_parts = parts(memory)
            state_grad_parts = parts(state_grad)
            products = mm_nt(parts(jnp.concatenate([queries, probes], 0)), probe_parts)
            fade_query = jnp.where(col_index <= row_index, faded * products[:span], 0.0)
            fade_probe = jnp.where(col_index < row_index, faded * products[span:], 0.0)
            out_grad_parts = parts(out_grad)
            probe_state = mm(probe_parts, state_grad_parts)
            fresh_grad = (
                mm(parts(jnp.transpose(fade_query * weight_row)), out_grad_parts)
                + kept * probe_state
            )
            solved = mm(parts(jnp.transpose(inverse_ref[m, h])), parts(fresh_grad))
            turned_queries = parts(jnp.transpose(queries))
            turned_probes = parts(jnp.transpose(probes))
            state_ref[m, h] = (
                end_scale * state_grad
                + mm(turned_queries, parts(scale_in * out_grad))
                - mm(turned_probes, parts(scale_in * solved))
            )
            joined = parts(jnp.concatenate([out_grad, solved], 0))
            outer = mm_nt(joined, fresh_parts)
            mixing_grad = jnp.where(col_index <= row_index, outer[:span], 0.0)
            strict_grad = jnp.where(col_index < row_index, -outer[span:], 0.0)
            through = mm_nt(joined, memory_parts)
            out_state = scale_in * through[:span]
            solved_state = scale_in * through[span:]
            spread = faded * weight_row
            mix_fade = mixing_grad * spread
            strict_fade = strict_grad * spread
            on_probes = mm(parts(jnp.concatenate([mix_fade, strict_fade], 0)), probe_parts)
            query_grad = out_state + on_probes[:span]
            probe_grad = (
                kept * mm_nt(fresh_parts, state_grad_parts)
                - solved_state
                + on_probes[span:]
                + mm(parts(jnp.transpose(mix_fade)), query_parts)
                + mm(parts(jnp.transpose(strict_fade)), probe_parts)
            )
            pairs = mixing_grad * fade_query + strict_grad * fade_probe
            weighted_pairs = pairs * weight_row
            probe_fresh = jnp.sum(probe_state * fresh, -1, keepdims=True)
            run_col = (
                jnp.sum(out_state * queries - solved_state * probes, -1, keepdims=True)
                + jnp.sum(weighted_pairs, -1, keepdims=True)
                - kept * probe_fresh
            )
            last_grad = jnp.sum(kept * probe_fresh, 0, keepdims=True) + end_scale * jnp.sum(
                jnp.sum(state_grad * memory, -1, keepdims=True), 0, keepdims=True
            )
            run_col = run_col + jnp.where(row_index[:, 0:1] == span - 1, last_grad, 0.0)
            col_terms = jnp.where(col_index == h, run_col, col_terms)
            col_terms = jnp.where(col_index == heads + h, remaining * probe_fresh, col_terms)
            row_terms = jnp.where(
                row_index == h, -jnp.sum(weighted_pairs, 0, keepdims=True), row_terms
            )
            row_terms = jnp.where(
                row_index == heads + h, jnp.sum(pairs, 0, keepdims=True), row_terms
            )
            active_grads[h] = unit_back(raw_queries, query_scale, query_grad) * head_size ** (-0.5)
            active_grads[heads + h] = unit_back(raw_probes, probe_scale, probe_grad)
            active_grads[2 * heads + h] = solved

        terms = col_terms + jnp.transpose(row_terms)
        decay_grad = ones_dot(ones_back, terms)
        shifted_grad = decay_grad * -jnp.exp(param_ref[0:1, :]) * sigmoid(shifted_logit)
        logit_grad = jnp.where(
            col_index < heads,
            shifted_grad,
            jnp.where(col_index < 2 * heads, terms * strengths * (1.0 - strengths), 0.0),
        )
        logit_grad_ref[m] = logit_grad
        decay_lane = col_index[0:1] < heads
        param_grad_ref[0:1, :] += jnp.sum(
            jnp.where(decay_lane, decay_grad * decays, 0.0), 0, keepdims=True
        )
        param_grad_ref[1:2, :] += jnp.sum(
            jnp.where(decay_lane, shifted_grad, 0.0), 0, keepdims=True
        )
        conv_grad = jnp.concatenate(active_grads, 1) * (
            opening * (1.0 + convolved * (1.0 - opening))
        )
        extended = jnp.concatenate([conv_grad, halo_ref[m]], 0)
        halo_ref[m] = conv_grad[:8]
        mixed_grad = jnp.zeros_like(conv_grad)
        for j in range(tap_count):
            reach = tap_count - 1 - j
            mixed_grad = mixed_grad + taps[j : j + 1] * extended[reach : reach + span]
            taps_grad_ref[j : j + 1, :] += jnp.sum(conv_grad * shifts[j], 0, keepdims=True)
        error_ref[m] = jnp.concatenate([mixed_grad] + gate_grads, 1).astype(BF16)


def run_forward(mixed, gate, logits, taps, params, gain, heads):
    steps, seqs, span, _ = mixed.shape
    head_size = gain.shape[1]
    width = heads * head_size

    def rows(columns):
        return pl.BlockSpec((None, seqs, span, columns), lambda j: (j, 0, 0, 0))

    def squares():
        return pl.BlockSpec((None, seqs, heads, head_size, head_size), lambda j: (j, 0, 0, 0, 0))

    def whole(array):
        return pl.BlockSpec(array.shape, lambda j: (0, 0))

    square = jax.ShapeDtypeStruct((steps, seqs, heads, head_size, head_size), F32)
    lower = jax.ShapeDtypeStruct((steps, seqs, heads, span, span), F32)
    flat = jax.ShapeDtypeStruct((steps, seqs, span, width), F32)
    return pl.pallas_call(
        mixer_forward,
        grid=(steps,),
        in_specs=[
            rows(3 * width),
            rows(width),
            rows(logits.shape[-1]),
            whole(taps),
            whole(params),
            whole(gain),
        ],
        out_specs=[rows(width), squares(), squares(), rows(width), rows(width)],
        out_shape=[
            jax.ShapeDtypeStruct((steps, seqs, span, width), BF16),
            square,
            lower,
            flat,
            flat,
        ],
        scratch_shapes=[
            pltpu.VMEM((seqs, heads, head_size, head_size), F32),
            pltpu.VMEM((seqs, 8, 3 * width), F32),
        ],
        compiler_params=pltpu.CompilerParams(vmem_limit_bytes=VMEM_LIMIT),
        cost_estimate=pl.CostEstimate(
            flops=steps * seqs * heads * 120 * span**3,
            bytes_accessed=steps * seqs * span * width * 30,
            transcendentals=0,
        ),
        name="mixer_forward",
    )(mixed, gate, logits, taps, params, gain)


def run_backward(mixed, gate, logits, taps, params, gain, memory, inverse, fresh, out, grad):
    steps, seqs, span, _ = mixed.shape
    heads, head_size = memory.shape[2], memory.shape[3]
    width = heads * head_size
    edge = 16

    def rows(columns):
        return pl.BlockSpec((None, seqs, span, columns), lambda j: (steps - 1 - j, 0, 0, 0))

    def squares():
        return pl.BlockSpec(
            (None, seqs, heads, head_size, head_size), lambda j: (steps - 1 - j, 0, 0, 0, 0)
        )

    def whole(shape):
        return pl.BlockSpec(shape, lambda j: (0, 0))

    before = pl.BlockSpec(
        (None, seqs, edge, 3 * width),
        lambda j: (jnp.maximum(steps - 2 - j, 0), 0, span // edge - 1, 0),
    )
    return pl.pallas_call(
        mixer_backward,
        grid=(steps,),
        in_specs=[
            rows(3 * width),
            before,
            rows(width),
            rows(logits.shape[-1]),
            whole(taps.shape),
            whole(params.shape),
            whole(gain.shape),
            squares(),
            squares(),
            rows(width),
            rows(width),
            rows(width),
        ],
        out_specs=[
            rows(4 * width),
            rows(logits.shape[-1]),
            whole((8, 3 * width)),
            whole((8, logits.shape[-1])),
            whole((8, head_size)),
        ],
        out_shape=[
            jax.ShapeDtypeStruct((steps, seqs, span, 4 * width), BF16),
            jax.ShapeDtypeStruct(logits.shape, F32),
            jax.ShapeDtypeStruct((8, 3 * width), F32),
            jax.ShapeDtypeStruct((8, logits.shape[-1]), F32),
            jax.ShapeDtypeStruct((8, head_size), F32),
        ],
        scratch_shapes=[
            pltpu.VMEM((seqs, heads, head_size, head_size), F32),
            pltpu.VMEM((seqs, 8, 3 * width), F32),
        ],
        compiler_params=pltpu.CompilerParams(vmem_limit_bytes=VMEM_LIMIT),
        cost_estimate=pl.CostEstimate(
            flops=steps * seqs * heads * 120 * span**3,
            bytes_accessed=steps * seqs * span * width * 40,
            transcendentals=0,
        ),
        name="mixer_backward",
    )(mixed, mixed, gate, logits, taps, params, gain, memory, inverse, fresh, out, grad)


def gather_rows(value, axis):
    return lax.all_gather(value, axis, axis=0, tiled=True)


def scatter_rows(value, axis):
    return lax.psum_scatter(value, axis, scatter_dimension=0, tiled=True)


def plane_peers():
    me = lax.axis_index("seq")
    sibling = me + 1 - 2 * (me % 2)
    across = me + 2 - 4 * ((me // 2) % 2)
    along = me + 4 - 8 * (me // 4)
    return (me, sibling, across, along)


def greet(peers):
    barrier = pltpu.get_barrier_semaphore()
    for peer in peers:
        pl.semaphore_signal(
            barrier, inc=1, device_id={"seq": peer}, device_id_type=pl.DeviceIdType.MESH
        )
    pl.semaphore_wait(barrier, len(peers))


def send_to(peer, source, target, send_sem, recv_sem):
    return pltpu.make_async_remote_copy(
        src_ref=source,
        dst_ref=target,
        send_sem=send_sem,
        recv_sem=recv_sem,
        device_id={"seq": peer},
        device_id_type=pl.DeviceIdType.MESH,
    )


def gather_phases(own_ref, all_ref, send_sems, recv_sems, local_sem, start):
    me, sibling, across, along = plane_peers()
    far = along + across - me
    half = own_ref.shape[0] // 2
    upper, lower = pl.ds(0, half), pl.ds(half, half)
    copies = []

    def send(peer, source, target):
        k = start + len(copies)
        copy = send_to(peer, source, target, send_sems.at[k], recv_sems.at[k])
        copy.start()
        copies.append(copy)

    keep = pltpu.make_async_copy(own_ref, all_ref.at[me], local_sem)
    keep.start()
    send(across, own_ref, all_ref.at[me])
    send(along, own_ref, all_ref.at[me])
    send(sibling, own_ref, all_ref.at[me])
    yield
    copies[0].wait_recv()
    send(along, all_ref.at[across, upper], all_ref.at[across, upper])
    copies[1].wait_recv()
    send(across, all_ref.at[along, lower], all_ref.at[along, lower])
    send(sibling, all_ref.at[across], all_ref.at[across])
    send(sibling, all_ref.at[along], all_ref.at[along])
    yield
    copies[3].wait_recv()
    send(sibling, all_ref.at[far, upper], all_ref.at[far, upper])
    copies[4].wait_recv()
    send(sibling, all_ref.at[far, lower], all_ref.at[far, lower])
    yield
    for k in (2, 5, 6, 7, 8):
        copies[k].wait_recv()
    for copy in copies:
        copy.wait_send()
    keep.wait()
    yield


def plane_gather_kernel(own_ref, all_ref, send_sems, recv_sems, local_sem):
    greet(plane_peers()[1:])
    for _ in gather_phases(own_ref, all_ref, send_sems, recv_sems, local_sem, 0):
        pass


def chain_phases(all_ref, up_send, up_recv, down_send, down_recv):
    depth = all_ref.shape[0]
    place = lax.axis_index("dp")
    above, below = lax.rem(place + 1, depth), lax.rem(place + depth - 1, depth)

    def hop(slot, peer, send_sem, recv_sem):
        return pltpu.make_async_remote_copy(
            src_ref=all_ref.at[slot],
            dst_ref=all_ref.at[slot],
            send_sem=send_sem,
            recv_sem=recv_sem,
            device_id={"dp": peer},
            device_id_type=pl.DeviceIdType.MESH,
        )

    ups, downs = [], []
    for t in range(depth - 1):
        up = hop(lax.rem(place + depth - t, depth), above, up_send.at[t], up_recv.at[t])
        down = hop(lax.rem(place + t, depth), below, down_send.at[t], down_recv.at[t])
        ups.append(up)
        downs.append(down)
        pl.when((place < depth - 1) & (place >= t))(up.start)
        pl.when((place > 0) & (place + t < depth))(down.start)
        yield
        pl.when(place > t)(up.wait_recv)
        pl.when(place + t + 1 < depth)(down.wait_recv)
    for t in range(depth - 1):
        pl.when((place < depth - 1) & (place >= t))(ups[t].wait_send)
        pl.when((place > 0) & (place + t < depth))(downs[t].wait_send)
    yield


def exchange_copies(cut_ref, land, send_sems, recv_sems, start):
    ring = cut_ref.shape[0]
    me = lax.axis_index("seq")
    copies = []
    for k in range(1, ring):
        peer = lax.rem(me + k, ring)
        copy = send_to(
            peer, cut_ref.at[peer], land, send_sems.at[start + k - 1], recv_sems.at[start + k - 1]
        )
        copy.start()
        copies.append(copy)
    return copies


def plane_open_kernel(
    first_ref,
    second_ref,
    early_ref,
    later_ref,
    first_all_ref,
    second_all_ref,
    early_all_ref,
    later_all_ref,
    send_sems,
    recv_sems,
    local_sems,
    up_send,
    up_recv,
    down_send,
    down_recv,
):
    place, me = lax.axis_index("dp"), lax.axis_index("seq")
    depth, ring = early_all_ref.shape[0], early_ref.shape[0]
    rows = early_ref.shape[1]
    barrier = pltpu.get_barrier_semaphore()
    for k in range(1, ring):
        pl.semaphore_signal(
            barrier,
            inc=1,
            device_id={"seq": lax.rem(me + k, ring)},
            device_id_type=pl.DeviceIdType.MESH,
        )
    for k in range(1, depth):
        pl.semaphore_signal(
            barrier,
            inc=1,
            device_id={"dp": lax.rem(place + k, depth)},
            device_id_type=pl.DeviceIdType.MESH,
        )
    pl.semaphore_wait(barrier, ring + depth - 2)
    spot = early_all_ref.at[place, pl.ds(pl.multiple_of(me * rows, rows), rows)]
    keep_early = pltpu.make_async_copy(early_ref.at[me], spot, local_sems.at[0])
    keep_early.start()
    keep_later = pltpu.make_async_copy(later_ref.at[me], later_all_ref.at[me], local_sems.at[1])
    keep_later.start()
    early = exchange_copies(early_ref, spot, send_sems, recv_sems, 0)
    for copy in early:
        copy.wait_recv()
    keep_early.wait()
    chain = chain_phases(early_all_ref, up_send, up_recv, down_send, down_recv)
    first = gather_phases(first_ref, first_all_ref, send_sems, recv_sems, local_sems.at[2], ring)
    second = gather_phases(
        second_ref, second_all_ref, send_sems, recv_sems, local_sems.at[3], ring + 9
    )
    next(chain)
    next(first)
    next(first)
    next(second)
    later = exchange_copies(later_ref, later_all_ref.at[me], send_sems, recv_sems, ring + 18)
    next(chain)
    next(first)
    next(chain)
    next(second)
    next(first)
    next(second)
    for copy in later:
        copy.wait_recv()
    next(chain)
    next(second)
    for copy in early + later:
        copy.wait_send()
    keep_later.wait()


def plane_open(first, second, early, later, collective_id):
    ring, depth = lax.axis_size("seq"), lax.axis_size("dp")
    rows, columns = first.shape
    total = 2 * ring + 18
    return pl.pallas_call(
        plane_open_kernel,
        out_shape=[
            jax.ShapeDtypeStruct((ring, rows, columns), first.dtype),
            jax.ShapeDtypeStruct((ring, rows, columns), second.dtype),
            jax.ShapeDtypeStruct((depth, ring * early.shape[1], early.shape[2]), early.dtype),
            jax.ShapeDtypeStruct(later.shape, later.dtype),
        ],
        in_specs=[pl.BlockSpec(memory_space=pl.ANY)] * 4,
        out_specs=[pl.BlockSpec(memory_space=pl.ANY)] * 4,
        scratch_shapes=[
            pltpu.SemaphoreType.DMA((total,)),
            pltpu.SemaphoreType.DMA((total,)),
            pltpu.SemaphoreType.DMA((4,)),
        ]
        + [pltpu.SemaphoreType.DMA((depth - 1,))] * 4,
        compiler_params=pltpu.CompilerParams(collective_id=collective_id, has_side_effects=True),
        name="plane_open",
    )(first, second, early, later)


def plane_gather(own, collective_id):
    ring = lax.axis_size("seq")
    rows, columns = own.shape
    return pl.pallas_call(
        plane_gather_kernel,
        out_shape=jax.ShapeDtypeStruct((ring, rows, columns), own.dtype),
        in_specs=[pl.BlockSpec(memory_space=pl.ANY)],
        out_specs=pl.BlockSpec(memory_space=pl.ANY),
        scratch_shapes=[
            pltpu.SemaphoreType.DMA((9,)),
            pltpu.SemaphoreType.DMA((9,)),
            pltpu.SemaphoreType.DMA,
        ],
        compiler_params=pltpu.CompilerParams(collective_id=collective_id, has_side_effects=True),
        name="plane_gather",
    )(own)


def plane_scatter_kernel(
    part_ref,
    sum_ref,
    own_ref,
    near_ref,
    far_in_ref,
    side_in_ref,
    send_sems,
    recv_sems,
    load_sems,
):
    me, sibling, across, along = plane_peers()
    far = along + across - me
    flip = sibling - me
    rows = sum_ref.shape[0]
    half = rows // 2
    upper, lower = pl.ds(0, half), pl.ds(half, half)
    greet((sibling, across, along))
    slabs = (far, across, along, me)
    loads = []
    nears = []
    for k, slab in enumerate(slabs):
        load = pltpu.make_async_copy(part_ref.at[slab], own_ref.at[k], load_sems.at[k])
        load.start()
        loads.append(load)
        near = send_to(sibling, part_ref.at[slab + flip], near_ref.at[k], send_sems.at[k], recv_sems.at[k])
        near.start()
        nears.append(near)

    def send(k, peer, source, target):
        copy = send_to(peer, source, target, send_sems.at[k], recv_sems.at[k])
        copy.start()
        return copy

    step = 32

    def fold(target, other, start, count):
        @pl.loop(0, count // step)
        def _(i):
            at = pl.ds(pl.multiple_of(start + i * step, step), step)
            target[at] = (target[at].astype(F32) + other[at].astype(F32)).astype(BF16)

    def join(k):
        loads[k].wait()
        nears[k].wait_recv()

    join(0)
    fold(own_ref.at[0], near_ref.at[0], 0, rows)
    copies = [
        send(4, across, own_ref.at[0, upper], far_in_ref.at[upper]),
        send(5, along, own_ref.at[0, lower], far_in_ref.at[lower]),
    ]
    join(1)
    fold(own_ref.at[1], near_ref.at[1], 0, rows)
    copies.append(send(6, across, own_ref.at[1, upper], side_in_ref.at[0, upper]))
    join(2)
    fold(own_ref.at[2], near_ref.at[2], 0, rows)
    copies.append(send(7, along, own_ref.at[2, lower], side_in_ref.at[1, lower]))
    copies[0].wait_recv()
    fold(own_ref.at[2], far_in_ref, 0, half)
    copies.append(send(8, along, own_ref.at[2, upper], side_in_ref.at[1, upper]))
    copies[1].wait_recv()
    fold(own_ref.at[1], far_in_ref, half, half)
    copies.append(send(9, across, own_ref.at[1, lower], side_in_ref.at[0, lower]))
    join(3)
    for copy in copies[2:]:
        copy.wait_recv()

    @pl.loop(0, rows // step)
    def _(i):
        at = pl.ds(pl.multiple_of(i * step, step), step)
        sum_ref[at] = (
            own_ref[3, at].astype(F32)
            + near_ref[3, at].astype(F32)
            + side_in_ref[0, at].astype(F32)
            + side_in_ref[1, at].astype(F32)
        )

    for copy in nears + copies:
        copy.wait_send()


def plane_scatter(part, collective_id):
    ring, rows, columns = part.shape
    return pl.pallas_call(
        plane_scatter_kernel,
        out_shape=jax.ShapeDtypeStruct((rows, columns), F32),
        in_specs=[pl.BlockSpec(memory_space=pl.ANY)],
        out_specs=pl.BlockSpec(memory_space=pltpu.VMEM),
        scratch_shapes=[
            pltpu.VMEM((4, rows, columns), BF16),
            pltpu.VMEM((4, rows, columns), BF16),
            pltpu.VMEM((rows, columns), BF16),
            pltpu.VMEM((2, rows, columns), BF16),
            pltpu.SemaphoreType.DMA((10,)),
            pltpu.SemaphoreType.DMA((10,)),
            pltpu.SemaphoreType.DMA((4,)),
        ],
        compiler_params=pltpu.CompilerParams(
            collective_id=collective_id, has_side_effects=True, vmem_limit_bytes=VMEM_LIMIT
        ),
        name="plane_scatter",
    )(part)


def small_sum_kernel(own_ref, all_ref, stage_ref, total_ref, send_sems, recv_sems):
    depth, ring = stage_ref.shape[0], all_ref.shape[0]
    place, me = lax.axis_index("dp"), lax.axis_index("seq")
    barrier = pltpu.get_barrier_semaphore()
    mesh_ids = pl.DeviceIdType.MESH
    columns = [lax.rem(place + k, depth) for k in range(1, depth)]
    plane = [lax.rem(me + k, ring) for k in range(1, ring)]
    for peer in columns:
        pl.semaphore_signal(barrier, inc=1, device_id={"dp": peer}, device_id_type=mesh_ids)
    for peer in plane:
        pl.semaphore_signal(barrier, inc=1, device_id={"seq": peer}, device_id_type=mesh_ids)
    pl.semaphore_wait(barrier, depth + ring - 2)
    first = []
    for k, peer in enumerate(columns):
        copy = pltpu.make_async_remote_copy(
            src_ref=own_ref,
            dst_ref=stage_ref.at[place],
            send_sem=send_sems.at[k],
            recv_sem=recv_sems.at[k],
            device_id={"dp": peer},
            device_id_type=mesh_ids,
        )
        copy.start()
        first.append(copy)
    stage_ref[place] = own_ref[...]
    for copy in first:
        copy.wait_recv()
    total = stage_ref[0]
    for k in range(1, depth):
        total = total + stage_ref[k]
    total_ref[...] = total
    second = []
    for k, peer in enumerate(plane):
        copy = pltpu.make_async_remote_copy(
            src_ref=total_ref,
            dst_ref=all_ref.at[me],
            send_sem=send_sems.at[depth - 1 + k],
            recv_sem=recv_sems.at[depth - 1 + k],
            device_id={"seq": peer},
            device_id_type=mesh_ids,
        )
        copy.start()
        second.append(copy)
    all_ref[me] = total
    for copy in second:
        copy.wait_recv()
    for copy in first + second:
        copy.wait_send()


def small_sum(own, collective_id):
    depth, ring = lax.axis_size("dp"), lax.axis_size("seq")
    count = depth + ring - 2
    return pl.pallas_call(
        small_sum_kernel,
        out_shape=jax.ShapeDtypeStruct((ring,) + own.shape, F32),
        in_specs=[pl.BlockSpec(memory_space=pltpu.VMEM)],
        out_specs=pl.BlockSpec(memory_space=pltpu.VMEM),
        scratch_shapes=[
            pltpu.VMEM((depth,) + own.shape, F32),
            pltpu.VMEM(own.shape, F32),
            pltpu.SemaphoreType.DMA((count,)),
            pltpu.SemaphoreType.DMA((count,)),
        ],
        compiler_params=pltpu.CompilerParams(collective_id=collective_id, has_side_effects=True),
        name="small_sum",
    )(own)


def greet_plane(ring):
    me = lax.axis_index("seq")
    greet([lax.rem(me + k, ring) for k in range(1, ring)])


def plane_exchange_kernel(count, *refs):
    cuts, swaps = refs[:count], refs[count : 2 * count]
    send_sems, recv_sems, local_sems = refs[2 * count :]
    ring = cuts[0].shape[0]
    me = lax.axis_index("seq")
    greet_plane(ring)
    copies, keeps = [], []
    for k in range(count):
        keep = pltpu.make_async_copy(cuts[k].at[me], swaps[k].at[me], local_sems.at[k])
        keep.start()
        keeps.append(keep)
        copies += exchange_copies(cuts[k], swaps[k].at[me], send_sems, recv_sems, k * (ring - 1))
    for copy in copies:
        copy.wait_recv()
    for copy in copies:
        copy.wait_send()
    for keep in keeps:
        keep.wait()


def plane_exchange(cuts, collective_id):
    count = len(cuts)
    total = count * (cuts[0].shape[0] - 1)
    return pl.pallas_call(
        functools.partial(plane_exchange_kernel, count),
        out_shape=[jax.ShapeDtypeStruct(cut.shape, cut.dtype) for cut in cuts],
        in_specs=[pl.BlockSpec(memory_space=pl.ANY)] * count,
        out_specs=[pl.BlockSpec(memory_space=pl.ANY)] * count,
        scratch_shapes=[
            pltpu.SemaphoreType.DMA((total,)),
            pltpu.SemaphoreType.DMA((total,)),
            pltpu.SemaphoreType.DMA((count,)),
        ],
        compiler_params=pltpu.CompilerParams(collective_id=collective_id, has_side_effects=True),
        name="plane_exchange",
    )(*cuts)


def rms_back(values, gain, grad):
    scale = lax.rsqrt(jnp.mean(values * values, -1, keepdims=True) + 1e-05)
    weighted = grad * gain
    part = scale * weighted - values * (
        scale * scale * scale * jnp.mean(weighted * values, -1, keepdims=True)
    )
    return (part, jnp.sum(grad * values * scale, 0))


def low_dot(left, right, dims):
    return lax.dot_general(left, right, (dims, ((), ())), preferred_element_type=F32)


NN = ((1,), (0,))
NT = ((1,), (1,))
TN = ((0,), (0,))


def split_heads_device(
    inputs,
    lengths,
    first_gain,
    input_weight,
    decay_weight,
    conv_weight,
    decay_log,
    decay_bias,
    head_gain,
    output_weight,
    second_gain,
    gate_up_weight,
    down_weight,
    cotangent,
):
    micro_count, seq_local, span, model_width = inputs.shape
    ring = lax.axis_size("seq")
    depth = lax.axis_size("dp")
    rank = lax.axis_index("seq")
    seqs = micro_count * seq_local
    row_count = seqs * span
    all_rows = ring * row_count
    head_count = decay_log.shape[0]
    heads = head_count // ring
    head_size = head_gain.shape[0]
    key_width = head_count * head_size
    width = heads * head_size
    own_units = down_weight.shape[0]
    units = depth * own_units
    weight_rows = input_weight.shape[0]
    tap_count = conv_weight.shape[0]

    tokens = inputs.reshape(row_count, model_width).astype(F32)
    positions = rank * span + lax.broadcasted_iota(jnp.int32, (micro_count, seq_local, span), 2)
    valid_rows = (positions < lengths[:, :, None]).astype(F32).reshape(row_count, 1)
    normed_low = rms_norm(tokens, first_gain).astype(BF16)

    in_cut = jnp.transpose(input_weight.reshape(weight_rows, 4, ring, width), (2, 0, 1, 3))
    gate_up_cut = jnp.transpose(
        gate_up_weight.reshape(weight_rows, 2, depth, ring, own_units), (3, 1, 0, 2, 4)
    ).reshape(ring, 2, weight_rows, units)
    upstream = valid_rows * cotangent.reshape(row_count, model_width).astype(F32)
    out_err = upstream.astype(BF16)
    normed_all, out_err_all, in_own, gate_up_cut = plane_open(
        normed_low,
        out_err,
        in_cut.reshape(ring, weight_rows, 4 * width),
        gate_up_cut.reshape(ring, 2 * weight_rows, units),
        1,
    )
    gate_up_cut = gate_up_cut.reshape(ring, 2, weight_rows, units)
    normed_all = normed_all.reshape(all_rows, model_width)
    out_err_all = out_err_all.reshape(all_rows, model_width)
    in_own = in_own.reshape(model_width, 4 * width)
    in_own, output_weight, down_weight = lax.optimization_barrier(
        (in_own, output_weight, down_weight)
    )
    turns = [(depth * s + z, ring * z + s) for s in range(ring) for z in range(depth)]
    out_own = gather_rows(lax.ppermute(output_weight, ("dp", "seq"), turns), "dp")
    gate_own = gather_rows(gate_up_cut[:, 0].reshape(ring * weight_rows, units), "dp")
    up_own = gather_rows(gate_up_cut[:, 1].reshape(ring * weight_rows, units), "dp")
    down_own = gather_rows(down_weight, "dp")

    def own_lanes(pair):
        rows = pair.shape[0]
        decay_part = lax.dynamic_slice(pair, (0, rank * heads), (rows, heads))
        other = pair.shape[1] - head_count
        if other:
            strength_part = lax.dynamic_slice(pair, (0, head_count + rank * heads), (rows, heads))
            decay_part = jnp.concatenate([decay_part, strength_part], 1)
        return jnp.pad(decay_part, ((0, 0), (0, 128 - decay_part.shape[1])))

    decay_own = own_lanes(decay_weight)
    params = jnp.pad(own_lanes(jnp.stack([decay_log, decay_bias])), ((0, 6), (0, 0)))
    taps = lax.dynamic_slice(
        conv_weight.reshape(tap_count, 3, key_width), (0, 0, rank * width), (tap_count, 3, width)
    ).reshape(tap_count, 3 * width)
    gain = head_gain.reshape(1, head_size)

    def chunks(value):
        return value.reshape(ring, seqs, span, value.shape[-1])

    mixed = chunks(low_dot(normed_all, in_own[:, : 3 * width], NN).astype(BF16))
    gate_raw = chunks(low_dot(normed_all, in_own[:, 3 * width :], NN))
    logits = chunks(low_dot(normed_all, decay_own, NN))
    gated, memory, inverse, fresh, mixer_out = run_forward(
        mixed, gate_raw, logits, taps, params, gain, heads
    )
    gated_rows = gated.reshape(all_rows, width)
    hidden_part = low_dot(gated_rows, out_own, NN).astype(BF16)
    hidden = tokens + plane_scatter(hidden_part.reshape(ring, row_count, model_width), 2)
    second_low = rms_norm(hidden, second_gain).astype(BF16)
    second_all = plane_gather(second_low, 3).reshape(all_rows, model_width)
    gate_part = low_dot(second_all, gate_own, NN)
    up_part = low_dot(second_all, up_own, NN)
    gate_open = jax.nn.sigmoid(gate_part)
    activated = (gate_part * gate_open * up_part).astype(BF16)
    down_part = low_dot(activated, down_own, NN).astype(BF16)

    down_term = low_dot(activated, out_err_all, TN).astype(BF16)
    down_term, out_err_all = lax.optimization_barrier((down_term, out_err_all))
    activated_grad = low_dot(out_err_all, down_own, NT)
    gate_err = (
        activated_grad * up_part * gate_open * (1.0 + gate_part * (1.0 - gate_open))
    ).astype(BF16)
    up_err = (activated_grad * gate_part * gate_open).astype(BF16)
    gate_term = low_dot(second_all, gate_err, TN).astype(BF16)
    up_term = low_dot(second_all, up_err, TN).astype(BF16)
    gate_term, up_term, gate_err, up_err = lax.optimization_barrier(
        (gate_term, up_term, gate_err, up_err)
    )
    second_part = (low_dot(gate_err, gate_own, NT) + low_dot(up_err, up_own, NT)).astype(BF16)
    second_grad = plane_scatter(second_part.reshape(ring, row_count, model_width), 4)
    down_share = scatter_rows(down_term, "dp").astype(F32)
    result = valid_rows * (hidden + plane_scatter(down_part.reshape(ring, row_count, model_width), 5))
    gate_share = scatter_rows(gate_term, "dp")
    up_share = scatter_rows(up_term, "dp")
    hidden_part, second_gain_grad = rms_back(hidden, second_gain, second_grad)
    hidden_grad = upstream + hidden_part
    branch_err = hidden_grad.astype(BF16)
    branch_all = plane_gather(branch_err, 11).reshape(all_rows, model_width)
    output_term = low_dot(gated_rows, branch_all, TN).astype(BF16)
    gated_grad = low_dot(branch_all, out_own, NT).astype(BF16)
    output_term, gated_grad = lax.optimization_barrier((output_term, gated_grad))
    output_term, down_share, gate_share, up_share = lax.optimization_barrier(
        (output_term, down_share, gate_share, up_share)
    )
    output_share = lax.ppermute(
        scatter_rows(output_term, "dp"), ("dp", "seq"), [(b, a) for a, b in turns]
    ).astype(F32)
    gate_share, up_share = plane_exchange(
        [
            gate_share.reshape(ring, weight_rows, units),
            up_share.reshape(ring, weight_rows, units),
        ],
        9,
    )
    gate_up_share = jnp.stack([gate_share, up_share], 1)
    gate_up_share = jnp.transpose(
        gate_up_share.reshape(ring, 2, weight_rows, depth, own_units), (2, 1, 3, 0, 4)
    )
    gate_up_share = gate_up_share.reshape(weight_rows, -1).astype(F32)

    in_err, logit_grad, taps_grad, param_grad, gain_grad = run_backward(
        mixed,
        gate_raw,
        logits,
        taps,
        params,
        gain,
        memory,
        inverse,
        fresh,
        mixer_out,
        gated_grad.reshape(ring, seqs, span, width),
    )
    in_err = in_err.reshape(all_rows, 4 * width)
    logit_grad = logit_grad.reshape(all_rows, -1)
    input_term = low_dot(normed_all, in_err, TN).astype(BF16)
    input_term, in_err, logit_grad = lax.optimization_barrier((input_term, in_err, logit_grad))
    (input_share,) = plane_exchange(
        [scatter_rows(input_term, "dp").reshape(ring, weight_rows, 4 * width)], 10
    )
    input_share = jnp.transpose(
        input_share.reshape(ring, weight_rows, 4, width), (1, 2, 0, 3)
    )
    input_share = input_share.reshape(weight_rows, -1).astype(F32)
    logit_top, logit_rest = parts(logit_grad)
    normed_part = (
        low_dot(in_err, in_own, NT)
        + low_dot(logit_top, decay_own, NT)
        + low_dot(logit_rest, decay_own, NT)
    ).astype(BF16)
    normed_grad = plane_scatter(normed_part.reshape(ring, row_count, model_width), 6)
    token_part, first_gain_grad = rms_back(tokens, first_gain, normed_grad)
    inputs_grad = hidden_grad + token_part
    decay_term = (low_dot(normed_all, logit_top, TN) + low_dot(normed_all, logit_rest, TN))[
        :, : 2 * heads
    ]

    pieces = [
        jnp.transpose(decay_term),
        taps_grad[:tap_count],
        param_grad[:2, : 2 * heads],
        first_gain_grad,
        second_gain_grad,
        gain_grad[0],
    ]
    sizes = [piece.size for piece in pieces]
    packed = jnp.concatenate([piece.reshape(-1) for piece in pieces])
    packed = jnp.pad(packed, (0, -packed.size % 1024)).reshape(-1, 128)
    summed = small_sum(packed, 7).reshape(ring, -1)
    parted = []
    start = 0
    for size in sizes:
        parted.append(summed[:, start : start + size])
        start += size
    decay_sum, taps_sum, param_sum = parted[:3]
    first_gain_grad, second_gain_grad, gain_grad = [part.sum(0) for part in parted[3:]]
    decay_sum = decay_sum.reshape(ring, 2, heads, model_width)
    decay_weight_grad = jnp.transpose(decay_sum, (3, 1, 0, 2)).reshape(model_width, 2 * head_count)
    taps_sum = jnp.transpose(taps_sum.reshape(ring, tap_count, 3, width), (1, 2, 0, 3))
    param_sum = jnp.transpose(param_sum.reshape(ring, 2, 2 * heads)[..., :heads], (1, 0, 2))
    param_sum = param_sum.reshape(2, head_count)
    return (
        result.reshape(inputs.shape),
        inputs_grad.reshape(inputs.shape),
        first_gain_grad,
        input_share,
        decay_weight_grad,
        taps_sum.reshape(tap_count, 3 * key_width),
        param_sum[0],
        param_sum[1],
        gain_grad,
        output_share,
        second_gain_grad,
        gate_up_share,
        down_share,
    )


def solution(mesh):
    in_specs = (
        P(None, "dp", "seq", None),
        P(None, "dp"),
        P(),
        P(("dp", "seq"), None),
        P(),
        P(),
        P(),
        P(),
        P(),
        P(("dp", "seq"), None),
        P(),
        P(("dp", "seq"), None),
        P(("dp", "seq"), None),
        P(None, "dp", "seq", None),
    )
    out_specs = (
        P(None, "dp", "seq", None),
        P(None, "dp", "seq", None),
        P(),
        P(("dp", "seq"), None),
        P(),
        P(),
        P(),
        P(),
        P(),
        P(("dp", "seq"), None),
        P(),
        P(("dp", "seq"), None),
        P(("dp", "seq"), None),
    )
    ring = mesh.shape["seq"]

    def whole_device(*arrays):
        heads_divide = ring == 8 and arrays[6].shape[0] % ring == 0
        return (split_heads_device if heads_divide else per_device)(*arrays)

    return jax.shard_map(
        whole_device, mesh=mesh, in_specs=in_specs, out_specs=out_specs, check_vma=False
    )
```

```python
import functools

import jax
import jax.numpy as jnp
from jax import lax
from jax.experimental import pallas as pl
from jax.experimental.pallas import tpu as pltpu
from jax.sharding import PartitionSpec as P

SPAN = 64
VMEM_LIMIT = 56 * 1024 * 1024


HIGH = lax.Precision.HIGHEST


def shifted(value, axis, steps):
    count = lax.axis_size(axis)
    initial, last = (max(0, -steps), min(count, count - steps))
    return lax.ppermute(value, axis, [(source, source + steps) for source in range(initial, last)])


def rms_norm(values, gain):
    return values * lax.rsqrt(jnp.mean(values * values, -1, keepdims=True) + 1e-05) * gain


def unit_norm(vectors):
    return vectors * lax.rsqrt(jnp.sum(vectors * vectors, -1, keepdims=True) + 1e-06)


def swish_product(gate_part, up_part):
    return jax.nn.silu(gate_part) * up_part


def unit_inverse(strict_lower):
    extent = strict_lower.shape[-1]
    identity_matrix = jnp.eye(extent, dtype=jnp.float32)
    inverse = identity_matrix - strict_lower
    power_term = strict_lower
    for level_index in range(1, (extent - 1).bit_length()):
        power_term = jnp.einsum("bhij,bhjk->bhik", power_term, power_term, precision=HIGH)
        inverse = jnp.einsum(
            "bhij,bhjk->bhik", inverse, identity_matrix + power_term, precision=HIGH
        )
    return inverse


def span_step(memory, pieces):
    queries, probes, writes, decays, strengths = pieces
    extent = decays.shape[-1]
    running = jnp.cumsum(decays, axis=-1)
    spread = running[..., :, None] - running[..., None, :]
    row_index = lax.broadcasted_iota(jnp.int32, (extent, extent), 0)
    col_index = lax.broadcasted_iota(jnp.int32, (extent, extent), 1)
    faded = jnp.exp(jnp.minimum(spread, 0.0))
    inclusive = jnp.where(col_index <= row_index, faded, 0.0) * strengths[..., None, :]
    strict_mask = jnp.where(col_index < row_index, faded, 0.0) * strengths[..., None, :]
    strict_lower = strict_mask * jnp.einsum("bhtd,bhsd->bhts", probes, probes, precision=HIGH)
    scale_in = jnp.exp(running)[..., None]
    target = writes - scale_in * jnp.einsum("bhtd,bhde->bhte", probes, memory, precision=HIGH)
    fresh_values = jnp.einsum("bhts,bhse->bhte", unit_inverse(strict_lower), target, precision=HIGH)
    mixing = inclusive * jnp.einsum("bhtd,bhsd->bhts", queries, probes, precision=HIGH)
    outputs = scale_in * jnp.einsum("bhtd,bhde->bhte", queries, memory, precision=HIGH)
    outputs = outputs + jnp.einsum("bhts,bhse->bhte", mixing, fresh_values, precision=HIGH)
    remaining = jnp.exp(running[..., -1:] - running) * strengths
    memory = jnp.exp(running[..., -1])[..., None, None] * memory + jnp.einsum(
        "bhsd,bhse->bhde", probes * remaining[..., None], fresh_values, precision=HIGH
    )
    return (memory, outputs)


def delta_local(queries, probes, writes, decays, strengths, memory):
    seq_count, head_count, length, head_size = queries.shape
    blocks = length // SPAN

    def arrange(tensor):
        shaped = tensor.reshape(tensor.shape[:2] + (blocks, SPAN) + tensor.shape[3:])
        return jnp.moveaxis(shaped, 2, 0)

    pieces = (
        arrange(queries),
        arrange(probes),
        arrange(writes),
        arrange(decays),
        arrange(strengths),
    )
    memory, outputs = lax.scan(span_step, memory, pieces)
    outputs = jnp.moveaxis(outputs, 0, 2)
    return (outputs.reshape(seq_count, head_count, length, outputs.shape[-1]), memory)


def prepare(packed, logits, conv_weight, decay_log, decay_bias):
    seq_count, length, logit_width = logits.shape
    head_count = decay_log.shape[0]
    tap_count = conv_weight.shape[0]
    convolved = conv_weight[0] * packed[:, 0:length]
    for tap_index in range(1, tap_count):
        convolved = convolved + conv_weight[tap_index] * packed[:, tap_index : tap_index + length]
    active = jax.nn.silu(convolved)
    key_width = active.shape[-1] // 3
    head_size = key_width // head_count

    def split_heads(portion):
        return jnp.transpose(
            portion.reshape(seq_count, length, head_count, head_size), (0, 2, 1, 3)
        )

    queries = unit_norm(split_heads(active[..., :key_width])) * head_size ** (-0.5)
    probes = unit_norm(split_heads(active[..., key_width : 2 * key_width]))
    writes = split_heads(active[..., 2 * key_width :])
    decays = jnp.transpose(
        -jnp.exp(decay_log) * jax.nn.softplus(logits[..., :head_count] + decay_bias), (0, 2, 1)
    )
    strengths = jnp.transpose(jax.nn.sigmoid(logits[..., head_count:]), (0, 2, 1))
    return (queries, probes, writes, decays, strengths)


def mixer_core(packed, logits, conv_weight, decay_log, decay_bias, memory):
    queries, probes, writes, decays, strengths = prepare(
        packed, logits, conv_weight, decay_log, decay_bias
    )
    return delta_local(queries, probes, writes, decays, strengths, memory)


def finish(mixer_out, gate_raw, head_gain):
    seq_count, head_count, length, head_size = mixer_out.shape
    normal_out = rms_norm(mixer_out, head_gain)
    flat_rows = jnp.transpose(normal_out, (0, 2, 1, 3)).reshape(
        seq_count, length, head_count * head_size
    )
    return flat_rows * jax.nn.silu(gate_raw)


def carry_forward(transfer, offset):

    def turn_step(step_index, incoming):
        leaving = jnp.einsum("bhij,bhjk->bhik", transfer, incoming, precision=HIGH) + offset
        return shifted(leaving.astype(jnp.bfloat16), "seq", 1).astype(leaving.dtype)

    return lax.fori_loop(0, lax.axis_size("seq") - 1, turn_step, jnp.zeros_like(offset))


def carry_back(transfer, source):
    flipped = jnp.swapaxes(transfer, 2, 3)

    def turn_step(step_index, incoming):
        leaving = jnp.einsum("bhij,bhjk->bhik", flipped, incoming, precision=HIGH) + source
        return shifted(leaving.astype(jnp.bfloat16), "seq", -1).astype(leaving.dtype)

    return lax.fori_loop(0, lax.axis_size("seq") - 1, turn_step, jnp.zeros_like(source))


def per_device(
    inputs,
    lengths,
    first_gain,
    input_weight,
    decay_weight,
    conv_weight,
    decay_log,
    decay_bias,
    head_gain,
    output_weight,
    second_gain,
    gate_up_weight,
    down_weight,
    cotangent,
):
    micro_count, seq_local, length, model_width = inputs.shape
    seq_count = micro_count * seq_local
    row_count = seq_count * length
    head_count = decay_log.shape[0]
    key_width = input_weight.shape[1] // 4
    head_size = key_width // head_count
    tap_count = conv_weight.shape[0]
    tokens = inputs.reshape(row_count, model_width).astype(jnp.float32)
    positions = lax.axis_index("seq") * length + lax.broadcasted_iota(
        jnp.int32, (micro_count, seq_local, length), 2
    )
    valid_rows = (positions < lengths[:, :, None]).astype(jnp.float32).reshape(row_count, 1)
    in_full, out_full, gate_up_full, down_full = (
        lax.all_gather(input_weight, ("dp", "seq"), axis=0, tiled=True),
        lax.all_gather(output_weight, ("dp", "seq"), axis=0, tiled=True),
        lax.all_gather(gate_up_weight, ("dp", "seq"), axis=0, tiled=True),
        lax.all_gather(down_weight, ("dp", "seq"), axis=0, tiled=True),
    )
    normed, first_pullback = jax.vjp(rms_norm, tokens, first_gain)
    normed_low = normed.astype(jnp.bfloat16)
    projected = jnp.dot(normed_low, in_full, preferred_element_type=jnp.float32)
    mixed_low = (
        projected[:, : 3 * key_width].astype(jnp.bfloat16).reshape(seq_count, length, 3 * key_width)
    )
    gate_raw = projected[:, 3 * key_width :].reshape(seq_count, length, key_width)
    logits = jnp.dot(normed_low, decay_weight, preferred_element_type=jnp.float32).reshape(
        seq_count, length, 2 * head_count
    )
    left_edge = shifted(mixed_low[:, length - tap_count + 1 :], "seq", 1)
    packed = jnp.concatenate([left_edge, mixed_low], 1).astype(jnp.float32)
    queries, probes, writes, decays, strengths = prepare(
        packed, logits, conv_weight, decay_log, decay_bias
    )
    blank_state = jnp.zeros((seq_count, head_count, head_size, head_size), jnp.float32)
    identity_maps = jnp.broadcast_to(jnp.eye(head_size, dtype=jnp.float32), blank_state.shape)
    joined_writes = jnp.concatenate([writes, jnp.zeros_like(writes)], -1)
    joined_outputs, joined_end = delta_local(
        queries,
        probes,
        joined_writes,
        decays,
        strengths,
        jnp.concatenate([blank_state, identity_maps], -1),
    )
    own_out = joined_outputs[..., :head_size]
    carry_out = joined_outputs[..., head_size:]
    offset = joined_end[..., :head_size]
    transfer = joined_end[..., head_size:]
    state_in = carry_forward(transfer, offset)
    mixer_out = own_out + jnp.einsum("bhtd,bhde->bhte", carry_out, state_in, precision=HIGH)
    gated_rows, finish_pullback = jax.vjp(finish, mixer_out, gate_raw, head_gain)
    gated_low = gated_rows.reshape(row_count, key_width).astype(jnp.bfloat16)
    hidden = tokens + jnp.dot(gated_low, out_full, preferred_element_type=jnp.float32)
    second, second_pullback = jax.vjp(rms_norm, hidden, second_gain)
    second_low = second.astype(jnp.bfloat16)
    gate_up = jnp.dot(second_low, gate_up_full, preferred_element_type=jnp.float32)
    ffn_width = gate_up.shape[1] // 2
    activated, swish_pullback = jax.vjp(
        swish_product, gate_up[:, :ffn_width], gate_up[:, ffn_width:]
    )
    activated_low = activated.astype(jnp.bfloat16)
    final_rows = hidden + jnp.dot(activated_low, down_full, preferred_element_type=jnp.float32)
    result = valid_rows * final_rows
    upstream = valid_rows * cotangent.reshape(row_count, model_width).astype(jnp.float32)
    out_err = upstream.astype(jnp.bfloat16)
    down_term = jnp.einsum("nf,nd->fd", activated_low, out_err, preferred_element_type=jnp.float32)
    activated_grad = jnp.einsum("nd,fd->nf", out_err, down_full, preferred_element_type=jnp.float32)
    gate_grad, up_grad = swish_pullback(activated_grad)
    gate_up_err = jnp.concatenate([gate_grad, up_grad], 1).astype(jnp.bfloat16)
    gate_up_term = jnp.einsum(
        "nd,nf->df", second_low, gate_up_err, preferred_element_type=jnp.float32
    )
    second_grad = jnp.einsum(
        "nf,df->nd", gate_up_err, gate_up_full, preferred_element_type=jnp.float32
    )
    hidden_part, second_gain_grad = second_pullback(second_grad)
    hidden_grad = upstream + hidden_part
    gate_up_share, down_share = (
        scatter_rows(gate_up_term.astype(BF16), ("dp", "seq")).astype(F32),
        scatter_rows(down_term.astype(BF16), ("dp", "seq")).astype(F32),
    )
    branch_err = hidden_grad.astype(jnp.bfloat16)
    output_term = jnp.einsum("nk,nd->kd", gated_low, branch_err, preferred_element_type=jnp.float32)
    gated_grad = jnp.einsum("nd,kd->nk", branch_err, out_full, preferred_element_type=jnp.float32)
    mixer_grad, gate_raw_grad, head_gain_grad = finish_pullback(
        gated_grad.reshape(seq_count, length, key_width)
    )
    source = jnp.einsum("bhtd,bhte->bhde", carry_out, mixer_grad, precision=HIGH)
    state_out_grad = carry_back(transfer, source)
    _, core_pullback = jax.vjp(
        mixer_core, packed, logits, conv_weight, decay_log, decay_bias, state_in
    )
    packed_grad, logits_grad, conv_grad, decay_log_grad, decay_bias_grad, _ = core_pullback(
        (mixer_grad, state_out_grad)
    )
    edge_grad = shifted(packed_grad[:, : tap_count - 1].astype(jnp.bfloat16), "seq", -1).astype(
        jnp.float32
    )
    mixed_grad = packed_grad[:, tap_count - 1 :] + jnp.pad(
        edge_grad, ((0, 0), (length - tap_count + 1, 0), (0, 0))
    )
    in_err = jnp.concatenate(
        [mixed_grad.reshape(row_count, 3 * key_width), gate_raw_grad.reshape(row_count, key_width)],
        1,
    ).astype(jnp.bfloat16)
    input_term = jnp.einsum("nd,nk->dk", normed_low, in_err, preferred_element_type=jnp.float32)
    logits_flat = logits_grad.reshape(row_count, 2 * head_count)
    decay_weight_grad = jnp.einsum(
        "nd,nk->dk", normed_low.astype(jnp.float32), logits_flat, precision=HIGH
    )
    normed_grad = jnp.einsum("nk,dk->nd", in_err, in_full, preferred_element_type=jnp.float32)
    normed_grad = normed_grad + jnp.einsum(
        "nk,dk->nd", logits_flat, decay_weight.astype(jnp.float32), precision=HIGH
    )
    token_part, first_gain_grad = first_pullback(normed_grad)
    inputs_grad = hidden_grad + token_part
    input_share, output_share = (
        scatter_rows(input_term.astype(BF16), ("dp", "seq")).astype(F32),
        scatter_rows(output_term.astype(BF16), ("dp", "seq")).astype(F32),
    )
    small_sums = lax.psum(
        (
            first_gain_grad,
            decay_weight_grad,
            conv_grad,
            decay_log_grad,
            decay_bias_grad,
            head_gain_grad,
            second_gain_grad,
        ),
        ("dp", "seq"),
    )
    return (
        result.reshape(inputs.shape),
        inputs_grad.reshape(inputs.shape),
        small_sums[0],
        input_share,
        small_sums[1],
        small_sums[2],
        small_sums[3],
        small_sums[4],
        small_sums[5],
        output_share,
        small_sums[6],
        gate_up_share,
        down_share,
    )


F32 = jnp.float32
BF16 = jnp.bfloat16


def lasting(microseconds):
    return pl.CostEstimate(flops=0, bytes_accessed=int(microseconds * 3.5e6), transcendentals=0)


def parts(value):
    top = value.astype(BF16)
    return (top, (value - top.astype(F32)).astype(BF16))


def contract(left, right, right_dim):
    lhs = jnp.concatenate([left[0], left[1], left[0]], 1)
    rhs = jnp.concatenate([right[0], right[0], right[1]], right_dim)
    return lax.dot_general(lhs, rhs, (((1,), (right_dim,)), ((), ())), preferred_element_type=F32)


def mm(left, right):
    return contract(left, right, 0)


def mm_nt(left, right):
    return contract(left, right, 1)


def ones_dot(ones, value):
    first = value.astype(BF16)
    rest = value - first.astype(F32)
    second = rest.astype(BF16)
    third = (rest - second.astype(F32)).astype(BF16)
    return (
        jnp.dot(ones, first, preferred_element_type=F32)
        + jnp.dot(ones, second, preferred_element_type=F32)
        + jnp.dot(ones, third, preferred_element_type=F32)
    )


def lower_inverse(strict_lower, row_index, col_index):
    extent = strict_lower.shape[0]

    def below(width):
        same = (row_index // (2 * width)) == (col_index // (2 * width))
        return same & ((row_index // width) % 2 == 1) & ((col_index // width) % 2 == 0)

    inverse = jnp.where(row_index == col_index, 1.0, 0.0) - jnp.where(below(1), strict_lower, 0.0)
    width = 2
    while width < extent:
        block = jnp.where(below(width), strict_lower, 0.0)
        split = parts(inverse)
        inverse = inverse - mm(parts(mm(split, parts(block))), split)
        width *= 2
    return inverse


def active_rows(before, rows, taps):
    extended = jnp.concatenate([before, rows], 0)
    count = rows.shape[0]
    tap_count = taps.shape[0]
    start = before.shape[0] - tap_count + 1
    shifts = [extended[start + j : start + j + count] for j in range(tap_count)]
    total = taps[0:1] * shifts[0]
    for j in range(1, tap_count):
        total = total + taps[j : j + 1] * shifts[j]
    return (total, shifts)


def soft_plus(value):
    return jnp.maximum(value, 0.0) + jnp.log(1.0 + jnp.exp(-jnp.abs(value)))


def sigmoid(value):
    return 1.0 / (1.0 + jnp.exp(-value))


def unit(vectors):
    scale = lax.rsqrt(jnp.sum(vectors * vectors, -1, keepdims=True) + 1e-06)
    return (vectors * scale, scale)


def unit_back(vectors, scale, grad):
    inner = jnp.sum(vectors * grad, -1, keepdims=True)
    return scale * grad - vectors * (scale * scale * scale * inner)


def decay_terms(logit, param_ref, heads, ones):
    shifted_logit = logit + param_ref[1:2, :]
    lane = lax.broadcasted_iota(jnp.int32, logit.shape, 1)
    decays = jnp.where(lane < heads, -jnp.exp(param_ref[0:1, :]) * soft_plus(shifted_logit), 0.0)
    strengths = sigmoid(logit)
    running = ones_dot(ones, decays)
    return (shifted_logit, decays, strengths, running)


def mixer_forward(
    mixed_ref,
    gate_ref,
    logit_ref,
    taps_ref,
    param_ref,
    gain_ref,
    own_ref,
    gated_ref,
    memory_ref,
    inverse_ref,
    fresh_ref,
    out_ref,
    all_ref,
    state_ref,
    halo_ref,
    send_sems,
    recv_sems,
    local_sem,
):
    seqs, span, _ = mixed_ref.shape
    heads, head_size = memory_ref.shape[1], memory_ref.shape[2]
    gather_in_steps(own_ref, all_ref, send_sems, recv_sems, local_sem)

    @pl.when(pl.program_id(0) == 0)
    def _():
        state_ref[...] = jnp.zeros_like(state_ref)
        halo_ref[...] = jnp.zeros_like(halo_ref)

    row_index = lax.broadcasted_iota(jnp.int32, (span, span), 0)
    col_index = lax.broadcasted_iota(jnp.int32, (span, span), 1)
    ones = jnp.where(col_index <= row_index, 1.0, 0.0).astype(BF16)
    taps = taps_ref[...]
    width = heads * head_size
    for m in range(seqs):
        rows = mixed_ref[m].astype(F32)
        convolved, _ = active_rows(halo_ref[m], rows, taps)
        halo_ref[m] = rows[span - 8 :]
        active = convolved * sigmoid(convolved)
        _, decays, strengths, running = decay_terms(logit_ref[m], param_ref, heads, ones)
        running_rows = jnp.transpose(running)
        strength_rows = jnp.transpose(strengths)
        for h in range(heads):
            own = slice(h * head_size, (h + 1) * head_size)
            queries = unit(active[:, own])[0] * head_size ** (-0.5)
            probes = unit(active[:, width + h * head_size : width + (h + 1) * head_size])[0]
            writes = active[:, 2 * width + h * head_size : 2 * width + (h + 1) * head_size]
            run = running[:, h : h + 1]
            last = running[span - 1 : span, h : h + 1]
            weight_row = strength_rows[heads + h : heads + h + 1, :]
            weight_col = strengths[:, heads + h : heads + h + 1]
            faded = jnp.exp(jnp.minimum(run - running_rows[h : h + 1, :], 0.0)) * weight_row
            probe_parts = parts(probes)
            query_parts = parts(queries)
            strict = jnp.where(col_index < row_index, faded * mm_nt(probe_parts, probe_parts), 0.0)
            mixing = jnp.where(col_index <= row_index, faded * mm_nt(query_parts, probe_parts), 0.0)
            inverse = lower_inverse(strict, row_index, col_index)
            scale_in = jnp.exp(run)
            both = mm(
                parts(inverse), parts(jnp.concatenate([writes, scale_in * probes], 1))
            )
            memory = state_ref[m, h]
            memory_parts = parts(memory)
            reads = mm(
                parts(jnp.concatenate([both[:, head_size:], scale_in * queries], 0)), memory_parts
            )
            fresh = both[:, :head_size] - reads[:span]
            fresh_parts = parts(fresh)
            mixer_out = reads[span:] + mm(parts(mixing), fresh_parts)
            kept = jnp.transpose(jnp.exp(last - run) * weight_col * probes)
            state_ref[m, h] = jnp.exp(last) * memory + mm(parts(kept), fresh_parts)
            memory_ref[m, h] = memory
            inverse_ref[m, h] = inverse
            fresh_ref[m, :, own] = fresh
            out_ref[m, :, own] = mixer_out
            scale = lax.rsqrt(jnp.mean(mixer_out * mixer_out, -1, keepdims=True) + 1e-05)
            gate = gate_ref[m, :, own]
            gated_ref[m, :, own] = (
                mixer_out * scale * gain_ref[...] * (gate * sigmoid(gate))
            ).astype(BF16)


def mixer_backward(
    mixed_ref,
    before_ref,
    gate_ref,
    logit_ref,
    taps_ref,
    param_ref,
    gain_ref,
    memory_ref,
    inverse_ref,
    fresh_ref,
    out_ref,
    grad_ref,
    part_ref,
    error_ref,
    logit_grad_ref,
    taps_grad_ref,
    param_grad_ref,
    gain_grad_ref,
    sum_ref,
    state_ref,
    halo_ref,
    *scatter_refs,
):
    seqs, span, _ = mixed_ref.shape
    heads, head_size = memory_ref.shape[1], memory_ref.shape[2]
    step = pl.program_id(0)
    scatter_in_steps(part_ref, sum_ref, *scatter_refs)

    @pl.when(step == 0)
    def _():
        state_ref[...] = jnp.zeros_like(state_ref)
        halo_ref[...] = jnp.zeros_like(halo_ref)
        taps_grad_ref[...] = jnp.zeros_like(taps_grad_ref)
        param_grad_ref[...] = jnp.zeros_like(param_grad_ref)
        gain_grad_ref[...] = jnp.zeros_like(gain_grad_ref)

    first = step == pl.num_programs(0) - 1
    row_index = lax.broadcasted_iota(jnp.int32, (span, span), 0)
    col_index = lax.broadcasted_iota(jnp.int32, (span, span), 1)
    ones = jnp.where(col_index <= row_index, 1.0, 0.0).astype(BF16)
    ones_back = jnp.where(col_index >= row_index, 1.0, 0.0).astype(BF16)
    taps = taps_ref[...]
    tap_count = taps.shape[0]
    width = heads * head_size
    gain = gain_ref[...]
    edge = before_ref.shape[1]
    for m in range(seqs):
        rows = mixed_ref[m].astype(F32)
        before = jnp.where(first, 0.0, before_ref[m].astype(F32))[edge - 8 :]
        convolved, shifts = active_rows(before, rows, taps)
        opening = sigmoid(convolved)
        active = convolved * opening
        logit = logit_ref[m]
        shifted_logit, decays, strengths, running = decay_terms(logit, param_ref, heads, ones)
        running_rows = jnp.transpose(running)
        strength_rows = jnp.transpose(strengths)
        active_grads = [None] * (3 * heads)
        gate_grads = [None] * heads
        col_terms = jnp.zeros((span, span), F32)
        row_terms = jnp.zeros((span, span), F32)
        for h in range(heads):
            own = slice(h * head_size, (h + 1) * head_size)
            raw_queries = active[:, own]
            raw_probes = active[:, width + h * head_size : width + (h + 1) * head_size]
            queries, query_scale = unit(raw_queries)
            queries = queries * head_size ** (-0.5)
            probes, probe_scale = unit(raw_probes)
            mixer_out = out_ref[m, :, own]
            gate = gate_ref[m, :, own]
            gated_grad = grad_ref[m, :, own].astype(F32)
            scale = lax.rsqrt(jnp.mean(mixer_out * mixer_out, -1, keepdims=True) + 1e-05)
            gate_open = sigmoid(gate)
            normal = mixer_out * scale
            gate_grads[h] = gated_grad * normal * gain * (gate_open * (1.0 + gate * (1.0 - gate_open)))
            normal_grad = gated_grad * (gate * gate_open)
            gain_grad_ref[0:1, :] += jnp.sum(normal_grad * normal, 0, keepdims=True)
            weighted = normal_grad * gain
            out_grad = scale * (
                weighted - normal * jnp.mean(weighted * normal, -1, keepdims=True)
            )

            run = running[:, h : h + 1]
            last = running[span - 1 : span, h : h + 1]
            weight_row = strength_rows[heads + h : heads + h + 1, :]
            weight_col = strengths[:, heads + h : heads + h + 1]
            faded = jnp.exp(jnp.minimum(run - running_rows[h : h + 1, :], 0.0))
            scale_in = jnp.exp(run)
            end_scale = jnp.exp(last)
            remaining = jnp.exp(last - run)
            kept = remaining * weight_col

            memory = memory_ref[m, h]
            fresh = fresh_ref[m, :, own]
            state_grad = state_ref[m, h]
            probe_parts = parts(probes)
            query_parts = parts(queries)
            fresh_parts = parts(fresh)
            memory_parts = parts(memory)
            state_grad_parts = parts(state_grad)
            products = mm_nt(parts(jnp.concatenate([queries, probes], 0)), probe_parts)
            fade_query = jnp.where(col_index <= row_index, faded * products[:span], 0.0)
            fade_probe = jnp.where(col_index < row_index, faded * products[span:], 0.0)
            out_grad_parts = parts(out_grad)
            probe_state = mm(probe_parts, state_grad_parts)
            fresh_grad = (
                mm(parts(jnp.transpose(fade_query * weight_row)), out_grad_parts)
                + kept * probe_state
            )
            solved = mm(parts(jnp.transpose(inverse_ref[m, h])), parts(fresh_grad))
            turned_queries = parts(jnp.transpose(queries))
            turned_probes = parts(jnp.transpose(probes))
            state_ref[m, h] = (
                end_scale * state_grad
                + mm(turned_queries, parts(scale_in * out_grad))
                - mm(turned_probes, parts(scale_in * solved))
            )
            joined = parts(jnp.concatenate([out_grad, solved], 0))
            outer = mm_nt(joined, fresh_parts)
            mixing_grad = jnp.where(col_index <= row_index, outer[:span], 0.0)
            strict_grad = jnp.where(col_index < row_index, -outer[span:], 0.0)
            through = mm_nt(joined, memory_parts)
            out_state = scale_in * through[:span]
            solved_state = scale_in * through[span:]
            spread = faded * weight_row
            mix_fade = mixing_grad * spread
            strict_fade = strict_grad * spread
            on_probes = mm(parts(jnp.concatenate([mix_fade, strict_fade], 0)), probe_parts)
            query_grad = out_state + on_probes[:span]
            probe_grad = (
                kept * mm_nt(fresh_parts, state_grad_parts)
                - solved_state
                + on_probes[span:]
                + mm(parts(jnp.transpose(mix_fade)), query_parts)
                + mm(parts(jnp.transpose(strict_fade)), probe_parts)
            )
            pairs = mixing_grad * fade_query + strict_grad * fade_probe
            weighted_pairs = pairs * weight_row
            probe_fresh = jnp.sum(probe_state * fresh, -1, keepdims=True)
            run_col = (
                jnp.sum(out_state * queries - solved_state * probes, -1, keepdims=True)
                + jnp.sum(weighted_pairs, -1, keepdims=True)
                - kept * probe_fresh
            )
            last_grad = jnp.sum(kept * probe_fresh, 0, keepdims=True) + end_scale * jnp.sum(
                jnp.sum(state_grad * memory, -1, keepdims=True), 0, keepdims=True
            )
            run_col = run_col + jnp.where(row_index[:, 0:1] == span - 1, last_grad, 0.0)
            col_terms = jnp.where(col_index == h, run_col, col_terms)
            col_terms = jnp.where(col_index == heads + h, remaining * probe_fresh, col_terms)
            row_terms = jnp.where(
                row_index == h, -jnp.sum(weighted_pairs, 0, keepdims=True), row_terms
            )
            row_terms = jnp.where(
                row_index == heads + h, jnp.sum(pairs, 0, keepdims=True), row_terms
            )
            active_grads[h] = unit_back(raw_queries, query_scale, query_grad) * head_size ** (-0.5)
            active_grads[heads + h] = unit_back(raw_probes, probe_scale, probe_grad)
            active_grads[2 * heads + h] = solved

        terms = col_terms + jnp.transpose(row_terms)
        decay_grad = ones_dot(ones_back, terms)
        shifted_grad = decay_grad * -jnp.exp(param_ref[0:1, :]) * sigmoid(shifted_logit)
        logit_grad = jnp.where(
            col_index < heads,
            shifted_grad,
            jnp.where(col_index < 2 * heads, terms * strengths * (1.0 - strengths), 0.0),
        )
        logit_top, logit_rest = parts(logit_grad)
        logit_grad_ref[m] = (
            logit_top.astype(F32) + pltpu.roll(logit_rest.astype(F32), span // 2, 1)
        ).astype(BF16)
        decay_lane = col_index[0:1] < heads
        param_grad_ref[0:1, :] += jnp.sum(
            jnp.where(decay_lane, decay_grad * decays, 0.0), 0, keepdims=True
        )
        param_grad_ref[1:2, :] += jnp.sum(
            jnp.where(decay_lane, shifted_grad, 0.0), 0, keepdims=True
        )
        conv_grad = jnp.concatenate(active_grads, 1) * (
            opening * (1.0 + convolved * (1.0 - opening))
        )
        extended = jnp.concatenate([conv_grad, halo_ref[m]], 0)
        halo_ref[m] = conv_grad[:8]
        mixed_grad = jnp.zeros_like(conv_grad)
        for j in range(tap_count):
            reach = tap_count - 1 - j
            mixed_grad = mixed_grad + taps[j : j + 1] * extended[reach : reach + span]
            taps_grad_ref[j : j + 1, :] += jnp.sum(conv_grad * shifts[j], 0, keepdims=True)
        error_ref[m] = jnp.concatenate([mixed_grad] + gate_grads, 1).astype(BF16)


def run_forward(mixed, gate, logits, taps, params, gain, heads, own, collective_id):
    steps, seqs, span, _ = mixed.shape
    anywhere = pl.BlockSpec(memory_space=pl.ANY)
    head_size = gain.shape[1]
    width = heads * head_size

    def rows(columns):
        return pl.BlockSpec((None, seqs, span, columns), lambda j: (j, 0, 0, 0))

    def squares():
        return pl.BlockSpec((None, seqs, heads, head_size, head_size), lambda j: (j, 0, 0, 0, 0))

    def whole(array):
        return pl.BlockSpec(array.shape, lambda j: (0, 0))

    square = jax.ShapeDtypeStruct((steps, seqs, heads, head_size, head_size), F32)
    lower = jax.ShapeDtypeStruct((steps, seqs, heads, span, span), F32)
    flat = jax.ShapeDtypeStruct((steps, seqs, span, width), F32)
    return pl.pallas_call(
        mixer_forward,
        grid=(steps,),
        in_specs=[
            rows(3 * width),
            rows(width),
            rows(logits.shape[-1]),
            whole(taps),
            whole(params),
            whole(gain),
            anywhere,
        ],
        out_specs=[rows(width), squares(), squares(), rows(width), rows(width), anywhere],
        out_shape=[
            jax.ShapeDtypeStruct((steps, seqs, span, width), BF16),
            square,
            lower,
            flat,
            flat,
            jax.ShapeDtypeStruct((steps,) + own.shape, own.dtype),
        ],
        scratch_shapes=[
            pltpu.VMEM((seqs, heads, head_size, head_size), F32),
            pltpu.VMEM((seqs, 8, 3 * width), F32),
            pltpu.SemaphoreType.DMA((9,)),
            pltpu.SemaphoreType.DMA((9,)),
            pltpu.SemaphoreType.DMA,
        ],
        compiler_params=pltpu.CompilerParams(
            collective_id=collective_id, has_side_effects=True, vmem_limit_bytes=VMEM_LIMIT
        ),
        cost_estimate=lasting(75),
        name="mixer_forward",
    )(mixed, gate, logits, taps, params, gain, own)


def run_backward(
    mixed, gate, logits, taps, params, gain, memory, inverse, fresh, out, grad, part, collective_id
):
    steps, seqs, span, _ = mixed.shape
    _, part_rows, columns = part.shape
    heads, head_size = memory.shape[2], memory.shape[3]
    width = heads * head_size
    edge = 16

    def rows(columns):
        return pl.BlockSpec((None, seqs, span, columns), lambda j: (steps - 1 - j, 0, 0, 0))

    def squares():
        return pl.BlockSpec(
            (None, seqs, heads, head_size, head_size), lambda j: (steps - 1 - j, 0, 0, 0, 0)
        )

    def whole(shape):
        return pl.BlockSpec(shape, lambda j: (0, 0))

    before = pl.BlockSpec(
        (None, seqs, edge, 3 * width),
        lambda j: (jnp.maximum(steps - 2 - j, 0), 0, span // edge - 1, 0),
    )
    return pl.pallas_call(
        mixer_backward,
        grid=(steps,),
        in_specs=[
            rows(3 * width),
            before,
            rows(width),
            rows(logits.shape[-1]),
            whole(taps.shape),
            whole(params.shape),
            whole(gain.shape),
            squares(),
            squares(),
            rows(width),
            rows(width),
            rows(width),
            pl.BlockSpec(memory_space=pl.ANY),
        ],
        out_specs=[
            rows(4 * width),
            rows(logits.shape[-1]),
            whole((8, 3 * width)),
            whole((8, logits.shape[-1])),
            whole((8, head_size)),
            whole((part_rows, columns)),
        ],
        out_shape=[
            jax.ShapeDtypeStruct((steps, seqs, span, 4 * width), BF16),
            jax.ShapeDtypeStruct(logits.shape, BF16),
            jax.ShapeDtypeStruct((8, 3 * width), F32),
            jax.ShapeDtypeStruct((8, logits.shape[-1]), F32),
            jax.ShapeDtypeStruct((8, head_size), F32),
            jax.ShapeDtypeStruct((part_rows, columns), F32),
        ],
        scratch_shapes=[
            pltpu.VMEM((seqs, heads, head_size, head_size), F32),
            pltpu.VMEM((seqs, 8, 3 * width), F32),
            pltpu.VMEM((4, part_rows, columns), BF16),
            pltpu.VMEM((4, part_rows, columns), BF16),
            pltpu.VMEM((part_rows, columns), BF16),
            pltpu.VMEM((2, part_rows, columns), BF16),
            pltpu.SemaphoreType.DMA((10,)),
            pltpu.SemaphoreType.DMA((10,)),
            pltpu.SemaphoreType.DMA((4,)),
        ],
        compiler_params=pltpu.CompilerParams(
            collective_id=collective_id, has_side_effects=True, vmem_limit_bytes=VMEM_LIMIT
        ),
        cost_estimate=lasting(55),
        name="mixer_backward",
    )(mixed, mixed, gate, logits, taps, params, gain, memory, inverse, fresh, out, grad, part)


def gather_rows(value, axis):
    return lax.all_gather(value, axis, axis=0, tiled=True)


def scatter_rows(value, axis):
    return lax.psum_scatter(value, axis, scatter_dimension=0, tiled=True)


def plane_peers():
    me = lax.axis_index("seq")
    sibling = me + 1 - 2 * (me % 2)
    across = me + 2 - 4 * ((me // 2) % 2)
    along = me + 4 - 8 * (me // 4)
    return (me, sibling, across, along)


def greet(peers):
    barrier = pltpu.get_barrier_semaphore()
    for peer in peers:
        pl.semaphore_signal(
            barrier, inc=1, device_id={"seq": peer}, device_id_type=pl.DeviceIdType.MESH
        )
    pl.semaphore_wait(barrier, len(peers))


def send_to(peer, source, target, send_sem, recv_sem):
    return pltpu.make_async_remote_copy(
        src_ref=source,
        dst_ref=target,
        send_sem=send_sem,
        recv_sem=recv_sem,
        device_id={"seq": peer},
        device_id_type=pl.DeviceIdType.MESH,
    )


def gather_phases(own_ref, all_ref, send_sems, recv_sems, local_sem, start):
    me, sibling, across, along = plane_peers()
    far = along + across - me
    half = own_ref.shape[0] // 2
    upper, lower = pl.ds(0, half), pl.ds(half, half)
    copies = []

    def send(peer, source, target):
        k = start + len(copies)
        copy = send_to(peer, source, target, send_sems.at[k], recv_sems.at[k])
        copy.start()
        copies.append(copy)

    keep = pltpu.make_async_copy(own_ref, all_ref.at[me], local_sem)
    keep.start()
    send(across, own_ref, all_ref.at[me])
    send(along, own_ref, all_ref.at[me])
    send(sibling, own_ref, all_ref.at[me])
    yield
    copies[0].wait_recv()
    send(along, all_ref.at[across, upper], all_ref.at[across, upper])
    copies[1].wait_recv()
    send(across, all_ref.at[along, lower], all_ref.at[along, lower])
    send(sibling, all_ref.at[across], all_ref.at[across])
    send(sibling, all_ref.at[along], all_ref.at[along])
    yield
    copies[3].wait_recv()
    send(sibling, all_ref.at[far, upper], all_ref.at[far, upper])
    copies[4].wait_recv()
    send(sibling, all_ref.at[far, lower], all_ref.at[far, lower])
    yield
    for k in (2, 5, 6, 7, 8):
        copies[k].wait_recv()
    for copy in copies:
        copy.wait_send()
    keep.wait()
    yield


def chain_phases(all_ref, up_send, up_recv, down_send, down_recv):
    depth = all_ref.shape[0]
    place = lax.axis_index("dp")
    above, below = lax.rem(place + 1, depth), lax.rem(place + depth - 1, depth)

    def hop(slot, peer, send_sem, recv_sem):
        return pltpu.make_async_remote_copy(
            src_ref=all_ref.at[slot],
            dst_ref=all_ref.at[slot],
            send_sem=send_sem,
            recv_sem=recv_sem,
            device_id={"dp": peer},
            device_id_type=pl.DeviceIdType.MESH,
        )

    ups, downs = [], []
    for t in range(depth - 1):
        up = hop(lax.rem(place + depth - t, depth), above, up_send.at[t], up_recv.at[t])
        down = hop(lax.rem(place + t, depth), below, down_send.at[t], down_recv.at[t])
        ups.append(up)
        downs.append(down)
        pl.when((place < depth - 1) & (place >= t))(up.start)
        pl.when((place > 0) & (place + t < depth))(down.start)
        yield
        pl.when(place > t)(up.wait_recv)
        pl.when(place + t + 1 < depth)(down.wait_recv)
    for t in range(depth - 1):
        pl.when((place < depth - 1) & (place >= t))(ups[t].wait_send)
        pl.when((place > 0) & (place + t < depth))(downs[t].wait_send)
    yield


def exchange_copies(cut_ref, land, send_sems, recv_sems, start):
    ring = cut_ref.shape[0]
    me = lax.axis_index("seq")
    copies = []
    for k in range(1, ring):
        peer = lax.rem(me + k, ring)
        copy = send_to(
            peer, cut_ref.at[peer], land, send_sems.at[start + k - 1], recv_sems.at[start + k - 1]
        )
        copy.start()
        copies.append(copy)
    return copies


def plane_open_kernel(
    first_ref,
    early_ref,
    later_ref,
    first_all_ref,
    early_all_ref,
    later_all_ref,
    send_sems,
    recv_sems,
    local_sems,
    up_send,
    up_recv,
    down_send,
    down_recv,
):
    place, me = lax.axis_index("dp"), lax.axis_index("seq")
    depth, ring = early_all_ref.shape[0], early_ref.shape[0]
    rows = early_ref.shape[1]
    barrier = pltpu.get_barrier_semaphore()
    for k in range(1, ring):
        pl.semaphore_signal(
            barrier,
            inc=1,
            device_id={"seq": lax.rem(me + k, ring)},
            device_id_type=pl.DeviceIdType.MESH,
        )
    for k in range(1, depth):
        pl.semaphore_signal(
            barrier,
            inc=1,
            device_id={"dp": lax.rem(place + k, depth)},
            device_id_type=pl.DeviceIdType.MESH,
        )
    pl.semaphore_wait(barrier, ring + depth - 2)
    spot = early_all_ref.at[place, pl.ds(pl.multiple_of(me * rows, rows), rows)]
    keep_early = pltpu.make_async_copy(early_ref.at[me], spot, local_sems.at[0])
    keep_early.start()
    keep_later = pltpu.make_async_copy(later_ref.at[me], later_all_ref.at[me], local_sems.at[1])
    keep_later.start()
    early = exchange_copies(early_ref, spot, send_sems, recv_sems, 0)
    for copy in early:
        copy.wait_recv()
    keep_early.wait()
    chain = chain_phases(early_all_ref, up_send, up_recv, down_send, down_recv)
    first = gather_phases(first_ref, first_all_ref, send_sems, recv_sems, local_sems.at[2], ring)
    next(chain)
    next(first)
    later = exchange_copies(later_ref, later_all_ref.at[me], send_sems, recv_sems, ring + 9)
    next(chain)
    next(first)
    next(chain)
    next(first)
    next(first)
    for copy in later:
        copy.wait_recv()
    next(chain)
    for copy in early + later:
        copy.wait_send()
    keep_later.wait()


def plane_open(first, early, later, collective_id):
    ring, depth = lax.axis_size("seq"), lax.axis_size("dp")
    rows, columns = first.shape
    total = 2 * ring + 9
    return pl.pallas_call(
        plane_open_kernel,
        out_shape=[
            jax.ShapeDtypeStruct((ring, rows, columns), first.dtype),
            jax.ShapeDtypeStruct((depth, ring * early.shape[1], early.shape[2]), early.dtype),
            jax.ShapeDtypeStruct(later.shape, later.dtype),
        ],
        in_specs=[pl.BlockSpec(memory_space=pl.ANY)] * 3,
        out_specs=[pl.BlockSpec(memory_space=pl.ANY)] * 3,
        scratch_shapes=[
            pltpu.SemaphoreType.DMA((total,)),
            pltpu.SemaphoreType.DMA((total,)),
            pltpu.SemaphoreType.DMA((3,)),
        ]
        + [pltpu.SemaphoreType.DMA((depth - 1,))] * 4,
        compiler_params=pltpu.CompilerParams(collective_id=collective_id, has_side_effects=True),
        cost_estimate=lasting(90),
        name="plane_open",
    )(first, early, later)


def gather_in_steps(own_ref, all_ref, send_sems, recv_sems, local_sem):
    me, sibling, across, along = plane_peers()
    far = along + across - me
    half = own_ref.shape[0] // 2
    upper, lower = pl.ds(0, half), pl.ds(half, half)
    keep = pltpu.make_async_copy(own_ref, all_ref.at[me], local_sem)
    plan = [
        (across, own_ref, all_ref.at[me]),
        (along, own_ref, all_ref.at[me]),
        (sibling, own_ref, all_ref.at[me]),
        (along, all_ref.at[across, upper], all_ref.at[across, upper]),
        (across, all_ref.at[along, lower], all_ref.at[along, lower]),
        (sibling, all_ref.at[across], all_ref.at[across]),
        (sibling, all_ref.at[along], all_ref.at[along]),
        (sibling, all_ref.at[far, upper], all_ref.at[far, upper]),
        (sibling, all_ref.at[far, lower], all_ref.at[far, lower]),
    ]
    copies = [
        send_to(peer, source, target, send_sems.at[k], recv_sems.at[k])
        for k, (peer, source, target) in enumerate(plan)
    ]
    step, steps = pl.program_id(0), pl.num_programs(0)

    @pl.when(step == 0)
    def _():
        greet((sibling, across, along))
        keep.start()
        for k in (0, 1, 2):
            copies[k].start()

    @pl.when(step == 3)
    def _():
        copies[0].wait_recv()
        copies[1].wait_recv()
        for k in (3, 4, 5, 6):
            copies[k].start()

    @pl.when(step == 5)
    def _():
        copies[3].wait_recv()
        copies[4].wait_recv()
        for k in (7, 8):
            copies[k].start()

    @pl.when(step == steps - 1)
    def _():
        for k in (2, 5, 6, 7, 8):
            copies[k].wait_recv()
        for copy in copies:
            copy.wait_send()
        keep.wait()


def scatter_in_steps(
    part_ref,
    sum_ref,
    own_ref,
    near_ref,
    far_in_ref,
    side_in_ref,
    send_sems,
    recv_sems,
    load_sems,
):
    me, sibling, across, along = plane_peers()
    far = along + across - me
    flip = sibling - me
    rows = sum_ref.shape[0]
    half = rows // 2
    upper, lower = pl.ds(0, half), pl.ds(half, half)
    slabs = (far, across, along, me)
    loads = [
        pltpu.make_async_copy(part_ref.at[slab], own_ref.at[k], load_sems.at[k])
        for k, slab in enumerate(slabs)
    ]
    plan = [(sibling, part_ref.at[slab + flip], near_ref.at[k]) for k, slab in enumerate(slabs)]
    plan += [
        (across, own_ref.at[0, upper], far_in_ref.at[upper]),
        (along, own_ref.at[0, lower], far_in_ref.at[lower]),
        (across, own_ref.at[1, upper], side_in_ref.at[0, upper]),
        (along, own_ref.at[2, lower], side_in_ref.at[1, lower]),
        (along, own_ref.at[2, upper], side_in_ref.at[1, upper]),
        (across, own_ref.at[1, lower], side_in_ref.at[0, lower]),
    ]
    copies = [
        send_to(peer, source, target, send_sems.at[k], recv_sems.at[k])
        for k, (peer, source, target) in enumerate(plan)
    ]
    step, steps = pl.program_id(0), pl.num_programs(0)
    tall = 32

    def fold(target, other, start, size):
        @pl.loop(0, size // tall)
        def _(i):
            at = pl.ds(pl.multiple_of(start + i * tall, tall), tall)
            target[at] = (target[at].astype(F32) + other[at].astype(F32)).astype(BF16)

    def join(k):
        loads[k].wait()
        copies[k].wait_recv()
        fold(own_ref.at[k], near_ref.at[k], 0, rows)

    @pl.when(step == 0)
    def _():
        greet((sibling, across, along))
        for k in range(4):
            loads[k].start()
            copies[k].start()

    @pl.when(step == 1)
    def _():
        join(0)
        copies[4].start()
        copies[5].start()
        join(1)
        copies[6].start()
        join(2)
        copies[7].start()

    @pl.when(step == 3)
    def _():
        copies[4].wait_recv()
        fold(own_ref.at[2], far_in_ref, 0, half)
        copies[8].start()
        copies[5].wait_recv()
        fold(own_ref.at[1], far_in_ref, half, half)
        copies[9].start()

    @pl.when(step == steps - 1)
    def _():
        loads[3].wait()
        copies[3].wait_recv()
        for copy in copies[6:]:
            copy.wait_recv()

        @pl.loop(0, rows // tall)
        def _(i):
            at = pl.ds(pl.multiple_of(i * tall, tall), tall)
            sum_ref[at] = (
                own_ref[3, at].astype(F32)
                + near_ref[3, at].astype(F32)
                + side_in_ref[0, at].astype(F32)
                + side_in_ref[1, at].astype(F32)
            )

        for copy in copies:
            copy.wait_send()


def small_sum_kernel(
    own_ref, cut_ref, all_ref, swapped_ref, stage_ref, total_ref, send_sems, recv_sems, local_sem
):
    depth, ring = stage_ref.shape[0], all_ref.shape[0]
    place, me = lax.axis_index("dp"), lax.axis_index("seq")
    barrier = pltpu.get_barrier_semaphore()
    mesh_ids = pl.DeviceIdType.MESH
    columns = [lax.rem(place + k, depth) for k in range(1, depth)]
    plane = [lax.rem(me + k, ring) for k in range(1, ring)]
    for peer in columns:
        pl.semaphore_signal(barrier, inc=1, device_id={"dp": peer}, device_id_type=mesh_ids)
    for peer in plane:
        pl.semaphore_signal(barrier, inc=1, device_id={"seq": peer}, device_id_type=mesh_ids)
    pl.semaphore_wait(barrier, depth + ring - 2)
    keep = pltpu.make_async_copy(cut_ref.at[me], swapped_ref.at[me], local_sem)
    keep.start()
    first = []
    for k, peer in enumerate(columns):
        copy = pltpu.make_async_remote_copy(
            src_ref=own_ref,
            dst_ref=stage_ref.at[place],
            send_sem=send_sems.at[k],
            recv_sem=recv_sems.at[k],
            device_id={"dp": peer},
            device_id_type=mesh_ids,
        )
        copy.start()
        first.append(copy)
    swaps = exchange_copies(
        cut_ref, swapped_ref.at[me], send_sems, recv_sems, depth + ring - 2
    )
    stage_ref[place] = own_ref[...]
    for copy in first:
        copy.wait_recv()
    total = stage_ref[0]
    for k in range(1, depth):
        total = total + stage_ref[k]
    total_ref[...] = total
    second = []
    for k, peer in enumerate(plane):
        copy = pltpu.make_async_remote_copy(
            src_ref=total_ref,
            dst_ref=all_ref.at[me],
            send_sem=send_sems.at[depth - 1 + k],
            recv_sem=recv_sems.at[depth - 1 + k],
            device_id={"seq": peer},
            device_id_type=mesh_ids,
        )
        copy.start()
        second.append(copy)
    all_ref[me] = total
    for copy in second + swaps:
        copy.wait_recv()
    for copy in first + second + swaps:
        copy.wait_send()
    keep.wait()


def small_sum(own, cut, collective_id):
    depth, ring = lax.axis_size("dp"), lax.axis_size("seq")
    count = depth + 2 * ring - 3
    vmem, anywhere = pl.BlockSpec(memory_space=pltpu.VMEM), pl.BlockSpec(memory_space=pl.ANY)
    return pl.pallas_call(
        small_sum_kernel,
        out_shape=[
            jax.ShapeDtypeStruct((ring,) + own.shape, F32),
            jax.ShapeDtypeStruct(cut.shape, cut.dtype),
        ],
        in_specs=[vmem, anywhere],
        out_specs=[vmem, anywhere],
        scratch_shapes=[
            pltpu.VMEM((depth,) + own.shape, F32),
            pltpu.VMEM(own.shape, F32),
            pltpu.SemaphoreType.DMA((count,)),
            pltpu.SemaphoreType.DMA((count,)),
            pltpu.SemaphoreType.DMA,
        ],
        compiler_params=pltpu.CompilerParams(collective_id=collective_id, has_side_effects=True),
        cost_estimate=lasting(20),
        name="small_sum",
    )(own, cut)


def greet_plane(ring):
    me = lax.axis_index("seq")
    greet([lax.rem(me + k, ring) for k in range(1, ring)])


def plane_scatter_dot_kernel(count, dims, fill, swaps, *refs):
    refs = list(refs)

    def take(size):
        taken = refs[:size]
        del refs[:size]
        return taken

    left_hbm, right_hbm, fill_hbm = take(count), take(count), take(int(fill))
    cut_refs = take(swaps)
    (sum_ref,) = take(1)
    terms = take(count if fill else 0)
    swapped_refs = take(swaps)
    lefts, rights, fill_refs = take(count), take(count), take(int(fill))
    out_ref, own_ref, near_ref, far_in_ref, side_in_ref = take(5)
    send_sems, recv_sems, load_sems = refs
    loads = []
    for k in range(count):
        for source, target in ((left_hbm[k], lefts[k]), (right_hbm[k], rights[k])):
            load = pltpu.make_async_copy(source, target, load_sems.at[len(loads)])
            load.start()
            loads.append(load)
    if fill:
        fill_load = pltpu.make_async_copy(fill_hbm[0], fill_refs[0], load_sems.at[2 * count])
        fill_load.start()
    me, sibling, across, along = plane_peers()
    far = along + across - me
    flip = sibling - me
    rows, columns = sum_ref.shape
    half = rows // 2
    upper, lower = pl.ds(0, half), pl.ds(half, half)
    swapped, keeps = [], []
    if swaps:
        ring = cut_refs[0].shape[0]
        greet_plane(ring)
        for k in range(swaps):
            keep = pltpu.make_async_copy(
                cut_refs[k].at[me], swapped_refs[k].at[me], load_sems.at[2 * count + k]
            )
            keep.start()
            keeps.append(keep)
            swapped += exchange_copies(
                cut_refs[k], swapped_refs[k].at[me], send_sems, recv_sems, 10 + k * (ring - 1)
            )
    else:
        greet((sibling, across, along))
    for load in loads:
        load.wait()
    wide = 512

    def slab_dot(slab, target):
        @pl.loop(0, columns // wide)
        def _(i):
            at = pl.ds(pl.multiple_of(i * wide, wide), wide)
            total = None
            for k in range(count):
                right = rights[k][:, at] if dims[1] == (0,) else rights[k][at, :]
                term = low_dot(lefts[k][slab], right, dims)
                total = term if total is None else total + term
            target[:, at] = total.astype(BF16)

    def send(k, peer, source, target):
        copy = send_to(peer, source, target, send_sems.at[k], recv_sems.at[k])
        copy.start()
        return copy

    step = 32

    def fold(target, other, start, size):
        @pl.loop(0, size // step)
        def _(i):
            at = pl.ds(pl.multiple_of(start + i * step, step), step)
            target[at] = (target[at].astype(F32) + other[at].astype(F32)).astype(BF16)

    nears = []

    def near_slab(k, slab):
        slab_dot(slab + flip, out_ref.at[k])
        nears.append(send(k, sibling, out_ref.at[k], near_ref.at[k]))

    near_slab(0, far)
    slab_dot(far, own_ref.at[0])
    near_slab(1, across)
    nears[0].wait_recv()
    fold(own_ref.at[0], near_ref.at[0], 0, rows)
    copies = [
        send(4, across, own_ref.at[0, upper], far_in_ref.at[upper]),
        send(5, along, own_ref.at[0, lower], far_in_ref.at[lower]),
    ]
    slab_dot(across, own_ref.at[1])
    near_slab(2, along)
    nears[1].wait_recv()
    fold(own_ref.at[1], near_ref.at[1], 0, rows)
    copies.append(send(6, across, own_ref.at[1, upper], side_in_ref.at[0, upper]))
    slab_dot(along, own_ref.at[2])
    near_slab(3, me)
    nears[2].wait_recv()
    fold(own_ref.at[2], near_ref.at[2], 0, rows)
    copies.append(send(7, along, own_ref.at[2, lower], side_in_ref.at[1, lower]))
    slab_dot(me, own_ref.at[3])
    copies[0].wait_recv()
    fold(own_ref.at[2], far_in_ref, 0, half)
    copies.append(send(8, along, own_ref.at[2, upper], side_in_ref.at[1, upper]))
    copies[1].wait_recv()
    fold(own_ref.at[1], far_in_ref, half, half)
    copies.append(send(9, across, own_ref.at[1, lower], side_in_ref.at[0, lower]))
    if fill:
        fill_load.wait()
        tall = 256

        @pl.loop(0, terms[0].shape[0] // tall)
        def _(i):
            at = pl.ds(pl.multiple_of(i * tall, tall), tall)
            turned = fill_refs[0][:, at]
            for k in range(count):
                wide_left = lefts[k][...].reshape(-1, lefts[k].shape[2])
                terms[k][at, :] = low_dot(turned, wide_left, TN).astype(BF16)

    nears[3].wait_recv()

    def finish(a, start):
        @pl.loop(0, half // step)
        def _(i):
            at = pl.ds(pl.multiple_of(start + i * step, step), step)
            sum_ref[at] = (
                own_ref[3, at].astype(F32)
                + near_ref[3, at].astype(F32)
                + side_in_ref[0, at].astype(F32)
                + side_in_ref[1, at].astype(F32)
            )

    for copy in copies[2:]:
        copy.wait_recv()
    finish(0, 0)
    finish(1, half)
    for copy in swapped:
        copy.wait_recv()
    for copy in nears + copies + swapped:
        copy.wait_send()
    for keep in keeps:
        keep.wait()


def plane_scatter_dot(lefts, rights, dims, collective_id, fill=None, cuts=()):
    count = len(lefts)
    ring, rows, _ = lefts[0].shape
    columns = rights[0].shape[1 - dims[1][0]]
    filled = fill is not None
    fills = [fill] if filled else []
    vmem, anywhere = pl.BlockSpec(memory_space=pltpu.VMEM), pl.BlockSpec(memory_space=pl.ANY)
    total = 10 + len(cuts) * (ring - 1)
    term_shapes = [
        jax.ShapeDtypeStruct((fill.shape[1], left.shape[2]), BF16) for left in lefts if filled
    ]
    return pl.pallas_call(
        functools.partial(plane_scatter_dot_kernel, count, dims, filled, len(cuts)),
        out_shape=[jax.ShapeDtypeStruct((rows, columns), F32)]
        + term_shapes
        + [jax.ShapeDtypeStruct(cut.shape, cut.dtype) for cut in cuts],
        in_specs=[anywhere] * (2 * count + len(fills) + len(cuts)),
        out_specs=[vmem] * (1 + len(term_shapes)) + [anywhere] * len(cuts),
        scratch_shapes=[pltpu.VMEM(left.shape, BF16) for left in lefts]
        + [pltpu.VMEM(right.shape, BF16) for right in rights]
        + [pltpu.VMEM(value.shape, BF16) for value in fills]
        + [
            pltpu.VMEM((4, rows, columns), BF16),
            pltpu.VMEM((4, rows, columns), BF16),
            pltpu.VMEM((4, rows, columns), BF16),
            pltpu.VMEM((rows, columns), BF16),
            pltpu.VMEM((2, rows, columns), BF16),
            pltpu.SemaphoreType.DMA((total,)),
            pltpu.SemaphoreType.DMA((total,)),
            pltpu.SemaphoreType.DMA((2 * count + len(fills) + len(cuts),)),
        ],
        compiler_params=pltpu.CompilerParams(
            collective_id=collective_id, has_side_effects=True, vmem_limit_bytes=VMEM_LIMIT
        ),
        cost_estimate=lasting(45),
        name="plane_scatter_dot",
    )(*lefts, *rights, *fills, *cuts)


def gather_in_turn(own_ref, all_ref, send_sems, recv_sems, use):
    me, sibling, across, along = plane_peers()
    far = along + across - me
    flip = sibling - me
    half = own_ref.shape[0] // 2
    upper, lower = pl.ds(0, half), pl.ds(half, half)
    copies = []

    def send(peer, source, target):
        k = len(copies)
        copy = send_to(peer, source, target, send_sems.at[k], recv_sems.at[k])
        copy.start()
        copies.append(copy)

    send(across, own_ref, all_ref.at[me])
    send(along, own_ref, all_ref.at[me])
    send(sibling, own_ref, all_ref.at[me])
    all_ref[me] = own_ref[...]
    use(me)
    copies[2].wait_recv()
    use(sibling)
    copies[0].wait_recv()
    send(along, all_ref.at[across, upper], all_ref.at[across, upper])
    copies[1].wait_recv()
    send(across, all_ref.at[along, lower], all_ref.at[along, lower])
    send(sibling, all_ref.at[across], all_ref.at[across])
    send(sibling, all_ref.at[along], all_ref.at[along])
    use(across)
    use(along)
    copies[5].wait_recv()
    use(across + flip)
    copies[6].wait_recv()
    use(along + flip)
    copies[3].wait_recv()
    send(sibling, all_ref.at[far, upper], all_ref.at[far, upper])
    copies[4].wait_recv()
    send(sibling, all_ref.at[far, lower], all_ref.at[far, lower])
    use(far)
    copies[7].wait_recv()
    copies[8].wait_recv()
    use(far + flip)
    for copy in copies:
        copy.wait_send()


def gather_feed_kernel(
    own_hbm,
    gate_hbm,
    up_hbm,
    down_hbm,
    error_hbm,
    all_hbm,
    activated_hbm,
    gate_err_hbm,
    up_err_hbm,
    down_term_ref,
    own_ref,
    gate_ref,
    up_ref,
    down_ref,
    error_ref,
    all_ref,
    activated_out,
    gate_out,
    up_out,
    total_ref,
    send_sems,
    recv_sems,
    load_sems,
    save_sems,
):
    loads = []
    for source, target in (
        (own_hbm, own_ref),
        (gate_hbm, gate_ref),
        (up_hbm, up_ref),
        (down_hbm, down_ref),
        (error_hbm, error_ref),
    ):
        load = pltpu.make_async_copy(source, target, load_sems.at[len(loads)])
        load.start()
        loads.append(load)
    greet(plane_peers()[1:])
    loads[0].wait()
    waiting = loads[1:]
    saves = []
    tall = 128
    wide = 512
    rows, columns = own_ref.shape

    def use(slab):
        first = bool(waiting)
        while waiting:
            waiting.pop().wait()
        turn = len(saves) % 2
        if len(saves) > 1:
            for save in saves[-2]:
                save.wait()

        @pl.loop(0, rows // tall)
        def _(i):
            at = pl.ds(pl.multiple_of(i * tall, tall), tall)
            values = all_ref[slab, at, :]
            gate = low_dot(values, gate_ref[...], NN)
            up = low_dot(values, up_ref[...], NN)
            grad = low_dot(error_ref[slab, at, :], down_ref[...], NT)
            opening = sigmoid(gate)
            gate_open = gate * opening
            activated_out[turn, at, :] = (gate_open * up).astype(BF16)
            gate_out[turn, at, :] = (
                grad * up * (opening * (1.0 + gate * (1.0 - opening)))
            ).astype(BF16)
            up_out[turn, at, :] = (grad * gate_open).astype(BF16)

        batch = []
        for k, (source, target) in enumerate(
            (
                (activated_out.at[turn], activated_hbm.at[slab]),
                (gate_out.at[turn], gate_err_hbm.at[slab]),
                (up_out.at[turn], up_err_hbm.at[slab]),
                (all_ref.at[slab], all_hbm.at[slab]),
            )
        ):
            save = pltpu.make_async_copy(source, target, save_sems.at[turn, k])
            save.start()
            batch.append(save)
        saves.append(batch)

        @pl.loop(0, columns // wide)
        def _(i):
            at = pl.ds(pl.multiple_of(i * wide, wide), wide)
            term = low_dot(activated_out[turn], error_ref[slab, :, at], TN)
            if first:
                total_ref[:, at] = term
            else:
                total_ref[:, at] += term

    gather_in_turn(own_ref, all_ref, send_sems, recv_sems, use)
    down_term_ref[...] = total_ref[...].astype(BF16)
    for batch in saves[-2:]:
        for save in batch:
            save.wait()


def gather_feed(own, gate_own, up_own, down_own, error_all, collective_id):
    ring = lax.axis_size("seq")
    rows, columns = own.shape
    units = gate_own.shape[1]
    anywhere = pl.BlockSpec(memory_space=pl.ANY)
    parted = jax.ShapeDtypeStruct((ring, rows, units), BF16)
    return pl.pallas_call(
        gather_feed_kernel,
        out_shape=[
            jax.ShapeDtypeStruct((ring, rows, columns), BF16),
            parted,
            parted,
            parted,
            jax.ShapeDtypeStruct(down_own.shape, BF16),
        ],
        in_specs=[anywhere] * 5,
        out_specs=[anywhere] * 4 + [pl.BlockSpec(memory_space=pltpu.VMEM)],
        scratch_shapes=[
            pltpu.VMEM((rows, columns), BF16),
            pltpu.VMEM(gate_own.shape, BF16),
            pltpu.VMEM(up_own.shape, BF16),
            pltpu.VMEM(down_own.shape, BF16),
            pltpu.VMEM((ring, rows, columns), BF16),
            pltpu.VMEM((ring, rows, columns), BF16),
            pltpu.VMEM((2, rows, units), BF16),
            pltpu.VMEM((2, rows, units), BF16),
            pltpu.VMEM((2, rows, units), BF16),
            pltpu.VMEM(down_own.shape, F32),
            pltpu.SemaphoreType.DMA((9,)),
            pltpu.SemaphoreType.DMA((9,)),
            pltpu.SemaphoreType.DMA((5,)),
            pltpu.SemaphoreType.DMA((2, 4)),
        ],
        compiler_params=pltpu.CompilerParams(
            collective_id=collective_id, has_side_effects=True, vmem_limit_bytes=VMEM_LIMIT
        ),
        cost_estimate=lasting(60),
        name="gather_feed",
    )(own, gate_own, up_own, down_own, error_all)


def gather_branch_kernel(
    own_hbm,
    gated_hbm,
    weight_hbm,
    activated_hbm,
    down_hbm,
    grad_ref,
    term_ref,
    part_hbm,
    own_ref,
    gated_ref,
    weight_ref,
    activated_ref,
    down_ref,
    all_ref,
    total_ref,
    part_out,
    send_sems,
    recv_sems,
    load_sems,
    save_sems,
):
    loads = []
    for source, target in (
        (own_hbm, own_ref),
        (gated_hbm, gated_ref),
        (weight_hbm, weight_ref),
        (activated_hbm, activated_ref),
        (down_hbm, down_ref),
    ):
        load = pltpu.make_async_copy(source, target, load_sems.at[len(loads)])
        load.start()
        loads.append(load)
    greet(plane_peers()[1:])
    loads[0].wait()
    waiting = loads[1:]
    total_ref[...] = jnp.zeros_like(total_ref)
    wide = 512
    saves = []

    def use(slab):
        while waiting:
            waiting.pop().wait()
        turn = len(saves) % 2
        if len(saves) > 1:
            saves[-2].wait()
        grad_ref[slab] = low_dot(all_ref[slab], weight_ref[...], NT).astype(BF16)

        @pl.loop(0, total_ref.shape[1] // wide)
        def _(i):
            at = pl.ds(pl.multiple_of(i * wide, wide), wide)
            total_ref[:, at] += low_dot(gated_ref[slab], all_ref[slab, :, at], TN)
            part_out[turn, :, at] = low_dot(activated_ref[slab], down_ref[:, at], NN).astype(BF16)

        save = pltpu.make_async_copy(part_out.at[turn], part_hbm.at[slab], save_sems.at[turn])
        save.start()
        saves.append(save)

    gather_in_turn(own_ref, all_ref, send_sems, recv_sems, use)
    term_ref[...] = total_ref[...].astype(BF16)
    for save in saves[-2:]:
        save.wait()


def gather_branch(own, gated, weight, activated, down_own, collective_id):
    ring, rows, width = gated.shape
    columns = own.shape[1]
    vmem = pl.BlockSpec(memory_space=pltpu.VMEM)
    anywhere = pl.BlockSpec(memory_space=pl.ANY)
    return pl.pallas_call(
        gather_branch_kernel,
        out_shape=[
            jax.ShapeDtypeStruct((ring, rows, width), BF16),
            jax.ShapeDtypeStruct((width, columns), BF16),
            jax.ShapeDtypeStruct((ring, rows, columns), BF16),
        ],
        in_specs=[anywhere] * 5,
        out_specs=[vmem, vmem, anywhere],
        scratch_shapes=[
            pltpu.VMEM(own.shape, BF16),
            pltpu.VMEM(gated.shape, BF16),
            pltpu.VMEM(weight.shape, BF16),
            pltpu.VMEM(activated.shape, BF16),
            pltpu.VMEM(down_own.shape, BF16),
            pltpu.VMEM((ring, rows, columns), BF16),
            pltpu.VMEM((width, columns), F32),
            pltpu.VMEM((2, rows, columns), BF16),
            pltpu.SemaphoreType.DMA((9,)),
            pltpu.SemaphoreType.DMA((9,)),
            pltpu.SemaphoreType.DMA((5,)),
            pltpu.SemaphoreType.DMA((2,)),
        ],
        compiler_params=pltpu.CompilerParams(
            collective_id=collective_id, has_side_effects=True, vmem_limit_bytes=VMEM_LIMIT
        ),
        cost_estimate=lasting(45),
        name="gather_branch",
    )(own, gated, weight, activated, down_own)


def rms_back(values, gain, grad):
    scale = lax.rsqrt(jnp.mean(values * values, -1, keepdims=True) + 1e-05)
    weighted = grad * gain
    part = scale * weighted - values * (
        scale * scale * scale * jnp.mean(weighted * values, -1, keepdims=True)
    )
    return (part, jnp.sum(grad * values * scale, 0))


def low_dot(left, right, dims):
    return lax.dot_general(left, right, (dims, ((), ())), preferred_element_type=F32)


NN = ((1,), (0,))
NT = ((1,), (1,))
TN = ((0,), (0,))


def split_heads_device(
    inputs,
    lengths,
    first_gain,
    input_weight,
    decay_weight,
    conv_weight,
    decay_log,
    decay_bias,
    head_gain,
    output_weight,
    second_gain,
    gate_up_weight,
    down_weight,
    cotangent,
):
    micro_count, seq_local, span, model_width = inputs.shape
    ring = lax.axis_size("seq")
    depth = lax.axis_size("dp")
    rank = lax.axis_index("seq")
    seqs = micro_count * seq_local
    row_count = seqs * span
    all_rows = ring * row_count
    head_count = decay_log.shape[0]
    heads = head_count // ring
    head_size = head_gain.shape[0]
    key_width = head_count * head_size
    width = heads * head_size
    own_units = down_weight.shape[0]
    units = depth * own_units
    weight_rows = input_weight.shape[0]
    tap_count = conv_weight.shape[0]

    tokens = inputs.reshape(row_count, model_width).astype(F32)
    positions = rank * span + lax.broadcasted_iota(jnp.int32, (micro_count, seq_local, span), 2)
    valid_rows = (positions < lengths[:, :, None]).astype(F32).reshape(row_count, 1)
    normed_low = rms_norm(tokens, first_gain).astype(BF16)

    in_cut = jnp.transpose(input_weight.reshape(weight_rows, 4, ring, width), (2, 0, 1, 3))
    gate_up_cut = jnp.transpose(
        gate_up_weight.reshape(weight_rows, 2, depth, ring, own_units), (3, 1, 0, 2, 4)
    ).reshape(ring, 2, weight_rows, units)
    upstream = valid_rows * cotangent.reshape(row_count, model_width).astype(F32)
    out_err = upstream.astype(BF16)
    turns = [(depth * s + z, ring * z + s) for s in range(ring) for z in range(depth)]
    down_own = gather_rows(down_weight, "dp")
    out_cut = lax.ppermute(output_weight, ("dp", "seq"), turns)
    normed_all, in_own, gate_up_cut = plane_open(
        normed_low,
        in_cut.reshape(ring, weight_rows, 4 * width),
        gate_up_cut.reshape(ring, 2 * weight_rows, units),
        1,
    )
    gate_up_cut = gate_up_cut.reshape(ring, 2, weight_rows, units)
    normed_all = normed_all.reshape(all_rows, model_width)
    in_own = in_own.reshape(model_width, 4 * width)
    in_own, out_cut, down_own = lax.optimization_barrier((in_own, out_cut, down_own))
    out_own = gather_rows(out_cut, "dp")
    gate_own = gather_rows(gate_up_cut[:, 0].reshape(ring * weight_rows, units), "dp")
    up_own = gather_rows(gate_up_cut[:, 1].reshape(ring * weight_rows, units), "dp")

    def own_lanes(pair):
        rows = pair.shape[0]
        decay_part = lax.dynamic_slice(pair, (0, rank * heads), (rows, heads))
        other = pair.shape[1] - head_count
        if other:
            strength_part = lax.dynamic_slice(pair, (0, head_count + rank * heads), (rows, heads))
            decay_part = jnp.concatenate([decay_part, strength_part], 1)
        return jnp.pad(decay_part, ((0, 0), (0, 128 - decay_part.shape[1])))

    decay_own = own_lanes(decay_weight)
    params = jnp.pad(own_lanes(jnp.stack([decay_log, decay_bias])), ((0, 6), (0, 0)))
    taps = lax.dynamic_slice(
        conv_weight.reshape(tap_count, 3, key_width), (0, 0, rank * width), (tap_count, 3, width)
    ).reshape(tap_count, 3 * width)
    gain = head_gain.reshape(1, head_size)

    def chunks(value):
        return value.reshape(ring, seqs, span, value.shape[-1])

    mixed = chunks(low_dot(normed_all, in_own[:, : 3 * width], NN).astype(BF16))
    gate_raw = chunks(low_dot(normed_all, in_own[:, 3 * width :], NN))
    logits = chunks(low_dot(normed_all, decay_own, NN))
    gated, memory, inverse, fresh, mixer_out, out_err_all = run_forward(
        mixed, gate_raw, logits, taps, params, gain, heads, out_err, 5
    )
    gated = gated.reshape(ring, row_count, width)
    hidden = tokens + plane_scatter_dot([gated], [out_own], NN, 2)[0]
    second_low = rms_norm(hidden, second_gain).astype(BF16)
    second_all, activated, gate_err, up_err, down_term = gather_feed(
        second_low, gate_own, up_own, down_own, out_err_all, 3
    )
    down_share = scatter_rows(down_term, "dp").astype(F32)
    second_grad, gate_term, up_term = plane_scatter_dot(
        [gate_err, up_err],
        [gate_own, up_own],
        NT,
        4,
        second_all.reshape(all_rows, model_width),
    )
    gate_share = scatter_rows(gate_term, "dp")
    up_share = scatter_rows(up_term, "dp")
    hidden_part, second_gain_grad = rms_back(hidden, second_gain, second_grad)
    hidden_grad = upstream + hidden_part
    branch_err = hidden_grad.astype(BF16)
    gated_grad, output_term, down_part = gather_branch(
        branch_err, gated, out_own, activated, down_own, 11
    )
    in_err, logit_grad, taps_grad, param_grad, gain_grad, final_part = run_backward(
        mixed,
        gate_raw,
        logits,
        taps,
        params,
        gain,
        memory,
        inverse,
        fresh,
        mixer_out,
        gated_grad.reshape(ring, seqs, span, width),
        down_part,
        12,
    )
    result = valid_rows * (hidden + final_part)
    input_term = low_dot(normed_all, in_err.reshape(all_rows, 4 * width), TN).astype(BF16)
    input_term, in_err, logit_grad, down_share, gate_share, up_share = lax.optimization_barrier(
        (input_term, in_err, logit_grad, down_share, gate_share, up_share)
    )
    input_cut = scatter_rows(input_term, "dp")
    lanes = logit_grad.shape[-1]
    decay_twice = decay_own + jnp.roll(decay_own, lanes // 2, 1)
    normed_grad, gate_share, up_share = plane_scatter_dot(
        [
            in_err.reshape(ring, row_count, 4 * width),
            logit_grad.reshape(ring, row_count, lanes),
        ],
        [in_own, decay_twice],
        NT,
        6,
        cuts=[
            gate_share.reshape(ring, weight_rows, units),
            up_share.reshape(ring, weight_rows, units),
        ],
    )
    output_term, input_cut, normed_grad = lax.optimization_barrier(
        (output_term, input_cut, normed_grad)
    )
    output_share = lax.ppermute(
        scatter_rows(output_term, "dp"), ("dp", "seq"), [(b, a) for a, b in turns]
    ).astype(F32)
    gate_up_share = jnp.stack([gate_share, up_share], 1)
    gate_up_share = jnp.transpose(
        gate_up_share.reshape(ring, 2, weight_rows, depth, own_units), (2, 1, 3, 0, 4)
    )
    gate_up_share = gate_up_share.reshape(weight_rows, -1).astype(F32)
    token_part, first_gain_grad = rms_back(tokens, first_gain, normed_grad)
    inputs_grad = hidden_grad + token_part
    decay_term = low_dot(normed_all, logit_grad.reshape(all_rows, lanes), TN)
    decay_term = decay_term[:, : 2 * heads] + decay_term[:, lanes // 2 : lanes // 2 + 2 * heads]
    pieces = [
        jnp.transpose(decay_term),
        taps_grad[:tap_count],
        param_grad[:2, : 2 * heads],
        first_gain_grad,
        second_gain_grad,
        gain_grad[0],
    ]
    sizes = [piece.size for piece in pieces]
    packed = jnp.concatenate([piece.reshape(-1) for piece in pieces])
    packed = jnp.pad(packed, (0, -packed.size % 1024)).reshape(-1, 128)
    summed, input_share = small_sum(packed, input_cut.reshape(ring, weight_rows, 4 * width), 7)
    input_share = jnp.transpose(input_share.reshape(ring, weight_rows, 4, width), (1, 2, 0, 3))
    input_share = input_share.reshape(weight_rows, -1).astype(F32)
    summed = summed.reshape(ring, -1)
    parted = []
    start = 0
    for size in sizes:
        parted.append(summed[:, start : start + size])
        start += size
    decay_sum, taps_sum, param_sum = parted[:3]
    first_gain_grad, second_gain_grad, gain_grad = [part.sum(0) for part in parted[3:]]
    decay_sum = decay_sum.reshape(ring, 2, heads, model_width)
    decay_weight_grad = jnp.transpose(decay_sum, (3, 1, 0, 2)).reshape(model_width, 2 * head_count)
    taps_sum = jnp.transpose(taps_sum.reshape(ring, tap_count, 3, width), (1, 2, 0, 3))
    param_sum = jnp.transpose(param_sum.reshape(ring, 2, 2 * heads)[..., :heads], (1, 0, 2))
    param_sum = param_sum.reshape(2, head_count)
    return (
        result.reshape(inputs.shape),
        inputs_grad.reshape(inputs.shape),
        first_gain_grad,
        input_share,
        decay_weight_grad,
        taps_sum.reshape(tap_count, 3 * key_width),
        param_sum[0],
        param_sum[1],
        gain_grad,
        output_share,
        second_gain_grad,
        gate_up_share,
        down_share,
    )


def solution(mesh):
    in_specs = (
        P(None, "dp", "seq", None),
        P(None, "dp"),
        P(),
        P(("dp", "seq"), None),
        P(),
        P(),
        P(),
        P(),
        P(),
        P(("dp", "seq"), None),
        P(),
        P(("dp", "seq"), None),
        P(("dp", "seq"), None),
        P(None, "dp", "seq", None),
    )
    out_specs = (
        P(None, "dp", "seq", None),
        P(None, "dp", "seq", None),
        P(),
        P(("dp", "seq"), None),
        P(),
        P(),
        P(),
        P(),
        P(),
        P(("dp", "seq"), None),
        P(),
        P(("dp", "seq"), None),
        P(("dp", "seq"), None),
    )
    ring = mesh.shape["seq"]

    def whole_device(*arrays):
        heads_divide = ring == 8 and arrays[6].shape[0] % ring == 0
        return (split_heads_device if heads_divide else per_device)(*arrays)

    return jax.shard_map(
        whole_device, mesh=mesh, in_specs=in_specs, out_specs=out_specs, check_vma=False
    )
```

```python
import functools

import jax
import jax.numpy as jnp
from jax import lax
from jax.experimental import pallas as pl
from jax.experimental.pallas import tpu as pltpu
from jax.sharding import PartitionSpec as P

SPAN = 64
VMEM_LIMIT = 56 * 1024 * 1024


HIGH = lax.Precision.HIGHEST


def shifted(value, axis, steps):
    count = lax.axis_size(axis)
    initial, last = (max(0, -steps), min(count, count - steps))
    return lax.ppermute(value, axis, [(source, source + steps) for source in range(initial, last)])


def rms_norm(values, gain):
    return values * lax.rsqrt(jnp.mean(values * values, -1, keepdims=True) + 1e-05) * gain


def unit_norm(vectors):
    return vectors * lax.rsqrt(jnp.sum(vectors * vectors, -1, keepdims=True) + 1e-06)


def swish_product(gate_part, up_part):
    return jax.nn.silu(gate_part) * up_part


def unit_inverse(strict_lower):
    extent = strict_lower.shape[-1]
    identity_matrix = jnp.eye(extent, dtype=jnp.float32)
    inverse = identity_matrix - strict_lower
    power_term = strict_lower
    for level_index in range(1, (extent - 1).bit_length()):
        power_term = jnp.einsum("bhij,bhjk->bhik", power_term, power_term, precision=HIGH)
        inverse = jnp.einsum(
            "bhij,bhjk->bhik", inverse, identity_matrix + power_term, precision=HIGH
        )
    return inverse


def span_step(memory, pieces):
    queries, probes, writes, decays, strengths = pieces
    extent = decays.shape[-1]
    running = jnp.cumsum(decays, axis=-1)
    spread = running[..., :, None] - running[..., None, :]
    row_index = lax.broadcasted_iota(jnp.int32, (extent, extent), 0)
    col_index = lax.broadcasted_iota(jnp.int32, (extent, extent), 1)
    faded = jnp.exp(jnp.minimum(spread, 0.0))
    inclusive = jnp.where(col_index <= row_index, faded, 0.0) * strengths[..., None, :]
    strict_mask = jnp.where(col_index < row_index, faded, 0.0) * strengths[..., None, :]
    strict_lower = strict_mask * jnp.einsum("bhtd,bhsd->bhts", probes, probes, precision=HIGH)
    scale_in = jnp.exp(running)[..., None]
    target = writes - scale_in * jnp.einsum("bhtd,bhde->bhte", probes, memory, precision=HIGH)
    fresh_values = jnp.einsum("bhts,bhse->bhte", unit_inverse(strict_lower), target, precision=HIGH)
    mixing = inclusive * jnp.einsum("bhtd,bhsd->bhts", queries, probes, precision=HIGH)
    outputs = scale_in * jnp.einsum("bhtd,bhde->bhte", queries, memory, precision=HIGH)
    outputs = outputs + jnp.einsum("bhts,bhse->bhte", mixing, fresh_values, precision=HIGH)
    remaining = jnp.exp(running[..., -1:] - running) * strengths
    memory = jnp.exp(running[..., -1])[..., None, None] * memory + jnp.einsum(
        "bhsd,bhse->bhde", probes * remaining[..., None], fresh_values, precision=HIGH
    )
    return (memory, outputs)


def delta_local(queries, probes, writes, decays, strengths, memory):
    seq_count, head_count, length, head_size = queries.shape
    blocks = length // SPAN

    def arrange(tensor):
        shaped = tensor.reshape(tensor.shape[:2] + (blocks, SPAN) + tensor.shape[3:])
        return jnp.moveaxis(shaped, 2, 0)

    pieces = (
        arrange(queries),
        arrange(probes),
        arrange(writes),
        arrange(decays),
        arrange(strengths),
    )
    memory, outputs = lax.scan(span_step, memory, pieces)
    outputs = jnp.moveaxis(outputs, 0, 2)
    return (outputs.reshape(seq_count, head_count, length, outputs.shape[-1]), memory)


def prepare(packed, logits, conv_weight, decay_log, decay_bias):
    seq_count, length, logit_width = logits.shape
    head_count = decay_log.shape[0]
    tap_count = conv_weight.shape[0]
    convolved = conv_weight[0] * packed[:, 0:length]
    for tap_index in range(1, tap_count):
        convolved = convolved + conv_weight[tap_index] * packed[:, tap_index : tap_index + length]
    active = jax.nn.silu(convolved)
    key_width = active.shape[-1] // 3
    head_size = key_width // head_count

    def split_heads(portion):
        return jnp.transpose(
            portion.reshape(seq_count, length, head_count, head_size), (0, 2, 1, 3)
        )

    queries = unit_norm(split_heads(active[..., :key_width])) * head_size ** (-0.5)
    probes = unit_norm(split_heads(active[..., key_width : 2 * key_width]))
    writes = split_heads(active[..., 2 * key_width :])
    decays = jnp.transpose(
        -jnp.exp(decay_log) * jax.nn.softplus(logits[..., :head_count] + decay_bias), (0, 2, 1)
    )
    strengths = jnp.transpose(jax.nn.sigmoid(logits[..., head_count:]), (0, 2, 1))
    return (queries, probes, writes, decays, strengths)


def mixer_core(packed, logits, conv_weight, decay_log, decay_bias, memory):
    queries, probes, writes, decays, strengths = prepare(
        packed, logits, conv_weight, decay_log, decay_bias
    )
    return delta_local(queries, probes, writes, decays, strengths, memory)


def finish(mixer_out, gate_raw, head_gain):
    seq_count, head_count, length, head_size = mixer_out.shape
    normal_out = rms_norm(mixer_out, head_gain)
    flat_rows = jnp.transpose(normal_out, (0, 2, 1, 3)).reshape(
        seq_count, length, head_count * head_size
    )
    return flat_rows * jax.nn.silu(gate_raw)


def carry_forward(transfer, offset):

    def turn_step(step_index, incoming):
        leaving = jnp.einsum("bhij,bhjk->bhik", transfer, incoming, precision=HIGH) + offset
        return shifted(leaving.astype(jnp.bfloat16), "seq", 1).astype(leaving.dtype)

    return lax.fori_loop(0, lax.axis_size("seq") - 1, turn_step, jnp.zeros_like(offset))


def carry_back(transfer, source):
    flipped = jnp.swapaxes(transfer, 2, 3)

    def turn_step(step_index, incoming):
        leaving = jnp.einsum("bhij,bhjk->bhik", flipped, incoming, precision=HIGH) + source
        return shifted(leaving.astype(jnp.bfloat16), "seq", -1).astype(leaving.dtype)

    return lax.fori_loop(0, lax.axis_size("seq") - 1, turn_step, jnp.zeros_like(source))


def per_device(
    inputs,
    lengths,
    first_gain,
    input_weight,
    decay_weight,
    conv_weight,
    decay_log,
    decay_bias,
    head_gain,
    output_weight,
    second_gain,
    gate_up_weight,
    down_weight,
    cotangent,
):
    micro_count, seq_local, length, model_width = inputs.shape
    seq_count = micro_count * seq_local
    row_count = seq_count * length
    head_count = decay_log.shape[0]
    key_width = input_weight.shape[1] // 4
    head_size = key_width // head_count
    tap_count = conv_weight.shape[0]
    tokens = inputs.reshape(row_count, model_width).astype(jnp.float32)
    positions = lax.axis_index("seq") * length + lax.broadcasted_iota(
        jnp.int32, (micro_count, seq_local, length), 2
    )
    valid_rows = (positions < lengths[:, :, None]).astype(jnp.float32).reshape(row_count, 1)
    in_full, out_full, gate_up_full, down_full = (
        lax.all_gather(input_weight, ("dp", "seq"), axis=0, tiled=True),
        lax.all_gather(output_weight, ("dp", "seq"), axis=0, tiled=True),
        lax.all_gather(gate_up_weight, ("dp", "seq"), axis=0, tiled=True),
        lax.all_gather(down_weight, ("dp", "seq"), axis=0, tiled=True),
    )
    normed, first_pullback = jax.vjp(rms_norm, tokens, first_gain)
    normed_low = normed.astype(jnp.bfloat16)
    projected = jnp.dot(normed_low, in_full, preferred_element_type=jnp.float32)
    mixed_low = (
        projected[:, : 3 * key_width].astype(jnp.bfloat16).reshape(seq_count, length, 3 * key_width)
    )
    gate_raw = projected[:, 3 * key_width :].reshape(seq_count, length, key_width)
    logits = jnp.dot(normed_low, decay_weight, preferred_element_type=jnp.float32).reshape(
        seq_count, length, 2 * head_count
    )
    left_edge = shifted(mixed_low[:, length - tap_count + 1 :], "seq", 1)
    packed = jnp.concatenate([left_edge, mixed_low], 1).astype(jnp.float32)
    queries, probes, writes, decays, strengths = prepare(
        packed, logits, conv_weight, decay_log, decay_bias
    )
    blank_state = jnp.zeros((seq_count, head_count, head_size, head_size), jnp.float32)
    identity_maps = jnp.broadcast_to(jnp.eye(head_size, dtype=jnp.float32), blank_state.shape)
    joined_writes = jnp.concatenate([writes, jnp.zeros_like(writes)], -1)
    joined_outputs, joined_end = delta_local(
        queries,
        probes,
        joined_writes,
        decays,
        strengths,
        jnp.concatenate([blank_state, identity_maps], -1),
    )
    own_out = joined_outputs[..., :head_size]
    carry_out = joined_outputs[..., head_size:]
    offset = joined_end[..., :head_size]
    transfer = joined_end[..., head_size:]
    state_in = carry_forward(transfer, offset)
    mixer_out = own_out + jnp.einsum("bhtd,bhde->bhte", carry_out, state_in, precision=HIGH)
    gated_rows, finish_pullback = jax.vjp(finish, mixer_out, gate_raw, head_gain)
    gated_low = gated_rows.reshape(row_count, key_width).astype(jnp.bfloat16)
    hidden = tokens + jnp.dot(gated_low, out_full, preferred_element_type=jnp.float32)
    second, second_pullback = jax.vjp(rms_norm, hidden, second_gain)
    second_low = second.astype(jnp.bfloat16)
    gate_up = jnp.dot(second_low, gate_up_full, preferred_element_type=jnp.float32)
    ffn_width = gate_up.shape[1] // 2
    activated, swish_pullback = jax.vjp(
        swish_product, gate_up[:, :ffn_width], gate_up[:, ffn_width:]
    )
    activated_low = activated.astype(jnp.bfloat16)
    final_rows = hidden + jnp.dot(activated_low, down_full, preferred_element_type=jnp.float32)
    result = valid_rows * final_rows
    upstream = valid_rows * cotangent.reshape(row_count, model_width).astype(jnp.float32)
    out_err = upstream.astype(jnp.bfloat16)
    down_term = jnp.einsum("nf,nd->fd", activated_low, out_err, preferred_element_type=jnp.float32)
    activated_grad = jnp.einsum("nd,fd->nf", out_err, down_full, preferred_element_type=jnp.float32)
    gate_grad, up_grad = swish_pullback(activated_grad)
    gate_up_err = jnp.concatenate([gate_grad, up_grad], 1).astype(jnp.bfloat16)
    gate_up_term = jnp.einsum(
        "nd,nf->df", second_low, gate_up_err, preferred_element_type=jnp.float32
    )
    second_grad = jnp.einsum(
        "nf,df->nd", gate_up_err, gate_up_full, preferred_element_type=jnp.float32
    )
    hidden_part, second_gain_grad = second_pullback(second_grad)
    hidden_grad = upstream + hidden_part
    gate_up_share, down_share = (
        scatter_rows(gate_up_term.astype(BF16), ("dp", "seq")).astype(F32),
        scatter_rows(down_term.astype(BF16), ("dp", "seq")).astype(F32),
    )
    branch_err = hidden_grad.astype(jnp.bfloat16)
    output_term = jnp.einsum("nk,nd->kd", gated_low, branch_err, preferred_element_type=jnp.float32)
    gated_grad = jnp.einsum("nd,kd->nk", branch_err, out_full, preferred_element_type=jnp.float32)
    mixer_grad, gate_raw_grad, head_gain_grad = finish_pullback(
        gated_grad.reshape(seq_count, length, key_width)
    )
    source = jnp.einsum("bhtd,bhte->bhde", carry_out, mixer_grad, precision=HIGH)
    state_out_grad = carry_back(transfer, source)
    _, core_pullback = jax.vjp(
        mixer_core, packed, logits, conv_weight, decay_log, decay_bias, state_in
    )
    packed_grad, logits_grad, conv_grad, decay_log_grad, decay_bias_grad, _ = core_pullback(
        (mixer_grad, state_out_grad)
    )
    edge_grad = shifted(packed_grad[:, : tap_count - 1].astype(jnp.bfloat16), "seq", -1).astype(
        jnp.float32
    )
    mixed_grad = packed_grad[:, tap_count - 1 :] + jnp.pad(
        edge_grad, ((0, 0), (length - tap_count + 1, 0), (0, 0))
    )
    in_err = jnp.concatenate(
        [mixed_grad.reshape(row_count, 3 * key_width), gate_raw_grad.reshape(row_count, key_width)],
        1,
    ).astype(jnp.bfloat16)
    input_term = jnp.einsum("nd,nk->dk", normed_low, in_err, preferred_element_type=jnp.float32)
    logits_flat = logits_grad.reshape(row_count, 2 * head_count)
    decay_weight_grad = jnp.einsum(
        "nd,nk->dk", normed_low.astype(jnp.float32), logits_flat, precision=HIGH
    )
    normed_grad = jnp.einsum("nk,dk->nd", in_err, in_full, preferred_element_type=jnp.float32)
    normed_grad = normed_grad + jnp.einsum(
        "nk,dk->nd", logits_flat, decay_weight.astype(jnp.float32), precision=HIGH
    )
    token_part, first_gain_grad = first_pullback(normed_grad)
    inputs_grad = hidden_grad + token_part
    input_share, output_share = (
        scatter_rows(input_term.astype(BF16), ("dp", "seq")).astype(F32),
        scatter_rows(output_term.astype(BF16), ("dp", "seq")).astype(F32),
    )
    small_sums = lax.psum(
        (
            first_gain_grad,
            decay_weight_grad,
            conv_grad,
            decay_log_grad,
            decay_bias_grad,
            head_gain_grad,
            second_gain_grad,
        ),
        ("dp", "seq"),
    )
    return (
        result.reshape(inputs.shape),
        inputs_grad.reshape(inputs.shape),
        small_sums[0],
        input_share,
        small_sums[1],
        small_sums[2],
        small_sums[3],
        small_sums[4],
        small_sums[5],
        output_share,
        small_sums[6],
        gate_up_share,
        down_share,
    )


F32 = jnp.float32
BF16 = jnp.bfloat16


def lasting(microseconds):
    return pl.CostEstimate(flops=0, bytes_accessed=int(microseconds * 3.5e6), transcendentals=0)


def parts(value):
    top = value.astype(BF16)
    return (top, (value - top.astype(F32)).astype(BF16))


def contract(left, right, right_dim):
    lhs = jnp.concatenate([left[0], left[1], left[0]], 1)
    rhs = jnp.concatenate([right[0], right[0], right[1]], right_dim)
    return lax.dot_general(lhs, rhs, (((1,), (right_dim,)), ((), ())), preferred_element_type=F32)


def mm(left, right):
    return contract(left, right, 0)


def mm_nt(left, right):
    return contract(left, right, 1)


def ones_dot(ones, value):
    first = value.astype(BF16)
    rest = value - first.astype(F32)
    second = rest.astype(BF16)
    third = (rest - second.astype(F32)).astype(BF16)
    return (
        jnp.dot(ones, first, preferred_element_type=F32)
        + jnp.dot(ones, second, preferred_element_type=F32)
        + jnp.dot(ones, third, preferred_element_type=F32)
    )


def lower_inverses(strict_lowers, row_index, col_index):
    extent = row_index.shape[0]

    def below(width):
        same = (row_index // (2 * width)) == (col_index // (2 * width))
        return same & ((row_index // width) % 2 == 1) & ((col_index // width) % 2 == 0)

    mask = below(1)
    identity = jnp.where(row_index == col_index, 1.0, 0.0)
    inverses = [identity - jnp.where(mask, strict, 0.0) for strict in strict_lowers]
    width = 2
    while width < extent:
        mask = below(width)
        splits = [parts(inverse) for inverse in inverses]
        blocks = [parts(jnp.where(mask, strict, 0.0)) for strict in strict_lowers]
        halves = [mm(split, block) for split, block in zip(splits, blocks)]
        inverses = [
            inverse - mm(parts(half), split)
            for inverse, half, split in zip(inverses, halves, splits)
        ]
        width *= 2
    return inverses


def active_rows(before, rows, taps):
    extended = jnp.concatenate([before, rows], 0)
    count = rows.shape[0]
    tap_count = taps.shape[0]
    start = before.shape[0] - tap_count + 1
    shifts = [extended[start + j : start + j + count] for j in range(tap_count)]
    total = taps[0:1] * shifts[0]
    for j in range(1, tap_count):
        total = total + taps[j : j + 1] * shifts[j]
    return (total, shifts)


def soft_plus(value):
    return jnp.maximum(value, 0.0) + jnp.log(1.0 + jnp.exp(-jnp.abs(value)))


def sigmoid(value):
    return 1.0 / (1.0 + jnp.exp(-value))


def unit(vectors):
    scale = lax.rsqrt(jnp.sum(vectors * vectors, -1, keepdims=True) + 1e-06)
    return (vectors * scale, scale)


def unit_back(vectors, scale, grad):
    inner = jnp.sum(vectors * grad, -1, keepdims=True)
    return scale * grad - vectors * (scale * scale * scale * inner)


def decay_terms(logit, param_ref, heads, ones):
    shifted_logit = logit + param_ref[1:2, :]
    lane = lax.broadcasted_iota(jnp.int32, logit.shape, 1)
    decays = jnp.where(lane < heads, -jnp.exp(param_ref[0:1, :]) * soft_plus(shifted_logit), 0.0)
    strengths = sigmoid(logit)
    running = ones_dot(ones, decays)
    return (shifted_logit, decays, strengths, running)


def mixer_forward(
    mixed_ref,
    gate_ref,
    logit_ref,
    taps_ref,
    param_ref,
    gain_ref,
    own_ref,
    gated_ref,
    memory_ref,
    inverse_ref,
    fresh_ref,
    out_ref,
    all_ref,
    state_ref,
    halo_ref,
    send_sems,
    recv_sems,
    local_sem,
):
    seqs, span, _ = mixed_ref.shape
    heads, head_size = memory_ref.shape[1], memory_ref.shape[2]
    gather_in_steps(own_ref, all_ref, send_sems, recv_sems, local_sem)

    @pl.when(pl.program_id(0) == 0)
    def _():
        state_ref[...] = jnp.zeros_like(state_ref)
        halo_ref[...] = jnp.zeros_like(halo_ref)

    row_index = lax.broadcasted_iota(jnp.int32, (span, span), 0)
    col_index = lax.broadcasted_iota(jnp.int32, (span, span), 1)
    ones = jnp.where(col_index <= row_index, 1.0, 0.0).astype(BF16)
    taps = taps_ref[...]
    width = heads * head_size
    pairs = [(m, h) for m in range(seqs) for h in range(heads)]
    active, decay_parts = [], []
    for m in range(seqs):
        rows = mixed_ref[m].astype(F32)
        convolved, _ = active_rows(halo_ref[m], rows, taps)
        halo_ref[m] = rows[span - 8 :]
        active.append(convolved * sigmoid(convolved))
        _, _, strengths, running = decay_terms(logit_ref[m], param_ref, heads, ones)
        decay_parts.append((strengths, running, jnp.transpose(strengths), jnp.transpose(running)))

    def columns(m, h, block):
        start = block * width + h * head_size
        return active[m][:, start : start + head_size]

    queries = [unit(columns(m, h, 0))[0] * head_size ** (-0.5) for m, h in pairs]
    probes = [unit(columns(m, h, 1))[0] for m, h in pairs]
    products = [
        mm_nt(parts(jnp.concatenate([query, probe], 0)), parts(probe))
        for query, probe in zip(queries, probes)
    ]
    stricts, mixings, scales, kepts, lasts = [], [], [], [], []
    for (m, h), probe, product in zip(pairs, probes, products):
        strengths, running, strength_rows, running_rows = decay_parts[m]
        run = running[:, h : h + 1]
        last = running[span - 1 : span, h : h + 1]
        weight_row = strength_rows[heads + h : heads + h + 1, :]
        weight_col = strengths[:, heads + h : heads + h + 1]
        faded = jnp.exp(jnp.minimum(run - running_rows[h : h + 1, :], 0.0)) * weight_row
        mixings.append(jnp.where(col_index <= row_index, faded * product[:span], 0.0))
        stricts.append(jnp.where(col_index < row_index, faded * product[span:], 0.0))
        scales.append(jnp.exp(run))
        kepts.append(jnp.transpose(jnp.exp(last - run) * weight_col * probe))
        lasts.append(jnp.exp(last))
    inverses = lower_inverses(stricts, row_index, col_index)
    boths = [
        mm(parts(inverse), parts(jnp.concatenate([columns(m, h, 2), scale * probe], 1)))
        for (m, h), inverse, scale, probe in zip(pairs, inverses, scales, probes)
    ]
    memories = [state_ref[m, h] for m, h in pairs]
    reads = [
        mm(parts(jnp.concatenate([both[:, head_size:], scale * query], 0)), parts(memory))
        for both, scale, query, memory in zip(boths, scales, queries, memories)
    ]
    freshes = [both[:, :head_size] - read[:span] for both, read in zip(boths, reads)]
    fresh_parts = [parts(fresh) for fresh in freshes]
    for (m, h), last, memory, kept, fresh in zip(pairs, lasts, memories, kepts, fresh_parts):
        state_ref[m, h] = last * memory + mm(parts(kept), fresh)
    outs = [
        read[span:] + mm(parts(mixing), fresh)
        for read, mixing, fresh in zip(reads, mixings, fresh_parts)
    ]
    for (m, h), memory, inverse, fresh, mixer_out in zip(pairs, memories, inverses, freshes, outs):
        own = slice(h * head_size, (h + 1) * head_size)
        memory_ref[m, h] = memory
        inverse_ref[m, h] = inverse
        fresh_ref[m, :, own] = fresh
        out_ref[m, :, own] = mixer_out
        scale = lax.rsqrt(jnp.mean(mixer_out * mixer_out, -1, keepdims=True) + 1e-05)
        gate = gate_ref[m, :, own]
        gated_ref[m, :, own] = (
            mixer_out * scale * gain_ref[...] * (gate * sigmoid(gate))
        ).astype(BF16)


def mixer_backward(
    mixed_ref,
    before_ref,
    gate_ref,
    logit_ref,
    taps_ref,
    param_ref,
    gain_ref,
    memory_ref,
    inverse_ref,
    fresh_ref,
    out_ref,
    grad_ref,
    part_ref,
    error_ref,
    logit_grad_ref,
    taps_grad_ref,
    param_grad_ref,
    gain_grad_ref,
    sum_ref,
    state_ref,
    halo_ref,
    *scatter_refs,
):
    seqs, span, _ = mixed_ref.shape
    heads, head_size = memory_ref.shape[1], memory_ref.shape[2]
    step = pl.program_id(0)
    scatter_in_steps(part_ref, sum_ref, *scatter_refs)

    @pl.when(step == 0)
    def _():
        state_ref[...] = jnp.zeros_like(state_ref)
        halo_ref[...] = jnp.zeros_like(halo_ref)
        taps_grad_ref[...] = jnp.zeros_like(taps_grad_ref)
        param_grad_ref[...] = jnp.zeros_like(param_grad_ref)
        gain_grad_ref[...] = jnp.zeros_like(gain_grad_ref)

    first = step == pl.num_programs(0) - 1
    row_index = lax.broadcasted_iota(jnp.int32, (span, span), 0)
    col_index = lax.broadcasted_iota(jnp.int32, (span, span), 1)
    ones = jnp.where(col_index <= row_index, 1.0, 0.0).astype(BF16)
    ones_back = jnp.where(col_index >= row_index, 1.0, 0.0).astype(BF16)
    taps = taps_ref[...]
    tap_count = taps.shape[0]
    width = heads * head_size
    gain = gain_ref[...]
    edge = before_ref.shape[1]
    pairs = [(m, h) for m in range(seqs) for h in range(heads)]
    everyone = range(len(pairs))
    active, openings, curves, shifts, decay_parts = [], [], [], [], []
    for m in range(seqs):
        rows = mixed_ref[m].astype(F32)
        before = jnp.where(first, 0.0, before_ref[m].astype(F32))[edge - 8 :]
        convolved, moved = active_rows(before, rows, taps)
        opening = sigmoid(convolved)
        active.append(convolved * opening)
        curves.append(convolved)
        openings.append(opening)
        shifts.append(moved)
        shifted_logit, decays, strengths, running = decay_terms(
            logit_ref[m], param_ref, heads, ones
        )
        decay_parts.append(
            (
                shifted_logit,
                decays,
                strengths,
                running,
                jnp.transpose(strengths),
                jnp.transpose(running),
            )
        )

    def columns(m, h, block):
        start = block * width + h * head_size
        return active[m][:, start : start + head_size]

    raw_queries = [columns(m, h, 0) for m, h in pairs]
    raw_probes = [columns(m, h, 1) for m, h in pairs]
    query_units = [unit(value) for value in raw_queries]
    probe_units = [unit(value) for value in raw_probes]
    queries = [value * head_size ** (-0.5) for value, _ in query_units]
    probes = [value for value, _ in probe_units]
    gate_grads, out_grads = [], []
    for m, h in pairs:
        own = slice(h * head_size, (h + 1) * head_size)
        mixer_out = out_ref[m, :, own]
        gate = gate_ref[m, :, own]
        gated_grad = grad_ref[m, :, own].astype(F32)
        scale = lax.rsqrt(jnp.mean(mixer_out * mixer_out, -1, keepdims=True) + 1e-05)
        gate_open = sigmoid(gate)
        normal = mixer_out * scale
        gate_grads.append(
            gated_grad * normal * gain * (gate_open * (1.0 + gate * (1.0 - gate_open)))
        )
        normal_grad = gated_grad * (gate * gate_open)
        gain_grad_ref[0:1, :] += jnp.sum(normal_grad * normal, 0, keepdims=True)
        weighted = normal_grad * gain
        out_grads.append(
            scale * (weighted - normal * jnp.mean(weighted * normal, -1, keepdims=True))
        )

    probe_parts = [parts(value) for value in probes]
    query_parts = [parts(value) for value in queries]
    out_grad_parts = [parts(value) for value in out_grads]
    state_grads = [state_ref[m, h] for m, h in pairs]
    state_grad_parts = [parts(value) for value in state_grads]
    products = [
        mm_nt(parts(jnp.concatenate([query, probe], 0)), probe_part)
        for query, probe, probe_part in zip(queries, probes, probe_parts)
    ]
    probe_states = [mm(left, right) for left, right in zip(probe_parts, state_grad_parts)]
    weight_rows, spreads, fade_queries, fade_probes = [], [], [], []
    scales, end_scales, remainings, kepts = [], [], [], []
    for (m, h), product in zip(pairs, products):
        _, _, strengths, running, strength_rows, running_rows = decay_parts[m]
        run = running[:, h : h + 1]
        last = running[span - 1 : span, h : h + 1]
        weight_row = strength_rows[heads + h : heads + h + 1, :]
        weight_rows.append(weight_row)
        faded = jnp.exp(jnp.minimum(run - running_rows[h : h + 1, :], 0.0))
        spreads.append(faded * weight_row)
        fade_queries.append(jnp.where(col_index <= row_index, faded * product[:span], 0.0))
        fade_probes.append(jnp.where(col_index < row_index, faded * product[span:], 0.0))
        scales.append(jnp.exp(run))
        end_scales.append(jnp.exp(last))
        remaining = jnp.exp(last - run)
        remainings.append(remaining)
        kepts.append(remaining * strengths[:, heads + h : heads + h + 1])
    fresh_grads = [
        mm(parts(jnp.transpose(fade * weight_row)), out_grad) + kept * probe_state
        for fade, weight_row, out_grad, kept, probe_state in zip(
            fade_queries, weight_rows, out_grad_parts, kepts, probe_states
        )
    ]
    solves = [
        mm(parts(jnp.transpose(inverse_ref[m, h])), parts(fresh_grad))
        for (m, h), fresh_grad in zip(pairs, fresh_grads)
    ]
    for k in everyone:
        m, h = pairs[k]
        state_ref[m, h] = (
            end_scales[k] * state_grads[k]
            + mm(parts(jnp.transpose(queries[k])), parts(scales[k] * out_grads[k]))
            - mm(parts(jnp.transpose(probes[k])), parts(scales[k] * solves[k]))
        )
    freshes = [fresh_ref[m, :, h * head_size : (h + 1) * head_size] for m, h in pairs]
    memories = [memory_ref[m, h] for m, h in pairs]
    fresh_parts = [parts(value) for value in freshes]
    joined = [
        parts(jnp.concatenate([out_grad, solved], 0)) for out_grad, solved in zip(out_grads, solves)
    ]
    outers = [mm_nt(both, fresh) for both, fresh in zip(joined, fresh_parts)]
    throughs = [mm_nt(both, parts(memory)) for both, memory in zip(joined, memories)]
    mixing_grads = [jnp.where(col_index <= row_index, outer[:span], 0.0) for outer in outers]
    strict_grads = [jnp.where(col_index < row_index, -outer[span:], 0.0) for outer in outers]
    mix_fades = [grad * spread for grad, spread in zip(mixing_grads, spreads)]
    strict_fades = [grad * spread for grad, spread in zip(strict_grads, spreads)]
    on_probes = [
        mm(parts(jnp.concatenate([mix, strict], 0)), probe)
        for mix, strict, probe in zip(mix_fades, strict_fades, probe_parts)
    ]
    fresh_states = [mm_nt(fresh, grad) for fresh, grad in zip(fresh_parts, state_grad_parts)]
    turned = [
        mm(parts(jnp.transpose(mix)), query) + mm(parts(jnp.transpose(strict)), probe)
        for mix, strict, query, probe in zip(mix_fades, strict_fades, query_parts, probe_parts)
    ]
    active_grads = [[None] * (3 * heads) for _ in range(seqs)]
    col_terms = [jnp.zeros((span, span), F32)] * seqs
    row_terms = [jnp.zeros((span, span), F32)] * seqs
    for k in everyone:
        m, h = pairs[k]
        out_state = scales[k] * throughs[k][:span]
        solved_state = scales[k] * throughs[k][span:]
        query_grad = out_state + on_probes[k][:span]
        probe_grad = kepts[k] * fresh_states[k] - solved_state + on_probes[k][span:] + turned[k]
        pair_terms = mixing_grads[k] * fade_queries[k] + strict_grads[k] * fade_probes[k]
        weighted_pairs = pair_terms * weight_rows[k]
        probe_fresh = jnp.sum(probe_states[k] * freshes[k], -1, keepdims=True)
        run_col = (
            jnp.sum(out_state * queries[k] - solved_state * probes[k], -1, keepdims=True)
            + jnp.sum(weighted_pairs, -1, keepdims=True)
            - kepts[k] * probe_fresh
        )
        last_grad = jnp.sum(kepts[k] * probe_fresh, 0, keepdims=True) + end_scales[k] * jnp.sum(
            jnp.sum(state_grads[k] * memories[k], -1, keepdims=True), 0, keepdims=True
        )
        run_col = run_col + jnp.where(row_index[:, 0:1] == span - 1, last_grad, 0.0)
        col_terms[m] = jnp.where(col_index == h, run_col, col_terms[m])
        col_terms[m] = jnp.where(
            col_index == heads + h, remainings[k] * probe_fresh, col_terms[m]
        )
        row_terms[m] = jnp.where(
            row_index == h, -jnp.sum(weighted_pairs, 0, keepdims=True), row_terms[m]
        )
        row_terms[m] = jnp.where(
            row_index == heads + h, jnp.sum(pair_terms, 0, keepdims=True), row_terms[m]
        )
        active_grads[m][h] = unit_back(
            raw_queries[k], query_units[k][1], query_grad
        ) * head_size ** (-0.5)
        active_grads[m][heads + h] = unit_back(raw_probes[k], probe_units[k][1], probe_grad)
        active_grads[m][2 * heads + h] = solves[k]

    for m in range(seqs):
        shifted_logit, decays, strengths = decay_parts[m][:3]
        terms = col_terms[m] + jnp.transpose(row_terms[m])
        decay_grad = ones_dot(ones_back, terms)
        shifted_grad = decay_grad * -jnp.exp(param_ref[0:1, :]) * sigmoid(shifted_logit)
        logit_grad = jnp.where(
            col_index < heads,
            shifted_grad,
            jnp.where(col_index < 2 * heads, terms * strengths * (1.0 - strengths), 0.0),
        )
        logit_top, logit_rest = parts(logit_grad)
        logit_grad_ref[m] = (
            logit_top.astype(F32) + pltpu.roll(logit_rest.astype(F32), span // 2, 1)
        ).astype(BF16)
        decay_lane = col_index[0:1] < heads
        param_grad_ref[0:1, :] += jnp.sum(
            jnp.where(decay_lane, decay_grad * decays, 0.0), 0, keepdims=True
        )
        param_grad_ref[1:2, :] += jnp.sum(
            jnp.where(decay_lane, shifted_grad, 0.0), 0, keepdims=True
        )
        conv_grad = jnp.concatenate(active_grads[m], 1) * (
            openings[m] * (1.0 + curves[m] * (1.0 - openings[m]))
        )
        extended = jnp.concatenate([conv_grad, halo_ref[m]], 0)
        halo_ref[m] = conv_grad[:8]
        mixed_grad = jnp.zeros_like(conv_grad)
        for j in range(tap_count):
            reach = tap_count - 1 - j
            mixed_grad = mixed_grad + taps[j : j + 1] * extended[reach : reach + span]
            taps_grad_ref[j : j + 1, :] += jnp.sum(conv_grad * shifts[m][j], 0, keepdims=True)
        error_ref[m] = jnp.concatenate(
            [mixed_grad] + gate_grads[m * heads : (m + 1) * heads], 1
        ).astype(BF16)


def run_forward(mixed, gate, logits, taps, params, gain, heads, own, collective_id):
    steps, seqs, span, _ = mixed.shape
    anywhere = pl.BlockSpec(memory_space=pl.ANY)
    head_size = gain.shape[1]
    width = heads * head_size

    def rows(columns):
        return pl.BlockSpec((None, seqs, span, columns), lambda j: (j, 0, 0, 0))

    def squares():
        return pl.BlockSpec((None, seqs, heads, head_size, head_size), lambda j: (j, 0, 0, 0, 0))

    def whole(array):
        return pl.BlockSpec(array.shape, lambda j: (0, 0))

    square = jax.ShapeDtypeStruct((steps, seqs, heads, head_size, head_size), F32)
    lower = jax.ShapeDtypeStruct((steps, seqs, heads, span, span), F32)
    flat = jax.ShapeDtypeStruct((steps, seqs, span, width), F32)
    return pl.pallas_call(
        mixer_forward,
        grid=(steps,),
        in_specs=[
            rows(3 * width),
            rows(width),
            rows(logits.shape[-1]),
            whole(taps),
            whole(params),
            whole(gain),
            anywhere,
        ],
        out_specs=[rows(width), squares(), squares(), rows(width), rows(width), anywhere],
        out_shape=[
            jax.ShapeDtypeStruct((steps, seqs, span, width), BF16),
            square,
            lower,
            flat,
            flat,
            jax.ShapeDtypeStruct((steps,) + own.shape, own.dtype),
        ],
        scratch_shapes=[
            pltpu.VMEM((seqs, heads, head_size, head_size), F32),
            pltpu.VMEM((seqs, 8, 3 * width), F32),
            pltpu.SemaphoreType.DMA((9,)),
            pltpu.SemaphoreType.DMA((9,)),
            pltpu.SemaphoreType.DMA,
        ],
        compiler_params=pltpu.CompilerParams(
            collective_id=collective_id, has_side_effects=True, vmem_limit_bytes=VMEM_LIMIT
        ),
        cost_estimate=lasting(55),
        name="mixer_forward",
    )(mixed, gate, logits, taps, params, gain, own)


def run_backward(
    mixed, gate, logits, taps, params, gain, memory, inverse, fresh, out, grad, part, collective_id
):
    steps, seqs, span, _ = mixed.shape
    _, part_rows, columns = part.shape
    heads, head_size = memory.shape[2], memory.shape[3]
    width = heads * head_size
    edge = 16

    def rows(columns):
        return pl.BlockSpec((None, seqs, span, columns), lambda j: (steps - 1 - j, 0, 0, 0))

    def squares():
        return pl.BlockSpec(
            (None, seqs, heads, head_size, head_size), lambda j: (steps - 1 - j, 0, 0, 0, 0)
        )

    def whole(shape):
        return pl.BlockSpec(shape, lambda j: (0, 0))

    before = pl.BlockSpec(
        (None, seqs, edge, 3 * width),
        lambda j: (jnp.maximum(steps - 2 - j, 0), 0, span // edge - 1, 0),
    )
    return pl.pallas_call(
        mixer_backward,
        grid=(steps,),
        in_specs=[
            rows(3 * width),
            before,
            rows(width),
            rows(logits.shape[-1]),
            whole(taps.shape),
            whole(params.shape),
            whole(gain.shape),
            squares(),
            squares(),
            rows(width),
            rows(width),
            rows(width),
            pl.BlockSpec(memory_space=pl.ANY),
        ],
        out_specs=[
            rows(4 * width),
            rows(logits.shape[-1]),
            whole((8, 3 * width)),
            whole((8, logits.shape[-1])),
            whole((8, head_size)),
            whole((part_rows, columns)),
        ],
        out_shape=[
            jax.ShapeDtypeStruct((steps, seqs, span, 4 * width), BF16),
            jax.ShapeDtypeStruct(logits.shape, BF16),
            jax.ShapeDtypeStruct((8, 3 * width), F32),
            jax.ShapeDtypeStruct((8, logits.shape[-1]), F32),
            jax.ShapeDtypeStruct((8, head_size), F32),
            jax.ShapeDtypeStruct((part_rows, columns), F32),
        ],
        scratch_shapes=[
            pltpu.VMEM((seqs, heads, head_size, head_size), F32),
            pltpu.VMEM((seqs, 8, 3 * width), F32),
            pltpu.VMEM((4, part_rows, columns), BF16),
            pltpu.VMEM((4, part_rows, columns), BF16),
            pltpu.VMEM((part_rows, columns), BF16),
            pltpu.VMEM((2, part_rows, columns), BF16),
            pltpu.SemaphoreType.DMA((10,)),
            pltpu.SemaphoreType.DMA((10,)),
            pltpu.SemaphoreType.DMA((4,)),
        ],
        compiler_params=pltpu.CompilerParams(
            collective_id=collective_id, has_side_effects=True, vmem_limit_bytes=VMEM_LIMIT
        ),
        cost_estimate=lasting(55),
        name="mixer_backward",
    )(mixed, mixed, gate, logits, taps, params, gain, memory, inverse, fresh, out, grad, part)


def gather_rows(value, axis):
    return lax.all_gather(value, axis, axis=0, tiled=True)


def scatter_rows(value, axis):
    return lax.psum_scatter(value, axis, scatter_dimension=0, tiled=True)


def plane_peers():
    me = lax.axis_index("seq")
    sibling = me + 1 - 2 * (me % 2)
    across = me + 2 - 4 * ((me // 2) % 2)
    along = me + 4 - 8 * (me // 4)
    return (me, sibling, across, along)


def greet(peers):
    barrier = pltpu.get_barrier_semaphore()
    for peer in peers:
        pl.semaphore_signal(
            barrier, inc=1, device_id={"seq": peer}, device_id_type=pl.DeviceIdType.MESH
        )
    pl.semaphore_wait(barrier, len(peers))


def send_to(peer, source, target, send_sem, recv_sem):
    return pltpu.make_async_remote_copy(
        src_ref=source,
        dst_ref=target,
        send_sem=send_sem,
        recv_sem=recv_sem,
        device_id={"seq": peer},
        device_id_type=pl.DeviceIdType.MESH,
    )


def gather_phases(own_ref, all_ref, send_sems, recv_sems, local_sem, start):
    me, sibling, across, along = plane_peers()
    far = along + across - me
    half = own_ref.shape[0] // 2
    upper, lower = pl.ds(0, half), pl.ds(half, half)
    copies = []

    def send(peer, source, target):
        k = start + len(copies)
        copy = send_to(peer, source, target, send_sems.at[k], recv_sems.at[k])
        copy.start()
        copies.append(copy)

    keep = pltpu.make_async_copy(own_ref, all_ref.at[me], local_sem)
    keep.start()
    send(across, own_ref, all_ref.at[me])
    send(along, own_ref, all_ref.at[me])
    send(sibling, own_ref, all_ref.at[me])
    yield
    copies[0].wait_recv()
    send(along, all_ref.at[across, upper], all_ref.at[across, upper])
    copies[1].wait_recv()
    send(across, all_ref.at[along, lower], all_ref.at[along, lower])
    send(sibling, all_ref.at[across], all_ref.at[across])
    send(sibling, all_ref.at[along], all_ref.at[along])
    yield
    copies[3].wait_recv()
    send(sibling, all_ref.at[far, upper], all_ref.at[far, upper])
    copies[4].wait_recv()
    send(sibling, all_ref.at[far, lower], all_ref.at[far, lower])
    yield
    for k in (2, 5, 6, 7, 8):
        copies[k].wait_recv()
    for copy in copies:
        copy.wait_send()
    keep.wait()
    yield


def chain_hops(all_ref, up_send, up_recv, down_send, down_recv):
    depth = all_ref.shape[0]
    place = lax.axis_index("dp")
    above, below = lax.rem(place + 1, depth), lax.rem(place + depth - 1, depth)

    def hop(slot, peer, send_sem, recv_sem):
        return pltpu.make_async_remote_copy(
            src_ref=all_ref.at[slot],
            dst_ref=all_ref.at[slot],
            send_sem=send_sem,
            recv_sem=recv_sem,
            device_id={"dp": peer},
            device_id_type=pl.DeviceIdType.MESH,
        )

    hops = []
    for t in range(depth - 1):
        up = hop(lax.rem(place + depth - t, depth), above, up_send.at[t], up_recv.at[t])
        down = hop(lax.rem(place + t, depth), below, down_send.at[t], down_recv.at[t])
        below_slot, above_slot = place + depth - 1 - t, place + 1 + t
        hops.append(
            (
                (up, (place < depth - 1) & (place >= t), place > t, lax.rem(below_slot, depth)),
                (
                    down,
                    (place > 0) & (place + t < depth),
                    above_slot < depth,
                    lax.rem(above_slot, depth),
                ),
            )
        )
    return hops


def hop_start(hop):
    for copy, leaves, _, _ in hop:
        pl.when(leaves)(copy.start)


def hop_arrive(hop):
    for copy, _, arrives, _ in hop:
        pl.when(arrives)(copy.wait_recv)


def hop_finish(hops):
    for hop in hops:
        for copy, leaves, _, _ in hop:
            pl.when(leaves)(copy.wait_send)


def greet_all(ring, depth):
    me, place = lax.axis_index("seq"), lax.axis_index("dp")
    barrier = pltpu.get_barrier_semaphore()
    for axis, index, size in (("seq", me, ring), ("dp", place, depth)):
        for k in range(1, size):
            pl.semaphore_signal(
                barrier,
                inc=1,
                device_id={axis: lax.rem(index + k, size)},
                device_id_type=pl.DeviceIdType.MESH,
            )
    pl.semaphore_wait(barrier, ring + depth - 2)


def spread_units(piece, target_ref, depth):
    ring, _, columns = piece.shape
    own = columns // (2 * depth)
    for k in range(2 * depth):
        block = jnp.concatenate([piece[s, :, k * own : (k + 1) * own] for s in range(ring)], 1)
        target_ref[:, k * ring * own : (k + 1) * ring * own] = block.astype(target_ref.dtype)


def exchange_copies(cut_ref, land, send_sems, recv_sems, start):
    ring = cut_ref.shape[0]
    me = lax.axis_index("seq")
    copies = []
    for k in range(1, ring):
        peer = lax.rem(me + k, ring)
        copy = send_to(
            peer, cut_ref.at[peer], land, send_sems.at[start + k - 1], recv_sems.at[start + k - 1]
        )
        copy.start()
        copies.append(copy)
    return copies


def plane_open_kernel(
    first_ref,
    weight_hbm,
    pair_hbm,
    lanes_hbm,
    first_all_hbm,
    weight_all_hbm,
    pair_all_ref,
    mixed_ref,
    gate_ref,
    logit_ref,
    first_all_ref,
    weight_all_ref,
    pair_ref,
    cut_ref,
    lanes_ref,
    total_ref,
    send_sems,
    recv_sems,
    local_sems,
    *chain_sems,
):
    place, me = lax.axis_index("dp"), lax.axis_index("seq")
    depth, rows = weight_all_ref.shape[0], weight_hbm.shape[0]
    ring, units = cut_ref.shape[0], cut_ref.shape[2] // 2
    width = weight_all_ref.shape[2] // 4
    load = pltpu.make_async_copy(pair_hbm, pair_ref, local_sems.at[0])
    load.start()
    lanes_load = pltpu.make_async_copy(lanes_hbm, lanes_ref, local_sems.at[3])
    lanes_load.start()
    greet_all(ring, depth)
    keeps, early = [], []
    own_rows = pl.ds(pl.multiple_of(me * rows, rows), rows)
    for block in range(4):
        target = weight_all_ref.at[place, own_rows, pl.ds(block * width, width)]

        def source(peer, block=block):
            start = pl.multiple_of((block * ring + peer) * width, width)
            return weight_hbm.at[:, pl.ds(start, width)]

        keep = pltpu.make_async_copy(source(me), target, local_sems.at[4 + block])
        keep.start()
        keeps.append(keep)
        for k in range(1, ring):
            peer = lax.rem(me + k, ring)
            spot = block * (ring - 1) + k - 1
            copy = send_to(peer, source(peer), target, send_sems.at[spot], recv_sems.at[spot])
            copy.start()
            early.append(copy)
    load.wait()
    own = units // depth
    half = pair_ref.shape[1] // 2
    for s in range(ring):
        pieces = []
        for g in range(2):
            for z in range(depth):
                start = g * half + (z * ring + s) * own
                pieces.append(pair_ref[:, start : start + own])
        cut_ref[s] = jnp.concatenate(pieces, 1)
    for copy in early:
        copy.wait_recv()
    for keep in keeps:
        keep.wait()
    base = 4 * (ring - 1)
    hops = chain_hops(weight_all_ref, *chain_sems)
    first = gather_phases(first_ref, first_all_ref, send_sems, recv_sems, local_sems.at[1], base)
    hop_start(hops[0])
    next(first)
    pair_keep = pltpu.make_async_copy(cut_ref.at[me], pair_all_ref.at[me], local_sems.at[2])
    pair_keep.start()
    later = exchange_copies(cut_ref, pair_all_ref.at[me], send_sems, recv_sems, base + 9)
    next(first)
    hop_arrive(hops[0])
    hop_start(hops[1])
    next(first)
    next(first)
    lanes_load.wait()
    deep = weight_all_ref.shape[1]

    def spread_slot(slot, fresh=False):
        def run():
            at = pl.ds(pl.multiple_of(slot * deep, deep), deep)

            @pl.loop(0, ring)
            def _(r):
                term = low_dot(first_all_ref[r, :, at], weight_all_ref[slot], NN)
                total_ref[r] = term if fresh else total_ref[r] + term

        return run

    @pl.loop(0, ring)
    def _(r):
        logit_ref[r] = low_dot(first_all_ref[r], lanes_ref[...], NN)

    spread_slot(place, True)()
    for _, _, arrives, slot in hops[0]:
        pl.when(arrives)(spread_slot(slot))
    saves = [pltpu.make_async_copy(first_all_ref, first_all_hbm, local_sems.at[0])]
    saves[0].start()
    for t in range(1, depth - 1):
        hop_arrive(hops[t])
        if t + 1 < depth - 1:
            hop_start(hops[t + 1])
        else:
            saves.append(pltpu.make_async_copy(weight_all_ref, weight_all_hbm, local_sems.at[1]))
            saves[1].start()
        for _, _, arrives, slot in hops[t]:
            pl.when(arrives)(spread_slot(slot))

    @pl.loop(0, ring)
    def _(r):
        mixed_ref[r] = total_ref[r, :, : 3 * width].astype(BF16)
        gate_ref[r] = total_ref[r, :, 3 * width :]

    for copy in later:
        copy.wait_recv()
    hop_finish(hops)
    for copy in early + later:
        copy.wait_send()
    pair_keep.wait()
    for save in saves:
        save.wait()


def plane_open(first, weight, pair, lanes, collective_id):
    ring, depth = lax.axis_size("seq"), lax.axis_size("dp")
    rows, columns = first.shape
    weight_rows = weight.shape[0]
    width = weight.shape[1] // (4 * ring)
    total = 5 * (ring - 1) + 9
    cut = jax.ShapeDtypeStruct((ring, weight_rows, pair.shape[1] // ring), pair.dtype)
    first_shape, weight_shape = (ring, rows, columns), (depth, ring * weight_rows, 4 * width)
    vmem, anywhere = pl.BlockSpec(memory_space=pltpu.VMEM), pl.BlockSpec(memory_space=pl.ANY)
    return pl.pallas_call(
        plane_open_kernel,
        out_shape=[
            jax.ShapeDtypeStruct(first_shape, BF16),
            jax.ShapeDtypeStruct(weight_shape, BF16),
            cut,
            jax.ShapeDtypeStruct((ring, rows, 3 * width), BF16),
            jax.ShapeDtypeStruct((ring, rows, width), F32),
            jax.ShapeDtypeStruct((ring, rows, lanes.shape[1]), F32),
        ],
        in_specs=[anywhere] * 4,
        out_specs=[anywhere] * 3 + [vmem] * 3,
        scratch_shapes=[
            pltpu.VMEM(first_shape, BF16),
            pltpu.VMEM(weight_shape, BF16),
            pltpu.VMEM(pair.shape, BF16),
            pltpu.VMEM(cut.shape, BF16),
            pltpu.VMEM(lanes.shape, BF16),
            pltpu.VMEM((ring, rows, 4 * width), F32),
            pltpu.SemaphoreType.DMA((total,)),
            pltpu.SemaphoreType.DMA((total,)),
            pltpu.SemaphoreType.DMA((8,)),
        ]
        + [pltpu.SemaphoreType.DMA((depth - 1,))] * 4,
        compiler_params=pltpu.CompilerParams(
            collective_id=collective_id, has_side_effects=True, vmem_limit_bytes=VMEM_LIMIT
        ),
        cost_estimate=lasting(150),
        name="plane_open",
    )(first, weight, pair, lanes)


def gather_in_steps(own_ref, all_ref, send_sems, recv_sems, local_sem):
    me, sibling, across, along = plane_peers()
    far = along + across - me
    half = own_ref.shape[0] // 2
    upper, lower = pl.ds(0, half), pl.ds(half, half)
    keep = pltpu.make_async_copy(own_ref, all_ref.at[me], local_sem)
    plan = [
        (across, own_ref, all_ref.at[me]),
        (along, own_ref, all_ref.at[me]),
        (sibling, own_ref, all_ref.at[me]),
        (along, all_ref.at[across, upper], all_ref.at[across, upper]),
        (across, all_ref.at[along, lower], all_ref.at[along, lower]),
        (sibling, all_ref.at[across], all_ref.at[across]),
        (sibling, all_ref.at[along], all_ref.at[along]),
        (sibling, all_ref.at[far, upper], all_ref.at[far, upper]),
        (sibling, all_ref.at[far, lower], all_ref.at[far, lower]),
    ]
    copies = [
        send_to(peer, source, target, send_sems.at[k], recv_sems.at[k])
        for k, (peer, source, target) in enumerate(plan)
    ]
    step, steps = pl.program_id(0), pl.num_programs(0)

    @pl.when(step == 0)
    def _():
        greet((sibling, across, along))
        keep.start()
        for k in (0, 1, 2):
            copies[k].start()

    @pl.when(step == 3)
    def _():
        copies[0].wait_recv()
        copies[1].wait_recv()
        for k in (3, 4, 5, 6):
            copies[k].start()

    @pl.when(step == 5)
    def _():
        copies[3].wait_recv()
        copies[4].wait_recv()
        for k in (7, 8):
            copies[k].start()

    @pl.when(step == steps - 1)
    def _():
        for k in (2, 5, 6, 7, 8):
            copies[k].wait_recv()
        for copy in copies:
            copy.wait_send()
        keep.wait()


def scatter_in_steps(
    part_ref,
    sum_ref,
    own_ref,
    near_ref,
    far_in_ref,
    side_in_ref,
    send_sems,
    recv_sems,
    load_sems,
):
    me, sibling, across, along = plane_peers()
    far = along + across - me
    flip = sibling - me
    rows = sum_ref.shape[0]
    half = rows // 2
    upper, lower = pl.ds(0, half), pl.ds(half, half)
    slabs = (far, across, along, me)
    loads = [
        pltpu.make_async_copy(part_ref.at[slab], own_ref.at[k], load_sems.at[k])
        for k, slab in enumerate(slabs)
    ]
    plan = [(sibling, part_ref.at[slab + flip], near_ref.at[k]) for k, slab in enumerate(slabs)]
    plan += [
        (across, own_ref.at[0, upper], far_in_ref.at[upper]),
        (along, own_ref.at[0, lower], far_in_ref.at[lower]),
        (across, own_ref.at[1, upper], side_in_ref.at[0, upper]),
        (along, own_ref.at[2, lower], side_in_ref.at[1, lower]),
        (along, own_ref.at[2, upper], side_in_ref.at[1, upper]),
        (across, own_ref.at[1, lower], side_in_ref.at[0, lower]),
    ]
    copies = [
        send_to(peer, source, target, send_sems.at[k], recv_sems.at[k])
        for k, (peer, source, target) in enumerate(plan)
    ]
    step, steps = pl.program_id(0), pl.num_programs(0)
    tall = 32

    def fold(target, other, start, size):
        @pl.loop(0, size // tall)
        def _(i):
            at = pl.ds(pl.multiple_of(start + i * tall, tall), tall)
            target[at] = (target[at].astype(F32) + other[at].astype(F32)).astype(BF16)

    def join(k):
        loads[k].wait()
        copies[k].wait_recv()
        fold(own_ref.at[k], near_ref.at[k], 0, rows)

    @pl.when(step == 0)
    def _():
        greet((sibling, across, along))
        for k in range(4):
            loads[k].start()
            copies[k].start()

    @pl.when(step == 1)
    def _():
        join(0)
        copies[4].start()
        copies[5].start()
        join(1)
        copies[6].start()
        join(2)
        copies[7].start()

    @pl.when(step == 3)
    def _():
        copies[4].wait_recv()
        fold(own_ref.at[2], far_in_ref, 0, half)
        copies[8].start()
        copies[5].wait_recv()
        fold(own_ref.at[1], far_in_ref, half, half)
        copies[9].start()

    @pl.when(step == steps - 1)
    def _():
        loads[3].wait()
        copies[3].wait_recv()
        for copy in copies[6:]:
            copy.wait_recv()

        @pl.loop(0, rows // tall)
        def _(i):
            at = pl.ds(pl.multiple_of(i * tall, tall), tall)
            sum_ref[at] = (
                own_ref[3, at].astype(F32)
                + near_ref[3, at].astype(F32)
                + side_in_ref[0, at].astype(F32)
                + side_in_ref[1, at].astype(F32)
            )

        for copy in copies:
            copy.wait_send()


def small_sum_kernel(
    own_ref, cut_ref, all_ref, joined_ref, swapped_ref, stage_ref, total_ref, send_sems, recv_sems, local_sem
):
    depth, ring = stage_ref.shape[0], all_ref.shape[0]
    place, me = lax.axis_index("dp"), lax.axis_index("seq")
    mesh_ids = pl.DeviceIdType.MESH
    columns = [lax.rem(place + k, depth) for k in range(1, depth)]
    plane = [lax.rem(me + k, ring) for k in range(1, ring)]
    greet_all(ring, depth)
    keep = pltpu.make_async_copy(cut_ref.at[me], swapped_ref.at[me], local_sem)
    keep.start()
    first = []
    for k, peer in enumerate(columns):
        copy = pltpu.make_async_remote_copy(
            src_ref=own_ref,
            dst_ref=stage_ref.at[place],
            send_sem=send_sems.at[k],
            recv_sem=recv_sems.at[k],
            device_id={"dp": peer},
            device_id_type=mesh_ids,
        )
        copy.start()
        first.append(copy)
    swaps = exchange_copies(
        cut_ref, swapped_ref.at[me], send_sems, recv_sems, depth + ring - 2
    )
    stage_ref[place] = own_ref[...]
    for copy in first:
        copy.wait_recv()
    total = stage_ref[0]
    for k in range(1, depth):
        total = total + stage_ref[k]
    total_ref[...] = total
    second = []
    for k, peer in enumerate(plane):
        copy = pltpu.make_async_remote_copy(
            src_ref=total_ref,
            dst_ref=all_ref.at[me],
            send_sem=send_sems.at[depth - 1 + k],
            recv_sem=recv_sems.at[depth - 1 + k],
            device_id={"seq": peer},
            device_id_type=mesh_ids,
        )
        copy.start()
        second.append(copy)
    all_ref[me] = total
    for copy in second + swaps:
        copy.wait_recv()
    keep.wait()
    width = cut_ref.shape[2] // 4
    for block in range(4):
        for s in range(ring):
            start = (block * ring + s) * width
            joined_ref[:, start : start + width] = swapped_ref[
                s, :, block * width : (block + 1) * width
            ].astype(F32)
    for copy in first + second + swaps:
        copy.wait_send()


def small_sum(own, cut, collective_id):
    depth, ring = lax.axis_size("dp"), lax.axis_size("seq")
    count = depth + 2 * ring - 3
    vmem, anywhere = pl.BlockSpec(memory_space=pltpu.VMEM), pl.BlockSpec(memory_space=pl.ANY)
    return pl.pallas_call(
        small_sum_kernel,
        out_shape=[
            jax.ShapeDtypeStruct((ring,) + own.shape, F32),
            jax.ShapeDtypeStruct((cut.shape[1], ring * cut.shape[2]), F32),
        ],
        in_specs=[vmem, anywhere],
        out_specs=[vmem, vmem],
        scratch_shapes=[
            pltpu.VMEM(cut.shape, cut.dtype),
            pltpu.VMEM((depth,) + own.shape, F32),
            pltpu.VMEM(own.shape, F32),
            pltpu.SemaphoreType.DMA((count,)),
            pltpu.SemaphoreType.DMA((count,)),
            pltpu.SemaphoreType.DMA,
        ],
        compiler_params=pltpu.CompilerParams(collective_id=collective_id, has_side_effects=True),
        cost_estimate=lasting(20),
        name="small_sum",
    )(own, cut)


def greet_plane(ring):
    me = lax.axis_index("seq")
    greet([lax.rem(me + k, ring) for k in range(1, ring)])


def plane_scatter_dot_kernel(count, dims, fill, swaps, *refs):
    refs = list(refs)

    def take(size):
        taken = refs[:size]
        del refs[:size]
        return taken

    left_hbm, right_hbm, fill_hbm = take(count), take(count), take(int(fill))
    cut_refs = take(swaps)
    (sum_ref,) = take(1)
    terms = take(count if fill else 0)
    spread_refs, swapped_refs = take(swaps), take(swaps)
    lefts, rights, fill_refs = take(count), take(count), take(int(fill))
    out_ref, own_ref, near_ref, far_in_ref, side_in_ref = take(5)
    send_sems, recv_sems, load_sems = refs
    loads = []
    for k in range(count):
        for source, target in ((left_hbm[k], lefts[k]), (right_hbm[k], rights[k])):
            load = pltpu.make_async_copy(source, target, load_sems.at[len(loads)])
            load.start()
            loads.append(load)
    if fill:
        fill_load = pltpu.make_async_copy(fill_hbm[0], fill_refs[0], load_sems.at[2 * count])
        fill_load.start()
    me, sibling, across, along = plane_peers()
    far = along + across - me
    flip = sibling - me
    rows, columns = sum_ref.shape
    half = rows // 2
    upper, lower = pl.ds(0, half), pl.ds(half, half)
    swapped = []
    if swaps:
        greet_plane(lefts[0].shape[0])
        keep = pltpu.make_async_copy(
            cut_refs[0].at[me], swapped_refs[0].at[me], load_sems.at[2 * count]
        )
        keep.start()
        swapped = exchange_copies(
            cut_refs[0], swapped_refs[0].at[me], send_sems, recv_sems, 10
        )
    else:
        greet((sibling, across, along))
    for load in loads:
        load.wait()
    wide = 512

    def slab_dot(slab, target):
        @pl.loop(0, columns // wide)
        def _(i):
            at = pl.ds(pl.multiple_of(i * wide, wide), wide)
            total = None
            for k in range(count):
                right = rights[k][:, at] if dims[1] == (0,) else rights[k][at, :]
                term = low_dot(lefts[k][slab], right, dims)
                total = term if total is None else total + term
            target[:, at] = total.astype(BF16)

    def send(k, peer, source, target):
        copy = send_to(peer, source, target, send_sems.at[k], recv_sems.at[k])
        copy.start()
        return copy

    step = 32

    def fold(target, other, start, size):
        @pl.loop(0, size // step)
        def _(i):
            at = pl.ds(pl.multiple_of(start + i * step, step), step)
            target[at] = (target[at].astype(F32) + other[at].astype(F32)).astype(BF16)

    nears = []

    def near_slab(k, slab):
        slab_dot(slab + flip, out_ref.at[k])
        nears.append(send(k, sibling, out_ref.at[k], near_ref.at[k]))

    near_slab(0, far)
    slab_dot(far, own_ref.at[0])
    near_slab(1, across)
    nears[0].wait_recv()
    fold(own_ref.at[0], near_ref.at[0], 0, rows)
    copies = [
        send(4, across, own_ref.at[0, upper], far_in_ref.at[upper]),
        send(5, along, own_ref.at[0, lower], far_in_ref.at[lower]),
    ]
    slab_dot(across, own_ref.at[1])
    near_slab(2, along)
    nears[1].wait_recv()
    fold(own_ref.at[1], near_ref.at[1], 0, rows)
    copies.append(send(6, across, own_ref.at[1, upper], side_in_ref.at[0, upper]))
    slab_dot(along, own_ref.at[2])
    near_slab(3, me)
    nears[2].wait_recv()
    fold(own_ref.at[2], near_ref.at[2], 0, rows)
    copies.append(send(7, along, own_ref.at[2, lower], side_in_ref.at[1, lower]))
    slab_dot(me, own_ref.at[3])
    copies[0].wait_recv()
    fold(own_ref.at[2], far_in_ref, 0, half)
    copies.append(send(8, along, own_ref.at[2, upper], side_in_ref.at[1, upper]))
    copies[1].wait_recv()
    fold(own_ref.at[1], far_in_ref, half, half)
    copies.append(send(9, across, own_ref.at[1, lower], side_in_ref.at[0, lower]))
    if swaps:
        for copy in swapped:
            copy.wait_recv()
        keep.wait()
        spread_units(swapped_refs[0], spread_refs[0], lax.axis_size("dp"))
    if fill:
        fill_load.wait()
        tall = 256

        @pl.loop(0, terms[0].shape[0] // tall)
        def _(i):
            at = pl.ds(pl.multiple_of(i * tall, tall), tall)
            turned = fill_refs[0][:, at]
            for k in range(count):
                wide_left = lefts[k][...].reshape(-1, lefts[k].shape[2])
                terms[k][at, :] = low_dot(turned, wide_left, TN).astype(BF16)

    nears[3].wait_recv()

    def finish(a, start):
        @pl.loop(0, half // step)
        def _(i):
            at = pl.ds(pl.multiple_of(start + i * step, step), step)
            sum_ref[at] = (
                own_ref[3, at].astype(F32)
                + near_ref[3, at].astype(F32)
                + side_in_ref[0, at].astype(F32)
                + side_in_ref[1, at].astype(F32)
            )

    for copy in copies[2:]:
        copy.wait_recv()
    finish(0, 0)
    finish(1, half)
    for copy in nears + copies + swapped:
        copy.wait_send()


def plane_scatter_dot(lefts, rights, dims, collective_id, fill=None, cut=None):
    count = len(lefts)
    ring, rows, _ = lefts[0].shape
    columns = rights[0].shape[1 - dims[1][0]]
    filled = fill is not None
    fills = [fill] if filled else []
    vmem, anywhere = pl.BlockSpec(memory_space=pltpu.VMEM), pl.BlockSpec(memory_space=pl.ANY)
    cuts = [] if cut is None else [cut]
    total = 10 + len(cuts) * (ring - 1)
    term_shapes = [
        jax.ShapeDtypeStruct((fill.shape[1], left.shape[2]), BF16) for left in lefts if filled
    ]
    return pl.pallas_call(
        functools.partial(plane_scatter_dot_kernel, count, dims, filled, len(cuts)),
        out_shape=[jax.ShapeDtypeStruct((rows, columns), F32)]
        + term_shapes
        + [jax.ShapeDtypeStruct((cut.shape[1], ring * cut.shape[2]), F32) for cut in cuts],
        in_specs=[anywhere] * (2 * count + len(fills) + len(cuts)),
        out_specs=[vmem] * (1 + len(term_shapes) + len(cuts)),
        scratch_shapes=[pltpu.VMEM(cut.shape, BF16) for cut in cuts]
        + [pltpu.VMEM(left.shape, BF16) for left in lefts]
        + [pltpu.VMEM(right.shape, BF16) for right in rights]
        + [pltpu.VMEM(value.shape, BF16) for value in fills]
        + [
            pltpu.VMEM((4, rows, columns), BF16),
            pltpu.VMEM((4, rows, columns), BF16),
            pltpu.VMEM((4, rows, columns), BF16),
            pltpu.VMEM((rows, columns), BF16),
            pltpu.VMEM((2, rows, columns), BF16),
            pltpu.SemaphoreType.DMA((total,)),
            pltpu.SemaphoreType.DMA((total,)),
            pltpu.SemaphoreType.DMA((2 * count + len(fills) + len(cuts),)),
        ],
        compiler_params=pltpu.CompilerParams(
            collective_id=collective_id, has_side_effects=True, vmem_limit_bytes=VMEM_LIMIT
        ),
        cost_estimate=lasting(45),
        name="plane_scatter_dot",
    )(*lefts, *rights, *fills, *cuts)


def gather_in_turn(own_ref, all_ref, send_sems, recv_sems, use):
    me, sibling, across, along = plane_peers()
    far = along + across - me
    flip = sibling - me
    half = own_ref.shape[0] // 2
    upper, lower = pl.ds(0, half), pl.ds(half, half)
    copies = []

    def send(peer, source, target):
        k = len(copies)
        copy = send_to(peer, source, target, send_sems.at[k], recv_sems.at[k])
        copy.start()
        copies.append(copy)

    send(across, own_ref, all_ref.at[me])
    send(along, own_ref, all_ref.at[me])
    send(sibling, own_ref, all_ref.at[me])
    all_ref[me] = own_ref[...]
    use(me)
    copies[2].wait_recv()
    use(sibling)
    copies[0].wait_recv()
    send(along, all_ref.at[across, upper], all_ref.at[across, upper])
    copies[1].wait_recv()
    send(across, all_ref.at[along, lower], all_ref.at[along, lower])
    send(sibling, all_ref.at[across], all_ref.at[across])
    send(sibling, all_ref.at[along], all_ref.at[along])
    use(across)
    use(along)
    copies[5].wait_recv()
    use(across + flip)
    copies[6].wait_recv()
    use(along + flip)
    copies[3].wait_recv()
    send(sibling, all_ref.at[far, upper], all_ref.at[far, upper])
    copies[4].wait_recv()
    send(sibling, all_ref.at[far, lower], all_ref.at[far, lower])
    use(far)
    copies[7].wait_recv()
    copies[8].wait_recv()
    use(far + flip)
    for copy in copies:
        copy.wait_send()


def gather_feed_kernel(
    own_hbm,
    pair_hbm,
    down_hbm,
    error_hbm,
    all_hbm,
    activated_hbm,
    pair_err_hbm,
    down_term_ref,
    own_ref,
    pair_ref,
    down_ref,
    error_ref,
    all_ref,
    activated_out,
    pair_out,
    total_ref,
    send_sems,
    recv_sems,
    load_sems,
    save_sems,
):
    loads = []
    for source, target in (
        (own_hbm, own_ref),
        (pair_hbm, pair_ref),
        (down_hbm, down_ref),
        (error_hbm, error_ref),
    ):
        load = pltpu.make_async_copy(source, target, load_sems.at[len(loads)])
        load.start()
        loads.append(load)
    greet(plane_peers()[1:])
    loads[0].wait()
    waiting = loads[1:]
    saves = []
    tall = 256
    wide = 512
    rows, columns = own_ref.shape
    units = down_ref.shape[0]


    def use(slab):
        first = bool(waiting)
        while waiting:
            waiting.pop().wait()
        turn = len(saves) % 2
        if len(saves) > 1:
            for save in saves[-2]:
                save.wait()

        @pl.loop(0, rows // tall)
        def _(i):
            at = pl.ds(pl.multiple_of(i * tall, tall), tall)
            values = all_ref[slab, at, :]
            pair = low_dot(values, pair_ref[...], NN)
            gate, up = pair[:, :units], pair[:, units:]
            grad = low_dot(error_ref[slab, at, :], down_ref[...], NT)
            opening = sigmoid(gate)
            gate_open = gate * opening
            activated_out[turn, at, :] = (gate_open * up).astype(BF16)
            gate_err = grad * up * (opening * (1.0 + gate * (1.0 - opening)))
            pair_out[turn, at, :] = jnp.concatenate([gate_err, grad * gate_open], 1).astype(BF16)

        batch = []
        for k, (source, target) in enumerate(
            (
                (activated_out.at[turn], activated_hbm.at[slab]),
                (pair_out.at[turn], pair_err_hbm.at[slab]),
                (all_ref.at[slab], all_hbm.at[slab]),
            )
        ):
            save = pltpu.make_async_copy(source, target, save_sems.at[turn, k])
            save.start()
            batch.append(save)
        saves.append(batch)

        @pl.loop(0, columns // wide)
        def _(i):
            at = pl.ds(pl.multiple_of(i * wide, wide), wide)
            term = low_dot(activated_out[turn], error_ref[slab, :, at], TN)
            if first:
                total_ref[:, at] = term
            else:
                total_ref[:, at] += term

    gather_in_turn(own_ref, all_ref, send_sems, recv_sems, use)
    down_term_ref[...] = total_ref[...].astype(BF16)
    for batch in saves[-2:]:
        for save in batch:
            save.wait()


def gather_feed(own, pair_own, down_own, error_all, collective_id):
    ring = lax.axis_size("seq")
    rows, columns = own.shape
    units = down_own.shape[0]
    anywhere = pl.BlockSpec(memory_space=pl.ANY)
    return pl.pallas_call(
        gather_feed_kernel,
        out_shape=[
            jax.ShapeDtypeStruct((ring, rows, columns), BF16),
            jax.ShapeDtypeStruct((ring, rows, units), BF16),
            jax.ShapeDtypeStruct((ring, rows, 2 * units), BF16),
            jax.ShapeDtypeStruct(down_own.shape, BF16),
        ],
        in_specs=[anywhere] * 4,
        out_specs=[anywhere] * 3 + [pl.BlockSpec(memory_space=pltpu.VMEM)],
        scratch_shapes=[
            pltpu.VMEM((rows, columns), BF16),
            pltpu.VMEM(pair_own.shape, BF16),
            pltpu.VMEM(down_own.shape, BF16),
            pltpu.VMEM((ring, rows, columns), BF16),
            pltpu.VMEM((ring, rows, columns), BF16),
            pltpu.VMEM((2, rows, units), BF16),
            pltpu.VMEM((2, rows, 2 * units), BF16),
            pltpu.VMEM(down_own.shape, F32),
            pltpu.SemaphoreType.DMA((9,)),
            pltpu.SemaphoreType.DMA((9,)),
            pltpu.SemaphoreType.DMA((4,)),
            pltpu.SemaphoreType.DMA((2, 3)),
        ],
        compiler_params=pltpu.CompilerParams(
            collective_id=collective_id, has_side_effects=True, vmem_limit_bytes=VMEM_LIMIT
        ),
        cost_estimate=lasting(60),
        name="gather_feed",
    )(own, pair_own, down_own, error_all)


def gather_branch_kernel(
    own_hbm,
    gated_hbm,
    weight_hbm,
    activated_hbm,
    down_hbm,
    grad_ref,
    term_ref,
    part_hbm,
    own_ref,
    gated_ref,
    weight_ref,
    activated_ref,
    down_ref,
    all_ref,
    total_ref,
    part_out,
    send_sems,
    recv_sems,
    load_sems,
    save_sems,
):
    loads = []
    for source, target in (
        (own_hbm, own_ref),
        (gated_hbm, gated_ref),
        (weight_hbm, weight_ref),
        (activated_hbm, activated_ref),
        (down_hbm, down_ref),
    ):
        load = pltpu.make_async_copy(source, target, load_sems.at[len(loads)])
        load.start()
        loads.append(load)
    greet(plane_peers()[1:])
    loads[0].wait()
    waiting = loads[1:]
    total_ref[...] = jnp.zeros_like(total_ref)
    wide = 512
    saves = []

    def use(slab):
        while waiting:
            waiting.pop().wait()
        turn = len(saves) % 2
        if len(saves) > 1:
            saves[-2].wait()
        grad_ref[slab] = low_dot(all_ref[slab], weight_ref[...], NT).astype(BF16)

        @pl.loop(0, total_ref.shape[1] // wide)
        def _(i):
            at = pl.ds(pl.multiple_of(i * wide, wide), wide)
            total_ref[:, at] += low_dot(gated_ref[slab], all_ref[slab, :, at], TN)
            part_out[turn, :, at] = low_dot(activated_ref[slab], down_ref[:, at], NN).astype(BF16)

        save = pltpu.make_async_copy(part_out.at[turn], part_hbm.at[slab], save_sems.at[turn])
        save.start()
        saves.append(save)

    gather_in_turn(own_ref, all_ref, send_sems, recv_sems, use)
    term_ref[...] = total_ref[...].astype(BF16)
    for save in saves[-2:]:
        save.wait()


def gather_branch(own, gated, weight, activated, down_own, collective_id):
    ring, rows, width = gated.shape
    columns = own.shape[1]
    vmem = pl.BlockSpec(memory_space=pltpu.VMEM)
    anywhere = pl.BlockSpec(memory_space=pl.ANY)
    return pl.pallas_call(
        gather_branch_kernel,
        out_shape=[
            jax.ShapeDtypeStruct((ring, rows, width), BF16),
            jax.ShapeDtypeStruct((width, columns), BF16),
            jax.ShapeDtypeStruct((ring, rows, columns), BF16),
        ],
        in_specs=[anywhere] * 5,
        out_specs=[vmem, vmem, anywhere],
        scratch_shapes=[
            pltpu.VMEM(own.shape, BF16),
            pltpu.VMEM(gated.shape, BF16),
            pltpu.VMEM(weight.shape, BF16),
            pltpu.VMEM(activated.shape, BF16),
            pltpu.VMEM(down_own.shape, BF16),
            pltpu.VMEM((ring, rows, columns), BF16),
            pltpu.VMEM((width, columns), F32),
            pltpu.VMEM((2, rows, columns), BF16),
            pltpu.SemaphoreType.DMA((9,)),
            pltpu.SemaphoreType.DMA((9,)),
            pltpu.SemaphoreType.DMA((5,)),
            pltpu.SemaphoreType.DMA((2,)),
        ],
        compiler_params=pltpu.CompilerParams(
            collective_id=collective_id, has_side_effects=True, vmem_limit_bytes=VMEM_LIMIT
        ),
        cost_estimate=lasting(45),
        name="gather_branch",
    )(own, gated, weight, activated, down_own)


def rms_back(values, gain, grad):
    scale = lax.rsqrt(jnp.mean(values * values, -1, keepdims=True) + 1e-05)
    weighted = grad * gain
    part = scale * weighted - values * (
        scale * scale * scale * jnp.mean(weighted * values, -1, keepdims=True)
    )
    return (part, jnp.sum(grad * values * scale, 0))


def low_dot(left, right, dims):
    return lax.dot_general(left, right, (dims, ((), ())), preferred_element_type=F32)


NN = ((1,), (0,))
NT = ((1,), (1,))
TN = ((0,), (0,))


def split_heads_device(
    inputs,
    lengths,
    first_gain,
    input_weight,
    decay_weight,
    conv_weight,
    decay_log,
    decay_bias,
    head_gain,
    output_weight,
    second_gain,
    gate_up_weight,
    down_weight,
    cotangent,
):
    micro_count, seq_local, span, model_width = inputs.shape
    ring = lax.axis_size("seq")
    depth = lax.axis_size("dp")
    rank = lax.axis_index("seq")
    seqs = micro_count * seq_local
    row_count = seqs * span
    all_rows = ring * row_count
    head_count = decay_log.shape[0]
    heads = head_count // ring
    head_size = head_gain.shape[0]
    key_width = head_count * head_size
    width = heads * head_size
    own_units = down_weight.shape[0]
    units = depth * own_units
    weight_rows = input_weight.shape[0]
    tap_count = conv_weight.shape[0]

    tokens = inputs.reshape(row_count, model_width).astype(F32)
    positions = rank * span + lax.broadcasted_iota(jnp.int32, (micro_count, seq_local, span), 2)
    valid_rows = (positions < lengths[:, :, None]).astype(F32).reshape(row_count, 1)
    normed_low = rms_norm(tokens, first_gain).astype(BF16)

    upstream = valid_rows * cotangent.reshape(row_count, model_width).astype(F32)
    out_err = upstream.astype(BF16)
    turns = [(depth * s + z, ring * z + s) for s in range(ring) for z in range(depth)]
    down_own = gather_rows(down_weight, "dp")
    out_own = gather_rows(lax.ppermute(output_weight, ("dp", "seq"), turns), "dp")

    def own_lanes(pair):
        rows = pair.shape[0]
        decay_part = lax.dynamic_slice(pair, (0, rank * heads), (rows, heads))
        other = pair.shape[1] - head_count
        if other:
            strength_part = lax.dynamic_slice(pair, (0, head_count + rank * heads), (rows, heads))
            decay_part = jnp.concatenate([decay_part, strength_part], 1)
        return jnp.pad(decay_part, ((0, 0), (0, 128 - decay_part.shape[1])))

    decay_own = own_lanes(decay_weight)
    params = jnp.pad(own_lanes(jnp.stack([decay_log, decay_bias])), ((0, 6), (0, 0)))
    taps = lax.dynamic_slice(
        conv_weight.reshape(tap_count, 3, key_width), (0, 0, rank * width), (tap_count, 3, width)
    ).reshape(tap_count, 3 * width)
    gain = head_gain.reshape(1, head_size)

    def chunks(value):
        return value.reshape(ring, seqs, span, value.shape[-1])

    normed_all, in_own, pair_cut, mixed, gate_raw, logits = plane_open(
        normed_low, input_weight, gate_up_weight, decay_own, 1
    )
    normed_all = normed_all.reshape(all_rows, model_width)
    in_own = in_own.reshape(model_width, 4 * width)
    pair_own = gather_rows(pair_cut.reshape(ring * weight_rows, 2 * units), "dp")
    mixed, out_own, down_own = lax.optimization_barrier((mixed, out_own, down_own))
    mixed, gate_raw, logits = chunks(mixed), chunks(gate_raw), chunks(logits)
    gated, memory, inverse, fresh, mixer_out, out_err_all = run_forward(
        mixed, gate_raw, logits, taps, params, gain, heads, out_err, 5
    )
    gated = gated.reshape(ring, row_count, width)
    hidden = tokens + plane_scatter_dot([gated], [out_own], NN, 2)[0]
    second_low = rms_norm(hidden, second_gain).astype(BF16)
    second_all, activated, pair_err, down_term = gather_feed(
        second_low, pair_own, down_own, out_err_all, 3
    )
    down_share = scatter_rows(down_term, "dp").astype(F32)
    second_grad, pair_term = plane_scatter_dot(
        [pair_err], [pair_own], NT, 4, second_all.reshape(all_rows, model_width)
    )
    pair_share = scatter_rows(pair_term, "dp")
    hidden_part, second_gain_grad = rms_back(hidden, second_gain, second_grad)
    hidden_grad = upstream + hidden_part
    branch_err = hidden_grad.astype(BF16)
    gated_grad, output_term, down_part = gather_branch(
        branch_err, gated, out_own, activated, down_own, 11
    )
    in_err, logit_grad, taps_grad, param_grad, gain_grad, final_part = run_backward(
        mixed,
        gate_raw,
        logits,
        taps,
        params,
        gain,
        memory,
        inverse,
        fresh,
        mixer_out,
        gated_grad.reshape(ring, seqs, span, width),
        down_part,
        12,
    )
    result = valid_rows * (hidden + final_part)
    input_term = low_dot(normed_all, in_err.reshape(all_rows, 4 * width), TN).astype(BF16)
    input_term, in_err, logit_grad, down_share, pair_share = lax.optimization_barrier(
        (input_term, in_err, logit_grad, down_share, pair_share)
    )
    input_cut = scatter_rows(input_term, "dp")
    lanes = logit_grad.shape[-1]
    decay_twice = decay_own + jnp.roll(decay_own, lanes // 2, 1)
    normed_grad, gate_up_share = plane_scatter_dot(
        [
            in_err.reshape(ring, row_count, 4 * width),
            logit_grad.reshape(ring, row_count, lanes),
        ],
        [in_own, decay_twice],
        NT,
        6,
        cut=pair_share.reshape(ring, weight_rows, 2 * units),
    )
    output_term, input_cut, normed_grad = lax.optimization_barrier(
        (output_term, input_cut, normed_grad)
    )
    output_share = lax.ppermute(
        scatter_rows(output_term, "dp"), ("dp", "seq"), [(b, a) for a, b in turns]
    ).astype(F32)
    token_part, first_gain_grad = rms_back(tokens, first_gain, normed_grad)
    inputs_grad = hidden_grad + token_part
    decay_term = low_dot(normed_all, logit_grad.reshape(all_rows, lanes), TN)
    decay_term = decay_term[:, : 2 * heads] + decay_term[:, lanes // 2 : lanes // 2 + 2 * heads]
    pieces = [
        jnp.transpose(decay_term),
        taps_grad[:tap_count],
        param_grad[:2, : 2 * heads],
        first_gain_grad,
        second_gain_grad,
        gain_grad[0],
    ]
    sizes = [piece.size for piece in pieces]
    packed = jnp.concatenate([piece.reshape(-1) for piece in pieces])
    packed = jnp.pad(packed, (0, -packed.size % 1024)).reshape(-1, 128)
    summed, input_share = small_sum(packed, input_cut.reshape(ring, weight_rows, 4 * width), 7)
    summed = summed.reshape(ring, -1)
    parted = []
    start = 0
    for size in sizes:
        parted.append(summed[:, start : start + size])
        start += size
    decay_sum, taps_sum, param_sum = parted[:3]
    first_gain_grad, second_gain_grad, gain_grad = [part.sum(0) for part in parted[3:]]
    decay_sum = decay_sum.reshape(ring, 2, heads, model_width)
    decay_weight_grad = jnp.transpose(decay_sum, (3, 1, 0, 2)).reshape(model_width, 2 * head_count)
    taps_sum = jnp.transpose(taps_sum.reshape(ring, tap_count, 3, width), (1, 2, 0, 3))
    param_sum = jnp.transpose(param_sum.reshape(ring, 2, 2 * heads)[..., :heads], (1, 0, 2))
    param_sum = param_sum.reshape(2, head_count)
    return (
        result.reshape(inputs.shape),
        inputs_grad.reshape(inputs.shape),
        first_gain_grad,
        input_share,
        decay_weight_grad,
        taps_sum.reshape(tap_count, 3 * key_width),
        param_sum[0],
        param_sum[1],
        gain_grad,
        output_share,
        second_gain_grad,
        gate_up_share,
        down_share,
    )


def solution(mesh):
    in_specs = (
        P(None, "dp", "seq", None),
        P(None, "dp"),
        P(),
        P(("dp", "seq"), None),
        P(),
        P(),
        P(),
        P(),
        P(),
        P(("dp", "seq"), None),
        P(),
        P(("dp", "seq"), None),
        P(("dp", "seq"), None),
        P(None, "dp", "seq", None),
    )
    out_specs = (
        P(None, "dp", "seq", None),
        P(None, "dp", "seq", None),
        P(),
        P(("dp", "seq"), None),
        P(),
        P(),
        P(),
        P(),
        P(),
        P(("dp", "seq"), None),
        P(),
        P(("dp", "seq"), None),
        P(("dp", "seq"), None),
    )
    ring = mesh.shape["seq"]

    def whole_device(*arrays):
        heads_divide = ring == 8 and arrays[6].shape[0] % ring == 0
        return (split_heads_device if heads_divide else per_device)(*arrays)

    return jax.shard_map(
        whole_device, mesh=mesh, in_specs=in_specs, out_specs=out_specs, check_vma=False
    )
```

```python
import functools

import jax
import jax.numpy as jnp
from jax import lax
from jax.experimental import pallas as pl
from jax.experimental.pallas import tpu as pltpu
from jax.sharding import PartitionSpec as P

SPAN = 64
VMEM_LIMIT = 56 * 1024 * 1024


HIGH = lax.Precision.HIGHEST


def shifted(value, axis, steps):
    count = lax.axis_size(axis)
    initial, last = (max(0, -steps), min(count, count - steps))
    return lax.ppermute(value, axis, [(source, source + steps) for source in range(initial, last)])


def rms_norm(values, gain):
    return values * lax.rsqrt(jnp.mean(values * values, -1, keepdims=True) + 1e-05) * gain


def unit_norm(vectors):
    return vectors * lax.rsqrt(jnp.sum(vectors * vectors, -1, keepdims=True) + 1e-06)


def swish_product(gate_part, up_part):
    return jax.nn.silu(gate_part) * up_part


def unit_inverse(strict_lower):
    extent = strict_lower.shape[-1]
    identity_matrix = jnp.eye(extent, dtype=jnp.float32)
    inverse = identity_matrix - strict_lower
    power_term = strict_lower
    for level_index in range(1, (extent - 1).bit_length()):
        power_term = jnp.einsum("bhij,bhjk->bhik", power_term, power_term, precision=HIGH)
        inverse = jnp.einsum(
            "bhij,bhjk->bhik", inverse, identity_matrix + power_term, precision=HIGH
        )
    return inverse


def span_step(memory, pieces):
    queries, probes, writes, decays, strengths = pieces
    extent = decays.shape[-1]
    running = jnp.cumsum(decays, axis=-1)
    spread = running[..., :, None] - running[..., None, :]
    row_index = lax.broadcasted_iota(jnp.int32, (extent, extent), 0)
    col_index = lax.broadcasted_iota(jnp.int32, (extent, extent), 1)
    faded = jnp.exp(jnp.minimum(spread, 0.0))
    inclusive = jnp.where(col_index <= row_index, faded, 0.0) * strengths[..., None, :]
    strict_mask = jnp.where(col_index < row_index, faded, 0.0) * strengths[..., None, :]
    strict_lower = strict_mask * jnp.einsum("bhtd,bhsd->bhts", probes, probes, precision=HIGH)
    scale_in = jnp.exp(running)[..., None]
    target = writes - scale_in * jnp.einsum("bhtd,bhde->bhte", probes, memory, precision=HIGH)
    fresh_values = jnp.einsum("bhts,bhse->bhte", unit_inverse(strict_lower), target, precision=HIGH)
    mixing = inclusive * jnp.einsum("bhtd,bhsd->bhts", queries, probes, precision=HIGH)
    outputs = scale_in * jnp.einsum("bhtd,bhde->bhte", queries, memory, precision=HIGH)
    outputs = outputs + jnp.einsum("bhts,bhse->bhte", mixing, fresh_values, precision=HIGH)
    remaining = jnp.exp(running[..., -1:] - running) * strengths
    memory = jnp.exp(running[..., -1])[..., None, None] * memory + jnp.einsum(
        "bhsd,bhse->bhde", probes * remaining[..., None], fresh_values, precision=HIGH
    )
    return (memory, outputs)


def delta_local(queries, probes, writes, decays, strengths, memory):
    seq_count, head_count, length, head_size = queries.shape
    blocks = length // SPAN

    def arrange(tensor):
        shaped = tensor.reshape(tensor.shape[:2] + (blocks, SPAN) + tensor.shape[3:])
        return jnp.moveaxis(shaped, 2, 0)

    pieces = (
        arrange(queries),
        arrange(probes),
        arrange(writes),
        arrange(decays),
        arrange(strengths),
    )
    memory, outputs = lax.scan(span_step, memory, pieces)
    outputs = jnp.moveaxis(outputs, 0, 2)
    return (outputs.reshape(seq_count, head_count, length, outputs.shape[-1]), memory)


def prepare(packed, logits, conv_weight, decay_log, decay_bias):
    seq_count, length, logit_width = logits.shape
    head_count = decay_log.shape[0]
    tap_count = conv_weight.shape[0]
    convolved = conv_weight[0] * packed[:, 0:length]
    for tap_index in range(1, tap_count):
        convolved = convolved + conv_weight[tap_index] * packed[:, tap_index : tap_index + length]
    active = jax.nn.silu(convolved)
    key_width = active.shape[-1] // 3
    head_size = key_width // head_count

    def split_heads(portion):
        return jnp.transpose(
            portion.reshape(seq_count, length, head_count, head_size), (0, 2, 1, 3)
        )

    queries = unit_norm(split_heads(active[..., :key_width])) * head_size ** (-0.5)
    probes = unit_norm(split_heads(active[..., key_width : 2 * key_width]))
    writes = split_heads(active[..., 2 * key_width :])
    decays = jnp.transpose(
        -jnp.exp(decay_log) * jax.nn.softplus(logits[..., :head_count] + decay_bias), (0, 2, 1)
    )
    strengths = jnp.transpose(jax.nn.sigmoid(logits[..., head_count:]), (0, 2, 1))
    return (queries, probes, writes, decays, strengths)


def mixer_core(packed, logits, conv_weight, decay_log, decay_bias, memory):
    queries, probes, writes, decays, strengths = prepare(
        packed, logits, conv_weight, decay_log, decay_bias
    )
    return delta_local(queries, probes, writes, decays, strengths, memory)


def finish(mixer_out, gate_raw, head_gain):
    seq_count, head_count, length, head_size = mixer_out.shape
    normal_out = rms_norm(mixer_out, head_gain)
    flat_rows = jnp.transpose(normal_out, (0, 2, 1, 3)).reshape(
        seq_count, length, head_count * head_size
    )
    return flat_rows * jax.nn.silu(gate_raw)


def carry_forward(transfer, offset):

    def turn_step(step_index, incoming):
        leaving = jnp.einsum("bhij,bhjk->bhik", transfer, incoming, precision=HIGH) + offset
        return shifted(leaving.astype(jnp.bfloat16), "seq", 1).astype(leaving.dtype)

    return lax.fori_loop(0, lax.axis_size("seq") - 1, turn_step, jnp.zeros_like(offset))


def carry_back(transfer, source):
    flipped = jnp.swapaxes(transfer, 2, 3)

    def turn_step(step_index, incoming):
        leaving = jnp.einsum("bhij,bhjk->bhik", flipped, incoming, precision=HIGH) + source
        return shifted(leaving.astype(jnp.bfloat16), "seq", -1).astype(leaving.dtype)

    return lax.fori_loop(0, lax.axis_size("seq") - 1, turn_step, jnp.zeros_like(source))


def per_device(
    inputs,
    lengths,
    first_gain,
    input_weight,
    decay_weight,
    conv_weight,
    decay_log,
    decay_bias,
    head_gain,
    output_weight,
    second_gain,
    gate_up_weight,
    down_weight,
    cotangent,
):
    micro_count, seq_local, length, model_width = inputs.shape
    seq_count = micro_count * seq_local
    row_count = seq_count * length
    head_count = decay_log.shape[0]
    key_width = input_weight.shape[1] // 4
    head_size = key_width // head_count
    tap_count = conv_weight.shape[0]
    tokens = inputs.reshape(row_count, model_width).astype(jnp.float32)
    positions = lax.axis_index("seq") * length + lax.broadcasted_iota(
        jnp.int32, (micro_count, seq_local, length), 2
    )
    valid_rows = (positions < lengths[:, :, None]).astype(jnp.float32).reshape(row_count, 1)
    in_full, out_full, gate_up_full, down_full = (
        lax.all_gather(input_weight, ("dp", "seq"), axis=0, tiled=True),
        lax.all_gather(output_weight, ("dp", "seq"), axis=0, tiled=True),
        lax.all_gather(gate_up_weight, ("dp", "seq"), axis=0, tiled=True),
        lax.all_gather(down_weight, ("dp", "seq"), axis=0, tiled=True),
    )
    normed, first_pullback = jax.vjp(rms_norm, tokens, first_gain)
    normed_low = normed.astype(jnp.bfloat16)
    projected = jnp.dot(normed_low, in_full, preferred_element_type=jnp.float32)
    mixed_low = (
        projected[:, : 3 * key_width].astype(jnp.bfloat16).reshape(seq_count, length, 3 * key_width)
    )
    gate_raw = projected[:, 3 * key_width :].reshape(seq_count, length, key_width)
    logits = jnp.dot(normed_low, decay_weight, preferred_element_type=jnp.float32).reshape(
        seq_count, length, 2 * head_count
    )
    left_edge = shifted(mixed_low[:, length - tap_count + 1 :], "seq", 1)
    packed = jnp.concatenate([left_edge, mixed_low], 1).astype(jnp.float32)
    queries, probes, writes, decays, strengths = prepare(
        packed, logits, conv_weight, decay_log, decay_bias
    )
    blank_state = jnp.zeros((seq_count, head_count, head_size, head_size), jnp.float32)
    identity_maps = jnp.broadcast_to(jnp.eye(head_size, dtype=jnp.float32), blank_state.shape)
    joined_writes = jnp.concatenate([writes, jnp.zeros_like(writes)], -1)
    joined_outputs, joined_end = delta_local(
        queries,
        probes,
        joined_writes,
        decays,
        strengths,
        jnp.concatenate([blank_state, identity_maps], -1),
    )
    own_out = joined_outputs[..., :head_size]
    carry_out = joined_outputs[..., head_size:]
    offset = joined_end[..., :head_size]
    transfer = joined_end[..., head_size:]
    state_in = carry_forward(transfer, offset)
    mixer_out = own_out + jnp.einsum("bhtd,bhde->bhte", carry_out, state_in, precision=HIGH)
    gated_rows, finish_pullback = jax.vjp(finish, mixer_out, gate_raw, head_gain)
    gated_low = gated_rows.reshape(row_count, key_width).astype(jnp.bfloat16)
    hidden = tokens + jnp.dot(gated_low, out_full, preferred_element_type=jnp.float32)
    second, second_pullback = jax.vjp(rms_norm, hidden, second_gain)
    second_low = second.astype(jnp.bfloat16)
    gate_up = jnp.dot(second_low, gate_up_full, preferred_element_type=jnp.float32)
    ffn_width = gate_up.shape[1] // 2
    activated, swish_pullback = jax.vjp(
        swish_product, gate_up[:, :ffn_width], gate_up[:, ffn_width:]
    )
    activated_low = activated.astype(jnp.bfloat16)
    final_rows = hidden + jnp.dot(activated_low, down_full, preferred_element_type=jnp.float32)
    result = valid_rows * final_rows
    upstream = valid_rows * cotangent.reshape(row_count, model_width).astype(jnp.float32)
    out_err = upstream.astype(jnp.bfloat16)
    down_term = jnp.einsum("nf,nd->fd", activated_low, out_err, preferred_element_type=jnp.float32)
    activated_grad = jnp.einsum("nd,fd->nf", out_err, down_full, preferred_element_type=jnp.float32)
    gate_grad, up_grad = swish_pullback(activated_grad)
    gate_up_err = jnp.concatenate([gate_grad, up_grad], 1).astype(jnp.bfloat16)
    gate_up_term = jnp.einsum(
        "nd,nf->df", second_low, gate_up_err, preferred_element_type=jnp.float32
    )
    second_grad = jnp.einsum(
        "nf,df->nd", gate_up_err, gate_up_full, preferred_element_type=jnp.float32
    )
    hidden_part, second_gain_grad = second_pullback(second_grad)
    hidden_grad = upstream + hidden_part
    gate_up_share, down_share = (
        scatter_rows(gate_up_term.astype(BF16), ("dp", "seq")).astype(F32),
        scatter_rows(down_term.astype(BF16), ("dp", "seq")).astype(F32),
    )
    branch_err = hidden_grad.astype(jnp.bfloat16)
    output_term = jnp.einsum("nk,nd->kd", gated_low, branch_err, preferred_element_type=jnp.float32)
    gated_grad = jnp.einsum("nd,kd->nk", branch_err, out_full, preferred_element_type=jnp.float32)
    mixer_grad, gate_raw_grad, head_gain_grad = finish_pullback(
        gated_grad.reshape(seq_count, length, key_width)
    )
    source = jnp.einsum("bhtd,bhte->bhde", carry_out, mixer_grad, precision=HIGH)
    state_out_grad = carry_back(transfer, source)
    _, core_pullback = jax.vjp(
        mixer_core, packed, logits, conv_weight, decay_log, decay_bias, state_in
    )
    packed_grad, logits_grad, conv_grad, decay_log_grad, decay_bias_grad, _ = core_pullback(
        (mixer_grad, state_out_grad)
    )
    edge_grad = shifted(packed_grad[:, : tap_count - 1].astype(jnp.bfloat16), "seq", -1).astype(
        jnp.float32
    )
    mixed_grad = packed_grad[:, tap_count - 1 :] + jnp.pad(
        edge_grad, ((0, 0), (length - tap_count + 1, 0), (0, 0))
    )
    in_err = jnp.concatenate(
        [mixed_grad.reshape(row_count, 3 * key_width), gate_raw_grad.reshape(row_count, key_width)],
        1,
    ).astype(jnp.bfloat16)
    input_term = jnp.einsum("nd,nk->dk", normed_low, in_err, preferred_element_type=jnp.float32)
    logits_flat = logits_grad.reshape(row_count, 2 * head_count)
    decay_weight_grad = jnp.einsum(
        "nd,nk->dk", normed_low.astype(jnp.float32), logits_flat, precision=HIGH
    )
    normed_grad = jnp.einsum("nk,dk->nd", in_err, in_full, preferred_element_type=jnp.float32)
    normed_grad = normed_grad + jnp.einsum(
        "nk,dk->nd", logits_flat, decay_weight.astype(jnp.float32), precision=HIGH
    )
    token_part, first_gain_grad = first_pullback(normed_grad)
    inputs_grad = hidden_grad + token_part
    input_share, output_share = (
        scatter_rows(input_term.astype(BF16), ("dp", "seq")).astype(F32),
        scatter_rows(output_term.astype(BF16), ("dp", "seq")).astype(F32),
    )
    small_sums = lax.psum(
        (
            first_gain_grad,
            decay_weight_grad,
            conv_grad,
            decay_log_grad,
            decay_bias_grad,
            head_gain_grad,
            second_gain_grad,
        ),
        ("dp", "seq"),
    )
    return (
        result.reshape(inputs.shape),
        inputs_grad.reshape(inputs.shape),
        small_sums[0],
        input_share,
        small_sums[1],
        small_sums[2],
        small_sums[3],
        small_sums[4],
        small_sums[5],
        output_share,
        small_sums[6],
        gate_up_share,
        down_share,
    )


F32 = jnp.float32
BF16 = jnp.bfloat16


def lasting(microseconds):
    return pl.CostEstimate(flops=0, bytes_accessed=int(microseconds * 3.5e6), transcendentals=0)


def parts(value):
    top = value.astype(BF16)
    return (top, (value - top.astype(F32)).astype(BF16))


def contract(left, right, right_dim):
    lhs = jnp.concatenate([left[0], left[1], left[0]], 1)
    rhs = jnp.concatenate([right[0], right[0], right[1]], right_dim)
    return lax.dot_general(lhs, rhs, (((1,), (right_dim,)), ((), ())), preferred_element_type=F32)


def mm(left, right):
    return contract(left, right, 0)


def mm_nt(left, right):
    return contract(left, right, 1)


def ones_dot(ones, value):
    first = value.astype(BF16)
    rest = value - first.astype(F32)
    second = rest.astype(BF16)
    third = (rest - second.astype(F32)).astype(BF16)
    return (
        jnp.dot(ones, first, preferred_element_type=F32)
        + jnp.dot(ones, second, preferred_element_type=F32)
        + jnp.dot(ones, third, preferred_element_type=F32)
    )


def lower_inverses(strict_lowers, row_index, col_index):
    extent = row_index.shape[0]

    def below(width):
        same = (row_index // (2 * width)) == (col_index // (2 * width))
        return same & ((row_index // width) % 2 == 1) & ((col_index // width) % 2 == 0)

    mask = below(1)
    identity = jnp.where(row_index == col_index, 1.0, 0.0)
    inverses = [identity - jnp.where(mask, strict, 0.0) for strict in strict_lowers]
    width = 2
    while width < extent:
        mask = below(width)
        splits = [parts(inverse) for inverse in inverses]
        blocks = [parts(jnp.where(mask, strict, 0.0)) for strict in strict_lowers]
        halves = [mm(split, block) for split, block in zip(splits, blocks)]
        inverses = [
            inverse - mm(parts(half), split)
            for inverse, half, split in zip(inverses, halves, splits)
        ]
        width *= 2
    return inverses


def active_rows(before, rows, taps):
    extended = jnp.concatenate([before, rows], 0)
    count = rows.shape[0]
    tap_count = taps.shape[0]
    start = before.shape[0] - tap_count + 1
    shifts = [extended[start + j : start + j + count] for j in range(tap_count)]
    total = taps[0:1] * shifts[0]
    for j in range(1, tap_count):
        total = total + taps[j : j + 1] * shifts[j]
    return (total, shifts)


def soft_plus(value):
    return jnp.maximum(value, 0.0) + jnp.log(1.0 + jnp.exp(-jnp.abs(value)))


def sigmoid(value):
    return 1.0 / (1.0 + jnp.exp(-value))


def unit(vectors):
    scale = lax.rsqrt(jnp.sum(vectors * vectors, -1, keepdims=True) + 1e-06)
    return (vectors * scale, scale)


def unit_back(vectors, scale, grad):
    inner = jnp.sum(vectors * grad, -1, keepdims=True)
    return scale * grad - vectors * (scale * scale * scale * inner)


def decay_terms(logit, param_ref, heads, ones):
    shifted_logit = logit + param_ref[1:2, :]
    lane = lax.broadcasted_iota(jnp.int32, logit.shape, 1)
    decays = jnp.where(lane < heads, -jnp.exp(param_ref[0:1, :]) * soft_plus(shifted_logit), 0.0)
    strengths = sigmoid(logit)
    running = ones_dot(ones, decays)
    return (shifted_logit, decays, strengths, running)


def mixer_forward(
    mixed_ref,
    gate_ref,
    logit_ref,
    taps_ref,
    param_ref,
    gain_ref,
    own_ref,
    rows_ref,
    gated_ref,
    memory_ref,
    inverse_ref,
    fresh_ref,
    out_ref,
    all_ref,
    rows_out_ref,
    state_ref,
    halo_ref,
    send_sems,
    recv_sems,
    local_sems,
):
    seqs, span, _ = mixed_ref.shape
    heads, head_size = memory_ref.shape[1], memory_ref.shape[2]
    gather_in_steps(own_ref, all_ref, send_sems, recv_sems, local_sems.at[0])
    trade_in_steps(rows_ref, rows_out_ref, send_sems, recv_sems, local_sems, heads)

    @pl.when(pl.program_id(0) == 0)
    def _():
        state_ref[...] = jnp.zeros_like(state_ref)
        halo_ref[...] = jnp.zeros_like(halo_ref)

    row_index = lax.broadcasted_iota(jnp.int32, (span, span), 0)
    col_index = lax.broadcasted_iota(jnp.int32, (span, span), 1)
    ones = jnp.where(col_index <= row_index, 1.0, 0.0).astype(BF16)
    taps = taps_ref[...]
    width = heads * head_size
    pairs = [(m, h) for m in range(seqs) for h in range(heads)]
    active, decay_parts = [], []
    for m in range(seqs):
        rows = mixed_ref[m].astype(F32)
        convolved, _ = active_rows(halo_ref[m], rows, taps)
        halo_ref[m] = rows[span - 8 :]
        active.append(convolved * sigmoid(convolved))
        _, _, strengths, running = decay_terms(logit_ref[m], param_ref, heads, ones)
        decay_parts.append((strengths, running, jnp.transpose(strengths), jnp.transpose(running)))

    def columns(m, h, block):
        start = block * width + h * head_size
        return active[m][:, start : start + head_size]

    queries = [unit(columns(m, h, 0))[0] * head_size ** (-0.5) for m, h in pairs]
    probes = [unit(columns(m, h, 1))[0] for m, h in pairs]
    products = [
        mm_nt(parts(jnp.concatenate([query, probe], 0)), parts(probe))
        for query, probe in zip(queries, probes)
    ]
    stricts, mixings, scales, kepts, lasts = [], [], [], [], []
    for (m, h), probe, product in zip(pairs, probes, products):
        strengths, running, strength_rows, running_rows = decay_parts[m]
        run = running[:, h : h + 1]
        last = running[span - 1 : span, h : h + 1]
        weight_row = strength_rows[heads + h : heads + h + 1, :]
        weight_col = strengths[:, heads + h : heads + h + 1]
        faded = jnp.exp(jnp.minimum(run - running_rows[h : h + 1, :], 0.0)) * weight_row
        mixings.append(jnp.where(col_index <= row_index, faded * product[:span], 0.0))
        stricts.append(jnp.where(col_index < row_index, faded * product[span:], 0.0))
        scales.append(jnp.exp(run))
        kepts.append(jnp.transpose(jnp.exp(last - run) * weight_col * probe))
        lasts.append(jnp.exp(last))
    inverses = lower_inverses(stricts, row_index, col_index)
    boths = [
        mm(parts(inverse), parts(jnp.concatenate([columns(m, h, 2), scale * probe], 1)))
        for (m, h), inverse, scale, probe in zip(pairs, inverses, scales, probes)
    ]
    memories = [state_ref[m, h] for m, h in pairs]
    reads = [
        mm(parts(jnp.concatenate([both[:, head_size:], scale * query], 0)), parts(memory))
        for both, scale, query, memory in zip(boths, scales, queries, memories)
    ]
    freshes = [both[:, :head_size] - read[:span] for both, read in zip(boths, reads)]
    fresh_parts = [parts(fresh) for fresh in freshes]
    for (m, h), last, memory, kept, fresh in zip(pairs, lasts, memories, kepts, fresh_parts):
        state_ref[m, h] = last * memory + mm(parts(kept), fresh)
    outs = [
        read[span:] + mm(parts(mixing), fresh)
        for read, mixing, fresh in zip(reads, mixings, fresh_parts)
    ]
    for (m, h), memory, inverse, fresh, mixer_out in zip(pairs, memories, inverses, freshes, outs):
        own = slice(h * head_size, (h + 1) * head_size)
        memory_ref[m, h] = memory
        inverse_ref[m, h] = inverse
        fresh_ref[m, :, own] = fresh
        out_ref[m, :, own] = mixer_out
        scale = lax.rsqrt(jnp.mean(mixer_out * mixer_out, -1, keepdims=True) + 1e-05)
        gate = gate_ref[m, :, own]
        gated_ref[m, :, own] = (
            mixer_out * scale * gain_ref[...] * (gate * sigmoid(gate))
        ).astype(BF16)


def mixer_backward(
    mixed_ref,
    before_ref,
    gate_ref,
    logit_ref,
    taps_ref,
    param_ref,
    gain_ref,
    memory_ref,
    inverse_ref,
    fresh_ref,
    out_ref,
    grad_ref,
    part_ref,
    term_ref,
    error_ref,
    logit_grad_ref,
    taps_grad_ref,
    param_grad_ref,
    gain_grad_ref,
    sum_ref,
    share_ref,
    state_ref,
    halo_ref,
    *scatter_refs,
):
    seqs, span, _ = mixed_ref.shape
    heads, head_size = memory_ref.shape[1], memory_ref.shape[2]
    step = pl.program_id(0)
    scatter_in_steps(part_ref, sum_ref, *scatter_refs[:7])
    sums_in_steps(term_ref, share_ref, *scatter_refs[7:])

    @pl.when(step == 0)
    def _():
        state_ref[...] = jnp.zeros_like(state_ref)
        halo_ref[...] = jnp.zeros_like(halo_ref)
        taps_grad_ref[...] = jnp.zeros_like(taps_grad_ref)
        param_grad_ref[...] = jnp.zeros_like(param_grad_ref)
        gain_grad_ref[...] = jnp.zeros_like(gain_grad_ref)

    first = step == pl.num_programs(0) - 1
    row_index = lax.broadcasted_iota(jnp.int32, (span, span), 0)
    col_index = lax.broadcasted_iota(jnp.int32, (span, span), 1)
    ones = jnp.where(col_index <= row_index, 1.0, 0.0).astype(BF16)
    ones_back = jnp.where(col_index >= row_index, 1.0, 0.0).astype(BF16)
    taps = taps_ref[...]
    tap_count = taps.shape[0]
    width = heads * head_size
    gain = gain_ref[...]
    edge = before_ref.shape[1]
    pairs = [(m, h) for m in range(seqs) for h in range(heads)]
    everyone = range(len(pairs))
    active, openings, curves, shifts, decay_parts = [], [], [], [], []
    for m in range(seqs):
        rows = mixed_ref[m].astype(F32)
        before = jnp.where(first, 0.0, before_ref[m].astype(F32))[edge - 8 :]
        convolved, moved = active_rows(before, rows, taps)
        opening = sigmoid(convolved)
        active.append(convolved * opening)
        curves.append(convolved)
        openings.append(opening)
        shifts.append(moved)
        shifted_logit, decays, strengths, running = decay_terms(
            logit_ref[m], param_ref, heads, ones
        )
        decay_parts.append(
            (
                shifted_logit,
                decays,
                strengths,
                running,
                jnp.transpose(strengths),
                jnp.transpose(running),
            )
        )

    def columns(m, h, block):
        start = block * width + h * head_size
        return active[m][:, start : start + head_size]

    raw_queries = [columns(m, h, 0) for m, h in pairs]
    raw_probes = [columns(m, h, 1) for m, h in pairs]
    query_units = [unit(value) for value in raw_queries]
    probe_units = [unit(value) for value in raw_probes]
    queries = [value * head_size ** (-0.5) for value, _ in query_units]
    probes = [value for value, _ in probe_units]
    gate_grads, out_grads = [], []
    for m, h in pairs:
        own = slice(h * head_size, (h + 1) * head_size)
        mixer_out = out_ref[m, :, own]
        gate = gate_ref[m, :, own]
        gated_grad = grad_ref[m, :, own].astype(F32)
        scale = lax.rsqrt(jnp.mean(mixer_out * mixer_out, -1, keepdims=True) + 1e-05)
        gate_open = sigmoid(gate)
        normal = mixer_out * scale
        gate_grads.append(
            gated_grad * normal * gain * (gate_open * (1.0 + gate * (1.0 - gate_open)))
        )
        normal_grad = gated_grad * (gate * gate_open)
        gain_grad_ref[0:1, :] += jnp.sum(normal_grad * normal, 0, keepdims=True)
        weighted = normal_grad * gain
        out_grads.append(
            scale * (weighted - normal * jnp.mean(weighted * normal, -1, keepdims=True))
        )

    probe_parts = [parts(value) for value in probes]
    query_parts = [parts(value) for value in queries]
    out_grad_parts = [parts(value) for value in out_grads]
    state_grads = [state_ref[m, h] for m, h in pairs]
    state_grad_parts = [parts(value) for value in state_grads]
    products = [
        mm_nt(parts(jnp.concatenate([query, probe], 0)), probe_part)
        for query, probe, probe_part in zip(queries, probes, probe_parts)
    ]
    probe_states = [mm(left, right) for left, right in zip(probe_parts, state_grad_parts)]
    weight_rows, spreads, fade_queries, fade_probes = [], [], [], []
    scales, end_scales, remainings, kepts = [], [], [], []
    for (m, h), product in zip(pairs, products):
        _, _, strengths, running, strength_rows, running_rows = decay_parts[m]
        run = running[:, h : h + 1]
        last = running[span - 1 : span, h : h + 1]
        weight_row = strength_rows[heads + h : heads + h + 1, :]
        weight_rows.append(weight_row)
        faded = jnp.exp(jnp.minimum(run - running_rows[h : h + 1, :], 0.0))
        spreads.append(faded * weight_row)
        fade_queries.append(jnp.where(col_index <= row_index, faded * product[:span], 0.0))
        fade_probes.append(jnp.where(col_index < row_index, faded * product[span:], 0.0))
        scales.append(jnp.exp(run))
        end_scales.append(jnp.exp(last))
        remaining = jnp.exp(last - run)
        remainings.append(remaining)
        kepts.append(remaining * strengths[:, heads + h : heads + h + 1])
    fresh_grads = [
        mm(parts(jnp.transpose(fade * weight_row)), out_grad) + kept * probe_state
        for fade, weight_row, out_grad, kept, probe_state in zip(
            fade_queries, weight_rows, out_grad_parts, kepts, probe_states
        )
    ]
    solves = [
        mm(parts(jnp.transpose(inverse_ref[m, h])), parts(fresh_grad))
        for (m, h), fresh_grad in zip(pairs, fresh_grads)
    ]
    for k in everyone:
        m, h = pairs[k]
        state_ref[m, h] = (
            end_scales[k] * state_grads[k]
            + mm(parts(jnp.transpose(queries[k])), parts(scales[k] * out_grads[k]))
            - mm(parts(jnp.transpose(probes[k])), parts(scales[k] * solves[k]))
        )
    freshes = [fresh_ref[m, :, h * head_size : (h + 1) * head_size] for m, h in pairs]
    memories = [memory_ref[m, h] for m, h in pairs]
    fresh_parts = [parts(value) for value in freshes]
    joined = [
        parts(jnp.concatenate([out_grad, solved], 0)) for out_grad, solved in zip(out_grads, solves)
    ]
    outers = [mm_nt(both, fresh) for both, fresh in zip(joined, fresh_parts)]
    throughs = [mm_nt(both, parts(memory)) for both, memory in zip(joined, memories)]
    mixing_grads = [jnp.where(col_index <= row_index, outer[:span], 0.0) for outer in outers]
    strict_grads = [jnp.where(col_index < row_index, -outer[span:], 0.0) for outer in outers]
    mix_fades = [grad * spread for grad, spread in zip(mixing_grads, spreads)]
    strict_fades = [grad * spread for grad, spread in zip(strict_grads, spreads)]
    on_probes = [
        mm(parts(jnp.concatenate([mix, strict], 0)), probe)
        for mix, strict, probe in zip(mix_fades, strict_fades, probe_parts)
    ]
    fresh_states = [mm_nt(fresh, grad) for fresh, grad in zip(fresh_parts, state_grad_parts)]
    turned = [
        mm(parts(jnp.transpose(mix)), query) + mm(parts(jnp.transpose(strict)), probe)
        for mix, strict, query, probe in zip(mix_fades, strict_fades, query_parts, probe_parts)
    ]
    active_grads = [[None] * (3 * heads) for _ in range(seqs)]
    col_terms = [jnp.zeros((span, span), F32)] * seqs
    row_terms = [jnp.zeros((span, span), F32)] * seqs
    for k in everyone:
        m, h = pairs[k]
        out_state = scales[k] * throughs[k][:span]
        solved_state = scales[k] * throughs[k][span:]
        query_grad = out_state + on_probes[k][:span]
        probe_grad = kepts[k] * fresh_states[k] - solved_state + on_probes[k][span:] + turned[k]
        pair_terms = mixing_grads[k] * fade_queries[k] + strict_grads[k] * fade_probes[k]
        weighted_pairs = pair_terms * weight_rows[k]
        probe_fresh = jnp.sum(probe_states[k] * freshes[k], -1, keepdims=True)
        run_col = (
            jnp.sum(out_state * queries[k] - solved_state * probes[k], -1, keepdims=True)
            + jnp.sum(weighted_pairs, -1, keepdims=True)
            - kepts[k] * probe_fresh
        )
        last_grad = jnp.sum(kepts[k] * probe_fresh, 0, keepdims=True) + end_scales[k] * jnp.sum(
            jnp.sum(state_grads[k] * memories[k], -1, keepdims=True), 0, keepdims=True
        )
        run_col = run_col + jnp.where(row_index[:, 0:1] == span - 1, last_grad, 0.0)
        col_terms[m] = jnp.where(col_index == h, run_col, col_terms[m])
        col_terms[m] = jnp.where(
            col_index == heads + h, remainings[k] * probe_fresh, col_terms[m]
        )
        row_terms[m] = jnp.where(
            row_index == h, -jnp.sum(weighted_pairs, 0, keepdims=True), row_terms[m]
        )
        row_terms[m] = jnp.where(
            row_index == heads + h, jnp.sum(pair_terms, 0, keepdims=True), row_terms[m]
        )
        active_grads[m][h] = unit_back(
            raw_queries[k], query_units[k][1], query_grad
        ) * head_size ** (-0.5)
        active_grads[m][heads + h] = unit_back(raw_probes[k], probe_units[k][1], probe_grad)
        active_grads[m][2 * heads + h] = solves[k]

    for m in range(seqs):
        shifted_logit, decays, strengths = decay_parts[m][:3]
        terms = col_terms[m] + jnp.transpose(row_terms[m])
        decay_grad = ones_dot(ones_back, terms)
        shifted_grad = decay_grad * -jnp.exp(param_ref[0:1, :]) * sigmoid(shifted_logit)
        logit_grad = jnp.where(
            col_index < heads,
            shifted_grad,
            jnp.where(col_index < 2 * heads, terms * strengths * (1.0 - strengths), 0.0),
        )
        logit_top, logit_rest = parts(logit_grad)
        logit_grad_ref[m] = (
            logit_top.astype(F32) + pltpu.roll(logit_rest.astype(F32), span // 2, 1)
        ).astype(BF16)
        decay_lane = col_index[0:1] < heads
        param_grad_ref[0:1, :] += jnp.sum(
            jnp.where(decay_lane, decay_grad * decays, 0.0), 0, keepdims=True
        )
        param_grad_ref[1:2, :] += jnp.sum(
            jnp.where(decay_lane, shifted_grad, 0.0), 0, keepdims=True
        )
        conv_grad = jnp.concatenate(active_grads[m], 1) * (
            openings[m] * (1.0 + curves[m] * (1.0 - openings[m]))
        )
        extended = jnp.concatenate([conv_grad, halo_ref[m]], 0)
        halo_ref[m] = conv_grad[:8]
        mixed_grad = jnp.zeros_like(conv_grad)
        for j in range(tap_count):
            reach = tap_count - 1 - j
            mixed_grad = mixed_grad + taps[j : j + 1] * extended[reach : reach + span]
            taps_grad_ref[j : j + 1, :] += jnp.sum(conv_grad * shifts[m][j], 0, keepdims=True)
        error_ref[m] = jnp.concatenate(
            [mixed_grad] + gate_grads[m * heads : (m + 1) * heads], 1
        ).astype(BF16)


def run_forward(mixed, gate, logits, taps, params, gain, heads, own, out_rows, collective_id):
    steps, seqs, span, _ = mixed.shape
    anywhere = pl.BlockSpec(memory_space=pl.ANY)
    head_size = gain.shape[1]
    width = heads * head_size

    def rows(columns):
        return pl.BlockSpec((None, seqs, span, columns), lambda j: (j, 0, 0, 0))

    def squares():
        return pl.BlockSpec((None, seqs, heads, head_size, head_size), lambda j: (j, 0, 0, 0, 0))

    def whole(array):
        return pl.BlockSpec(array.shape, lambda j: (0, 0))

    square = jax.ShapeDtypeStruct((steps, seqs, heads, head_size, head_size), F32)
    lower = jax.ShapeDtypeStruct((steps, seqs, heads, span, span), F32)
    flat = jax.ShapeDtypeStruct((steps, seqs, span, width), F32)
    return pl.pallas_call(
        mixer_forward,
        grid=(steps,),
        in_specs=[
            rows(3 * width),
            rows(width),
            rows(logits.shape[-1]),
            whole(taps),
            whole(params),
            whole(gain),
            anywhere,
            anywhere,
        ],
        out_specs=[rows(width), squares(), squares(), rows(width), rows(width)] + [anywhere] * 2,
        out_shape=[
            jax.ShapeDtypeStruct((steps, seqs, span, width), BF16),
            square,
            lower,
            flat,
            flat,
            jax.ShapeDtypeStruct((steps,) + own.shape, own.dtype),
            jax.ShapeDtypeStruct(out_rows.shape, out_rows.dtype),
        ],
        scratch_shapes=[
            pltpu.VMEM((seqs, heads, head_size, head_size), F32),
            pltpu.VMEM((seqs, 8, 3 * width), F32),
            pltpu.SemaphoreType.DMA((9 + heads,)),
            pltpu.SemaphoreType.DMA((9 + heads,)),
            pltpu.SemaphoreType.DMA((1 + heads,)),
        ],
        compiler_params=pltpu.CompilerParams(
            collective_id=collective_id, has_side_effects=True, vmem_limit_bytes=VMEM_LIMIT
        ),
        cost_estimate=lasting(55),
        name="mixer_forward",
    )(mixed, gate, logits, taps, params, gain, own, out_rows)


def run_backward(
    mixed, gate, logits, taps, params, gain, memory, inverse, fresh, out, grad, part, term, collective_id
):
    steps, seqs, span, _ = mixed.shape
    _, part_rows, columns = part.shape
    depth = lax.axis_size("dp")
    term_rows = term.shape[0] // depth
    heads, head_size = memory.shape[2], memory.shape[3]
    width = heads * head_size
    edge = 16

    def rows(columns):
        return pl.BlockSpec((None, seqs, span, columns), lambda j: (steps - 1 - j, 0, 0, 0))

    def squares():
        return pl.BlockSpec(
            (None, seqs, heads, head_size, head_size), lambda j: (steps - 1 - j, 0, 0, 0, 0)
        )

    def whole(shape):
        return pl.BlockSpec(shape, lambda j: (0, 0))

    before = pl.BlockSpec(
        (None, seqs, edge, 3 * width),
        lambda j: (jnp.maximum(steps - 2 - j, 0), 0, span // edge - 1, 0),
    )
    return pl.pallas_call(
        mixer_backward,
        grid=(steps,),
        in_specs=[
            rows(3 * width),
            before,
            rows(width),
            rows(logits.shape[-1]),
            whole(taps.shape),
            whole(params.shape),
            whole(gain.shape),
            squares(),
            squares(),
            rows(width),
            rows(width),
            rows(width),
            pl.BlockSpec(memory_space=pl.ANY),
            pl.BlockSpec(memory_space=pl.ANY),
        ],
        out_specs=[
            rows(4 * width),
            rows(logits.shape[-1]),
            whole((8, 3 * width)),
            whole((8, logits.shape[-1])),
            whole((8, head_size)),
            whole((part_rows, columns)),
            whole((term_rows, columns)),
        ],
        out_shape=[
            jax.ShapeDtypeStruct((steps, seqs, span, 4 * width), BF16),
            jax.ShapeDtypeStruct(logits.shape, BF16),
            jax.ShapeDtypeStruct((8, 3 * width), F32),
            jax.ShapeDtypeStruct((8, logits.shape[-1]), F32),
            jax.ShapeDtypeStruct((8, head_size), F32),
            jax.ShapeDtypeStruct((part_rows, columns), F32),
            jax.ShapeDtypeStruct((term_rows, columns), BF16),
        ],
        scratch_shapes=[
            pltpu.VMEM((seqs, heads, head_size, head_size), F32),
            pltpu.VMEM((seqs, 8, 3 * width), F32),
            pltpu.VMEM((4, part_rows, columns), BF16),
            pltpu.VMEM((4, part_rows, columns), BF16),
            pltpu.VMEM((part_rows, columns), BF16),
            pltpu.VMEM((2, part_rows, columns), BF16),
            pltpu.SemaphoreType.DMA((10,)),
            pltpu.SemaphoreType.DMA((10,)),
            pltpu.SemaphoreType.DMA((4,)),
            pltpu.VMEM((depth, term_rows, columns), BF16),
            pltpu.VMEM((depth - 1, 2, term_rows, columns), BF16),
            pltpu.SemaphoreType.DMA((2, depth - 1)),
            pltpu.SemaphoreType.DMA((2, depth - 1)),
            pltpu.SemaphoreType.DMA((depth // 2,)),
            pltpu.SemaphoreType.DMA((2, depth // 2)),
        ],
        compiler_params=pltpu.CompilerParams(
            collective_id=collective_id, has_side_effects=True, vmem_limit_bytes=VMEM_LIMIT
        ),
        cost_estimate=lasting(55),
        name="mixer_backward",
    )(mixed, mixed, gate, logits, taps, params, gain, memory, inverse, fresh, out, grad, part, term)


def gather_rows(value, axis):
    return lax.all_gather(value, axis, axis=0, tiled=True)


def scatter_rows(value, axis):
    return lax.psum_scatter(value, axis, scatter_dimension=0, tiled=True)


def plane_peers():
    me = lax.axis_index("seq")
    sibling = me + 1 - 2 * (me % 2)
    across = me + 2 - 4 * ((me // 2) % 2)
    along = me + 4 - 8 * (me // 4)
    return (me, sibling, across, along)


def greet(peers):
    barrier = pltpu.get_barrier_semaphore()
    for peer in peers:
        pl.semaphore_signal(
            barrier, inc=1, device_id={"seq": peer}, device_id_type=pl.DeviceIdType.MESH
        )
    pl.semaphore_wait(barrier, len(peers))


def send_to(peer, source, target, send_sem, recv_sem):
    return pltpu.make_async_remote_copy(
        src_ref=source,
        dst_ref=target,
        send_sem=send_sem,
        recv_sem=recv_sem,
        device_id={"seq": peer},
        device_id_type=pl.DeviceIdType.MESH,
    )


def gather_phases(own_ref, all_ref, send_sems, recv_sems, local_sem, start):
    me, sibling, across, along = plane_peers()
    far = along + across - me
    half = own_ref.shape[0] // 2
    upper, lower = pl.ds(0, half), pl.ds(half, half)
    copies = []

    def send(peer, source, target):
        k = start + len(copies)
        copy = send_to(peer, source, target, send_sems.at[k], recv_sems.at[k])
        copy.start()
        copies.append(copy)

    keep = pltpu.make_async_copy(own_ref, all_ref.at[me], local_sem)
    keep.start()
    send(across, own_ref, all_ref.at[me])
    send(along, own_ref, all_ref.at[me])
    send(sibling, own_ref, all_ref.at[me])
    yield
    copies[0].wait_recv()
    send(along, all_ref.at[across, upper], all_ref.at[across, upper])
    copies[1].wait_recv()
    send(across, all_ref.at[along, lower], all_ref.at[along, lower])
    send(sibling, all_ref.at[across], all_ref.at[across])
    send(sibling, all_ref.at[along], all_ref.at[along])
    yield
    copies[3].wait_recv()
    send(sibling, all_ref.at[far, upper], all_ref.at[far, upper])
    copies[4].wait_recv()
    send(sibling, all_ref.at[far, lower], all_ref.at[far, lower])
    yield
    for k in (2, 5, 6, 7, 8):
        copies[k].wait_recv()
    for copy in copies:
        copy.wait_send()
    keep.wait()
    yield


def chain_hops(all_ref, up_send, up_recv, down_send, down_recv):
    depth = all_ref.shape[0]
    place = lax.axis_index("dp")
    above, below = lax.rem(place + 1, depth), lax.rem(place + depth - 1, depth)

    def hop(slot, peer, send_sem, recv_sem):
        return pltpu.make_async_remote_copy(
            src_ref=all_ref.at[slot],
            dst_ref=all_ref.at[slot],
            send_sem=send_sem,
            recv_sem=recv_sem,
            device_id={"dp": peer},
            device_id_type=pl.DeviceIdType.MESH,
        )

    hops = []
    for t in range(depth - 1):
        up = hop(lax.rem(place + depth - t, depth), above, up_send.at[t], up_recv.at[t])
        down = hop(lax.rem(place + t, depth), below, down_send.at[t], down_recv.at[t])
        below_slot, above_slot = place + depth - 1 - t, place + 1 + t
        hops.append(
            (
                (up, (place < depth - 1) & (place >= t), place > t, lax.rem(below_slot, depth)),
                (
                    down,
                    (place > 0) & (place + t < depth),
                    above_slot < depth,
                    lax.rem(above_slot, depth),
                ),
            )
        )
    return hops


def hop_start(hop):
    for copy, leaves, _, _ in hop:
        pl.when(leaves)(copy.start)


def hop_arrive(hop):
    for copy, _, arrives, _ in hop:
        pl.when(arrives)(copy.wait_recv)


def hop_finish(hops):
    for hop in hops:
        for copy, leaves, _, _ in hop:
            pl.when(leaves)(copy.wait_send)


def greet_near(peers):
    place, depth = lax.axis_index("dp"), lax.axis_size("dp")
    barrier = pltpu.get_barrier_semaphore()
    mesh_ids = pl.DeviceIdType.MESH
    for peer in peers:
        pl.semaphore_signal(barrier, inc=1, device_id={"seq": peer}, device_id_type=mesh_ids)
    for peer in (lax.rem(place + 1, depth), lax.rem(place + depth - 1, depth)):
        pl.semaphore_signal(barrier, inc=1, device_id={"dp": peer}, device_id_type=mesh_ids)
    pl.semaphore_wait(barrier, len(peers) + 2)


def greet_all(ring, depth):
    me, place = lax.axis_index("seq"), lax.axis_index("dp")
    barrier = pltpu.get_barrier_semaphore()
    for axis, index, size in (("seq", me, ring), ("dp", place, depth)):
        for k in range(1, size):
            pl.semaphore_signal(
                barrier,
                inc=1,
                device_id={axis: lax.rem(index + k, size)},
                device_id_type=pl.DeviceIdType.MESH,
            )
    pl.semaphore_wait(barrier, ring + depth - 2)


def spread_units(piece, target_ref, depth):
    ring, _, columns = piece.shape
    own = columns // (2 * depth)
    for k in range(2 * depth):
        block = jnp.concatenate([piece[s, :, k * own : (k + 1) * own] for s in range(ring)], 1)
        target_ref[:, k * ring * own : (k + 1) * ring * own] = block.astype(target_ref.dtype)


def exchange_copies(cut_ref, land, send_sems, recv_sems, start):
    ring = cut_ref.shape[0]
    me = lax.axis_index("seq")
    copies = []
    for k in range(1, ring):
        peer = lax.rem(me + k, ring)
        copy = send_to(
            peer, cut_ref.at[peer], land, send_sems.at[start + k - 1], recv_sems.at[start + k - 1]
        )
        copy.start()
        copies.append(copy)
    return copies


def rank_head(rank, j, heads):
    return rank // 2 + lax.axis_size("seq") // 2 * (heads * (rank % 2) + j)


def plane_open_kernel(
    heads,
    first_ref,
    weight_hbm,
    pair_hbm,
    lanes_hbm,
    first_all_hbm,
    weight_all_hbm,
    pair_all_ref,
    mixed_ref,
    gate_ref,
    logit_ref,
    first_all_ref,
    weight_all_ref,
    pair_ref,
    cut_ref,
    lanes_ref,
    total_ref,
    send_sems,
    recv_sems,
    local_sems,
    *chain_sems,
):
    place, me = lax.axis_index("dp"), lax.axis_index("seq")
    depth, rows = weight_all_ref.shape[0], weight_hbm.shape[0]
    ring, units = cut_ref.shape[0], cut_ref.shape[2] // 2
    width = weight_all_ref.shape[2] // 4
    load = pltpu.make_async_copy(pair_hbm, pair_ref, local_sems.at[0])
    load.start()
    lanes_load = pltpu.make_async_copy(lanes_hbm, lanes_ref, local_sems.at[3])
    lanes_load.start()
    greet_all(ring, depth)
    keeps, early = [], []
    own_rows = pl.ds(pl.multiple_of(me * rows, rows), rows)
    size = width // heads
    for part in range(4 * heads):
        block, j = part // heads, part % heads
        target = weight_all_ref.at[place, own_rows, pl.ds(part * size, size)]

        def source(peer, block=block, j=j):
            start = (block * ring * heads + rank_head(peer, j, heads)) * size
            return weight_hbm.at[:, pl.ds(pl.multiple_of(start, size), size)]

        keep = pltpu.make_async_copy(source(me), target, local_sems.at[4 + part])
        keep.start()
        keeps.append(keep)
        for k in range(1, ring):
            peer = lax.rem(me + k, ring)
            spot = part * (ring - 1) + k - 1
            copy = send_to(peer, source(peer), target, send_sems.at[spot], recv_sems.at[spot])
            copy.start()
            early.append(copy)
    for copy in early:
        copy.wait_recv()
    for keep in keeps:
        keep.wait()
    base = 4 * heads * (ring - 1)
    hops = chain_hops(weight_all_ref, *chain_sems)
    first = gather_phases(first_ref, first_all_ref, send_sems, recv_sems, local_sems.at[1], base)
    hop_start(hops[0])
    next(first)
    load.wait()
    own = units // depth
    half = pair_ref.shape[1] // 2
    for s in range(ring):
        pieces = []
        for g in range(2):
            for z in range(depth):
                start = g * half + (z * ring + s) * own
                pieces.append(pair_ref[:, start : start + own])
        cut_ref[s] = jnp.concatenate(pieces, 1)
    pair_keep = pltpu.make_async_copy(cut_ref.at[me], pair_all_ref.at[me], local_sems.at[2])
    pair_keep.start()
    later = exchange_copies(cut_ref, pair_all_ref.at[me], send_sems, recv_sems, base + 9)
    hop_arrive(hops[0])
    hop_start(hops[1])
    next(first)
    for t in range(1, depth - 2):
        hop_arrive(hops[t])
        hop_start(hops[t + 1])
    next(first)
    next(first)
    lanes_load.wait()
    deep = weight_all_ref.shape[1]

    def spread_slot(slot, fresh=False):
        def run():
            at = pl.ds(pl.multiple_of(slot * deep, deep), deep)

            @pl.loop(0, ring)
            def _(r):
                term = low_dot(first_all_ref[r, :, at], weight_all_ref[slot], NN)
                total_ref[r] = term if fresh else total_ref[r] + term

        return run

    @pl.loop(0, ring)
    def _(r):
        logit_ref[r] = low_dot(first_all_ref[r], lanes_ref[...], NN)

    saves = [pltpu.make_async_copy(first_all_ref, first_all_hbm, local_sems.at[0])]
    saves[0].start()
    spread_slot(place, True)()
    for hop in hops[:-1]:
        for _, _, arrives, slot in hop:
            pl.when(arrives)(spread_slot(slot))
    hop_arrive(hops[-1])
    saves.append(pltpu.make_async_copy(weight_all_ref, weight_all_hbm, local_sems.at[1]))
    saves[1].start()
    for _, _, arrives, slot in hops[-1]:
        pl.when(arrives)(spread_slot(slot))

    @pl.loop(0, ring)
    def _(r):
        mixed_ref[r] = total_ref[r, :, : 3 * width].astype(BF16)
        gate_ref[r] = total_ref[r, :, 3 * width :]

    for copy in later:
        copy.wait_recv()
    hop_finish(hops)
    for copy in early + later:
        copy.wait_send()
    pair_keep.wait()
    for save in saves:
        save.wait()


def plane_open(first, weight, pair, lanes, heads, collective_id):
    ring, depth = lax.axis_size("seq"), lax.axis_size("dp")
    rows, columns = first.shape
    weight_rows = weight.shape[0]
    width = weight.shape[1] // (4 * ring)
    total = (4 * heads + 1) * (ring - 1) + 9
    cut = jax.ShapeDtypeStruct((ring, weight_rows, pair.shape[1] // ring), pair.dtype)
    first_shape, weight_shape = (ring, rows, columns), (depth, ring * weight_rows, 4 * width)
    vmem, anywhere = pl.BlockSpec(memory_space=pltpu.VMEM), pl.BlockSpec(memory_space=pl.ANY)
    return pl.pallas_call(
        functools.partial(plane_open_kernel, heads),
        out_shape=[
            jax.ShapeDtypeStruct(first_shape, BF16),
            jax.ShapeDtypeStruct(weight_shape, BF16),
            cut,
            jax.ShapeDtypeStruct((ring, rows, 3 * width), BF16),
            jax.ShapeDtypeStruct((ring, rows, width), F32),
            jax.ShapeDtypeStruct((ring, rows, lanes.shape[1]), F32),
        ],
        in_specs=[anywhere] * 4,
        out_specs=[anywhere] * 3 + [vmem] * 3,
        scratch_shapes=[
            pltpu.VMEM(first_shape, BF16),
            pltpu.VMEM(weight_shape, BF16),
            pltpu.VMEM(pair.shape, BF16),
            pltpu.VMEM(cut.shape, BF16),
            pltpu.VMEM(lanes.shape, BF16),
            pltpu.VMEM((ring, rows, 4 * width), F32),
            pltpu.SemaphoreType.DMA((total,)),
            pltpu.SemaphoreType.DMA((total,)),
            pltpu.SemaphoreType.DMA((4 + 4 * heads,)),
        ]
        + [pltpu.SemaphoreType.DMA((depth - 1,))] * 4,
        compiler_params=pltpu.CompilerParams(
            collective_id=collective_id, has_side_effects=True, vmem_limit_bytes=VMEM_LIMIT
        ),
        cost_estimate=lasting(150),
        name="plane_open",
    )(first, weight, pair, lanes)


def trade_in_steps(rows_ref, rows_out_ref, send_sems, recv_sems, local_sems, heads):
    me = lax.axis_index("seq")
    core = lax.rem(me, 2)
    sibling = me + 1 - 2 * core
    rows = rows_out_ref.shape[0] // (2 * heads)

    def rows_of(ref, spot):
        return ref.at[pl.ds(pl.multiple_of(spot * rows, rows), rows)]

    copies, keeps = [], []
    for j in range(heads):
        target = rows_of(rows_out_ref, 2 * j + core)
        theirs = rows_of(rows_ref, heads * (1 - core) + j)
        copies.append(send_to(sibling, theirs, target, send_sems.at[9 + j], recv_sems.at[9 + j]))
        keeps.append(
            pltpu.make_async_copy(rows_of(rows_ref, heads * core + j), target, local_sems.at[1 + j])
        )
    step, steps = pl.program_id(0), pl.num_programs(0)

    @pl.when(step == 0)
    def _():
        for copy in copies + keeps:
            copy.start()

    @pl.when(step == steps - 1)
    def _():
        for copy in copies:
            copy.wait_recv()
            copy.wait_send()
        for keep in keeps:
            keep.wait()


def gather_in_steps(own_ref, all_ref, send_sems, recv_sems, local_sem):
    me, sibling, across, along = plane_peers()
    far = along + across - me
    half = own_ref.shape[0] // 2
    upper, lower = pl.ds(0, half), pl.ds(half, half)
    keep = pltpu.make_async_copy(own_ref, all_ref.at[me], local_sem)
    plan = [
        (across, own_ref, all_ref.at[me]),
        (along, own_ref, all_ref.at[me]),
        (sibling, own_ref, all_ref.at[me]),
        (along, all_ref.at[across, upper], all_ref.at[across, upper]),
        (across, all_ref.at[along, lower], all_ref.at[along, lower]),
        (sibling, all_ref.at[across], all_ref.at[across]),
        (sibling, all_ref.at[along], all_ref.at[along]),
        (sibling, all_ref.at[far, upper], all_ref.at[far, upper]),
        (sibling, all_ref.at[far, lower], all_ref.at[far, lower]),
    ]
    copies = [
        send_to(peer, source, target, send_sems.at[k], recv_sems.at[k])
        for k, (peer, source, target) in enumerate(plan)
    ]
    step, steps = pl.program_id(0), pl.num_programs(0)

    @pl.when(step == 0)
    def _():
        greet((sibling, across, along))
        keep.start()
        for k in (0, 1, 2):
            copies[k].start()

    @pl.when(step == 3)
    def _():
        copies[0].wait_recv()
        copies[1].wait_recv()
        for k in (3, 4, 5, 6):
            copies[k].start()

    @pl.when(step == 5)
    def _():
        copies[3].wait_recv()
        copies[4].wait_recv()
        for k in (7, 8):
            copies[k].start()

    @pl.when(step == steps - 1)
    def _():
        for k in (2, 5, 6, 7, 8):
            copies[k].wait_recv()
        for copy in copies:
            copy.wait_send()
        keep.wait()


def scatter_in_steps(
    part_ref,
    sum_ref,
    own_ref,
    near_ref,
    far_in_ref,
    side_in_ref,
    send_sems,
    recv_sems,
    load_sems,
):
    me, sibling, across, along = plane_peers()
    far = along + across - me
    flip = sibling - me
    rows = sum_ref.shape[0]
    half = rows // 2
    upper, lower = pl.ds(0, half), pl.ds(half, half)
    slabs = (far, across, along, me)
    loads = [
        pltpu.make_async_copy(part_ref.at[slab], own_ref.at[k], load_sems.at[k])
        for k, slab in enumerate(slabs)
    ]
    plan = [(sibling, part_ref.at[slab + flip], near_ref.at[k]) for k, slab in enumerate(slabs)]
    plan += [
        (across, own_ref.at[0, upper], far_in_ref.at[upper]),
        (along, own_ref.at[0, lower], far_in_ref.at[lower]),
        (across, own_ref.at[1, upper], side_in_ref.at[0, upper]),
        (along, own_ref.at[2, lower], side_in_ref.at[1, lower]),
        (along, own_ref.at[2, upper], side_in_ref.at[1, upper]),
        (across, own_ref.at[1, lower], side_in_ref.at[0, lower]),
    ]
    copies = [
        send_to(peer, source, target, send_sems.at[k], recv_sems.at[k])
        for k, (peer, source, target) in enumerate(plan)
    ]
    step, steps = pl.program_id(0), pl.num_programs(0)
    tall = 32

    def fold(target, other, start, size):
        @pl.loop(0, size // tall)
        def _(i):
            at = pl.ds(pl.multiple_of(start + i * tall, tall), tall)
            target[at] = (target[at].astype(F32) + other[at].astype(F32)).astype(BF16)

    def join(k):
        loads[k].wait()
        copies[k].wait_recv()
        fold(own_ref.at[k], near_ref.at[k], 0, rows)

    @pl.when(step == 0)
    def _():
        greet_near((sibling, across, along))
        for k in range(4):
            loads[k].start()
            copies[k].start()

    @pl.when(step == 1)
    def _():
        join(0)
        copies[4].start()
        copies[5].start()
        join(1)
        copies[6].start()
        join(2)
        copies[7].start()

    @pl.when(step == 3)
    def _():
        copies[4].wait_recv()
        fold(own_ref.at[2], far_in_ref, 0, half)
        copies[8].start()
        copies[5].wait_recv()
        fold(own_ref.at[1], far_in_ref, half, half)
        copies[9].start()

    @pl.when(step == steps - 1)
    def _():
        loads[3].wait()
        copies[3].wait_recv()
        for copy in copies[6:]:
            copy.wait_recv()

        @pl.loop(0, rows // tall)
        def _(i):
            at = pl.ds(pl.multiple_of(i * tall, tall), tall)
            sum_ref[at] = (
                own_ref[3, at].astype(F32)
                + near_ref[3, at].astype(F32)
                + side_in_ref[0, at].astype(F32)
                + side_in_ref[1, at].astype(F32)
            )

        for copy in copies:
            copy.wait_send()


def sums_in_steps(
    term_ref, share_ref, held_ref, land_ref, up_sems, down_sems, load_sems, trade_sems
):
    depth, rows, _ = held_ref.shape
    place = lax.axis_index("dp")
    above, below = lax.rem(place + 1, depth), lax.rem(place + depth - 1, depth)
    last = depth - 1
    mesh_ids = pl.DeviceIdType.MESH
    me = lax.axis_index("seq")
    core = lax.rem(me, 2)
    heads = depth // 2
    loads, trades = [], []
    for j in range(heads):
        target = held_ref.at[heads * core + j]

        def rows_of(spot):
            return term_ref.at[pl.ds(pl.multiple_of(spot * rows, rows), rows)]

        loads.append(pltpu.make_async_copy(rows_of(2 * j + core), target, load_sems.at[j]))
        trades.append(
            send_to(
                me + 1 - 2 * core,
                rows_of(2 * j + 1 - core),
                target,
                trade_sems.at[0, j],
                trade_sems.at[1, j],
            )
        )
    hops = []
    for r in range(last):
        hop = []
        for k, (peer, sems, block, leaves, mine, arrives) in enumerate(
            (
                (above, up_sems, place + last - r, place < r + 1, place + last - 1 - r, place > 0),
                (below, down_sems, place - last + r, place > last - 1 - r, place - last + 1 + r, place < last),
            )
        ):
            inside = (mine >= 0) & (mine <= last)
            spot = lax.rem(block + depth, depth)
            copy = pltpu.make_async_remote_copy(
                src_ref=held_ref.at[spot],
                dst_ref=land_ref.at[r, k],
                send_sem=sems.at[0, r],
                recv_sem=sems.at[1, r],
                device_id={"dp": peer},
                device_id_type=mesh_ids,
            )
            hop.append((copy, leaves, arrives & inside, lax.rem(mine + depth, depth)))
        hops.append(hop)
    step, steps = pl.program_id(0), pl.num_programs(0)

    def start(r):
        for copy, leaves, _, _ in hops[r]:
            pl.when(leaves)(copy.start)

    def arrive(r):
        for k, (copy, _, arrives, block) in enumerate(hops[r]):

            @pl.when(arrives)
            def _(copy=copy, block=block, k=k):
                copy.wait_recv()
                total = held_ref[block].astype(F32) + land_ref[r, k].astype(F32)
                held_ref[block] = total.astype(BF16)

    @pl.when(step == 0)
    def _():
        for copy in loads + trades:
            copy.start()

    @pl.when(step == 1)
    def _():
        for load in loads:
            load.wait()
        for trade in trades:
            trade.wait_recv()
            trade.wait_send()
        start(0)

    for r, turn in enumerate((3, 5, steps - 1)):

        @pl.when(step == turn)
        def _(r=r):
            arrive(r)
            if r + 1 < last:
                start(r + 1)
            else:
                for hop in hops:
                    for copy, leaves, _, _ in hop:
                        pl.when(leaves)(copy.wait_send)
                share_ref[...] = held_ref[place]


def small_sum_kernel(
    heads,
    own_ref,
    cut_ref,
    all_ref,
    shared_ref,
    joined_ref,
    swapped_ref,
    stage_ref,
    total_ref,
    send_sems,
    recv_sems,
    local_sem,
):
    depth, ring = stage_ref.shape[0], all_ref.shape[0]
    place, me = lax.axis_index("dp"), lax.axis_index("seq")
    mesh_ids = pl.DeviceIdType.MESH
    columns = [lax.rem(place + k, depth) for k in range(1, depth)]
    plane = [lax.rem(me + k, ring) for k in range(1, ring)]
    greet_all(ring, depth)
    keep = pltpu.make_async_copy(cut_ref.at[me], swapped_ref.at[me], local_sem)
    keep.start()
    first = []
    for k, peer in enumerate(columns):
        copy = pltpu.make_async_remote_copy(
            src_ref=own_ref,
            dst_ref=stage_ref.at[place],
            send_sem=send_sems.at[k],
            recv_sem=recv_sems.at[k],
            device_id={"dp": peer},
            device_id_type=mesh_ids,
        )
        copy.start()
        first.append(copy)
    swaps = exchange_copies(
        cut_ref, swapped_ref.at[me], send_sems, recv_sems, depth + ring - 2
    )
    stage_ref[place] = own_ref[...]
    for copy in first:
        copy.wait_recv()
    total = stage_ref[0]
    for k in range(1, depth):
        total = total + stage_ref[k]
    total_ref[...] = total
    second = []
    for k, peer in enumerate(plane):
        copy = pltpu.make_async_remote_copy(
            src_ref=total_ref,
            dst_ref=all_ref.at[me],
            send_sem=send_sems.at[depth - 1 + k],
            recv_sem=recv_sems.at[depth - 1 + k],
            device_id={"seq": peer},
            device_id_type=mesh_ids,
        )
        copy.start()
        second.append(copy)
    all_ref[me] = total
    for copy in second:
        copy.wait_recv()
    shared_rows = shared_ref.shape[0]
    shared = all_ref[0, :shared_rows]
    for s in range(1, ring):
        shared = shared + all_ref[s, :shared_rows]
    shared_ref[...] = shared
    for copy in swaps:
        copy.wait_recv()
    keep.wait()
    size = cut_ref.shape[2] // (4 * heads)
    for part in range(4 * heads):
        block, j = part // heads, part % heads
        for s in range(ring):
            start = (block * ring * heads + rank_head(s, j, heads)) * size
            joined_ref[:, start : start + size] = swapped_ref[
                s, :, part * size : (part + 1) * size
            ].astype(F32)
    for copy in first + second + swaps:
        copy.wait_send()


def small_sum(own, shared_rows, cut, heads, collective_id):
    depth, ring = lax.axis_size("dp"), lax.axis_size("seq")
    count = depth + 2 * ring - 3
    vmem, anywhere = pl.BlockSpec(memory_space=pltpu.VMEM), pl.BlockSpec(memory_space=pl.ANY)
    return pl.pallas_call(
        functools.partial(small_sum_kernel, heads),
        out_shape=[
            jax.ShapeDtypeStruct((ring,) + own.shape, F32),
            jax.ShapeDtypeStruct((shared_rows, own.shape[1]), F32),
            jax.ShapeDtypeStruct((cut.shape[1], ring * cut.shape[2]), F32),
        ],
        in_specs=[vmem, anywhere],
        out_specs=[vmem, vmem, vmem],
        scratch_shapes=[
            pltpu.VMEM(cut.shape, cut.dtype),
            pltpu.VMEM((depth,) + own.shape, F32),
            pltpu.VMEM(own.shape, F32),
            pltpu.SemaphoreType.DMA((count,)),
            pltpu.SemaphoreType.DMA((count,)),
            pltpu.SemaphoreType.DMA,
        ],
        compiler_params=pltpu.CompilerParams(collective_id=collective_id, has_side_effects=True),
        cost_estimate=lasting(20),
        name="small_sum",
    )(own, cut)


def greet_plane(ring):
    me = lax.axis_index("seq")
    greet([lax.rem(me + k, ring) for k in range(1, ring)])


def plane_scatter_dot_kernel(count, dims, fill, swaps, back, *refs):
    refs = list(refs)

    def take(size):
        taken = refs[:size]
        del refs[:size]
        return taken

    left_hbm, right_hbm, fill_hbm = take(count), take(count), take(int(fill))
    cut_refs, back_hbm = take(swaps), take(2 * back)
    (sum_ref,) = take(1)
    terms = take(count if fill else 0)
    spread_refs, swapped_refs = take(swaps), take(swaps)
    lefts, rights, fill_refs = take(count), take(count), take(int(fill))
    out_ref, own_ref, near_ref, far_in_ref, side_in_ref = take(5)
    send_sems, recv_sems, load_sems = take(3)
    loads = []
    for k in range(count):
        for source, target in ((left_hbm[k], lefts[k]), (right_hbm[k], rights[k])):
            load = pltpu.make_async_copy(source, target, load_sems.at[len(loads)])
            load.start()
            loads.append(load)
    me, sibling, across, along = plane_peers()
    far = along + across - me
    flip = sibling - me
    if back:
        error_ref, down_ref, error_sems, down_sem = refs
        error_order = [far + flip, far, across + flip, across, along + flip, along, sibling, me]
        down_load = pltpu.make_async_copy(back_hbm[1], down_ref, down_sem)
        down_load.start()
        error_loads = [
            pltpu.make_async_copy(back_hbm[0].at[slab], error_ref.at[k % 2], error_sems.at[k % 2])
            for k, slab in enumerate(error_order)
        ]
        error_loads[0].start()
        error_loads[1].start()
    if fill:
        fill_load = pltpu.make_async_copy(fill_hbm[0], fill_refs[0], load_sems.at[2 * count])
        fill_load.start()
    rows, columns = sum_ref.shape
    half = rows // 2
    upper, lower = pl.ds(0, half), pl.ds(half, half)
    swapped = []
    if swaps:
        greet_plane(lefts[0].shape[0])
        keep = pltpu.make_async_copy(
            cut_refs[0].at[me], swapped_refs[0].at[me], load_sems.at[2 * count]
        )
        keep.start()
        swapped = exchange_copies(
            cut_refs[0], swapped_refs[0].at[me], send_sems, recv_sems, 10
        )
    else:
        greet((sibling, across, along))
    for load in loads:
        load.wait()
    if back:
        down_load.wait()
    wide = 512
    turns = iter(range(8))

    def feed_back(slab):
        k = next(turns)
        error_loads[k].wait()
        units = down_ref.shape[0]
        grad = low_dot(error_ref[k % 2], down_ref[...], NT)
        gate = lefts[0][slab, :, :units].astype(F32)
        up = lefts[0][slab, :, units:].astype(F32)
        opening = sigmoid(gate)
        gate_err = grad * up * (opening * (1.0 + gate * (1.0 - opening)))
        up_err = grad * (gate * opening)
        lefts[0][slab] = jnp.concatenate([gate_err, up_err], 1).astype(BF16)
        if k + 2 < len(error_loads):
            error_loads[k + 2].start()

    def slab_dot(slab, target):
        if back:
            feed_back(slab)

        @pl.loop(0, columns // wide)
        def _(i):
            at = pl.ds(pl.multiple_of(i * wide, wide), wide)
            total = None
            for k in range(count):
                right = rights[k][:, at] if dims[1] == (0,) else rights[k][at, :]
                term = low_dot(lefts[k][slab], right, dims)
                total = term if total is None else total + term
            target[:, at] = total.astype(BF16)

    def send(k, peer, source, target):
        copy = send_to(peer, source, target, send_sems.at[k], recv_sems.at[k])
        copy.start()
        return copy

    step = 32

    def fold(target, other, start, size):
        @pl.loop(0, size // step)
        def _(i):
            at = pl.ds(pl.multiple_of(start + i * step, step), step)
            target[at] = (target[at].astype(F32) + other[at].astype(F32)).astype(BF16)

    nears = []

    def near_slab(k, slab):
        slab_dot(slab + flip, out_ref.at[k])
        nears.append(send(k, sibling, out_ref.at[k], near_ref.at[k]))

    near_slab(0, far)
    slab_dot(far, own_ref.at[0])
    near_slab(1, across)
    nears[0].wait_recv()
    fold(own_ref.at[0], near_ref.at[0], 0, rows)
    copies = [
        send(4, across, own_ref.at[0, upper], far_in_ref.at[upper]),
        send(5, along, own_ref.at[0, lower], far_in_ref.at[lower]),
    ]
    slab_dot(across, own_ref.at[1])
    near_slab(2, along)
    nears[1].wait_recv()
    fold(own_ref.at[1], near_ref.at[1], 0, rows)
    copies.append(send(6, across, own_ref.at[1, upper], side_in_ref.at[0, upper]))
    slab_dot(along, own_ref.at[2])
    near_slab(3, me)
    nears[2].wait_recv()
    fold(own_ref.at[2], near_ref.at[2], 0, rows)
    copies.append(send(7, along, own_ref.at[2, lower], side_in_ref.at[1, lower]))
    slab_dot(me, own_ref.at[3])
    copies[0].wait_recv()
    fold(own_ref.at[2], far_in_ref, 0, half)
    copies.append(send(8, along, own_ref.at[2, upper], side_in_ref.at[1, upper]))
    copies[1].wait_recv()
    fold(own_ref.at[1], far_in_ref, half, half)
    copies.append(send(9, across, own_ref.at[1, lower], side_in_ref.at[0, lower]))
    if swaps:
        for copy in swapped:
            copy.wait_recv()
        keep.wait()
        spread_units(swapped_refs[0], spread_refs[0], lax.axis_size("dp"))
    if fill:
        fill_load.wait()
        tall = 256

        @pl.loop(0, terms[0].shape[0] // tall)
        def _(i):
            at = pl.ds(pl.multiple_of(i * tall, tall), tall)
            turned = fill_refs[0][:, at]
            for k in range(count):
                wide_left = lefts[k][...].reshape(-1, lefts[k].shape[2])
                terms[k][at, :] = low_dot(turned, wide_left, TN).astype(BF16)

    nears[3].wait_recv()

    def finish(a, start):
        @pl.loop(0, half // step)
        def _(i):
            at = pl.ds(pl.multiple_of(start + i * step, step), step)
            sum_ref[at] = (
                own_ref[3, at].astype(F32)
                + near_ref[3, at].astype(F32)
                + side_in_ref[0, at].astype(F32)
                + side_in_ref[1, at].astype(F32)
            )

    for copy in copies[2:]:
        copy.wait_recv()
    finish(0, 0)
    finish(1, half)
    for copy in nears + copies + swapped:
        copy.wait_send()


def plane_scatter_dot(lefts, rights, dims, collective_id, fill=None, cut=None, back=()):
    count = len(lefts)
    ring, rows, _ = lefts[0].shape
    columns = rights[0].shape[1 - dims[1][0]]
    filled = fill is not None
    fills = [fill] if filled else []
    vmem, anywhere = pl.BlockSpec(memory_space=pltpu.VMEM), pl.BlockSpec(memory_space=pl.ANY)
    back_scratch = []
    if back:
        back_scratch = [
            pltpu.VMEM((2,) + back[0].shape[1:], BF16),
            pltpu.VMEM(back[1].shape, BF16),
            pltpu.SemaphoreType.DMA((2,)),
            pltpu.SemaphoreType.DMA,
        ]
    cuts = [] if cut is None else [cut]
    total = 10 + len(cuts) * (ring - 1)
    term_shapes = [
        jax.ShapeDtypeStruct((fill.shape[1], left.shape[2]), BF16) for left in lefts if filled
    ]
    return pl.pallas_call(
        functools.partial(plane_scatter_dot_kernel, count, dims, filled, len(cuts), len(back) // 2),
        out_shape=[jax.ShapeDtypeStruct((rows, columns), F32)]
        + term_shapes
        + [jax.ShapeDtypeStruct((cut.shape[1], ring * cut.shape[2]), F32) for cut in cuts],
        in_specs=[anywhere] * (2 * count + len(fills) + len(cuts) + len(back)),
        out_specs=[vmem] * (1 + len(term_shapes) + len(cuts)),
        scratch_shapes=[pltpu.VMEM(cut.shape, BF16) for cut in cuts]
        + [pltpu.VMEM(left.shape, BF16) for left in lefts]
        + [pltpu.VMEM(right.shape, BF16) for right in rights]
        + [pltpu.VMEM(value.shape, BF16) for value in fills]
        + [
            pltpu.VMEM((4, rows, columns), BF16),
            pltpu.VMEM((4, rows, columns), BF16),
            pltpu.VMEM((4, rows, columns), BF16),
            pltpu.VMEM((rows, columns), BF16),
            pltpu.VMEM((2, rows, columns), BF16),
            pltpu.SemaphoreType.DMA((total,)),
            pltpu.SemaphoreType.DMA((total,)),
            pltpu.SemaphoreType.DMA((2 * count + len(fills) + len(cuts),)),
        ]
        + back_scratch,
        compiler_params=pltpu.CompilerParams(
            collective_id=collective_id, has_side_effects=True, vmem_limit_bytes=VMEM_LIMIT
        ),
        cost_estimate=lasting(45),
        name="plane_scatter_dot",
    )(*lefts, *rights, *fills, *cuts, *back)


def gather_in_turn(own_ref, all_ref, send_sems, recv_sems, use):
    me, sibling, across, along = plane_peers()
    far = along + across - me
    flip = sibling - me
    half = own_ref.shape[0] // 2
    upper, lower = pl.ds(0, half), pl.ds(half, half)
    copies = []

    def send(peer, source, target):
        k = len(copies)
        copy = send_to(peer, source, target, send_sems.at[k], recv_sems.at[k])
        copy.start()
        copies.append(copy)

    send(across, own_ref, all_ref.at[me])
    send(along, own_ref, all_ref.at[me])
    send(sibling, own_ref, all_ref.at[me])
    all_ref[me] = own_ref[...]
    use(me)
    copies[2].wait_recv()
    use(sibling)
    copies[0].wait_recv()
    send(along, all_ref.at[across, upper], all_ref.at[across, upper])
    copies[1].wait_recv()
    send(across, all_ref.at[along, lower], all_ref.at[along, lower])
    send(sibling, all_ref.at[across], all_ref.at[across])
    send(sibling, all_ref.at[along], all_ref.at[along])
    use(across)
    use(along)
    copies[5].wait_recv()
    use(across + flip)
    copies[6].wait_recv()
    use(along + flip)
    copies[3].wait_recv()
    send(sibling, all_ref.at[far, upper], all_ref.at[far, upper])
    copies[4].wait_recv()
    send(sibling, all_ref.at[far, lower], all_ref.at[far, lower])
    use(far)
    copies[7].wait_recv()
    copies[8].wait_recv()
    use(far + flip)
    for copy in copies:
        copy.wait_send()


def gather_feed_kernel(
    own_hbm,
    pair_hbm,
    error_hbm,
    all_hbm,
    activated_hbm,
    pair_part_hbm,
    down_term_ref,
    own_ref,
    pair_ref,
    error_ref,
    all_ref,
    activated_out,
    pair_out,
    total_ref,
    send_sems,
    recv_sems,
    load_sems,
    save_sems,
):
    loads = []
    for source, target in (
        (own_hbm, own_ref),
        (pair_hbm, pair_ref),
        (error_hbm, error_ref),
    ):
        load = pltpu.make_async_copy(source, target, load_sems.at[len(loads)])
        load.start()
        loads.append(load)
    greet(plane_peers()[1:])
    loads[0].wait()
    waiting = loads[1:]
    saves = []
    tall = 256
    wide = 512
    rows, columns = own_ref.shape
    units = pair_ref.shape[1] // 2


    def use(slab):
        first = bool(waiting)
        while waiting:
            waiting.pop().wait()
        turn = len(saves) % 2
        if len(saves) > 1:
            for save in saves[-2]:
                save.wait()

        @pl.loop(0, rows // tall)
        def _(i):
            at = pl.ds(pl.multiple_of(i * tall, tall), tall)
            values = all_ref[slab, at, :]
            pair = low_dot(values, pair_ref[...], NN)
            gate, up = pair[:, :units], pair[:, units:]
            activated_out[turn, at, :] = (gate * sigmoid(gate) * up).astype(BF16)
            pair_out[turn, at, :] = pair.astype(BF16)

        batch = []
        for k, (source, target) in enumerate(
            (
                (activated_out.at[turn], activated_hbm.at[slab]),
                (pair_out.at[turn], pair_part_hbm.at[slab]),
                (all_ref.at[slab], all_hbm.at[slab]),
            )
        ):
            save = pltpu.make_async_copy(source, target, save_sems.at[turn, k])
            save.start()
            batch.append(save)
        saves.append(batch)

        @pl.loop(0, columns // wide)
        def _(i):
            at = pl.ds(pl.multiple_of(i * wide, wide), wide)
            term = low_dot(activated_out[turn], error_ref[slab, :, at], TN)
            if first:
                total_ref[:, at] = term
            else:
                total_ref[:, at] += term

    gather_in_turn(own_ref, all_ref, send_sems, recv_sems, use)
    down_term_ref[...] = total_ref[...].astype(BF16)
    for batch in saves[-2:]:
        for save in batch:
            save.wait()


def gather_feed(own, pair_own, error_all, collective_id):
    ring = lax.axis_size("seq")
    rows, columns = own.shape
    units = pair_own.shape[1] // 2
    anywhere = pl.BlockSpec(memory_space=pl.ANY)
    return pl.pallas_call(
        gather_feed_kernel,
        out_shape=[
            jax.ShapeDtypeStruct((ring, rows, columns), BF16),
            jax.ShapeDtypeStruct((ring, rows, units), BF16),
            jax.ShapeDtypeStruct((ring, rows, 2 * units), BF16),
            jax.ShapeDtypeStruct((units, columns), BF16),
        ],
        in_specs=[anywhere] * 3,
        out_specs=[anywhere] * 3 + [pl.BlockSpec(memory_space=pltpu.VMEM)],
        scratch_shapes=[
            pltpu.VMEM((rows, columns), BF16),
            pltpu.VMEM(pair_own.shape, BF16),
            pltpu.VMEM((ring, rows, columns), BF16),
            pltpu.VMEM((ring, rows, columns), BF16),
            pltpu.VMEM((2, rows, units), BF16),
            pltpu.VMEM((2, rows, 2 * units), BF16),
            pltpu.VMEM((units, columns), F32),
            pltpu.SemaphoreType.DMA((9,)),
            pltpu.SemaphoreType.DMA((9,)),
            pltpu.SemaphoreType.DMA((3,)),
            pltpu.SemaphoreType.DMA((2, 3)),
        ],
        compiler_params=pltpu.CompilerParams(
            collective_id=collective_id, has_side_effects=True, vmem_limit_bytes=VMEM_LIMIT
        ),
        cost_estimate=lasting(46),
        name="gather_feed",
    )(own, pair_own, error_all)


def gather_branch_kernel(
    own_hbm,
    gated_hbm,
    weight_hbm,
    activated_hbm,
    down_hbm,
    grad_ref,
    term_ref,
    part_hbm,
    own_ref,
    gated_ref,
    weight_ref,
    activated_ref,
    down_ref,
    all_ref,
    total_ref,
    part_out,
    send_sems,
    recv_sems,
    load_sems,
    save_sems,
):
    loads = []
    for source, target in (
        (own_hbm, own_ref),
        (gated_hbm, gated_ref),
        (weight_hbm, weight_ref),
        (activated_hbm, activated_ref),
        (down_hbm, down_ref),
    ):
        load = pltpu.make_async_copy(source, target, load_sems.at[len(loads)])
        load.start()
        loads.append(load)
    greet(plane_peers()[1:])
    loads[0].wait()
    waiting = loads[1:]
    total_ref[...] = jnp.zeros_like(total_ref)
    wide = 512
    saves = []

    def use(slab):
        while waiting:
            waiting.pop().wait()
        turn = len(saves) % 2
        if len(saves) > 1:
            saves[-2].wait()
        grad_ref[slab] = low_dot(all_ref[slab], weight_ref[...], NT).astype(BF16)

        @pl.loop(0, total_ref.shape[1] // wide)
        def _(i):
            at = pl.ds(pl.multiple_of(i * wide, wide), wide)
            total_ref[:, at] += low_dot(gated_ref[slab], all_ref[slab, :, at], TN)
            part_out[turn, :, at] = low_dot(activated_ref[slab], down_ref[:, at], NN).astype(BF16)

        save = pltpu.make_async_copy(part_out.at[turn], part_hbm.at[slab], save_sems.at[turn])
        save.start()
        saves.append(save)

    gather_in_turn(own_ref, all_ref, send_sems, recv_sems, use)
    term_ref[...] = total_ref[...].astype(BF16)
    for save in saves[-2:]:
        save.wait()


def gather_branch(own, gated, weight, activated, down_own, collective_id):
    ring, rows, width = gated.shape
    columns = own.shape[1]
    vmem = pl.BlockSpec(memory_space=pltpu.VMEM)
    anywhere = pl.BlockSpec(memory_space=pl.ANY)
    return pl.pallas_call(
        gather_branch_kernel,
        out_shape=[
            jax.ShapeDtypeStruct((ring, rows, width), BF16),
            jax.ShapeDtypeStruct((width, columns), BF16),
            jax.ShapeDtypeStruct((ring, rows, columns), BF16),
        ],
        in_specs=[anywhere] * 5,
        out_specs=[vmem, vmem, anywhere],
        scratch_shapes=[
            pltpu.VMEM(own.shape, BF16),
            pltpu.VMEM(gated.shape, BF16),
            pltpu.VMEM(weight.shape, BF16),
            pltpu.VMEM(activated.shape, BF16),
            pltpu.VMEM(down_own.shape, BF16),
            pltpu.VMEM((ring, rows, columns), BF16),
            pltpu.VMEM((width, columns), F32),
            pltpu.VMEM((2, rows, columns), BF16),
            pltpu.SemaphoreType.DMA((9,)),
            pltpu.SemaphoreType.DMA((9,)),
            pltpu.SemaphoreType.DMA((5,)),
            pltpu.SemaphoreType.DMA((2,)),
        ],
        compiler_params=pltpu.CompilerParams(
            collective_id=collective_id, has_side_effects=True, vmem_limit_bytes=VMEM_LIMIT
        ),
        cost_estimate=lasting(45),
        name="gather_branch",
    )(own, gated, weight, activated, down_own)


def rms_back(values, gain, grad):
    scale = lax.rsqrt(jnp.mean(values * values, -1, keepdims=True) + 1e-05)
    weighted = grad * gain
    part = scale * weighted - values * (
        scale * scale * scale * jnp.mean(weighted * values, -1, keepdims=True)
    )
    return (part, jnp.sum(grad * values * scale, 0))


def low_dot(left, right, dims):
    return lax.dot_general(left, right, (dims, ((), ())), preferred_element_type=F32)


NN = ((1,), (0,))
NT = ((1,), (1,))
TN = ((0,), (0,))


def split_heads_device(
    inputs,
    lengths,
    first_gain,
    input_weight,
    decay_weight,
    conv_weight,
    decay_log,
    decay_bias,
    head_gain,
    output_weight,
    second_gain,
    gate_up_weight,
    down_weight,
    cotangent,
):
    micro_count, seq_local, span, model_width = inputs.shape
    ring = lax.axis_size("seq")
    depth = lax.axis_size("dp")
    rank = lax.axis_index("seq")
    seqs = micro_count * seq_local
    row_count = seqs * span
    all_rows = ring * row_count
    head_count = decay_log.shape[0]
    heads = head_count // ring
    head_size = head_gain.shape[0]
    key_width = head_count * head_size
    width = heads * head_size
    own_units = down_weight.shape[0]
    units = depth * own_units
    weight_rows = input_weight.shape[0]
    tap_count = conv_weight.shape[0]

    tokens = inputs.reshape(row_count, model_width).astype(F32)
    positions = rank * span + lax.broadcasted_iota(jnp.int32, (micro_count, seq_local, span), 2)
    valid_rows = (positions < lengths[:, :, None]).astype(F32).reshape(row_count, 1)
    normed_low = rms_norm(tokens, first_gain).astype(BF16)

    upstream = valid_rows * cotangent.reshape(row_count, model_width).astype(F32)
    out_err = upstream.astype(BF16)
    out_rows = gather_rows(output_weight, "dp")
    own_heads = [rank_head(rank, j, heads) for j in range(heads)]

    def own_lanes(pair):
        rows = pair.shape[0]
        lanes = [
            lax.dynamic_slice(pair, (0, start + head), (rows, 1))
            for start in range(0, pair.shape[1], head_count)
            for head in own_heads
        ]
        return jnp.pad(jnp.concatenate(lanes, 1), ((0, 0), (0, 128 - len(lanes))))

    decay_own = own_lanes(decay_weight)
    params = jnp.pad(own_lanes(jnp.stack([decay_log, decay_bias])), ((0, 6), (0, 0)))
    taps = jnp.concatenate(
        [
            lax.dynamic_slice(
                conv_weight, (0, block * key_width + head * head_size), (tap_count, head_size)
            )
            for block in range(3)
            for head in own_heads
        ],
        1,
    )
    gain = head_gain.reshape(1, head_size)

    def chunks(value):
        return value.reshape(ring, seqs, span, value.shape[-1])

    normed_all, in_own, pair_cut, mixed, gate_raw, logits = plane_open(
        normed_low, input_weight, gate_up_weight, decay_own, heads, 1
    )
    normed_all = normed_all.reshape(all_rows, model_width)
    in_own = in_own.reshape(model_width, 4 * width)
    pair_own = gather_rows(pair_cut.reshape(ring * weight_rows, 2 * units), "dp")
    mixed, out_rows, down_weight = lax.optimization_barrier((mixed, out_rows, down_weight))
    down_own = gather_rows(down_weight, "dp")
    mixed, gate_raw, logits = chunks(mixed), chunks(gate_raw), chunks(logits)
    gated, memory, inverse, fresh, mixer_out, out_err_all, out_own = run_forward(
        mixed, gate_raw, logits, taps, params, gain, heads, out_err, out_rows, 5
    )
    gated = gated.reshape(ring, row_count, width)
    hidden = tokens + plane_scatter_dot([gated], [out_own], NN, 2)[0]
    second_low = rms_norm(hidden, second_gain).astype(BF16)
    second_all, activated, pair_part, down_term = gather_feed(
        second_low, pair_own, out_err_all, 3
    )
    down_share = scatter_rows(down_term, "dp").astype(F32)
    second_grad, pair_term = plane_scatter_dot(
        [pair_part],
        [pair_own],
        NT,
        4,
        second_all.reshape(all_rows, model_width),
        back=(out_err_all, down_own),
    )
    pair_share = scatter_rows(pair_term, "dp")
    hidden_part, second_gain_grad = rms_back(hidden, second_gain, second_grad)
    hidden_grad = upstream + hidden_part
    branch_err = hidden_grad.astype(BF16)
    gated_grad, output_term, down_part = gather_branch(
        branch_err, gated, out_own, activated, down_own, 11
    )
    in_err, logit_grad, taps_grad, param_grad, gain_grad, final_part, output_share = run_backward(
        mixed,
        gate_raw,
        logits,
        taps,
        params,
        gain,
        memory,
        inverse,
        fresh,
        mixer_out,
        gated_grad.reshape(ring, seqs, span, width),
        down_part,
        output_term,
        12,
    )
    result = valid_rows * (hidden + final_part)
    input_term = low_dot(normed_all, in_err.reshape(all_rows, 4 * width), TN).astype(BF16)
    input_term, in_err, logit_grad, down_share, pair_share = lax.optimization_barrier(
        (input_term, in_err, logit_grad, down_share, pair_share)
    )
    lanes = logit_grad.shape[-1]
    decay_term = low_dot(normed_all, logit_grad.reshape(all_rows, lanes), TN)
    decay_term, in_err = lax.optimization_barrier((decay_term, in_err))
    input_cut = scatter_rows(input_term, "dp")
    decay_twice = decay_own + jnp.roll(decay_own, lanes // 2, 1)
    normed_grad, gate_up_share = plane_scatter_dot(
        [
            in_err.reshape(ring, row_count, 4 * width),
            logit_grad.reshape(ring, row_count, lanes),
        ],
        [in_own, decay_twice],
        NT,
        6,
        cut=pair_share.reshape(ring, weight_rows, 2 * units),
    )
    token_part, first_gain_grad = rms_back(tokens, first_gain, normed_grad)
    inputs_grad = hidden_grad + token_part
    decay_term = decay_term[:, : 2 * heads] + decay_term[:, lanes // 2 : lanes // 2 + 2 * heads]
    shared = jnp.concatenate([first_gain_grad, second_gain_grad, gain_grad[0]])
    shared = jnp.pad(shared, (0, -shared.size % 1024))
    pieces = [jnp.transpose(decay_term), taps_grad[:tap_count], param_grad[:2]]
    packed = jnp.concatenate([shared] + [piece.reshape(-1) for piece in pieces])
    packed = jnp.pad(packed, (0, -packed.size % 1024)).reshape(-1, 128)
    packed, input_cut, inputs_grad, result = lax.optimization_barrier(
        (packed, input_cut, inputs_grad, result)
    )
    summed, shared_sum, input_share = small_sum(
        packed,
        shared.size // 128,
        input_cut.reshape(ring, weight_rows, 4 * width),
        heads,
        7,
    )
    shared_sum = shared_sum.reshape(-1)
    first_gain_grad = shared_sum[:model_width]
    second_gain_grad = shared_sum[model_width : 2 * model_width]
    gain_grad = shared_sum[2 * model_width : 2 * model_width + head_size]
    parted = []
    start = shared.size // 128
    for piece in pieces:
        count = piece.size // 128
        parted.append(summed[:, start : start + count])
        start += count
    decay_sum, taps_sum, param_sum = parted
    chips = ring // 2
    decay_sum = decay_sum.reshape(chips, 2, 2, heads, model_width)
    decay_weight_grad = jnp.transpose(decay_sum, (4, 2, 1, 3, 0)).reshape(model_width, -1)
    taps_sum = taps_sum.reshape(chips, 2, tap_count, 3, heads, head_size)
    taps_sum = jnp.transpose(taps_sum, (2, 3, 1, 4, 0, 5))
    param_sum = param_sum[:, :, :heads].reshape(chips, 2, 2, heads)
    param_sum = jnp.transpose(param_sum, (2, 1, 3, 0)).reshape(2, head_count)
    return (
        result.reshape(inputs.shape),
        inputs_grad.reshape(inputs.shape),
        first_gain_grad,
        input_share,
        decay_weight_grad,
        taps_sum.reshape(tap_count, 3 * key_width),
        param_sum[0],
        param_sum[1],
        gain_grad,
        output_share.astype(F32),
        second_gain_grad,
        gate_up_share,
        down_share,
    )


def solution(mesh):
    in_specs = (
        P(None, "dp", "seq", None),
        P(None, "dp"),
        P(),
        P(("dp", "seq"), None),
        P(),
        P(),
        P(),
        P(),
        P(),
        P(("dp", "seq"), None),
        P(),
        P(("dp", "seq"), None),
        P(("dp", "seq"), None),
        P(None, "dp", "seq", None),
    )
    out_specs = (
        P(None, "dp", "seq", None),
        P(None, "dp", "seq", None),
        P(),
        P(("dp", "seq"), None),
        P(),
        P(),
        P(),
        P(),
        P(),
        P(("dp", "seq"), None),
        P(),
        P(("dp", "seq"), None),
        P(("dp", "seq"), None),
    )
    ring = mesh.shape["seq"]

    def whole_device(*arrays):
        heads_divide = ring == 8 and 2 * arrays[6].shape[0] == ring * mesh.shape["dp"]
        return (split_heads_device if heads_divide else per_device)(*arrays)

    return jax.shard_map(
        whole_device, mesh=mesh, in_specs=in_specs, out_specs=out_specs, check_vma=False
    )
```

```python
import functools

import jax
import jax.numpy as jnp
from jax import lax
from jax.experimental import pallas as pl
from jax.experimental.pallas import tpu as pltpu
from jax.sharding import PartitionSpec as P

SPAN = 64
VMEM_LIMIT = 56 * 1024 * 1024


HIGH = lax.Precision.HIGHEST


def shifted(value, axis, steps):
    count = lax.axis_size(axis)
    initial, last = (max(0, -steps), min(count, count - steps))
    return lax.ppermute(value, axis, [(source, source + steps) for source in range(initial, last)])


def rms_norm(values, gain):
    return values * lax.rsqrt(jnp.mean(values * values, -1, keepdims=True) + 1e-05) * gain


def unit_norm(vectors):
    return vectors * lax.rsqrt(jnp.sum(vectors * vectors, -1, keepdims=True) + 1e-06)


def swish_product(gate_part, up_part):
    return jax.nn.silu(gate_part) * up_part


def unit_inverse(strict_lower):
    extent = strict_lower.shape[-1]
    identity_matrix = jnp.eye(extent, dtype=jnp.float32)
    inverse = identity_matrix - strict_lower
    power_term = strict_lower
    for level_index in range(1, (extent - 1).bit_length()):
        power_term = jnp.einsum("bhij,bhjk->bhik", power_term, power_term, precision=HIGH)
        inverse = jnp.einsum(
            "bhij,bhjk->bhik", inverse, identity_matrix + power_term, precision=HIGH
        )
    return inverse


def span_step(memory, pieces):
    queries, probes, writes, decays, strengths = pieces
    extent = decays.shape[-1]
    running = jnp.cumsum(decays, axis=-1)
    spread = running[..., :, None] - running[..., None, :]
    row_index = lax.broadcasted_iota(jnp.int32, (extent, extent), 0)
    col_index = lax.broadcasted_iota(jnp.int32, (extent, extent), 1)
    faded = jnp.exp(jnp.minimum(spread, 0.0))
    inclusive = jnp.where(col_index <= row_index, faded, 0.0) * strengths[..., None, :]
    strict_mask = jnp.where(col_index < row_index, faded, 0.0) * strengths[..., None, :]
    strict_lower = strict_mask * jnp.einsum("bhtd,bhsd->bhts", probes, probes, precision=HIGH)
    scale_in = jnp.exp(running)[..., None]
    target = writes - scale_in * jnp.einsum("bhtd,bhde->bhte", probes, memory, precision=HIGH)
    fresh_values = jnp.einsum("bhts,bhse->bhte", unit_inverse(strict_lower), target, precision=HIGH)
    mixing = inclusive * jnp.einsum("bhtd,bhsd->bhts", queries, probes, precision=HIGH)
    outputs = scale_in * jnp.einsum("bhtd,bhde->bhte", queries, memory, precision=HIGH)
    outputs = outputs + jnp.einsum("bhts,bhse->bhte", mixing, fresh_values, precision=HIGH)
    remaining = jnp.exp(running[..., -1:] - running) * strengths
    memory = jnp.exp(running[..., -1])[..., None, None] * memory + jnp.einsum(
        "bhsd,bhse->bhde", probes * remaining[..., None], fresh_values, precision=HIGH
    )
    return (memory, outputs)


def delta_local(queries, probes, writes, decays, strengths, memory):
    seq_count, head_count, length, head_size = queries.shape
    blocks = length // SPAN

    def arrange(tensor):
        shaped = tensor.reshape(tensor.shape[:2] + (blocks, SPAN) + tensor.shape[3:])
        return jnp.moveaxis(shaped, 2, 0)

    pieces = (
        arrange(queries),
        arrange(probes),
        arrange(writes),
        arrange(decays),
        arrange(strengths),
    )
    memory, outputs = lax.scan(span_step, memory, pieces)
    outputs = jnp.moveaxis(outputs, 0, 2)
    return (outputs.reshape(seq_count, head_count, length, outputs.shape[-1]), memory)


def prepare(packed, logits, conv_weight, decay_log, decay_bias):
    seq_count, length, logit_width = logits.shape
    head_count = decay_log.shape[0]
    tap_count = conv_weight.shape[0]
    convolved = conv_weight[0] * packed[:, 0:length]
    for tap_index in range(1, tap_count):
        convolved = convolved + conv_weight[tap_index] * packed[:, tap_index : tap_index + length]
    active = jax.nn.silu(convolved)
    key_width = active.shape[-1] // 3
    head_size = key_width // head_count

    def split_heads(portion):
        return jnp.transpose(
            portion.reshape(seq_count, length, head_count, head_size), (0, 2, 1, 3)
        )

    queries = unit_norm(split_heads(active[..., :key_width])) * head_size ** (-0.5)
    probes = unit_norm(split_heads(active[..., key_width : 2 * key_width]))
    writes = split_heads(active[..., 2 * key_width :])
    decays = jnp.transpose(
        -jnp.exp(decay_log) * jax.nn.softplus(logits[..., :head_count] + decay_bias), (0, 2, 1)
    )
    strengths = jnp.transpose(jax.nn.sigmoid(logits[..., head_count:]), (0, 2, 1))
    return (queries, probes, writes, decays, strengths)


def mixer_core(packed, logits, conv_weight, decay_log, decay_bias, memory):
    queries, probes, writes, decays, strengths = prepare(
        packed, logits, conv_weight, decay_log, decay_bias
    )
    return delta_local(queries, probes, writes, decays, strengths, memory)


def finish(mixer_out, gate_raw, head_gain):
    seq_count, head_count, length, head_size = mixer_out.shape
    normal_out = rms_norm(mixer_out, head_gain)
    flat_rows = jnp.transpose(normal_out, (0, 2, 1, 3)).reshape(
        seq_count, length, head_count * head_size
    )
    return flat_rows * jax.nn.silu(gate_raw)


def carry_forward(transfer, offset):

    def turn_step(step_index, incoming):
        leaving = jnp.einsum("bhij,bhjk->bhik", transfer, incoming, precision=HIGH) + offset
        return shifted(leaving.astype(jnp.bfloat16), "seq", 1).astype(leaving.dtype)

    return lax.fori_loop(0, lax.axis_size("seq") - 1, turn_step, jnp.zeros_like(offset))


def carry_back(transfer, source):
    flipped = jnp.swapaxes(transfer, 2, 3)

    def turn_step(step_index, incoming):
        leaving = jnp.einsum("bhij,bhjk->bhik", flipped, incoming, precision=HIGH) + source
        return shifted(leaving.astype(jnp.bfloat16), "seq", -1).astype(leaving.dtype)

    return lax.fori_loop(0, lax.axis_size("seq") - 1, turn_step, jnp.zeros_like(source))


def per_device(
    inputs,
    lengths,
    first_gain,
    input_weight,
    decay_weight,
    conv_weight,
    decay_log,
    decay_bias,
    head_gain,
    output_weight,
    second_gain,
    gate_up_weight,
    down_weight,
    cotangent,
):
    micro_count, seq_local, length, model_width = inputs.shape
    seq_count = micro_count * seq_local
    row_count = seq_count * length
    head_count = decay_log.shape[0]
    key_width = input_weight.shape[1] // 4
    head_size = key_width // head_count
    tap_count = conv_weight.shape[0]
    tokens = inputs.reshape(row_count, model_width).astype(jnp.float32)
    positions = lax.axis_index("seq") * length + lax.broadcasted_iota(
        jnp.int32, (micro_count, seq_local, length), 2
    )
    valid_rows = (positions < lengths[:, :, None]).astype(jnp.float32).reshape(row_count, 1)
    in_full, out_full, gate_up_full, down_full = (
        lax.all_gather(input_weight, ("dp", "seq"), axis=0, tiled=True),
        lax.all_gather(output_weight, ("dp", "seq"), axis=0, tiled=True),
        lax.all_gather(gate_up_weight, ("dp", "seq"), axis=0, tiled=True),
        lax.all_gather(down_weight, ("dp", "seq"), axis=0, tiled=True),
    )
    normed, first_pullback = jax.vjp(rms_norm, tokens, first_gain)
    normed_low = normed.astype(jnp.bfloat16)
    projected = jnp.dot(normed_low, in_full, preferred_element_type=jnp.float32)
    mixed_low = (
        projected[:, : 3 * key_width].astype(jnp.bfloat16).reshape(seq_count, length, 3 * key_width)
    )
    gate_raw = projected[:, 3 * key_width :].reshape(seq_count, length, key_width)
    logits = jnp.dot(normed_low, decay_weight, preferred_element_type=jnp.float32).reshape(
        seq_count, length, 2 * head_count
    )
    left_edge = shifted(mixed_low[:, length - tap_count + 1 :], "seq", 1)
    packed = jnp.concatenate([left_edge, mixed_low], 1).astype(jnp.float32)
    queries, probes, writes, decays, strengths = prepare(
        packed, logits, conv_weight, decay_log, decay_bias
    )
    blank_state = jnp.zeros((seq_count, head_count, head_size, head_size), jnp.float32)
    identity_maps = jnp.broadcast_to(jnp.eye(head_size, dtype=jnp.float32), blank_state.shape)
    joined_writes = jnp.concatenate([writes, jnp.zeros_like(writes)], -1)
    joined_outputs, joined_end = delta_local(
        queries,
        probes,
        joined_writes,
        decays,
        strengths,
        jnp.concatenate([blank_state, identity_maps], -1),
    )
    own_out = joined_outputs[..., :head_size]
    carry_out = joined_outputs[..., head_size:]
    offset = joined_end[..., :head_size]
    transfer = joined_end[..., head_size:]
    state_in = carry_forward(transfer, offset)
    mixer_out = own_out + jnp.einsum("bhtd,bhde->bhte", carry_out, state_in, precision=HIGH)
    gated_rows, finish_pullback = jax.vjp(finish, mixer_out, gate_raw, head_gain)
    gated_low = gated_rows.reshape(row_count, key_width).astype(jnp.bfloat16)
    hidden = tokens + jnp.dot(gated_low, out_full, preferred_element_type=jnp.float32)
    second, second_pullback = jax.vjp(rms_norm, hidden, second_gain)
    second_low = second.astype(jnp.bfloat16)
    gate_up = jnp.dot(second_low, gate_up_full, preferred_element_type=jnp.float32)
    ffn_width = gate_up.shape[1] // 2
    activated, swish_pullback = jax.vjp(
        swish_product, gate_up[:, :ffn_width], gate_up[:, ffn_width:]
    )
    activated_low = activated.astype(jnp.bfloat16)
    final_rows = hidden + jnp.dot(activated_low, down_full, preferred_element_type=jnp.float32)
    result = valid_rows * final_rows
    upstream = valid_rows * cotangent.reshape(row_count, model_width).astype(jnp.float32)
    out_err = upstream.astype(jnp.bfloat16)
    down_term = jnp.einsum("nf,nd->fd", activated_low, out_err, preferred_element_type=jnp.float32)
    activated_grad = jnp.einsum("nd,fd->nf", out_err, down_full, preferred_element_type=jnp.float32)
    gate_grad, up_grad = swish_pullback(activated_grad)
    gate_up_err = jnp.concatenate([gate_grad, up_grad], 1).astype(jnp.bfloat16)
    gate_up_term = jnp.einsum(
        "nd,nf->df", second_low, gate_up_err, preferred_element_type=jnp.float32
    )
    second_grad = jnp.einsum(
        "nf,df->nd", gate_up_err, gate_up_full, preferred_element_type=jnp.float32
    )
    hidden_part, second_gain_grad = second_pullback(second_grad)
    hidden_grad = upstream + hidden_part
    gate_up_share, down_share = (
        scatter_rows(gate_up_term.astype(BF16), ("dp", "seq")).astype(F32),
        scatter_rows(down_term.astype(BF16), ("dp", "seq")).astype(F32),
    )
    branch_err = hidden_grad.astype(jnp.bfloat16)
    output_term = jnp.einsum("nk,nd->kd", gated_low, branch_err, preferred_element_type=jnp.float32)
    gated_grad = jnp.einsum("nd,kd->nk", branch_err, out_full, preferred_element_type=jnp.float32)
    mixer_grad, gate_raw_grad, head_gain_grad = finish_pullback(
        gated_grad.reshape(seq_count, length, key_width)
    )
    source = jnp.einsum("bhtd,bhte->bhde", carry_out, mixer_grad, precision=HIGH)
    state_out_grad = carry_back(transfer, source)
    _, core_pullback = jax.vjp(
        mixer_core, packed, logits, conv_weight, decay_log, decay_bias, state_in
    )
    packed_grad, logits_grad, conv_grad, decay_log_grad, decay_bias_grad, _ = core_pullback(
        (mixer_grad, state_out_grad)
    )
    edge_grad = shifted(packed_grad[:, : tap_count - 1].astype(jnp.bfloat16), "seq", -1).astype(
        jnp.float32
    )
    mixed_grad = packed_grad[:, tap_count - 1 :] + jnp.pad(
        edge_grad, ((0, 0), (length - tap_count + 1, 0), (0, 0))
    )
    in_err = jnp.concatenate(
        [mixed_grad.reshape(row_count, 3 * key_width), gate_raw_grad.reshape(row_count, key_width)],
        1,
    ).astype(jnp.bfloat16)
    input_term = jnp.einsum("nd,nk->dk", normed_low, in_err, preferred_element_type=jnp.float32)
    logits_flat = logits_grad.reshape(row_count, 2 * head_count)
    decay_weight_grad = jnp.einsum(
        "nd,nk->dk", normed_low.astype(jnp.float32), logits_flat, precision=HIGH
    )
    normed_grad = jnp.einsum("nk,dk->nd", in_err, in_full, preferred_element_type=jnp.float32)
    normed_grad = normed_grad + jnp.einsum(
        "nk,dk->nd", logits_flat, decay_weight.astype(jnp.float32), precision=HIGH
    )
    token_part, first_gain_grad = first_pullback(normed_grad)
    inputs_grad = hidden_grad + token_part
    input_share, output_share = (
        scatter_rows(input_term.astype(BF16), ("dp", "seq")).astype(F32),
        scatter_rows(output_term.astype(BF16), ("dp", "seq")).astype(F32),
    )
    small_sums = lax.psum(
        (
            first_gain_grad,
            decay_weight_grad,
            conv_grad,
            decay_log_grad,
            decay_bias_grad,
            head_gain_grad,
            second_gain_grad,
        ),
        ("dp", "seq"),
    )
    return (
        result.reshape(inputs.shape),
        inputs_grad.reshape(inputs.shape),
        small_sums[0],
        input_share,
        small_sums[1],
        small_sums[2],
        small_sums[3],
        small_sums[4],
        small_sums[5],
        output_share,
        small_sums[6],
        gate_up_share,
        down_share,
    )


F32 = jnp.float32
BF16 = jnp.bfloat16


def lasting(microseconds):
    return pl.CostEstimate(flops=0, bytes_accessed=int(microseconds * 3.5e6), transcendentals=0)


def parts(value):
    top = value.astype(BF16)
    return (top, (value - top.astype(F32)).astype(BF16))


def contract(left, right, right_dim):
    lhs = jnp.concatenate([left[0], left[1], left[0]], 1)
    rhs = jnp.concatenate([right[0], right[0], right[1]], right_dim)
    return lax.dot_general(lhs, rhs, (((1,), (right_dim,)), ((), ())), preferred_element_type=F32)


def mm(left, right):
    return contract(left, right, 0)


def mm_nt(left, right):
    return contract(left, right, 1)


def ones_dot(ones, value):
    first = value.astype(BF16)
    rest = value - first.astype(F32)
    second = rest.astype(BF16)
    third = (rest - second.astype(F32)).astype(BF16)
    return (
        jnp.dot(ones, first, preferred_element_type=F32)
        + jnp.dot(ones, second, preferred_element_type=F32)
        + jnp.dot(ones, third, preferred_element_type=F32)
    )


def lower_inverses(strict_lowers, row_index, col_index):
    extent = row_index.shape[0]

    def below(width):
        same = (row_index // (2 * width)) == (col_index // (2 * width))
        return same & ((row_index // width) % 2 == 1) & ((col_index // width) % 2 == 0)

    mask = below(1)
    identity = jnp.where(row_index == col_index, 1.0, 0.0)
    inverses = [identity - jnp.where(mask, strict, 0.0) for strict in strict_lowers]
    width = 2
    while width < extent:
        mask = below(width)
        splits = [parts(inverse) for inverse in inverses]
        blocks = [parts(jnp.where(mask, strict, 0.0)) for strict in strict_lowers]
        halves = [mm(split, block) for split, block in zip(splits, blocks)]
        inverses = [
            inverse - mm(parts(half), split)
            for inverse, half, split in zip(inverses, halves, splits)
        ]
        width *= 2
    return inverses


def active_rows(before, rows, taps):
    extended = jnp.concatenate([before, rows], 0)
    count = rows.shape[0]
    tap_count = taps.shape[0]
    start = before.shape[0] - tap_count + 1
    shifts = [extended[start + j : start + j + count] for j in range(tap_count)]
    total = taps[0:1] * shifts[0]
    for j in range(1, tap_count):
        total = total + taps[j : j + 1] * shifts[j]
    return (total, shifts)


def soft_plus(value):
    return jnp.maximum(value, 0.0) + jnp.log(1.0 + jnp.exp(-jnp.abs(value)))


def sigmoid(value):
    return 1.0 / (1.0 + jnp.exp(-value))


def unit(vectors):
    scale = lax.rsqrt(jnp.sum(vectors * vectors, -1, keepdims=True) + 1e-06)
    return (vectors * scale, scale)


def unit_back(vectors, scale, grad):
    inner = jnp.sum(vectors * grad, -1, keepdims=True)
    return scale * grad - vectors * (scale * scale * scale * inner)


def decay_terms(logit, param_ref, heads, ones):
    shifted_logit = logit + param_ref[1:2, :]
    lane = lax.broadcasted_iota(jnp.int32, logit.shape, 1)
    decays = jnp.where(lane < heads, -jnp.exp(param_ref[0:1, :]) * soft_plus(shifted_logit), 0.0)
    strengths = sigmoid(logit)
    running = ones_dot(ones, decays)
    return (shifted_logit, decays, strengths, running)


def mixer_forward(
    mixed_ref,
    gate_ref,
    logit_ref,
    taps_ref,
    param_ref,
    gain_ref,
    own_ref,
    rows_ref,
    gated_ref,
    memory_ref,
    inverse_ref,
    fresh_ref,
    out_ref,
    all_ref,
    rows_out_ref,
    state_ref,
    halo_ref,
    send_sems,
    recv_sems,
    local_sems,
):
    seqs, span, _ = mixed_ref.shape
    heads, head_size = memory_ref.shape[1], memory_ref.shape[2]
    gather_in_steps(own_ref, all_ref, send_sems, recv_sems, local_sems.at[0])
    trade_in_steps(rows_ref, rows_out_ref, send_sems, recv_sems, local_sems, heads)

    @pl.when(pl.program_id(0) == 0)
    def _():
        state_ref[...] = jnp.zeros_like(state_ref)
        halo_ref[...] = jnp.zeros_like(halo_ref)

    row_index = lax.broadcasted_iota(jnp.int32, (span, span), 0)
    col_index = lax.broadcasted_iota(jnp.int32, (span, span), 1)
    ones = jnp.where(col_index <= row_index, 1.0, 0.0).astype(BF16)
    taps = taps_ref[...]
    width = heads * head_size
    pairs = [(m, h) for m in range(seqs) for h in range(heads)]
    active, decay_parts = [], []
    for m in range(seqs):
        rows = mixed_ref[m].astype(F32)
        convolved, _ = active_rows(halo_ref[m], rows, taps)
        halo_ref[m] = rows[span - 8 :]
        active.append(convolved * sigmoid(convolved))
        _, _, strengths, running = decay_terms(logit_ref[m], param_ref, heads, ones)
        decay_parts.append((strengths, running, jnp.transpose(strengths), jnp.transpose(running)))

    def columns(m, h, block):
        start = block * width + h * head_size
        return active[m][:, start : start + head_size]

    queries = [unit(columns(m, h, 0))[0] * head_size ** (-0.5) for m, h in pairs]
    probes = [unit(columns(m, h, 1))[0] for m, h in pairs]
    products = [
        mm_nt(parts(jnp.concatenate([query, probe], 0)), parts(probe))
        for query, probe in zip(queries, probes)
    ]
    stricts, mixings, scales, kepts, lasts = [], [], [], [], []
    for (m, h), probe, product in zip(pairs, probes, products):
        strengths, running, strength_rows, running_rows = decay_parts[m]
        run = running[:, h : h + 1]
        last = running[span - 1 : span, h : h + 1]
        weight_row = strength_rows[heads + h : heads + h + 1, :]
        weight_col = strengths[:, heads + h : heads + h + 1]
        faded = jnp.exp(jnp.minimum(run - running_rows[h : h + 1, :], 0.0)) * weight_row
        mixings.append(jnp.where(col_index <= row_index, faded * product[:span], 0.0))
        stricts.append(jnp.where(col_index < row_index, faded * product[span:], 0.0))
        scales.append(jnp.exp(run))
        kepts.append(jnp.transpose(jnp.exp(last - run) * weight_col * probe))
        lasts.append(jnp.exp(last))
    inverses = lower_inverses(stricts, row_index, col_index)
    boths = [
        mm(parts(inverse), parts(jnp.concatenate([columns(m, h, 2), scale * probe], 1)))
        for (m, h), inverse, scale, probe in zip(pairs, inverses, scales, probes)
    ]
    memories = [state_ref[m, h] for m, h in pairs]
    reads = [
        mm(parts(jnp.concatenate([both[:, head_size:], scale * query], 0)), parts(memory))
        for both, scale, query, memory in zip(boths, scales, queries, memories)
    ]
    freshes = [both[:, :head_size] - read[:span] for both, read in zip(boths, reads)]
    fresh_parts = [parts(fresh) for fresh in freshes]
    for (m, h), last, memory, kept, fresh in zip(pairs, lasts, memories, kepts, fresh_parts):
        state_ref[m, h] = last * memory + mm(parts(kept), fresh)
    outs = [
        read[span:] + mm(parts(mixing), fresh)
        for read, mixing, fresh in zip(reads, mixings, fresh_parts)
    ]
    for (m, h), memory, inverse, fresh, mixer_out in zip(pairs, memories, inverses, freshes, outs):
        own = slice(h * head_size, (h + 1) * head_size)
        memory_ref[m, h] = memory
        inverse_ref[m, h] = inverse
        fresh_ref[m, :, own] = fresh
        out_ref[m, :, own] = mixer_out
        scale = lax.rsqrt(jnp.mean(mixer_out * mixer_out, -1, keepdims=True) + 1e-05)
        gate = gate_ref[m, :, own]
        gated_ref[m, :, own] = (
            mixer_out * scale * gain_ref[...] * (gate * sigmoid(gate))
        ).astype(BF16)


def mixer_backward(
    mixed_ref,
    before_ref,
    gate_ref,
    logit_ref,
    taps_ref,
    param_ref,
    gain_ref,
    memory_ref,
    inverse_ref,
    fresh_ref,
    out_ref,
    grad_ref,
    part_ref,
    error_ref,
    logit_grad_ref,
    taps_grad_ref,
    param_grad_ref,
    gain_grad_ref,
    sum_ref,
    state_ref,
    halo_ref,
    *scatter_refs,
):
    seqs, span, _ = mixed_ref.shape
    heads, head_size = memory_ref.shape[1], memory_ref.shape[2]
    step = pl.program_id(0)
    scatter_in_steps(part_ref, sum_ref, *scatter_refs)

    @pl.when(step == 0)
    def _():
        state_ref[...] = jnp.zeros_like(state_ref)
        halo_ref[...] = jnp.zeros_like(halo_ref)
        taps_grad_ref[...] = jnp.zeros_like(taps_grad_ref)
        param_grad_ref[...] = jnp.zeros_like(param_grad_ref)
        gain_grad_ref[...] = jnp.zeros_like(gain_grad_ref)

    first = step == pl.num_programs(0) - 1
    row_index = lax.broadcasted_iota(jnp.int32, (span, span), 0)
    col_index = lax.broadcasted_iota(jnp.int32, (span, span), 1)
    ones = jnp.where(col_index <= row_index, 1.0, 0.0).astype(BF16)
    ones_back = jnp.where(col_index >= row_index, 1.0, 0.0).astype(BF16)
    taps = taps_ref[...]
    tap_count = taps.shape[0]
    width = heads * head_size
    gain = gain_ref[...]
    edge = before_ref.shape[1]
    pairs = [(m, h) for m in range(seqs) for h in range(heads)]
    everyone = range(len(pairs))
    active, openings, curves, shifts, decay_parts = [], [], [], [], []
    for m in range(seqs):
        rows = mixed_ref[m].astype(F32)
        before = jnp.where(first, 0.0, before_ref[m].astype(F32))[edge - 8 :]
        convolved, moved = active_rows(before, rows, taps)
        opening = sigmoid(convolved)
        active.append(convolved * opening)
        curves.append(convolved)
        openings.append(opening)
        shifts.append(moved)
        shifted_logit, decays, strengths, running = decay_terms(
            logit_ref[m], param_ref, heads, ones
        )
        decay_parts.append(
            (
                shifted_logit,
                decays,
                strengths,
                running,
                jnp.transpose(strengths),
                jnp.transpose(running),
            )
        )

    def columns(m, h, block):
        start = block * width + h * head_size
        return active[m][:, start : start + head_size]

    raw_queries = [columns(m, h, 0) for m, h in pairs]
    raw_probes = [columns(m, h, 1) for m, h in pairs]
    query_units = [unit(value) for value in raw_queries]
    probe_units = [unit(value) for value in raw_probes]
    queries = [value * head_size ** (-0.5) for value, _ in query_units]
    probes = [value for value, _ in probe_units]
    gate_grads, out_grads = [], []
    for m, h in pairs:
        own = slice(h * head_size, (h + 1) * head_size)
        mixer_out = out_ref[m, :, own]
        gate = gate_ref[m, :, own]
        gated_grad = grad_ref[m, :, own].astype(F32)
        scale = lax.rsqrt(jnp.mean(mixer_out * mixer_out, -1, keepdims=True) + 1e-05)
        gate_open = sigmoid(gate)
        normal = mixer_out * scale
        gate_grads.append(
            gated_grad * normal * gain * (gate_open * (1.0 + gate * (1.0 - gate_open)))
        )
        normal_grad = gated_grad * (gate * gate_open)
        gain_grad_ref[0:1, :] += jnp.sum(normal_grad * normal, 0, keepdims=True)
        weighted = normal_grad * gain
        out_grads.append(
            scale * (weighted - normal * jnp.mean(weighted * normal, -1, keepdims=True))
        )

    probe_parts = [parts(value) for value in probes]
    query_parts = [parts(value) for value in queries]
    out_grad_parts = [parts(value) for value in out_grads]
    state_grads = [state_ref[m, h] for m, h in pairs]
    state_grad_parts = [parts(value) for value in state_grads]
    products = [
        mm_nt(parts(jnp.concatenate([query, probe], 0)), probe_part)
        for query, probe, probe_part in zip(queries, probes, probe_parts)
    ]
    probe_states = [mm(left, right) for left, right in zip(probe_parts, state_grad_parts)]
    weight_rows, spreads, fade_queries, fade_probes = [], [], [], []
    scales, end_scales, remainings, kepts = [], [], [], []
    for (m, h), product in zip(pairs, products):
        _, _, strengths, running, strength_rows, running_rows = decay_parts[m]
        run = running[:, h : h + 1]
        last = running[span - 1 : span, h : h + 1]
        weight_row = strength_rows[heads + h : heads + h + 1, :]
        weight_rows.append(weight_row)
        faded = jnp.exp(jnp.minimum(run - running_rows[h : h + 1, :], 0.0))
        spreads.append(faded * weight_row)
        fade_queries.append(jnp.where(col_index <= row_index, faded * product[:span], 0.0))
        fade_probes.append(jnp.where(col_index < row_index, faded * product[span:], 0.0))
        scales.append(jnp.exp(run))
        end_scales.append(jnp.exp(last))
        remaining = jnp.exp(last - run)
        remainings.append(remaining)
        kepts.append(remaining * strengths[:, heads + h : heads + h + 1])
    fresh_grads = [
        mm(parts(jnp.transpose(fade * weight_row)), out_grad) + kept * probe_state
        for fade, weight_row, out_grad, kept, probe_state in zip(
            fade_queries, weight_rows, out_grad_parts, kepts, probe_states
        )
    ]
    solves = [
        mm(parts(jnp.transpose(inverse_ref[m, h])), parts(fresh_grad))
        for (m, h), fresh_grad in zip(pairs, fresh_grads)
    ]
    for k in everyone:
        m, h = pairs[k]
        state_ref[m, h] = (
            end_scales[k] * state_grads[k]
            + mm(parts(jnp.transpose(queries[k])), parts(scales[k] * out_grads[k]))
            - mm(parts(jnp.transpose(probes[k])), parts(scales[k] * solves[k]))
        )
    freshes = [fresh_ref[m, :, h * head_size : (h + 1) * head_size] for m, h in pairs]
    memories = [memory_ref[m, h] for m, h in pairs]
    fresh_parts = [parts(value) for value in freshes]
    joined = [
        parts(jnp.concatenate([out_grad, solved], 0)) for out_grad, solved in zip(out_grads, solves)
    ]
    outers = [mm_nt(both, fresh) for both, fresh in zip(joined, fresh_parts)]
    throughs = [mm_nt(both, parts(memory)) for both, memory in zip(joined, memories)]
    mixing_grads = [jnp.where(col_index <= row_index, outer[:span], 0.0) for outer in outers]
    strict_grads = [jnp.where(col_index < row_index, -outer[span:], 0.0) for outer in outers]
    mix_fades = [grad * spread for grad, spread in zip(mixing_grads, spreads)]
    strict_fades = [grad * spread for grad, spread in zip(strict_grads, spreads)]
    on_probes = [
        mm(parts(jnp.concatenate([mix, strict], 0)), probe)
        for mix, strict, probe in zip(mix_fades, strict_fades, probe_parts)
    ]
    fresh_states = [mm_nt(fresh, grad) for fresh, grad in zip(fresh_parts, state_grad_parts)]
    turned = [
        mm(parts(jnp.transpose(mix)), query) + mm(parts(jnp.transpose(strict)), probe)
        for mix, strict, query, probe in zip(mix_fades, strict_fades, query_parts, probe_parts)
    ]
    active_grads = [[None] * (3 * heads) for _ in range(seqs)]
    col_terms = [jnp.zeros((span, span), F32)] * seqs
    row_terms = [jnp.zeros((span, span), F32)] * seqs
    for k in everyone:
        m, h = pairs[k]
        out_state = scales[k] * throughs[k][:span]
        solved_state = scales[k] * throughs[k][span:]
        query_grad = out_state + on_probes[k][:span]
        probe_grad = kepts[k] * fresh_states[k] - solved_state + on_probes[k][span:] + turned[k]
        pair_terms = mixing_grads[k] * fade_queries[k] + strict_grads[k] * fade_probes[k]
        weighted_pairs = pair_terms * weight_rows[k]
        probe_fresh = jnp.sum(probe_states[k] * freshes[k], -1, keepdims=True)
        run_col = (
            jnp.sum(out_state * queries[k] - solved_state * probes[k], -1, keepdims=True)
            + jnp.sum(weighted_pairs, -1, keepdims=True)
            - kepts[k] * probe_fresh
        )
        last_grad = jnp.sum(kepts[k] * probe_fresh, 0, keepdims=True) + end_scales[k] * jnp.sum(
            jnp.sum(state_grads[k] * memories[k], -1, keepdims=True), 0, keepdims=True
        )
        run_col = run_col + jnp.where(row_index[:, 0:1] == span - 1, last_grad, 0.0)
        col_terms[m] = jnp.where(col_index == h, run_col, col_terms[m])
        col_terms[m] = jnp.where(
            col_index == heads + h, remainings[k] * probe_fresh, col_terms[m]
        )
        row_terms[m] = jnp.where(
            row_index == h, -jnp.sum(weighted_pairs, 0, keepdims=True), row_terms[m]
        )
        row_terms[m] = jnp.where(
            row_index == heads + h, jnp.sum(pair_terms, 0, keepdims=True), row_terms[m]
        )
        active_grads[m][h] = unit_back(
            raw_queries[k], query_units[k][1], query_grad
        ) * head_size ** (-0.5)
        active_grads[m][heads + h] = unit_back(raw_probes[k], probe_units[k][1], probe_grad)
        active_grads[m][2 * heads + h] = solves[k]

    for m in range(seqs):
        shifted_logit, decays, strengths = decay_parts[m][:3]
        terms = col_terms[m] + jnp.transpose(row_terms[m])
        decay_grad = ones_dot(ones_back, terms)
        shifted_grad = decay_grad * -jnp.exp(param_ref[0:1, :]) * sigmoid(shifted_logit)
        logit_grad = jnp.where(
            col_index < heads,
            shifted_grad,
            jnp.where(col_index < 2 * heads, terms * strengths * (1.0 - strengths), 0.0),
        )
        logit_top, logit_rest = parts(logit_grad)
        logit_grad_ref[m] = (
            logit_top.astype(F32) + pltpu.roll(logit_rest.astype(F32), span // 2, 1)
        ).astype(BF16)
        decay_lane = col_index[0:1] < heads
        param_grad_ref[0:1, :] += jnp.sum(
            jnp.where(decay_lane, decay_grad * decays, 0.0), 0, keepdims=True
        )
        param_grad_ref[1:2, :] += jnp.sum(
            jnp.where(decay_lane, shifted_grad, 0.0), 0, keepdims=True
        )
        conv_grad = jnp.concatenate(active_grads[m], 1) * (
            openings[m] * (1.0 + curves[m] * (1.0 - openings[m]))
        )
        extended = jnp.concatenate([conv_grad, halo_ref[m]], 0)
        halo_ref[m] = conv_grad[:8]
        mixed_grad = jnp.zeros_like(conv_grad)
        for j in range(tap_count):
            reach = tap_count - 1 - j
            mixed_grad = mixed_grad + taps[j : j + 1] * extended[reach : reach + span]
            taps_grad_ref[j : j + 1, :] += jnp.sum(conv_grad * shifts[m][j], 0, keepdims=True)
        error_ref[m] = jnp.concatenate(
            [mixed_grad] + gate_grads[m * heads : (m + 1) * heads], 1
        ).astype(BF16)


def run_forward(mixed, gate, logits, taps, params, gain, heads, own, out_rows, collective_id):
    steps, seqs, span, _ = mixed.shape
    anywhere = pl.BlockSpec(memory_space=pl.ANY)
    head_size = gain.shape[1]
    width = heads * head_size

    def rows(columns):
        return pl.BlockSpec((None, seqs, span, columns), lambda j: (j, 0, 0, 0))

    def squares():
        return pl.BlockSpec((None, seqs, heads, head_size, head_size), lambda j: (j, 0, 0, 0, 0))

    def whole(array):
        return pl.BlockSpec(array.shape, lambda j: (0, 0))

    square = jax.ShapeDtypeStruct((steps, seqs, heads, head_size, head_size), F32)
    lower = jax.ShapeDtypeStruct((steps, seqs, heads, span, span), F32)
    flat = jax.ShapeDtypeStruct((steps, seqs, span, width), F32)
    return pl.pallas_call(
        mixer_forward,
        grid=(steps,),
        in_specs=[
            rows(3 * width),
            rows(width),
            rows(logits.shape[-1]),
            whole(taps),
            whole(params),
            whole(gain),
            anywhere,
            anywhere,
        ],
        out_specs=[rows(width), squares(), squares(), rows(width), rows(width)] + [anywhere] * 2,
        out_shape=[
            jax.ShapeDtypeStruct((steps, seqs, span, width), BF16),
            square,
            lower,
            flat,
            flat,
            jax.ShapeDtypeStruct((steps,) + own.shape, own.dtype),
            jax.ShapeDtypeStruct(out_rows.shape, out_rows.dtype),
        ],
        scratch_shapes=[
            pltpu.VMEM((seqs, heads, head_size, head_size), F32),
            pltpu.VMEM((seqs, 8, 3 * width), F32),
            pltpu.SemaphoreType.DMA((9 + heads,)),
            pltpu.SemaphoreType.DMA((9 + heads,)),
            pltpu.SemaphoreType.DMA((1 + heads,)),
        ],
        compiler_params=pltpu.CompilerParams(
            collective_id=collective_id, has_side_effects=True, vmem_limit_bytes=VMEM_LIMIT
        ),
        cost_estimate=lasting(55),
        name="mixer_forward",
    )(mixed, gate, logits, taps, params, gain, own, out_rows)


def run_backward(
    mixed, gate, logits, taps, params, gain, memory, inverse, fresh, out, grad, part, collective_id
):
    steps, seqs, span, _ = mixed.shape
    _, part_rows, columns = part.shape
    heads, head_size = memory.shape[2], memory.shape[3]
    width = heads * head_size
    edge = 16

    def rows(columns):
        return pl.BlockSpec((None, seqs, span, columns), lambda j: (steps - 1 - j, 0, 0, 0))

    def squares():
        return pl.BlockSpec(
            (None, seqs, heads, head_size, head_size), lambda j: (steps - 1 - j, 0, 0, 0, 0)
        )

    def whole(shape):
        return pl.BlockSpec(shape, lambda j: (0, 0))

    before = pl.BlockSpec(
        (None, seqs, edge, 3 * width),
        lambda j: (jnp.maximum(steps - 2 - j, 0), 0, span // edge - 1, 0),
    )
    return pl.pallas_call(
        mixer_backward,
        grid=(steps,),
        in_specs=[
            rows(3 * width),
            before,
            rows(width),
            rows(logits.shape[-1]),
            whole(taps.shape),
            whole(params.shape),
            whole(gain.shape),
            squares(),
            squares(),
            rows(width),
            rows(width),
            rows(width),
            pl.BlockSpec(memory_space=pl.ANY),
        ],
        out_specs=[
            rows(4 * width),
            rows(logits.shape[-1]),
            whole((8, 3 * width)),
            whole((8, logits.shape[-1])),
            whole((8, head_size)),
            whole((part_rows, columns)),
        ],
        out_shape=[
            jax.ShapeDtypeStruct((steps, seqs, span, 4 * width), BF16),
            jax.ShapeDtypeStruct(logits.shape, BF16),
            jax.ShapeDtypeStruct((8, 3 * width), F32),
            jax.ShapeDtypeStruct((8, logits.shape[-1]), F32),
            jax.ShapeDtypeStruct((8, head_size), F32),
            jax.ShapeDtypeStruct((part_rows, columns), F32),
        ],
        scratch_shapes=[
            pltpu.VMEM((seqs, heads, head_size, head_size), F32),
            pltpu.VMEM((seqs, 8, 3 * width), F32),
            pltpu.VMEM((4, part_rows, columns), BF16),
            pltpu.VMEM((4, part_rows, columns), BF16),
            pltpu.VMEM((part_rows, columns), BF16),
            pltpu.VMEM((2, part_rows, columns), BF16),
            pltpu.SemaphoreType.DMA((10,)),
            pltpu.SemaphoreType.DMA((10,)),
            pltpu.SemaphoreType.DMA((4,)),
        ],
        compiler_params=pltpu.CompilerParams(
            collective_id=collective_id, has_side_effects=True, vmem_limit_bytes=VMEM_LIMIT
        ),
        cost_estimate=lasting(55),
        name="mixer_backward",
    )(mixed, mixed, gate, logits, taps, params, gain, memory, inverse, fresh, out, grad, part)


def gather_rows(value, axis):
    return lax.all_gather(value, axis, axis=0, tiled=True)


def scatter_rows(value, axis):
    return lax.psum_scatter(value, axis, scatter_dimension=0, tiled=True)


def plane_peers():
    me = lax.axis_index("seq")
    sibling = me + 1 - 2 * (me % 2)
    across = me + 2 - 4 * ((me // 2) % 2)
    along = me + 4 - 8 * (me // 4)
    return (me, sibling, across, along)


def greet(peers):
    barrier = pltpu.get_barrier_semaphore()
    for peer in peers:
        pl.semaphore_signal(
            barrier, inc=1, device_id={"seq": peer}, device_id_type=pl.DeviceIdType.MESH
        )
    pl.semaphore_wait(barrier, len(peers))


def send_to(peer, source, target, send_sem, recv_sem):
    return pltpu.make_async_remote_copy(
        src_ref=source,
        dst_ref=target,
        send_sem=send_sem,
        recv_sem=recv_sem,
        device_id={"seq": peer},
        device_id_type=pl.DeviceIdType.MESH,
    )


def gather_phases(own_ref, all_ref, send_sems, recv_sems, local_sem, start):
    me, sibling, across, along = plane_peers()
    far = along + across - me
    half = own_ref.shape[0] // 2
    upper, lower = pl.ds(0, half), pl.ds(half, half)
    copies = []

    def send(peer, source, target):
        k = start + len(copies)
        copy = send_to(peer, source, target, send_sems.at[k], recv_sems.at[k])
        copy.start()
        copies.append(copy)

    keep = pltpu.make_async_copy(own_ref, all_ref.at[me], local_sem)
    keep.start()
    send(across, own_ref, all_ref.at[me])
    send(along, own_ref, all_ref.at[me])
    send(sibling, own_ref, all_ref.at[me])
    yield
    copies[0].wait_recv()
    send(along, all_ref.at[across, upper], all_ref.at[across, upper])
    copies[1].wait_recv()
    send(across, all_ref.at[along, lower], all_ref.at[along, lower])
    send(sibling, all_ref.at[across], all_ref.at[across])
    send(sibling, all_ref.at[along], all_ref.at[along])
    yield
    copies[3].wait_recv()
    send(sibling, all_ref.at[far, upper], all_ref.at[far, upper])
    copies[4].wait_recv()
    send(sibling, all_ref.at[far, lower], all_ref.at[far, lower])
    yield
    for k in (2, 5, 6, 7, 8):
        copies[k].wait_recv()
    for copy in copies:
        copy.wait_send()
    keep.wait()
    yield


def chain_hops(all_ref, half, up_send, up_recv, down_send, down_recv):
    depth = all_ref.shape[0]
    columns = all_ref.shape[2] // 2
    own = pl.ds(half * columns, columns)
    place = lax.axis_index("dp")
    above, below = lax.rem(place + 1, depth), lax.rem(place + depth - 1, depth)

    def hop(slot, peer, send_sem, recv_sem):
        return pltpu.make_async_remote_copy(
            src_ref=all_ref.at[slot, :, own],
            dst_ref=all_ref.at[slot, :, own],
            send_sem=send_sem,
            recv_sem=recv_sem,
            device_id={"dp": peer},
            device_id_type=pl.DeviceIdType.MESH,
        )

    hops = []
    for t in range(depth - 1):
        spot = half * (depth - 1) + t
        up_slot, down_slot = lax.rem(place + depth - t, depth), lax.rem(place + t, depth)
        up = hop(up_slot, above, up_send.at[spot], up_recv.at[spot])
        down = hop(down_slot, below, down_send.at[spot], down_recv.at[spot])
        below_slot, above_slot = place + depth - 1 - t, place + 1 + t
        hops.append(
            (
                (up, (place < depth - 1) & (place >= t), place > t, lax.rem(below_slot, depth)),
                (
                    down,
                    (place > 0) & (place + t < depth),
                    above_slot < depth,
                    lax.rem(above_slot, depth),
                ),
            )
        )
    return hops


def hop_start(hop):
    for copy, leaves, _, _ in hop:
        pl.when(leaves)(copy.start)


def hop_arrive(hop):
    for copy, _, arrives, _ in hop:
        pl.when(arrives)(copy.wait_recv)


def hop_finish(hops):
    for hop in hops:
        for copy, leaves, _, _ in hop:
            pl.when(leaves)(copy.wait_send)


def greet_all(ring, depth):
    me, place = lax.axis_index("seq"), lax.axis_index("dp")
    barrier = pltpu.get_barrier_semaphore()
    peers = [{"seq": lax.rem(me + k, ring)} for k in range(1, ring)]
    peers += [{"dp": lax.rem(place + k, depth)} for k in range(1, depth)]
    for peer in peers:
        pl.semaphore_signal(barrier, inc=1, device_id=peer, device_id_type=pl.DeviceIdType.MESH)
    pl.semaphore_wait(barrier, len(peers))


def spread_units(piece, target_ref, depth):
    ring, _, columns = piece.shape
    own = columns // (2 * depth)
    for k in range(2 * depth):
        block = jnp.concatenate([piece[s, :, k * own : (k + 1) * own] for s in range(ring)], 1)
        target_ref[:, k * ring * own : (k + 1) * ring * own] = block.astype(target_ref.dtype)


def exchange_copies(cut_ref, land, send_sems, recv_sems, start):
    ring = cut_ref.shape[0]
    me = lax.axis_index("seq")
    copies = []
    for k in range(1, ring):
        peer = lax.rem(me + k, ring)
        copy = send_to(
            peer, cut_ref.at[peer], land, send_sems.at[start + k - 1], recv_sems.at[start + k - 1]
        )
        copy.start()
        copies.append(copy)
    return copies


def rank_head(rank, j, heads):
    return rank // 2 + lax.axis_size("seq") // 2 * (heads * (rank % 2) + j)


def plane_open_kernel(
    heads,
    first_ref,
    weight_hbm,
    pair_hbm,
    lanes_hbm,
    first_all_hbm,
    weight_all_hbm,
    pair_all_ref,
    mixed_ref,
    gate_ref,
    logit_ref,
    first_all_ref,
    weight_all_ref,
    pair_ref,
    cut_ref,
    lanes_ref,
    total_ref,
    send_sems,
    recv_sems,
    local_sems,
    *chain_sems,
):
    place, me = lax.axis_index("dp"), lax.axis_index("seq")
    depth, rows = weight_all_ref.shape[0], weight_hbm.shape[0]
    ring, units = cut_ref.shape[0], cut_ref.shape[2] // 2
    width = weight_all_ref.shape[2] // 4
    load = pltpu.make_async_copy(pair_hbm, pair_ref, local_sems.at[0])
    load.start()
    lanes_load = pltpu.make_async_copy(lanes_hbm, lanes_ref, local_sems.at[3])
    lanes_load.start()
    greet_all(ring, depth)
    keeps, early = [], []
    own_rows = pl.ds(pl.multiple_of(me * rows, rows), rows)
    size = width // heads
    for part in range(4 * heads):
        block, j = part // heads, part % heads
        target = weight_all_ref.at[place, own_rows, pl.ds(part * size, size)]

        def source(peer, block=block, j=j):
            start = (block * ring * heads + rank_head(peer, j, heads)) * size
            return weight_hbm.at[:, pl.ds(pl.multiple_of(start, size), size)]

        keep = pltpu.make_async_copy(source(me), target, local_sems.at[4 + part])
        keep.start()
        keeps.append(keep)
        for k in range(1, ring):
            peer = lax.rem(me + k, ring)
            spot = part * (ring - 1) + k - 1
            copy = send_to(peer, source(peer), target, send_sems.at[spot], recv_sems.at[spot])
            copy.start()
            early.append(copy)
    base = 4 * heads * (ring - 1)
    chains = [chain_hops(weight_all_ref, g, *chain_sems) for g in range(2)]
    for g, chain in enumerate(chains):
        for copy in early[g * base // 2 : (g + 1) * base // 2]:
            copy.wait_recv()
        for keep in keeps[2 * g * heads : 2 * (g + 1) * heads]:
            keep.wait()
        hop_start(chain[0])
    first = gather_phases(first_ref, first_all_ref, send_sems, recv_sems, local_sems.at[1], base)
    next(first)
    load.wait()
    own = units // depth
    half = pair_ref.shape[1] // 2
    for s in range(ring):
        pieces = []
        for g in range(2):
            for z in range(depth):
                start = g * half + (z * ring + s) * own
                pieces.append(pair_ref[:, start : start + own])
        cut_ref[s] = jnp.concatenate(pieces, 1)
    pair_keep = pltpu.make_async_copy(cut_ref.at[me], pair_all_ref.at[me], local_sems.at[2])
    pair_keep.start()
    later = exchange_copies(cut_ref, pair_all_ref.at[me], send_sems, recv_sems, base + 9)
    for t in range(depth - 2):
        for chain in chains:
            hop_arrive(chain[t])
            hop_start(chain[t + 1])
        if t == 0:
            next(first)
    next(first)
    next(first)
    lanes_load.wait()
    deep = weight_all_ref.shape[1]

    def spread_slot(slot, fresh=False):
        def run():
            at = pl.ds(pl.multiple_of(slot * deep, deep), deep)

            @pl.loop(0, ring)
            def _(r):
                term = low_dot(first_all_ref[r, :, at], weight_all_ref[slot], NN)
                total_ref[r] = term if fresh else total_ref[r] + term

        return run

    @pl.loop(0, ring)
    def _(r):
        logit_ref[r] = low_dot(first_all_ref[r], lanes_ref[...], NN)

    saves = [pltpu.make_async_copy(first_all_ref, first_all_hbm, local_sems.at[0])]
    saves[0].start()
    spread_slot(place, True)()
    for hop in chains[0][:-1]:
        for _, _, arrives, slot in hop:
            pl.when(arrives)(spread_slot(slot))
    for chain in chains:
        hop_arrive(chain[-1])
    saves.append(pltpu.make_async_copy(weight_all_ref, weight_all_hbm, local_sems.at[1]))
    saves[1].start()
    for _, _, arrives, slot in chains[0][-1]:
        pl.when(arrives)(spread_slot(slot))

    @pl.loop(0, ring)
    def _(r):
        mixed_ref[r] = total_ref[r, :, : 3 * width].astype(BF16)
        gate_ref[r] = total_ref[r, :, 3 * width :]

    for copy in later:
        copy.wait_recv()
    for chain in chains:
        hop_finish(chain)
    for copy in early + later:
        copy.wait_send()
    pair_keep.wait()
    for save in saves:
        save.wait()


def plane_open(first, weight, pair, lanes, heads, collective_id):
    ring, depth = lax.axis_size("seq"), lax.axis_size("dp")
    rows, columns = first.shape
    weight_rows = weight.shape[0]
    width = weight.shape[1] // (4 * ring)
    total = (4 * heads + 1) * (ring - 1) + 9
    cut = jax.ShapeDtypeStruct((ring, weight_rows, pair.shape[1] // ring), pair.dtype)
    first_shape, weight_shape = (ring, rows, columns), (depth, ring * weight_rows, 4 * width)
    vmem, anywhere = pl.BlockSpec(memory_space=pltpu.VMEM), pl.BlockSpec(memory_space=pl.ANY)
    return pl.pallas_call(
        functools.partial(plane_open_kernel, heads),
        out_shape=[
            jax.ShapeDtypeStruct(first_shape, BF16),
            jax.ShapeDtypeStruct(weight_shape, BF16),
            cut,
            jax.ShapeDtypeStruct((ring, rows, 3 * width), BF16),
            jax.ShapeDtypeStruct((ring, rows, width), F32),
            jax.ShapeDtypeStruct((ring, rows, lanes.shape[1]), F32),
        ],
        in_specs=[anywhere] * 4,
        out_specs=[anywhere] * 3 + [vmem] * 3,
        scratch_shapes=[
            pltpu.VMEM(first_shape, BF16),
            pltpu.VMEM(weight_shape, BF16),
            pltpu.VMEM(pair.shape, BF16),
            pltpu.VMEM(cut.shape, BF16),
            pltpu.VMEM(lanes.shape, BF16),
            pltpu.VMEM((ring, rows, 4 * width), F32),
            pltpu.SemaphoreType.DMA((total,)),
            pltpu.SemaphoreType.DMA((total,)),
            pltpu.SemaphoreType.DMA((4 + 4 * heads,)),
        ]
        + [pltpu.SemaphoreType.DMA((2 * (depth - 1),))] * 4,
        compiler_params=pltpu.CompilerParams(
            collective_id=collective_id, has_side_effects=True, vmem_limit_bytes=VMEM_LIMIT
        ),
        cost_estimate=lasting(150),
        name="plane_open",
    )(first, weight, pair, lanes)


def trade_in_steps(rows_ref, rows_out_ref, send_sems, recv_sems, local_sems, heads):
    me = lax.axis_index("seq")
    core = lax.rem(me, 2)
    sibling = me + 1 - 2 * core
    rows = rows_out_ref.shape[0] // (2 * heads)

    def rows_of(ref, spot):
        return ref.at[pl.ds(pl.multiple_of(spot * rows, rows), rows)]

    copies, keeps = [], []
    for j in range(heads):
        target = rows_of(rows_out_ref, 2 * j + core)
        theirs = rows_of(rows_ref, heads * (1 - core) + j)
        copies.append(send_to(sibling, theirs, target, send_sems.at[9 + j], recv_sems.at[9 + j]))
        keeps.append(
            pltpu.make_async_copy(rows_of(rows_ref, heads * core + j), target, local_sems.at[1 + j])
        )
    step, steps = pl.program_id(0), pl.num_programs(0)

    @pl.when(step == 0)
    def _():
        for copy in copies + keeps:
            copy.start()

    @pl.when(step == steps - 1)
    def _():
        for copy in copies:
            copy.wait_recv()
            copy.wait_send()
        for keep in keeps:
            keep.wait()


def gather_in_steps(own_ref, all_ref, send_sems, recv_sems, local_sem):
    me, sibling, across, along = plane_peers()
    far = along + across - me
    half = own_ref.shape[0] // 2
    upper, lower = pl.ds(0, half), pl.ds(half, half)
    keep = pltpu.make_async_copy(own_ref, all_ref.at[me], local_sem)
    plan = [
        (across, own_ref, all_ref.at[me]),
        (along, own_ref, all_ref.at[me]),
        (sibling, own_ref, all_ref.at[me]),
        (along, all_ref.at[across, upper], all_ref.at[across, upper]),
        (across, all_ref.at[along, lower], all_ref.at[along, lower]),
        (sibling, all_ref.at[across], all_ref.at[across]),
        (sibling, all_ref.at[along], all_ref.at[along]),
        (sibling, all_ref.at[far, upper], all_ref.at[far, upper]),
        (sibling, all_ref.at[far, lower], all_ref.at[far, lower]),
    ]
    copies = [
        send_to(peer, source, target, send_sems.at[k], recv_sems.at[k])
        for k, (peer, source, target) in enumerate(plan)
    ]
    step, steps = pl.program_id(0), pl.num_programs(0)

    @pl.when(step == 0)
    def _():
        greet((sibling, across, along))
        keep.start()
        for k in (0, 1, 2):
            copies[k].start()

    @pl.when(step == 3)
    def _():
        copies[0].wait_recv()
        copies[1].wait_recv()
        for k in (3, 4, 5, 6):
            copies[k].start()

    @pl.when(step == 5)
    def _():
        copies[3].wait_recv()
        copies[4].wait_recv()
        for k in (7, 8):
            copies[k].start()

    @pl.when(step == steps - 1)
    def _():
        for k in (2, 5, 6, 7, 8):
            copies[k].wait_recv()
        for copy in copies:
            copy.wait_send()
        keep.wait()


def scatter_in_steps(
    part_ref,
    sum_ref,
    own_ref,
    near_ref,
    far_in_ref,
    side_in_ref,
    send_sems,
    recv_sems,
    load_sems,
):
    me, sibling, across, along = plane_peers()
    far = along + across - me
    flip = sibling - me
    rows = sum_ref.shape[0]
    half = rows // 2
    upper, lower = pl.ds(0, half), pl.ds(half, half)
    slabs = (far, across, along, me)
    loads = [
        pltpu.make_async_copy(part_ref.at[slab], own_ref.at[k], load_sems.at[k])
        for k, slab in enumerate(slabs)
    ]
    plan = [(sibling, part_ref.at[slab + flip], near_ref.at[k]) for k, slab in enumerate(slabs)]
    plan += [
        (across, own_ref.at[0, upper], far_in_ref.at[upper]),
        (along, own_ref.at[0, lower], far_in_ref.at[lower]),
        (across, own_ref.at[1, upper], side_in_ref.at[0, upper]),
        (along, own_ref.at[2, lower], side_in_ref.at[1, lower]),
        (along, own_ref.at[2, upper], side_in_ref.at[1, upper]),
        (across, own_ref.at[1, lower], side_in_ref.at[0, lower]),
    ]
    copies = [
        send_to(peer, source, target, send_sems.at[k], recv_sems.at[k])
        for k, (peer, source, target) in enumerate(plan)
    ]
    step, steps = pl.program_id(0), pl.num_programs(0)
    tall = 32

    def fold(target, other, start, size):
        @pl.loop(0, size // tall)
        def _(i):
            at = pl.ds(pl.multiple_of(start + i * tall, tall), tall)
            target[at] = (target[at].astype(F32) + other[at].astype(F32)).astype(BF16)

    def join(k):
        loads[k].wait()
        copies[k].wait_recv()
        fold(own_ref.at[k], near_ref.at[k], 0, rows)

    @pl.when(step == 0)
    def _():
        greet((sibling, across, along))
        for k in range(4):
            loads[k].start()
            copies[k].start()

    @pl.when(step == 1)
    def _():
        join(0)
        copies[4].start()
        copies[5].start()
        join(1)
        copies[6].start()
        join(2)
        copies[7].start()

    @pl.when(step == 3)
    def _():
        copies[4].wait_recv()
        fold(own_ref.at[2], far_in_ref, 0, half)
        copies[8].start()
        copies[5].wait_recv()
        fold(own_ref.at[1], far_in_ref, half, half)
        copies[9].start()

    @pl.when(step == steps - 1)
    def _():
        loads[3].wait()
        copies[3].wait_recv()
        for copy in copies[6:]:
            copy.wait_recv()

        @pl.loop(0, rows // tall)
        def _(i):
            at = pl.ds(pl.multiple_of(i * tall, tall), tall)
            sum_ref[at] = (
                own_ref[3, at].astype(F32)
                + near_ref[3, at].astype(F32)
                + side_in_ref[0, at].astype(F32)
                + side_in_ref[1, at].astype(F32)
            )

        for copy in copies:
            copy.wait_send()


def sum_phases(
    term_ref, share_ref, held_ref, land_ref, up_sems, down_sems, load_sems, trade_sems
):
    depth, rows, _ = held_ref.shape
    place = lax.axis_index("dp")
    above, below = lax.rem(place + 1, depth), lax.rem(place + depth - 1, depth)
    last = depth - 1
    mesh_ids = pl.DeviceIdType.MESH
    me = lax.axis_index("seq")
    core = lax.rem(me, 2)
    heads = depth // 2
    loads, trades = [], []
    for j in range(heads):
        target = held_ref.at[heads * core + j]

        def rows_of(spot):
            return term_ref.at[pl.ds(pl.multiple_of(spot * rows, rows), rows)]

        loads.append(pltpu.make_async_copy(rows_of(2 * j + core), target, load_sems.at[j]))
        trades.append(
            send_to(
                me + 1 - 2 * core,
                rows_of(2 * j + 1 - core),
                target,
                trade_sems.at[0, j],
                trade_sems.at[1, j],
            )
        )
    hops = []
    for r in range(last):
        hop = []
        for k, (peer, sems, block, leaves, mine, arrives) in enumerate(
            (
                (above, up_sems, place + last - r, place < r + 1, place + last - 1 - r, place > 0),
                (below, down_sems, place - last + r, place > last - 1 - r, place - last + 1 + r, place < last),
            )
        ):
            inside = (mine >= 0) & (mine <= last)
            spot = lax.rem(block + depth, depth)
            copy = pltpu.make_async_remote_copy(
                src_ref=held_ref.at[spot],
                dst_ref=land_ref.at[r, k],
                send_sem=sems.at[0, r],
                recv_sem=sems.at[1, r],
                device_id={"dp": peer},
                device_id_type=mesh_ids,
            )
            hop.append((copy, leaves, arrives & inside, lax.rem(mine + depth, depth)))
        hops.append(hop)
    def start(r, from_end):
        for end, (copy, leaves, _, _) in zip((0, last), hops[r]):
            pl.when(leaves & ((place == end) == from_end))(copy.start)

    def arrive(r):
        for k, (copy, _, arrives, block) in enumerate(hops[r]):

            @pl.when(arrives)
            def _(copy=copy, block=block, k=k):
                copy.wait_recv()
                total = held_ref[block].astype(F32) + land_ref[r, k].astype(F32)
                held_ref[block] = total.astype(BF16)

    for copy in loads + trades:
        copy.start()
    yield
    for load in loads:
        load.wait()
    for trade in trades:
        trade.wait_recv()
    for r in range(last):
        start(r, True)
    for r in range(last):
        start(r, False)
        yield
        arrive(r)
    share_ref[...] = held_ref[place].astype(F32)
    for trade in trades:
        trade.wait_send()
    for hop in hops:
        for copy, leaves, _, _ in hop:
            pl.when(leaves)(copy.wait_send)
    yield


def small_sum_kernel(
    heads,
    own_ref,
    cut_ref,
    term_ref,
    first_ref,
    second_ref,
    third_ref,
    decay_ref,
    taps_ref,
    param_ref,
    joined_ref,
    share_ref,
    all_ref,
    swapped_ref,
    stage_ref,
    total_ref,
    send_sems,
    recv_sems,
    local_sem,
    *sum_refs,
):
    depth, ring = stage_ref.shape[0], cut_ref.shape[0]
    place, me = lax.axis_index("dp"), lax.axis_index("seq")
    mesh_ids = pl.DeviceIdType.MESH
    columns = [lax.rem(place + k, depth) for k in range(1, depth)]
    plane = [lax.rem(me + k, ring) for k in range(1, ring)]
    greet_all(ring, depth)
    sums = sum_phases(term_ref, share_ref, *sum_refs)
    next(sums)
    keep = pltpu.make_async_copy(cut_ref.at[me], swapped_ref.at[me], local_sem)
    keep.start()
    first = []
    for k, peer in enumerate(columns):
        copy = pltpu.make_async_remote_copy(
            src_ref=own_ref,
            dst_ref=stage_ref.at[place],
            send_sem=send_sems.at[k],
            recv_sem=recv_sems.at[k],
            device_id={"dp": peer},
            device_id_type=mesh_ids,
        )
        copy.start()
        first.append(copy)
    swaps = exchange_copies(
        cut_ref, swapped_ref.at[me], send_sems, recv_sems, depth + ring - 2
    )
    stage_ref[place] = own_ref[...]
    next(sums)
    for copy in first:
        copy.wait_recv()
    total = stage_ref[0]
    for k in range(1, depth):
        total = total + stage_ref[k]
    total_ref[...] = total
    second = []
    for k, peer in enumerate(plane):
        copy = pltpu.make_async_remote_copy(
            src_ref=total_ref,
            dst_ref=all_ref.at[me],
            send_sem=send_sems.at[depth - 1 + k],
            recv_sem=recv_sems.at[depth - 1 + k],
            device_id={"seq": peer},
            device_id_type=mesh_ids,
        )
        copy.start()
        second.append(copy)
    all_ref[me] = total
    next(sums)
    next(sums)
    for copy in second:
        copy.wait_recv()
    start = 0
    for target in (first_ref, second_ref, third_ref):
        rows = target.shape[0]
        shared = all_ref[0, start : start + rows]
        for s in range(1, ring):
            shared = shared + all_ref[s, start : start + rows]
        target[...] = shared
        start += rows
    for target in (decay_ref, taps_ref, param_ref):
        rows = target.shape[1]
        target[...] = all_ref[:, start : start + rows]
        start += rows
    for copy in swaps:
        copy.wait_recv()
    keep.wait()
    size = cut_ref.shape[2] // (4 * heads)
    for part in range(4 * heads):
        block, j = part // heads, part % heads
        for s in range(ring):
            start = (block * ring * heads + rank_head(s, j, heads)) * size
            joined_ref[:, start : start + size] = swapped_ref[
                s, :, part * size : (part + 1) * size
            ]
    next(sums)
    for copy in first + second + swaps:
        copy.wait_send()


def small_sum(own, shared_counts, own_counts, cut, term, heads, collective_id):
    depth, ring = lax.axis_size("dp"), lax.axis_size("seq")
    count = depth + 2 * ring - 3
    term_rows, columns = term.shape[0] // depth, term.shape[1]
    vmem, anywhere = pl.BlockSpec(memory_space=pltpu.VMEM), pl.BlockSpec(memory_space=pl.ANY)
    return pl.pallas_call(
        functools.partial(small_sum_kernel, heads),
        out_shape=[
            *[jax.ShapeDtypeStruct((count, own.shape[1]), F32) for count in shared_counts],
            *[jax.ShapeDtypeStruct((ring, count, own.shape[1]), F32) for count in own_counts],
            jax.ShapeDtypeStruct((cut.shape[1], ring * cut.shape[2]), cut.dtype),
            jax.ShapeDtypeStruct((term_rows, columns), F32),
        ],
        in_specs=[vmem, anywhere, anywhere],
        out_specs=[vmem] * 8,
        scratch_shapes=[
            pltpu.VMEM((ring,) + own.shape, F32),
            pltpu.VMEM(cut.shape, cut.dtype),
            pltpu.VMEM((depth,) + own.shape, F32),
            pltpu.VMEM(own.shape, F32),
            pltpu.SemaphoreType.DMA((count,)),
            pltpu.SemaphoreType.DMA((count,)),
            pltpu.SemaphoreType.DMA,
            pltpu.VMEM((depth, term_rows, columns), BF16),
            pltpu.VMEM((depth - 1, 2, term_rows, columns), BF16),
            pltpu.SemaphoreType.DMA((2, depth - 1)),
            pltpu.SemaphoreType.DMA((2, depth - 1)),
            pltpu.SemaphoreType.DMA((depth // 2,)),
            pltpu.SemaphoreType.DMA((2, depth // 2)),
        ],
        compiler_params=pltpu.CompilerParams(collective_id=collective_id, has_side_effects=True),
        cost_estimate=lasting(20),
        name="small_sum",
    )(own, cut, term)


def greet_plane(ring):
    me = lax.axis_index("seq")
    greet([lax.rem(me + k, ring) for k in range(1, ring)])


def plane_scatter_dot_kernel(count, dims, fill, swaps, back, ends, low, *refs):
    refs = list(refs)

    def take(size):
        taken = refs[:size]
        del refs[:size]
        return taken

    left_hbm, right_hbm, fill_hbm = take(count), take(count), take(int(len(fill) > 0))
    cut_refs, back_hbm, end_hbm = take(swaps), take(2 * back), take(3 * ends)
    (sum_ref,) = take(1)
    terms, spread_refs = take(len(fill)), take(swaps)
    gain_grads, low_refs = take(ends), take(int(low))
    swapped_refs = take(swaps)
    lefts, rights, fill_refs = take(count), take(count), take(int(len(fill) > 0))
    out_ref, own_ref, near_ref, far_in_ref, side_in_ref = take(5)
    send_sems, recv_sems, load_sems, slab_sems = take(4)
    me, sibling, across, along = plane_peers()
    far = along + across - me
    flip = sibling - me
    slab_order = [far + flip, far, across + flip, across, along + flip, along, sibling, me]
    loads, slab_loads = [], []
    for k in range(count):
        load = pltpu.make_async_copy(right_hbm[k], rights[k], load_sems.at[k])
        load.start()
        loads.append(load)
    for n, slab in enumerate(slab_order):
        for k in range(count):
            load = pltpu.make_async_copy(
                left_hbm[k].at[slab], lefts[k].at[slab], slab_sems.at[k * len(slab_order) + n]
            )
            load.start()
            slab_loads.append(load)
    if ends:
        base_ref, up_ref, end_sems = take(3)
        end_loads = [
            pltpu.make_async_copy(end_hbm[0], base_ref, end_sems.at[0]),
            pltpu.make_async_copy(end_hbm[1], up_ref, end_sems.at[1]),
        ]
        gain_grads[0][...] = jnp.zeros_like(gain_grads[0])
    if back:
        error_ref, down_ref, error_sems, down_sem = refs
        down_load = pltpu.make_async_copy(back_hbm[1], down_ref, down_sem)
        down_load.start()
        error_loads = [
            pltpu.make_async_copy(back_hbm[0].at[slab], error_ref.at[k % 2], error_sems.at[k % 2])
            for k, slab in enumerate(slab_order)
        ]
        error_loads[0].start()
        error_loads[1].start()
    if fill:
        fill_load = pltpu.make_async_copy(fill_hbm[0], fill_refs[0], load_sems.at[count])
    rows, columns = sum_ref.shape
    half = rows // 2
    upper, lower = pl.ds(0, half), pl.ds(half, half)
    swapped = []
    if swaps:
        greet_plane(lefts[0].shape[0])
        keep = pltpu.make_async_copy(
            cut_refs[0].at[me], swapped_refs[0].at[me], load_sems.at[count + 1]
        )
        keep.start()
        swapped = exchange_copies(
            cut_refs[0], swapped_refs[0].at[me], send_sems, recv_sems, 10
        )
    else:
        greet((sibling, across, along))
    for load in loads:
        load.wait()
    if ends:
        for load in end_loads:
            load.start()
    if back:
        down_load.wait()
    wide = 512
    turns = iter(range(8))

    def feed_back(slab):
        k = next(turns)
        error_loads[k].wait()
        units = down_ref.shape[0]
        grad = low_dot(error_ref[k % 2], down_ref[...], NT)
        gate = lefts[0][slab, :, :units].astype(F32)
        up = lefts[0][slab, :, units:].astype(F32)
        opening = sigmoid(gate)
        gate_err = grad * up * (opening * (1.0 + gate * (1.0 - opening)))
        up_err = grad * (gate * opening)
        lefts[0][slab] = jnp.concatenate([gate_err, up_err], 1).astype(BF16)
        if k + 2 < len(error_loads):
            error_loads[k + 2].start()

    def slab_dot(slab, target):
        for _ in range(count):
            slab_loads.pop(0).wait()
        if back:
            feed_back(slab)

        @pl.loop(0, columns // wide)
        def _(i):
            at = pl.ds(pl.multiple_of(i * wide, wide), wide)
            total = None
            for k in range(count):
                right = rights[k][:, at] if dims[1] == (0,) else rights[k][at, :]
                term = low_dot(lefts[k][slab], right, dims)
                total = term if total is None else total + term
            target[:, at] = total.astype(BF16)

    def send(k, peer, source, target):
        copy = send_to(peer, source, target, send_sems.at[k], recv_sems.at[k])
        copy.start()
        return copy

    step = 32

    def fold(target, other, start, size):
        @pl.loop(0, size // step)
        def _(i):
            at = pl.ds(pl.multiple_of(start + i * step, step), step)
            target[at] = (target[at].astype(F32) + other[at].astype(F32)).astype(BF16)

    nears = []

    def near_slab(k, slab):
        slab_dot(slab + flip, out_ref.at[k])
        nears.append(send(k, sibling, out_ref.at[k], near_ref.at[k]))

    near_slab(0, far)
    if fill:
        fill_load.start()
    slab_dot(far, own_ref.at[0])
    near_slab(1, across)
    nears[0].wait_recv()
    fold(own_ref.at[0], near_ref.at[0], 0, rows)
    copies = [
        send(4, across, own_ref.at[0, upper], far_in_ref.at[upper]),
        send(5, along, own_ref.at[0, lower], far_in_ref.at[lower]),
    ]
    slab_dot(across, own_ref.at[1])
    near_slab(2, along)
    nears[1].wait_recv()
    fold(own_ref.at[1], near_ref.at[1], 0, rows)
    copies.append(send(6, across, own_ref.at[1, upper], side_in_ref.at[0, upper]))
    slab_dot(along, own_ref.at[2])
    near_slab(3, me)
    nears[2].wait_recv()
    fold(own_ref.at[2], near_ref.at[2], 0, rows)
    copies.append(send(7, along, own_ref.at[2, lower], side_in_ref.at[1, lower]))
    slab_dot(me, own_ref.at[3])
    copies[0].wait_recv()
    fold(own_ref.at[2], far_in_ref, 0, half)
    copies.append(send(8, along, own_ref.at[2, upper], side_in_ref.at[1, upper]))
    copies[1].wait_recv()
    fold(own_ref.at[1], far_in_ref, half, half)
    copies.append(send(9, across, own_ref.at[1, lower], side_in_ref.at[0, lower]))
    if swaps:
        for copy in swapped:
            copy.wait_recv()
        keep.wait()
        spread_units(swapped_refs[0], spread_refs[0], lax.axis_size("dp"))
    if fill:
        fill_load.wait()
        tall = 256

        @pl.loop(0, terms[0].shape[0] // tall)
        def _(i):
            at = pl.ds(pl.multiple_of(i * tall, tall), tall)
            turned = fill_refs[0][:, at]
            for term, k in zip(terms, fill):
                wide_left = lefts[k][...].reshape(-1, lefts[k].shape[2])
                term[at, :] = low_dot(turned, wide_left, TN).astype(term.dtype)

    nears[3].wait_recv()

    def finish(a, start):
        @pl.loop(0, half // step)
        def _(i):
            at = pl.ds(pl.multiple_of(start + i * step, step), step)
            total = (
                own_ref[3, at].astype(F32)
                + near_ref[3, at].astype(F32)
                + side_in_ref[0, at].astype(F32)
                + side_in_ref[1, at].astype(F32)
            )
            if ends:
                base = base_ref[at].astype(F32)
                scale = lax.rsqrt(jnp.mean(base * base, -1, keepdims=True) + 1e-05)
                normal = base * scale
                weighted = total * end_hbm[2][...]
                inner = jnp.mean(weighted * normal, -1, keepdims=True)
                gain_grads[0][0:1, :] += jnp.sum(total * normal, 0, keepdims=True)
                total = up_ref[at].astype(F32) + scale * (weighted - normal * inner)
            sum_ref[at] = total
            if low:
                low_refs[0][at] = total.astype(BF16)

    for copy in copies[2:]:
        copy.wait_recv()
    if ends:
        for load in end_loads:
            load.wait()
    finish(0, 0)
    finish(1, half)
    for copy in nears + copies + swapped:
        copy.wait_send()


def plane_scatter_dot(lefts, rights, dims, collective_id, fill=None, fill_lefts=(0,), term_type=BF16, cut=None, back=(), ends=(), low=False):
    count = len(lefts)
    ring, rows, _ = lefts[0].shape
    columns = rights[0].shape[1 - dims[1][0]]
    filled = fill is not None
    fills = [fill] if filled else []
    vmem, anywhere = pl.BlockSpec(memory_space=pltpu.VMEM), pl.BlockSpec(memory_space=pl.ANY)
    back_scratch = []
    if back:
        back_scratch = [
            pltpu.VMEM((2,) + back[0].shape[1:], BF16),
            pltpu.VMEM(back[1].shape, BF16),
            pltpu.SemaphoreType.DMA((2,)),
            pltpu.SemaphoreType.DMA,
        ]
    cuts = [] if cut is None else [cut]
    total = 10 + len(cuts) * (ring - 1)
    fill_lefts = fill_lefts if filled else ()
    term_shapes = [
        jax.ShapeDtypeStruct((fill.shape[1], lefts[k].shape[2]), term_type) for k in fill_lefts
    ]
    end_shapes = [jax.ShapeDtypeStruct((8, columns), F32)] if ends else []
    end_shapes += [jax.ShapeDtypeStruct((rows, columns), BF16)] if low else []
    end_scratch = []
    if ends:
        end_scratch = [
            pltpu.VMEM(ends[0].shape, ends[0].dtype),
            pltpu.VMEM(ends[1].shape, ends[1].dtype),
            pltpu.SemaphoreType.DMA((2,)),
        ]
    return pl.pallas_call(
        functools.partial(
            plane_scatter_dot_kernel,
            count,
            dims,
            fill_lefts,
            len(cuts),
            len(back) // 2,
            len(ends) // 3,
            low,
        ),
        out_shape=[jax.ShapeDtypeStruct((rows, columns), F32)]
        + term_shapes
        + [jax.ShapeDtypeStruct((cut.shape[1], ring * cut.shape[2]), BF16) for cut in cuts]
        + end_shapes,
        in_specs=[anywhere] * (2 * count + len(fills) + len(cuts) + len(back) + len(ends[:2]))
        + [vmem] * len(ends[2:]),
        out_specs=[vmem] * (1 + len(term_shapes) + len(cuts) + len(end_shapes)),
        scratch_shapes=[pltpu.VMEM(cut.shape, BF16) for cut in cuts]
        + [pltpu.VMEM(left.shape, BF16) for left in lefts]
        + [pltpu.VMEM(right.shape, BF16) for right in rights]
        + [pltpu.VMEM(value.shape, BF16) for value in fills]
        + [
            pltpu.VMEM((4, rows, columns), BF16),
            pltpu.VMEM((4, rows, columns), BF16),
            pltpu.VMEM((4, rows, columns), BF16),
            pltpu.VMEM((rows, columns), BF16),
            pltpu.VMEM((2, rows, columns), BF16),
            pltpu.SemaphoreType.DMA((total,)),
            pltpu.SemaphoreType.DMA((total,)),
            pltpu.SemaphoreType.DMA((count + 2,)),
            pltpu.SemaphoreType.DMA((8 * count,)),
        ]
        + end_scratch
        + back_scratch,
        compiler_params=pltpu.CompilerParams(
            collective_id=collective_id, has_side_effects=True, vmem_limit_bytes=VMEM_LIMIT
        ),
        cost_estimate=lasting(45),
        name="plane_scatter_dot",
    )(*lefts, *rights, *fills, *cuts, *back, *ends)


def gather_in_turn(own_ref, all_ref, send_sems, recv_sems, use):
    me, sibling, across, along = plane_peers()
    far = along + across - me
    flip = sibling - me
    half = own_ref.shape[0] // 2
    upper, lower = pl.ds(0, half), pl.ds(half, half)
    copies = []

    def send(peer, source, target):
        k = len(copies)
        copy = send_to(peer, source, target, send_sems.at[k], recv_sems.at[k])
        copy.start()
        copies.append(copy)

    send(across, own_ref, all_ref.at[me])
    send(along, own_ref, all_ref.at[me])
    send(sibling, own_ref, all_ref.at[me])
    all_ref[me] = own_ref[...]
    use(me)
    copies[2].wait_recv()
    use(sibling)
    copies[0].wait_recv()
    send(along, all_ref.at[across, upper], all_ref.at[across, upper])
    copies[1].wait_recv()
    send(across, all_ref.at[along, lower], all_ref.at[along, lower])
    send(sibling, all_ref.at[across], all_ref.at[across])
    send(sibling, all_ref.at[along], all_ref.at[along])
    use(across)
    use(along)
    copies[5].wait_recv()
    use(across + flip)
    copies[6].wait_recv()
    use(along + flip)
    copies[3].wait_recv()
    send(sibling, all_ref.at[far, upper], all_ref.at[far, upper])
    copies[4].wait_recv()
    send(sibling, all_ref.at[far, lower], all_ref.at[far, lower])
    use(far)
    copies[7].wait_recv()
    copies[8].wait_recv()
    use(far + flip)
    for copy in copies:
        copy.wait_send()


def gather_feed_kernel(
    own_hbm,
    pair_hbm,
    error_hbm,
    all_hbm,
    activated_hbm,
    pair_part_hbm,
    down_term_ref,
    own_ref,
    pair_ref,
    error_ref,
    all_ref,
    activated_out,
    pair_out,
    total_ref,
    send_sems,
    recv_sems,
    load_sems,
    save_sems,
):
    loads = []
    for source, target in (
        (own_hbm, own_ref),
        (pair_hbm, pair_ref),
        (error_hbm, error_ref),
    ):
        load = pltpu.make_async_copy(source, target, load_sems.at[len(loads)])
        load.start()
        loads.append(load)
    greet(plane_peers()[1:])
    loads[0].wait()
    waiting = loads[1:]
    saves = []
    tall = 256
    wide = 512
    rows, columns = own_ref.shape
    units = pair_ref.shape[1] // 2


    def use(slab):
        first = bool(waiting)
        while waiting:
            waiting.pop().wait()
        turn = len(saves) % 2
        if len(saves) > 1:
            for save in saves[-2]:
                save.wait()

        @pl.loop(0, rows // tall)
        def _(i):
            at = pl.ds(pl.multiple_of(i * tall, tall), tall)
            values = all_ref[slab, at, :]
            pair = low_dot(values, pair_ref[...], NN)
            gate, up = pair[:, :units], pair[:, units:]
            activated_out[turn, at, :] = (gate * sigmoid(gate) * up).astype(BF16)
            pair_out[turn, at, :] = pair.astype(BF16)

        batch = []
        for k, (source, target) in enumerate(
            (
                (activated_out.at[turn], activated_hbm.at[slab]),
                (pair_out.at[turn], pair_part_hbm.at[slab]),
                (all_ref.at[slab], all_hbm.at[slab]),
            )
        ):
            save = pltpu.make_async_copy(source, target, save_sems.at[turn, k])
            save.start()
            batch.append(save)
        saves.append(batch)

        @pl.loop(0, columns // wide)
        def _(i):
            at = pl.ds(pl.multiple_of(i * wide, wide), wide)
            term = low_dot(activated_out[turn], error_ref[slab, :, at], TN)
            if first:
                total_ref[:, at] = term
            else:
                total_ref[:, at] += term

    gather_in_turn(own_ref, all_ref, send_sems, recv_sems, use)
    down_term_ref[...] = total_ref[...].astype(BF16)
    for batch in saves[-2:]:
        for save in batch:
            save.wait()


def gather_feed(own, pair_own, error_all, collective_id):
    ring = lax.axis_size("seq")
    rows, columns = own.shape
    units = pair_own.shape[1] // 2
    anywhere = pl.BlockSpec(memory_space=pl.ANY)
    return pl.pallas_call(
        gather_feed_kernel,
        out_shape=[
            jax.ShapeDtypeStruct((ring, rows, columns), BF16),
            jax.ShapeDtypeStruct((ring, rows, units), BF16),
            jax.ShapeDtypeStruct((ring, rows, 2 * units), BF16),
            jax.ShapeDtypeStruct((units, columns), BF16),
        ],
        in_specs=[anywhere] * 3,
        out_specs=[anywhere] * 3 + [pl.BlockSpec(memory_space=pltpu.VMEM)],
        scratch_shapes=[
            pltpu.VMEM((rows, columns), BF16),
            pltpu.VMEM(pair_own.shape, BF16),
            pltpu.VMEM((ring, rows, columns), BF16),
            pltpu.VMEM((ring, rows, columns), BF16),
            pltpu.VMEM((2, rows, units), BF16),
            pltpu.VMEM((2, rows, 2 * units), BF16),
            pltpu.VMEM((units, columns), F32),
            pltpu.SemaphoreType.DMA((9,)),
            pltpu.SemaphoreType.DMA((9,)),
            pltpu.SemaphoreType.DMA((3,)),
            pltpu.SemaphoreType.DMA((2, 3)),
        ],
        compiler_params=pltpu.CompilerParams(
            collective_id=collective_id, has_side_effects=True, vmem_limit_bytes=VMEM_LIMIT
        ),
        cost_estimate=lasting(46),
        name="gather_feed",
    )(own, pair_own, error_all)


def gather_branch_kernel(
    own_hbm,
    gated_hbm,
    weight_hbm,
    activated_hbm,
    down_hbm,
    grad_ref,
    term_ref,
    part_hbm,
    own_ref,
    gated_ref,
    weight_ref,
    activated_ref,
    down_ref,
    all_ref,
    total_ref,
    part_out,
    send_sems,
    recv_sems,
    load_sems,
    save_sems,
):
    loads = []
    for source, target in (
        (own_hbm, own_ref),
        (gated_hbm, gated_ref),
        (weight_hbm, weight_ref),
        (activated_hbm, activated_ref),
        (down_hbm, down_ref),
    ):
        load = pltpu.make_async_copy(source, target, load_sems.at[len(loads)])
        load.start()
        loads.append(load)
    greet(plane_peers()[1:])
    loads[0].wait()
    waiting = loads[1:]
    total_ref[...] = jnp.zeros_like(total_ref)
    wide = 512
    saves = []

    def use(slab):
        while waiting:
            waiting.pop().wait()
        turn = len(saves) % 2
        if len(saves) > 1:
            saves[-2].wait()
        grad_ref[slab] = low_dot(all_ref[slab], weight_ref[...], NT).astype(BF16)

        @pl.loop(0, total_ref.shape[1] // wide)
        def _(i):
            at = pl.ds(pl.multiple_of(i * wide, wide), wide)
            total_ref[:, at] += low_dot(gated_ref[slab], all_ref[slab, :, at], TN)
            part_out[turn, :, at] = low_dot(activated_ref[slab], down_ref[:, at], NN).astype(BF16)

        save = pltpu.make_async_copy(part_out.at[turn], part_hbm.at[slab], save_sems.at[turn])
        save.start()
        saves.append(save)

    gather_in_turn(own_ref, all_ref, send_sems, recv_sems, use)
    term_ref[...] = total_ref[...].astype(BF16)
    for save in saves[-2:]:
        save.wait()


def gather_branch(own, gated, weight, activated, down_own, collective_id):
    ring, rows, width = gated.shape
    columns = own.shape[1]
    vmem = pl.BlockSpec(memory_space=pltpu.VMEM)
    anywhere = pl.BlockSpec(memory_space=pl.ANY)
    return pl.pallas_call(
        gather_branch_kernel,
        out_shape=[
            jax.ShapeDtypeStruct((ring, rows, width), BF16),
            jax.ShapeDtypeStruct((width, columns), BF16),
            jax.ShapeDtypeStruct((ring, rows, columns), BF16),
        ],
        in_specs=[anywhere] * 5,
        out_specs=[vmem, vmem, anywhere],
        scratch_shapes=[
            pltpu.VMEM(own.shape, BF16),
            pltpu.VMEM(gated.shape, BF16),
            pltpu.VMEM(weight.shape, BF16),
            pltpu.VMEM(activated.shape, BF16),
            pltpu.VMEM(down_own.shape, BF16),
            pltpu.VMEM((ring, rows, columns), BF16),
            pltpu.VMEM((width, columns), F32),
            pltpu.VMEM((2, rows, columns), BF16),
            pltpu.SemaphoreType.DMA((9,)),
            pltpu.SemaphoreType.DMA((9,)),
            pltpu.SemaphoreType.DMA((5,)),
            pltpu.SemaphoreType.DMA((2,)),
        ],
        compiler_params=pltpu.CompilerParams(
            collective_id=collective_id, has_side_effects=True, vmem_limit_bytes=VMEM_LIMIT
        ),
        cost_estimate=lasting(45),
        name="gather_branch",
    )(own, gated, weight, activated, down_own)


def low_dot(left, right, dims):
    return lax.dot_general(left, right, (dims, ((), ())), preferred_element_type=F32)


NN = ((1,), (0,))
NT = ((1,), (1,))
TN = ((0,), (0,))


def split_heads_device(
    inputs,
    lengths,
    first_gain,
    input_weight,
    decay_weight,
    conv_weight,
    decay_log,
    decay_bias,
    head_gain,
    output_weight,
    second_gain,
    gate_up_weight,
    down_weight,
    cotangent,
):
    micro_count, seq_local, span, model_width = inputs.shape
    ring = lax.axis_size("seq")
    depth = lax.axis_size("dp")
    rank = lax.axis_index("seq")
    seqs = micro_count * seq_local
    row_count = seqs * span
    all_rows = ring * row_count
    head_count = decay_log.shape[0]
    heads = head_count // ring
    head_size = head_gain.shape[0]
    key_width = head_count * head_size
    width = heads * head_size
    own_units = down_weight.shape[0]
    units = depth * own_units
    weight_rows = input_weight.shape[0]
    tap_count = conv_weight.shape[0]

    tokens = inputs.reshape(row_count, model_width).astype(F32)
    positions = rank * span + lax.broadcasted_iota(jnp.int32, (micro_count, seq_local, span), 2)
    valid_rows = (positions < lengths[:, :, None]).astype(F32).reshape(row_count, 1)
    normed_low = rms_norm(tokens, first_gain).astype(BF16)

    upstream = valid_rows * cotangent.reshape(row_count, model_width).astype(F32)
    out_err = upstream.astype(BF16)
    out_rows = gather_rows(output_weight, "dp")
    own_heads = [rank_head(rank, j, heads) for j in range(heads)]

    def own_lanes(pair):
        rows = pair.shape[0]
        lanes = [
            lax.dynamic_slice(pair, (0, start + head), (rows, 1))
            for start in range(0, pair.shape[1], head_count)
            for head in own_heads
        ]
        return jnp.pad(jnp.concatenate(lanes, 1), ((0, 0), (0, 128 - len(lanes))))

    decay_own = own_lanes(decay_weight)
    params = jnp.pad(own_lanes(jnp.stack([decay_log, decay_bias])), ((0, 6), (0, 0)))
    taps = jnp.concatenate(
        [
            lax.dynamic_slice(
                conv_weight, (0, block * key_width + head * head_size), (tap_count, head_size)
            )
            for block in range(3)
            for head in own_heads
        ],
        1,
    )
    gain = head_gain.reshape(1, head_size)

    def chunks(value):
        return value.reshape(ring, seqs, span, value.shape[-1])

    normed_all, in_own, pair_cut, mixed, gate_raw, logits = plane_open(
        normed_low, input_weight, gate_up_weight, decay_own, heads, 1
    )
    normed_all = normed_all.reshape(all_rows, model_width)
    in_own = in_own.reshape(model_width, 4 * width)
    pair_own = gather_rows(pair_cut.reshape(ring * weight_rows, 2 * units), "dp")
    mixed, out_rows, down_weight = lax.optimization_barrier((mixed, out_rows, down_weight))
    down_own = gather_rows(down_weight, "dp")
    mixed, gate_raw, logits = chunks(mixed), chunks(gate_raw), chunks(logits)
    gated, memory, inverse, fresh, mixer_out, out_err_all, out_own = run_forward(
        mixed, gate_raw, logits, taps, params, gain, heads, out_err, out_rows, 5
    )
    gated = gated.reshape(ring, row_count, width)
    hidden = tokens + plane_scatter_dot([gated], [out_own], NN, 2)[0]
    second_low = rms_norm(hidden, second_gain).astype(BF16)
    second_all, activated, pair_part, down_term = gather_feed(
        second_low, pair_own, out_err_all, 3
    )
    down_share = scatter_rows(down_term, "dp").astype(F32)
    hidden_grad, pair_term, second_gain_grad, branch_err = plane_scatter_dot(
        [pair_part],
        [pair_own],
        NT,
        4,
        second_all.reshape(all_rows, model_width),
        back=(out_err_all, down_own),
        ends=(hidden, out_err, second_gain.reshape(1, model_width)),
        low=True,
    )
    pair_share = scatter_rows(pair_term, "dp")
    gated_grad, output_term, down_part = gather_branch(
        branch_err, gated, out_own, activated, down_own, 11
    )
    in_err, logit_grad, taps_grad, param_grad, gain_grad, final_part = run_backward(
        mixed,
        gate_raw,
        logits,
        taps,
        params,
        gain,
        memory,
        inverse,
        fresh,
        mixer_out,
        gated_grad.reshape(ring, seqs, span, width),
        down_part,
        12,
    )
    result = valid_rows * (hidden + final_part)
    input_term = low_dot(normed_all, in_err.reshape(all_rows, 4 * width), TN).astype(BF16)
    input_term, in_err, logit_grad, down_share, pair_share = lax.optimization_barrier(
        (input_term, in_err, logit_grad, down_share, pair_share)
    )
    lanes = logit_grad.shape[-1]
    input_cut = scatter_rows(input_term, "dp")
    decay_twice = decay_own + jnp.roll(decay_own, lanes // 2, 1)
    inputs_grad, decay_term, gate_up_share, first_gain_grad = plane_scatter_dot(
        [
            in_err.reshape(ring, row_count, 4 * width),
            logit_grad.reshape(ring, row_count, lanes),
        ],
        [in_own, decay_twice],
        NT,
        6,
        normed_all,
        (1,),
        F32,
        cut=pair_share.reshape(ring, weight_rows, 2 * units),
        ends=(
            inputs.reshape(row_count, model_width),
            hidden_grad,
            first_gain.reshape(1, model_width),
        ),
    )
    decay_term = decay_term[:, : 2 * heads] + decay_term[:, lanes // 2 : lanes // 2 + 2 * heads]
    pieces = [
        first_gain_grad[0],
        second_gain_grad[0],
        gain_grad[0],
        jnp.transpose(decay_term),
        taps_grad[:tap_count],
        param_grad[:2],
    ]
    counts = [piece.size // 128 for piece in pieces]
    packed = jnp.concatenate([piece.reshape(-1) for piece in pieces])
    packed = jnp.pad(packed, (0, -packed.size % 1024)).reshape(-1, 128)
    gate_up_share = gate_up_share.astype(F32)
    packed, input_cut, gate_up_share, result = lax.optimization_barrier(
        (packed, input_cut, gate_up_share, result)
    )
    (
        first_gain_grad,
        second_gain_grad,
        gain_grad,
        decay_sum,
        taps_sum,
        param_sum,
        input_share,
        output_share,
    ) = small_sum(
        packed,
        counts[:3],
        counts[3:],
        input_cut.reshape(ring, weight_rows, 4 * width),
        output_term,
        heads,
        7,
    )
    input_share = input_share.astype(F32)
    first_gain_grad, second_gain_grad, gain_grad = [
        total.reshape(-1) for total in (first_gain_grad, second_gain_grad, gain_grad)
    ]
    chips = ring // 2
    decay_sum = decay_sum.reshape(chips, 2, 2, heads, model_width)
    decay_weight_grad = jnp.transpose(decay_sum, (4, 2, 1, 3, 0)).reshape(model_width, -1)
    taps_sum = taps_sum.reshape(chips, 2, tap_count, 3, heads, head_size)
    taps_sum = jnp.transpose(taps_sum, (2, 3, 1, 4, 0, 5))
    param_sum = param_sum[:, :, :heads].reshape(chips, 2, 2, heads)
    param_sum = jnp.transpose(param_sum, (2, 1, 3, 0)).reshape(2, head_count)
    return (
        result.reshape(inputs.shape),
        inputs_grad.reshape(inputs.shape),
        first_gain_grad,
        input_share,
        decay_weight_grad,
        taps_sum.reshape(tap_count, 3 * key_width),
        param_sum[0],
        param_sum[1],
        gain_grad,
        output_share,
        second_gain_grad,
        gate_up_share,
        down_share,
    )


def solution(mesh):
    in_specs = (
        P(None, "dp", "seq", None),
        P(None, "dp"),
        P(),
        P(("dp", "seq"), None),
        P(),
        P(),
        P(),
        P(),
        P(),
        P(("dp", "seq"), None),
        P(),
        P(("dp", "seq"), None),
        P(("dp", "seq"), None),
        P(None, "dp", "seq", None),
    )
    out_specs = (
        P(None, "dp", "seq", None),
        P(None, "dp", "seq", None),
        P(),
        P(("dp", "seq"), None),
        P(),
        P(),
        P(),
        P(),
        P(),
        P(("dp", "seq"), None),
        P(),
        P(("dp", "seq"), None),
        P(("dp", "seq"), None),
    )
    ring = mesh.shape["seq"]

    def whole_device(*arrays):
        heads_divide = ring == 8 and 2 * arrays[6].shape[0] == ring * mesh.shape["dp"]
        return (split_heads_device if heads_divide else per_device)(*arrays)

    return jax.shard_map(
        whole_device, mesh=mesh, in_specs=in_specs, out_specs=out_specs, check_vma=False
    )
```

```python
import functools

import jax
import jax.numpy as jnp
from jax import lax
from jax.experimental import pallas as pl
from jax.experimental.pallas import tpu as pltpu
from jax.sharding import PartitionSpec as P

SPAN = 64
VMEM_LIMIT = 56 * 1024 * 1024


HIGH = lax.Precision.HIGHEST


def shifted(value, axis, steps):
    count = lax.axis_size(axis)
    initial, last = (max(0, -steps), min(count, count - steps))
    return lax.ppermute(value, axis, [(source, source + steps) for source in range(initial, last)])


def rms_norm(values, gain):
    return values * lax.rsqrt(jnp.mean(values * values, -1, keepdims=True) + 1e-05) * gain


def unit_norm(vectors):
    return vectors * lax.rsqrt(jnp.sum(vectors * vectors, -1, keepdims=True) + 1e-06)


def swish_product(gate_part, up_part):
    return jax.nn.silu(gate_part) * up_part


def unit_inverse(strict_lower):
    extent = strict_lower.shape[-1]
    identity_matrix = jnp.eye(extent, dtype=jnp.float32)
    inverse = identity_matrix - strict_lower
    power_term = strict_lower
    for level_index in range(1, (extent - 1).bit_length()):
        power_term = jnp.einsum("bhij,bhjk->bhik", power_term, power_term, precision=HIGH)
        inverse = jnp.einsum(
            "bhij,bhjk->bhik", inverse, identity_matrix + power_term, precision=HIGH
        )
    return inverse


def span_step(memory, pieces):
    queries, probes, writes, decays, strengths = pieces
    extent = decays.shape[-1]
    running = jnp.cumsum(decays, axis=-1)
    spread = running[..., :, None] - running[..., None, :]
    row_index = lax.broadcasted_iota(jnp.int32, (extent, extent), 0)
    col_index = lax.broadcasted_iota(jnp.int32, (extent, extent), 1)
    faded = jnp.exp(jnp.minimum(spread, 0.0))
    inclusive = jnp.where(col_index <= row_index, faded, 0.0) * strengths[..., None, :]
    strict_mask = jnp.where(col_index < row_index, faded, 0.0) * strengths[..., None, :]
    strict_lower = strict_mask * jnp.einsum("bhtd,bhsd->bhts", probes, probes, precision=HIGH)
    scale_in = jnp.exp(running)[..., None]
    target = writes - scale_in * jnp.einsum("bhtd,bhde->bhte", probes, memory, precision=HIGH)
    fresh_values = jnp.einsum("bhts,bhse->bhte", unit_inverse(strict_lower), target, precision=HIGH)
    mixing = inclusive * jnp.einsum("bhtd,bhsd->bhts", queries, probes, precision=HIGH)
    outputs = scale_in * jnp.einsum("bhtd,bhde->bhte", queries, memory, precision=HIGH)
    outputs = outputs + jnp.einsum("bhts,bhse->bhte", mixing, fresh_values, precision=HIGH)
    remaining = jnp.exp(running[..., -1:] - running) * strengths
    memory = jnp.exp(running[..., -1])[..., None, None] * memory + jnp.einsum(
        "bhsd,bhse->bhde", probes * remaining[..., None], fresh_values, precision=HIGH
    )
    return (memory, outputs)


def delta_local(queries, probes, writes, decays, strengths, memory):
    seq_count, head_count, length, head_size = queries.shape
    blocks = length // SPAN

    def arrange(tensor):
        shaped = tensor.reshape(tensor.shape[:2] + (blocks, SPAN) + tensor.shape[3:])
        return jnp.moveaxis(shaped, 2, 0)

    pieces = (
        arrange(queries),
        arrange(probes),
        arrange(writes),
        arrange(decays),
        arrange(strengths),
    )
    memory, outputs = lax.scan(span_step, memory, pieces)
    outputs = jnp.moveaxis(outputs, 0, 2)
    return (outputs.reshape(seq_count, head_count, length, outputs.shape[-1]), memory)


def prepare(packed, logits, conv_weight, decay_log, decay_bias):
    seq_count, length, logit_width = logits.shape
    head_count = decay_log.shape[0]
    tap_count = conv_weight.shape[0]
    convolved = conv_weight[0] * packed[:, 0:length]
    for tap_index in range(1, tap_count):
        convolved = convolved + conv_weight[tap_index] * packed[:, tap_index : tap_index + length]
    active = jax.nn.silu(convolved)
    key_width = active.shape[-1] // 3
    head_size = key_width // head_count

    def split_heads(portion):
        return jnp.transpose(
            portion.reshape(seq_count, length, head_count, head_size), (0, 2, 1, 3)
        )

    queries = unit_norm(split_heads(active[..., :key_width])) * head_size ** (-0.5)
    probes = unit_norm(split_heads(active[..., key_width : 2 * key_width]))
    writes = split_heads(active[..., 2 * key_width :])
    decays = jnp.transpose(
        -jnp.exp(decay_log) * jax.nn.softplus(logits[..., :head_count] + decay_bias), (0, 2, 1)
    )
    strengths = jnp.transpose(jax.nn.sigmoid(logits[..., head_count:]), (0, 2, 1))
    return (queries, probes, writes, decays, strengths)


def mixer_core(packed, logits, conv_weight, decay_log, decay_bias, memory):
    queries, probes, writes, decays, strengths = prepare(
        packed, logits, conv_weight, decay_log, decay_bias
    )
    return delta_local(queries, probes, writes, decays, strengths, memory)


def finish(mixer_out, gate_raw, head_gain):
    seq_count, head_count, length, head_size = mixer_out.shape
    normal_out = rms_norm(mixer_out, head_gain)
    flat_rows = jnp.transpose(normal_out, (0, 2, 1, 3)).reshape(
        seq_count, length, head_count * head_size
    )
    return flat_rows * jax.nn.silu(gate_raw)


def carry_forward(transfer, offset):

    def turn_step(step_index, incoming):
        leaving = jnp.einsum("bhij,bhjk->bhik", transfer, incoming, precision=HIGH) + offset
        return shifted(leaving.astype(jnp.bfloat16), "seq", 1).astype(leaving.dtype)

    return lax.fori_loop(0, lax.axis_size("seq") - 1, turn_step, jnp.zeros_like(offset))


def carry_back(transfer, source):
    flipped = jnp.swapaxes(transfer, 2, 3)

    def turn_step(step_index, incoming):
        leaving = jnp.einsum("bhij,bhjk->bhik", flipped, incoming, precision=HIGH) + source
        return shifted(leaving.astype(jnp.bfloat16), "seq", -1).astype(leaving.dtype)

    return lax.fori_loop(0, lax.axis_size("seq") - 1, turn_step, jnp.zeros_like(source))


def per_device(
    inputs,
    lengths,
    first_gain,
    input_weight,
    decay_weight,
    conv_weight,
    decay_log,
    decay_bias,
    head_gain,
    output_weight,
    second_gain,
    gate_up_weight,
    down_weight,
    cotangent,
):
    micro_count, seq_local, length, model_width = inputs.shape
    seq_count = micro_count * seq_local
    row_count = seq_count * length
    head_count = decay_log.shape[0]
    key_width = input_weight.shape[1] // 4
    head_size = key_width // head_count
    tap_count = conv_weight.shape[0]
    tokens = inputs.reshape(row_count, model_width).astype(jnp.float32)
    positions = lax.axis_index("seq") * length + lax.broadcasted_iota(
        jnp.int32, (micro_count, seq_local, length), 2
    )
    valid_rows = (positions < lengths[:, :, None]).astype(jnp.float32).reshape(row_count, 1)
    in_full, out_full, gate_up_full, down_full = (
        lax.all_gather(input_weight, ("dp", "seq"), axis=0, tiled=True),
        lax.all_gather(output_weight, ("dp", "seq"), axis=0, tiled=True),
        lax.all_gather(gate_up_weight, ("dp", "seq"), axis=0, tiled=True),
        lax.all_gather(down_weight, ("dp", "seq"), axis=0, tiled=True),
    )
    normed, first_pullback = jax.vjp(rms_norm, tokens, first_gain)
    normed_low = normed.astype(jnp.bfloat16)
    projected = jnp.dot(normed_low, in_full, preferred_element_type=jnp.float32)
    mixed_low = (
        projected[:, : 3 * key_width].astype(jnp.bfloat16).reshape(seq_count, length, 3 * key_width)
    )
    gate_raw = projected[:, 3 * key_width :].reshape(seq_count, length, key_width)
    logits = jnp.dot(normed_low, decay_weight, preferred_element_type=jnp.float32).reshape(
        seq_count, length, 2 * head_count
    )
    left_edge = shifted(mixed_low[:, length - tap_count + 1 :], "seq", 1)
    packed = jnp.concatenate([left_edge, mixed_low], 1).astype(jnp.float32)
    queries, probes, writes, decays, strengths = prepare(
        packed, logits, conv_weight, decay_log, decay_bias
    )
    blank_state = jnp.zeros((seq_count, head_count, head_size, head_size), jnp.float32)
    identity_maps = jnp.broadcast_to(jnp.eye(head_size, dtype=jnp.float32), blank_state.shape)
    joined_writes = jnp.concatenate([writes, jnp.zeros_like(writes)], -1)
    joined_outputs, joined_end = delta_local(
        queries,
        probes,
        joined_writes,
        decays,
        strengths,
        jnp.concatenate([blank_state, identity_maps], -1),
    )
    own_out = joined_outputs[..., :head_size]
    carry_out = joined_outputs[..., head_size:]
    offset = joined_end[..., :head_size]
    transfer = joined_end[..., head_size:]
    state_in = carry_forward(transfer, offset)
    mixer_out = own_out + jnp.einsum("bhtd,bhde->bhte", carry_out, state_in, precision=HIGH)
    gated_rows, finish_pullback = jax.vjp(finish, mixer_out, gate_raw, head_gain)
    gated_low = gated_rows.reshape(row_count, key_width).astype(jnp.bfloat16)
    hidden = tokens + jnp.dot(gated_low, out_full, preferred_element_type=jnp.float32)
    second, second_pullback = jax.vjp(rms_norm, hidden, second_gain)
    second_low = second.astype(jnp.bfloat16)
    gate_up = jnp.dot(second_low, gate_up_full, preferred_element_type=jnp.float32)
    ffn_width = gate_up.shape[1] // 2
    activated, swish_pullback = jax.vjp(
        swish_product, gate_up[:, :ffn_width], gate_up[:, ffn_width:]
    )
    activated_low = activated.astype(jnp.bfloat16)
    final_rows = hidden + jnp.dot(activated_low, down_full, preferred_element_type=jnp.float32)
    result = valid_rows * final_rows
    upstream = valid_rows * cotangent.reshape(row_count, model_width).astype(jnp.float32)
    out_err = upstream.astype(jnp.bfloat16)
    down_term = jnp.einsum("nf,nd->fd", activated_low, out_err, preferred_element_type=jnp.float32)
    activated_grad = jnp.einsum("nd,fd->nf", out_err, down_full, preferred_element_type=jnp.float32)
    gate_grad, up_grad = swish_pullback(activated_grad)
    gate_up_err = jnp.concatenate([gate_grad, up_grad], 1).astype(jnp.bfloat16)
    gate_up_term = jnp.einsum(
        "nd,nf->df", second_low, gate_up_err, preferred_element_type=jnp.float32
    )
    second_grad = jnp.einsum(
        "nf,df->nd", gate_up_err, gate_up_full, preferred_element_type=jnp.float32
    )
    hidden_part, second_gain_grad = second_pullback(second_grad)
    hidden_grad = upstream + hidden_part
    gate_up_share, down_share = (
        scatter_rows(gate_up_term.astype(BF16), ("dp", "seq")).astype(F32),
        scatter_rows(down_term.astype(BF16), ("dp", "seq")).astype(F32),
    )
    branch_err = hidden_grad.astype(jnp.bfloat16)
    output_term = jnp.einsum("nk,nd->kd", gated_low, branch_err, preferred_element_type=jnp.float32)
    gated_grad = jnp.einsum("nd,kd->nk", branch_err, out_full, preferred_element_type=jnp.float32)
    mixer_grad, gate_raw_grad, head_gain_grad = finish_pullback(
        gated_grad.reshape(seq_count, length, key_width)
    )
    source = jnp.einsum("bhtd,bhte->bhde", carry_out, mixer_grad, precision=HIGH)
    state_out_grad = carry_back(transfer, source)
    _, core_pullback = jax.vjp(
        mixer_core, packed, logits, conv_weight, decay_log, decay_bias, state_in
    )
    packed_grad, logits_grad, conv_grad, decay_log_grad, decay_bias_grad, _ = core_pullback(
        (mixer_grad, state_out_grad)
    )
    edge_grad = shifted(packed_grad[:, : tap_count - 1].astype(jnp.bfloat16), "seq", -1).astype(
        jnp.float32
    )
    mixed_grad = packed_grad[:, tap_count - 1 :] + jnp.pad(
        edge_grad, ((0, 0), (length - tap_count + 1, 0), (0, 0))
    )
    in_err = jnp.concatenate(
        [mixed_grad.reshape(row_count, 3 * key_width), gate_raw_grad.reshape(row_count, key_width)],
        1,
    ).astype(jnp.bfloat16)
    input_term = jnp.einsum("nd,nk->dk", normed_low, in_err, preferred_element_type=jnp.float32)
    logits_flat = logits_grad.reshape(row_count, 2 * head_count)
    decay_weight_grad = jnp.einsum(
        "nd,nk->dk", normed_low.astype(jnp.float32), logits_flat, precision=HIGH
    )
    normed_grad = jnp.einsum("nk,dk->nd", in_err, in_full, preferred_element_type=jnp.float32)
    normed_grad = normed_grad + jnp.einsum(
        "nk,dk->nd", logits_flat, decay_weight.astype(jnp.float32), precision=HIGH
    )
    token_part, first_gain_grad = first_pullback(normed_grad)
    inputs_grad = hidden_grad + token_part
    input_share, output_share = (
        scatter_rows(input_term.astype(BF16), ("dp", "seq")).astype(F32),
        scatter_rows(output_term.astype(BF16), ("dp", "seq")).astype(F32),
    )
    small_sums = lax.psum(
        (
            first_gain_grad,
            decay_weight_grad,
            conv_grad,
            decay_log_grad,
            decay_bias_grad,
            head_gain_grad,
            second_gain_grad,
        ),
        ("dp", "seq"),
    )
    return (
        result.reshape(inputs.shape),
        inputs_grad.reshape(inputs.shape),
        small_sums[0],
        input_share,
        small_sums[1],
        small_sums[2],
        small_sums[3],
        small_sums[4],
        small_sums[5],
        output_share,
        small_sums[6],
        gate_up_share,
        down_share,
    )


F32 = jnp.float32
BF16 = jnp.bfloat16


def lasting(microseconds):
    return pl.CostEstimate(flops=0, bytes_accessed=int(microseconds * 3.5e6), transcendentals=0)


def parts(value):
    top = value.astype(BF16)
    return (top, (value - top.astype(F32)).astype(BF16))


def contract(left, right, right_dim):
    lhs = jnp.concatenate([left[0], left[1], left[0]], 1)
    rhs = jnp.concatenate([right[0], right[0], right[1]], right_dim)
    return lax.dot_general(lhs, rhs, (((1,), (right_dim,)), ((), ())), preferred_element_type=F32)


def mm(left, right):
    return contract(left, right, 0)


def mm_nt(left, right):
    return contract(left, right, 1)


def ones_dot(ones, value):
    first = value.astype(BF16)
    rest = value - first.astype(F32)
    second = rest.astype(BF16)
    third = (rest - second.astype(F32)).astype(BF16)
    return (
        jnp.dot(ones, first, preferred_element_type=F32)
        + jnp.dot(ones, second, preferred_element_type=F32)
        + jnp.dot(ones, third, preferred_element_type=F32)
    )


def lower_inverses(strict_lowers, row_index, col_index):
    extent = row_index.shape[0]

    def below(width):
        same = (row_index // (2 * width)) == (col_index // (2 * width))
        return same & ((row_index // width) % 2 == 1) & ((col_index // width) % 2 == 0)

    mask = below(1)
    identity = jnp.where(row_index == col_index, 1.0, 0.0)
    inverses = [identity - jnp.where(mask, strict, 0.0) for strict in strict_lowers]
    width = 2
    while width < extent:
        mask = below(width)
        splits = [parts(inverse) for inverse in inverses]
        blocks = [parts(jnp.where(mask, strict, 0.0)) for strict in strict_lowers]
        halves = [mm(split, block) for split, block in zip(splits, blocks)]
        inverses = [
            inverse - mm(parts(half), split)
            for inverse, half, split in zip(inverses, halves, splits)
        ]
        width *= 2
    return inverses


def active_rows(before, rows, taps):
    extended = jnp.concatenate([before, rows], 0)
    count = rows.shape[0]
    tap_count = taps.shape[0]
    start = before.shape[0] - tap_count + 1
    shifts = [extended[start + j : start + j + count] for j in range(tap_count)]
    total = taps[0:1] * shifts[0]
    for j in range(1, tap_count):
        total = total + taps[j : j + 1] * shifts[j]
    return (total, shifts)


def soft_plus(value):
    return jnp.maximum(value, 0.0) + jnp.log(1.0 + jnp.exp(-jnp.abs(value)))


def sigmoid(value):
    return 1.0 / (1.0 + jnp.exp(-value))


def unit(vectors):
    scale = lax.rsqrt(jnp.sum(vectors * vectors, -1, keepdims=True) + 1e-06)
    return (vectors * scale, scale)


def unit_back(vectors, scale, grad):
    inner = jnp.sum(vectors * grad, -1, keepdims=True)
    return scale * grad - vectors * (scale * scale * scale * inner)


def decay_terms(logit, param_ref, heads, ones):
    shifted_logit = logit + param_ref[1:2, :]
    lane = lax.broadcasted_iota(jnp.int32, logit.shape, 1)
    decays = jnp.where(lane < heads, -jnp.exp(param_ref[0:1, :]) * soft_plus(shifted_logit), 0.0)
    strengths = sigmoid(logit)
    running = ones_dot(ones, decays)
    return (shifted_logit, decays, strengths, running)


def mixer_forward(
    mixed_ref,
    gate_ref,
    logit_ref,
    taps_ref,
    param_ref,
    gain_ref,
    own_ref,
    rows_ref,
    gated_ref,
    memory_ref,
    inverse_ref,
    fresh_ref,
    out_ref,
    all_ref,
    rows_out_ref,
    state_ref,
    halo_ref,
    send_sems,
    recv_sems,
    local_sems,
):
    seqs, span, _ = mixed_ref.shape
    heads, head_size = memory_ref.shape[1], memory_ref.shape[2]
    gather_in_steps(own_ref, all_ref, send_sems, recv_sems, local_sems.at[0])
    trade_in_steps(rows_ref, rows_out_ref, send_sems, recv_sems, local_sems, heads)

    @pl.when(pl.program_id(0) == 0)
    def _():
        state_ref[...] = jnp.zeros_like(state_ref)
        halo_ref[...] = jnp.zeros_like(halo_ref)

    row_index = lax.broadcasted_iota(jnp.int32, (span, span), 0)
    col_index = lax.broadcasted_iota(jnp.int32, (span, span), 1)
    ones = jnp.where(col_index <= row_index, 1.0, 0.0).astype(BF16)
    taps = taps_ref[...]
    width = heads * head_size
    pairs = [(m, h) for m in range(seqs) for h in range(heads)]
    active, decay_parts = [], []
    for m in range(seqs):
        rows = mixed_ref[m].astype(F32)
        convolved, _ = active_rows(halo_ref[m], rows, taps)
        halo_ref[m] = rows[span - 8 :]
        active.append(convolved * sigmoid(convolved))
        _, _, strengths, running = decay_terms(logit_ref[m], param_ref, heads, ones)
        decay_parts.append((strengths, running, jnp.transpose(strengths), jnp.transpose(running)))

    def columns(m, h, block):
        start = block * width + h * head_size
        return active[m][:, start : start + head_size]

    queries = [unit(columns(m, h, 0))[0] * head_size ** (-0.5) for m, h in pairs]
    probes = [unit(columns(m, h, 1))[0] for m, h in pairs]
    products = [
        mm_nt(parts(jnp.concatenate([query, probe], 0)), parts(probe))
        for query, probe in zip(queries, probes)
    ]
    stricts, mixings, scales, kepts, lasts = [], [], [], [], []
    for (m, h), probe, product in zip(pairs, probes, products):
        strengths, running, strength_rows, running_rows = decay_parts[m]
        run = running[:, h : h + 1]
        last = running[span - 1 : span, h : h + 1]
        weight_row = strength_rows[heads + h : heads + h + 1, :]
        weight_col = strengths[:, heads + h : heads + h + 1]
        faded = jnp.exp(jnp.minimum(run - running_rows[h : h + 1, :], 0.0)) * weight_row
        mixings.append(jnp.where(col_index <= row_index, faded * product[:span], 0.0))
        stricts.append(jnp.where(col_index < row_index, faded * product[span:], 0.0))
        scales.append(jnp.exp(run))
        kepts.append(jnp.transpose(jnp.exp(last - run) * weight_col * probe))
        lasts.append(jnp.exp(last))
    inverses = lower_inverses(stricts, row_index, col_index)
    boths = [
        mm(parts(inverse), parts(jnp.concatenate([columns(m, h, 2), scale * probe], 1)))
        for (m, h), inverse, scale, probe in zip(pairs, inverses, scales, probes)
    ]
    memories = [state_ref[m, h] for m, h in pairs]
    reads = [
        mm(parts(jnp.concatenate([both[:, head_size:], scale * query], 0)), parts(memory))
        for both, scale, query, memory in zip(boths, scales, queries, memories)
    ]
    freshes = [both[:, :head_size] - read[:span] for both, read in zip(boths, reads)]
    fresh_parts = [parts(fresh) for fresh in freshes]
    for (m, h), last, memory, kept, fresh in zip(pairs, lasts, memories, kepts, fresh_parts):
        state_ref[m, h] = last * memory + mm(parts(kept), fresh)
    outs = [
        read[span:] + mm(parts(mixing), fresh)
        for read, mixing, fresh in zip(reads, mixings, fresh_parts)
    ]
    for (m, h), memory, inverse, fresh, mixer_out in zip(pairs, memories, inverses, freshes, outs):
        own = slice(h * head_size, (h + 1) * head_size)
        memory_ref[m, h] = memory
        inverse_ref[m, h] = inverse
        fresh_ref[m, :, own] = fresh
        out_ref[m, :, own] = mixer_out
        scale = lax.rsqrt(jnp.mean(mixer_out * mixer_out, -1, keepdims=True) + 1e-05)
        gate = gate_ref[m, :, own]
        gated_ref[m, :, own] = (
            mixer_out * scale * gain_ref[...] * (gate * sigmoid(gate))
        ).astype(BF16)


def mixer_backward(
    mixed_ref,
    before_ref,
    gate_ref,
    logit_ref,
    taps_ref,
    param_ref,
    gain_ref,
    memory_ref,
    inverse_ref,
    fresh_ref,
    out_ref,
    grad_ref,
    part_ref,
    error_ref,
    logit_grad_ref,
    taps_grad_ref,
    param_grad_ref,
    gain_grad_ref,
    sum_ref,
    state_ref,
    halo_ref,
    *scatter_refs,
):
    seqs, span, _ = mixed_ref.shape
    heads, head_size = memory_ref.shape[1], memory_ref.shape[2]
    step = pl.program_id(0)
    scatter_in_steps(part_ref, sum_ref, *scatter_refs)

    @pl.when(step == 0)
    def _():
        state_ref[...] = jnp.zeros_like(state_ref)
        halo_ref[...] = jnp.zeros_like(halo_ref)
        taps_grad_ref[...] = jnp.zeros_like(taps_grad_ref)
        param_grad_ref[...] = jnp.zeros_like(param_grad_ref)
        gain_grad_ref[...] = jnp.zeros_like(gain_grad_ref)

    first = step == pl.num_programs(0) - 1
    row_index = lax.broadcasted_iota(jnp.int32, (span, span), 0)
    col_index = lax.broadcasted_iota(jnp.int32, (span, span), 1)
    ones = jnp.where(col_index <= row_index, 1.0, 0.0).astype(BF16)
    ones_back = jnp.where(col_index >= row_index, 1.0, 0.0).astype(BF16)
    taps = taps_ref[...]
    tap_count = taps.shape[0]
    width = heads * head_size
    gain = gain_ref[...]
    edge = before_ref.shape[1]
    pairs = [(m, h) for m in range(seqs) for h in range(heads)]
    everyone = range(len(pairs))
    active, openings, curves, shifts, decay_parts = [], [], [], [], []
    for m in range(seqs):
        rows = mixed_ref[m].astype(F32)
        before = jnp.where(first, 0.0, before_ref[m].astype(F32))[edge - 8 :]
        convolved, moved = active_rows(before, rows, taps)
        opening = sigmoid(convolved)
        active.append(convolved * opening)
        curves.append(convolved)
        openings.append(opening)
        shifts.append(moved)
        shifted_logit, decays, strengths, running = decay_terms(
            logit_ref[m], param_ref, heads, ones
        )
        decay_parts.append(
            (
                shifted_logit,
                decays,
                strengths,
                running,
                jnp.transpose(strengths),
                jnp.transpose(running),
            )
        )

    def columns(m, h, block):
        start = block * width + h * head_size
        return active[m][:, start : start + head_size]

    raw_queries = [columns(m, h, 0) for m, h in pairs]
    raw_probes = [columns(m, h, 1) for m, h in pairs]
    query_units = [unit(value) for value in raw_queries]
    probe_units = [unit(value) for value in raw_probes]
    queries = [value * head_size ** (-0.5) for value, _ in query_units]
    probes = [value for value, _ in probe_units]
    gate_grads, out_grads = [], []
    for m, h in pairs:
        own = slice(h * head_size, (h + 1) * head_size)
        mixer_out = out_ref[m, :, own]
        gate = gate_ref[m, :, own]
        gated_grad = grad_ref[m, :, own].astype(F32)
        scale = lax.rsqrt(jnp.mean(mixer_out * mixer_out, -1, keepdims=True) + 1e-05)
        gate_open = sigmoid(gate)
        normal = mixer_out * scale
        gate_grads.append(
            gated_grad * normal * gain * (gate_open * (1.0 + gate * (1.0 - gate_open)))
        )
        normal_grad = gated_grad * (gate * gate_open)
        gain_grad_ref[0:1, :] += jnp.sum(normal_grad * normal, 0, keepdims=True)
        weighted = normal_grad * gain
        out_grads.append(
            scale * (weighted - normal * jnp.mean(weighted * normal, -1, keepdims=True))
        )

    probe_parts = [parts(value) for value in probes]
    query_parts = [parts(value) for value in queries]
    out_grad_parts = [parts(value) for value in out_grads]
    state_grads = [state_ref[m, h] for m, h in pairs]
    state_grad_parts = [parts(value) for value in state_grads]
    products = [
        mm_nt(parts(jnp.concatenate([query, probe], 0)), probe_part)
        for query, probe, probe_part in zip(queries, probes, probe_parts)
    ]
    probe_states = [mm(left, right) for left, right in zip(probe_parts, state_grad_parts)]
    weight_rows, spreads, fade_queries, fade_probes = [], [], [], []
    scales, end_scales, remainings, kepts = [], [], [], []
    for (m, h), product in zip(pairs, products):
        _, _, strengths, running, strength_rows, running_rows = decay_parts[m]
        run = running[:, h : h + 1]
        last = running[span - 1 : span, h : h + 1]
        weight_row = strength_rows[heads + h : heads + h + 1, :]
        weight_rows.append(weight_row)
        faded = jnp.exp(jnp.minimum(run - running_rows[h : h + 1, :], 0.0))
        spreads.append(faded * weight_row)
        fade_queries.append(jnp.where(col_index <= row_index, faded * product[:span], 0.0))
        fade_probes.append(jnp.where(col_index < row_index, faded * product[span:], 0.0))
        scales.append(jnp.exp(run))
        end_scales.append(jnp.exp(last))
        remaining = jnp.exp(last - run)
        remainings.append(remaining)
        kepts.append(remaining * strengths[:, heads + h : heads + h + 1])
    fresh_grads = [
        mm(parts(jnp.transpose(fade * weight_row)), out_grad) + kept * probe_state
        for fade, weight_row, out_grad, kept, probe_state in zip(
            fade_queries, weight_rows, out_grad_parts, kepts, probe_states
        )
    ]
    solves = [
        mm(parts(jnp.transpose(inverse_ref[m, h])), parts(fresh_grad))
        for (m, h), fresh_grad in zip(pairs, fresh_grads)
    ]
    for k in everyone:
        m, h = pairs[k]
        state_ref[m, h] = (
            end_scales[k] * state_grads[k]
            + mm(parts(jnp.transpose(queries[k])), parts(scales[k] * out_grads[k]))
            - mm(parts(jnp.transpose(probes[k])), parts(scales[k] * solves[k]))
        )
    freshes = [fresh_ref[m, :, h * head_size : (h + 1) * head_size] for m, h in pairs]
    memories = [memory_ref[m, h] for m, h in pairs]
    fresh_parts = [parts(value) for value in freshes]
    joined = [
        parts(jnp.concatenate([out_grad, solved], 0)) for out_grad, solved in zip(out_grads, solves)
    ]
    outers = [mm_nt(both, fresh) for both, fresh in zip(joined, fresh_parts)]
    throughs = [mm_nt(both, parts(memory)) for both, memory in zip(joined, memories)]
    mixing_grads = [jnp.where(col_index <= row_index, outer[:span], 0.0) for outer in outers]
    strict_grads = [jnp.where(col_index < row_index, -outer[span:], 0.0) for outer in outers]
    mix_fades = [grad * spread for grad, spread in zip(mixing_grads, spreads)]
    strict_fades = [grad * spread for grad, spread in zip(strict_grads, spreads)]
    on_probes = [
        mm(parts(jnp.concatenate([mix, strict], 0)), probe)
        for mix, strict, probe in zip(mix_fades, strict_fades, probe_parts)
    ]
    fresh_states = [mm_nt(fresh, grad) for fresh, grad in zip(fresh_parts, state_grad_parts)]
    turned = [
        mm(parts(jnp.transpose(mix)), query) + mm(parts(jnp.transpose(strict)), probe)
        for mix, strict, query, probe in zip(mix_fades, strict_fades, query_parts, probe_parts)
    ]
    active_grads = [[None] * (3 * heads) for _ in range(seqs)]
    col_terms = [jnp.zeros((span, span), F32)] * seqs
    row_terms = [jnp.zeros((span, span), F32)] * seqs
    for k in everyone:
        m, h = pairs[k]
        out_state = scales[k] * throughs[k][:span]
        solved_state = scales[k] * throughs[k][span:]
        query_grad = out_state + on_probes[k][:span]
        probe_grad = kepts[k] * fresh_states[k] - solved_state + on_probes[k][span:] + turned[k]
        pair_terms = mixing_grads[k] * fade_queries[k] + strict_grads[k] * fade_probes[k]
        weighted_pairs = pair_terms * weight_rows[k]
        probe_fresh = jnp.sum(probe_states[k] * freshes[k], -1, keepdims=True)
        run_col = (
            jnp.sum(out_state * queries[k] - solved_state * probes[k], -1, keepdims=True)
            + jnp.sum(weighted_pairs, -1, keepdims=True)
            - kepts[k] * probe_fresh
        )
        last_grad = jnp.sum(kepts[k] * probe_fresh, 0, keepdims=True) + end_scales[k] * jnp.sum(
            jnp.sum(state_grads[k] * memories[k], -1, keepdims=True), 0, keepdims=True
        )
        run_col = run_col + jnp.where(row_index[:, 0:1] == span - 1, last_grad, 0.0)
        col_terms[m] = jnp.where(col_index == h, run_col, col_terms[m])
        col_terms[m] = jnp.where(
            col_index == heads + h, remainings[k] * probe_fresh, col_terms[m]
        )
        row_terms[m] = jnp.where(
            row_index == h, -jnp.sum(weighted_pairs, 0, keepdims=True), row_terms[m]
        )
        row_terms[m] = jnp.where(
            row_index == heads + h, jnp.sum(pair_terms, 0, keepdims=True), row_terms[m]
        )
        active_grads[m][h] = unit_back(
            raw_queries[k], query_units[k][1], query_grad
        ) * head_size ** (-0.5)
        active_grads[m][heads + h] = unit_back(raw_probes[k], probe_units[k][1], probe_grad)
        active_grads[m][2 * heads + h] = solves[k]

    for m in range(seqs):
        shifted_logit, decays, strengths = decay_parts[m][:3]
        terms = col_terms[m] + jnp.transpose(row_terms[m])
        decay_grad = ones_dot(ones_back, terms)
        shifted_grad = decay_grad * -jnp.exp(param_ref[0:1, :]) * sigmoid(shifted_logit)
        logit_grad = jnp.where(
            col_index < heads,
            shifted_grad,
            jnp.where(col_index < 2 * heads, terms * strengths * (1.0 - strengths), 0.0),
        )
        logit_top, logit_rest = parts(logit_grad)
        logit_grad_ref[m] = (
            logit_top.astype(F32) + pltpu.roll(logit_rest.astype(F32), span // 2, 1)
        ).astype(BF16)
        decay_lane = col_index[0:1] < heads
        param_grad_ref[0:1, :] += jnp.sum(
            jnp.where(decay_lane, decay_grad * decays, 0.0), 0, keepdims=True
        )
        param_grad_ref[1:2, :] += jnp.sum(
            jnp.where(decay_lane, shifted_grad, 0.0), 0, keepdims=True
        )
        conv_grad = jnp.concatenate(active_grads[m], 1) * (
            openings[m] * (1.0 + curves[m] * (1.0 - openings[m]))
        )
        extended = jnp.concatenate([conv_grad, halo_ref[m]], 0)
        halo_ref[m] = conv_grad[:8]
        mixed_grad = jnp.zeros_like(conv_grad)
        for j in range(tap_count):
            reach = tap_count - 1 - j
            mixed_grad = mixed_grad + taps[j : j + 1] * extended[reach : reach + span]
            taps_grad_ref[j : j + 1, :] += jnp.sum(conv_grad * shifts[m][j], 0, keepdims=True)
        error_ref[m] = jnp.concatenate(
            [mixed_grad] + gate_grads[m * heads : (m + 1) * heads], 1
        ).astype(BF16)


def run_forward(mixed, gate, logits, taps, params, gain, heads, own, out_rows, collective_id):
    steps, seqs, span, _ = mixed.shape
    anywhere = pl.BlockSpec(memory_space=pl.ANY)
    head_size = gain.shape[1]
    width = heads * head_size

    def rows(columns):
        return pl.BlockSpec((None, seqs, span, columns), lambda j: (j, 0, 0, 0))

    def squares():
        return pl.BlockSpec((None, seqs, heads, head_size, head_size), lambda j: (j, 0, 0, 0, 0))

    def whole(array):
        return pl.BlockSpec(array.shape, lambda j: (0, 0))

    square = jax.ShapeDtypeStruct((steps, seqs, heads, head_size, head_size), F32)
    lower = jax.ShapeDtypeStruct((steps, seqs, heads, span, span), F32)
    flat = jax.ShapeDtypeStruct((steps, seqs, span, width), F32)
    return pl.pallas_call(
        mixer_forward,
        grid=(steps,),
        in_specs=[
            rows(3 * width),
            rows(width),
            rows(logits.shape[-1]),
            whole(taps),
            whole(params),
            whole(gain),
            anywhere,
            anywhere,
        ],
        out_specs=[rows(width), squares(), squares(), rows(width), rows(width)] + [anywhere] * 2,
        out_shape=[
            jax.ShapeDtypeStruct((steps, seqs, span, width), BF16),
            square,
            lower,
            flat,
            flat,
            jax.ShapeDtypeStruct((steps,) + own.shape, own.dtype),
            jax.ShapeDtypeStruct(out_rows.shape, out_rows.dtype),
        ],
        scratch_shapes=[
            pltpu.VMEM((seqs, heads, head_size, head_size), F32),
            pltpu.VMEM((seqs, 8, 3 * width), F32),
            pltpu.SemaphoreType.DMA((9 + heads,)),
            pltpu.SemaphoreType.DMA((9 + heads,)),
            pltpu.SemaphoreType.DMA((1 + heads,)),
        ],
        compiler_params=pltpu.CompilerParams(
            collective_id=collective_id, has_side_effects=True, vmem_limit_bytes=VMEM_LIMIT
        ),
        cost_estimate=lasting(55),
        name="mixer_forward",
    )(mixed, gate, logits, taps, params, gain, own, out_rows)


def run_backward(
    mixed, gate, logits, taps, params, gain, memory, inverse, fresh, out, grad, part, collective_id
):
    steps, seqs, span, _ = mixed.shape
    _, part_rows, columns = part.shape
    heads, head_size = memory.shape[2], memory.shape[3]
    width = heads * head_size
    edge = 16

    def rows(columns):
        return pl.BlockSpec((None, seqs, span, columns), lambda j: (steps - 1 - j, 0, 0, 0))

    def squares():
        return pl.BlockSpec(
            (None, seqs, heads, head_size, head_size), lambda j: (steps - 1 - j, 0, 0, 0, 0)
        )

    def whole(shape):
        return pl.BlockSpec(shape, lambda j: (0, 0))

    before = pl.BlockSpec(
        (None, seqs, edge, 3 * width),
        lambda j: (jnp.maximum(steps - 2 - j, 0), 0, span // edge - 1, 0),
    )
    return pl.pallas_call(
        mixer_backward,
        grid=(steps,),
        in_specs=[
            rows(3 * width),
            before,
            rows(width),
            rows(logits.shape[-1]),
            whole(taps.shape),
            whole(params.shape),
            whole(gain.shape),
            squares(),
            squares(),
            rows(width),
            rows(width),
            rows(width),
            pl.BlockSpec(memory_space=pl.ANY),
        ],
        out_specs=[
            rows(4 * width),
            rows(logits.shape[-1]),
            whole((8, 3 * width)),
            whole((8, logits.shape[-1])),
            whole((8, head_size)),
            whole((part_rows, columns)),
        ],
        out_shape=[
            jax.ShapeDtypeStruct((steps, seqs, span, 4 * width), BF16),
            jax.ShapeDtypeStruct(logits.shape, BF16),
            jax.ShapeDtypeStruct((8, 3 * width), F32),
            jax.ShapeDtypeStruct((8, logits.shape[-1]), F32),
            jax.ShapeDtypeStruct((8, head_size), F32),
            jax.ShapeDtypeStruct((part_rows, columns), F32),
        ],
        scratch_shapes=[
            pltpu.VMEM((seqs, heads, head_size, head_size), F32),
            pltpu.VMEM((seqs, 8, 3 * width), F32),
            pltpu.VMEM((4, part_rows, columns), BF16),
            pltpu.VMEM((4, part_rows, columns), BF16),
            pltpu.VMEM((part_rows, columns), BF16),
            pltpu.VMEM((2, part_rows, columns), BF16),
            pltpu.SemaphoreType.DMA((10,)),
            pltpu.SemaphoreType.DMA((10,)),
            pltpu.SemaphoreType.DMA((4,)),
        ],
        compiler_params=pltpu.CompilerParams(
            collective_id=collective_id, has_side_effects=True, vmem_limit_bytes=VMEM_LIMIT
        ),
        cost_estimate=lasting(55),
        name="mixer_backward",
    )(mixed, mixed, gate, logits, taps, params, gain, memory, inverse, fresh, out, grad, part)


def gather_rows(value, axis):
    return lax.all_gather(value, axis, axis=0, tiled=True)


def scatter_rows(value, axis):
    return lax.psum_scatter(value, axis, scatter_dimension=0, tiled=True)


def plane_peers():
    me = lax.axis_index("seq")
    sibling = me + 1 - 2 * (me % 2)
    across = me + 2 - 4 * ((me // 2) % 2)
    along = me + 4 - 8 * (me // 4)
    return (me, sibling, across, along)


def greet(peers):
    barrier = pltpu.get_barrier_semaphore()
    for peer in peers:
        pl.semaphore_signal(
            barrier, inc=1, device_id={"seq": peer}, device_id_type=pl.DeviceIdType.MESH
        )
    pl.semaphore_wait(barrier, len(peers))


def send_to(peer, source, target, send_sem, recv_sem):
    return pltpu.make_async_remote_copy(
        src_ref=source,
        dst_ref=target,
        send_sem=send_sem,
        recv_sem=recv_sem,
        device_id={"seq": peer},
        device_id_type=pl.DeviceIdType.MESH,
    )


def gather_phases(own_ref, all_ref, send_sems, recv_sems, local_sem, start):
    me, sibling, across, along = plane_peers()
    far = along + across - me
    half = own_ref.shape[0] // 2
    upper, lower = pl.ds(0, half), pl.ds(half, half)
    copies = []

    def send(peer, source, target):
        k = start + len(copies)
        copy = send_to(peer, source, target, send_sems.at[k], recv_sems.at[k])
        copy.start()
        copies.append(copy)

    keep = pltpu.make_async_copy(own_ref, all_ref.at[me], local_sem)
    keep.start()
    send(across, own_ref, all_ref.at[me])
    send(along, own_ref, all_ref.at[me])
    send(sibling, own_ref, all_ref.at[me])
    yield
    copies[0].wait_recv()
    send(along, all_ref.at[across, upper], all_ref.at[across, upper])
    copies[1].wait_recv()
    send(across, all_ref.at[along, lower], all_ref.at[along, lower])
    send(sibling, all_ref.at[across], all_ref.at[across])
    send(sibling, all_ref.at[along], all_ref.at[along])
    yield
    copies[3].wait_recv()
    send(sibling, all_ref.at[far, upper], all_ref.at[far, upper])
    copies[4].wait_recv()
    send(sibling, all_ref.at[far, lower], all_ref.at[far, lower])
    yield
    for k in (2, 5, 6, 7, 8):
        copies[k].wait_recv()
    for copy in copies:
        copy.wait_send()
    keep.wait()
    yield


def chain_hops(all_ref, half, up_send, up_recv, down_send, down_recv):
    depth = all_ref.shape[0]
    columns = all_ref.shape[2] // 2
    own = pl.ds(half * columns, columns)
    place = lax.axis_index("dp")
    above, below = lax.rem(place + 1, depth), lax.rem(place + depth - 1, depth)

    def hop(slot, peer, send_sem, recv_sem):
        return pltpu.make_async_remote_copy(
            src_ref=all_ref.at[slot, :, own],
            dst_ref=all_ref.at[slot, :, own],
            send_sem=send_sem,
            recv_sem=recv_sem,
            device_id={"dp": peer},
            device_id_type=pl.DeviceIdType.MESH,
        )

    hops = []
    for t in range(depth - 1):
        spot = half * (depth - 1) + t
        up_slot, down_slot = lax.rem(place + depth - t, depth), lax.rem(place + t, depth)
        up = hop(up_slot, above, up_send.at[spot], up_recv.at[spot])
        down = hop(down_slot, below, down_send.at[spot], down_recv.at[spot])
        below_slot, above_slot = place + depth - 1 - t, place + 1 + t
        hops.append(
            (
                (up, (place < depth - 1) & (place >= t), place > t, lax.rem(below_slot, depth)),
                (
                    down,
                    (place > 0) & (place + t < depth),
                    above_slot < depth,
                    lax.rem(above_slot, depth),
                ),
            )
        )
    return hops


def hop_start(hop):
    for copy, leaves, _, _ in hop:
        pl.when(leaves)(copy.start)


def hop_arrive(hop):
    for copy, _, arrives, _ in hop:
        pl.when(arrives)(copy.wait_recv)


def hop_finish(hops):
    for hop in hops:
        for copy, leaves, _, _ in hop:
            pl.when(leaves)(copy.wait_send)


def greet_all(ring, depth):
    me, place = lax.axis_index("seq"), lax.axis_index("dp")
    barrier = pltpu.get_barrier_semaphore()
    peers = [{"seq": lax.rem(me + k, ring)} for k in range(1, ring)]
    peers += [{"dp": lax.rem(place + k, depth)} for k in range(1, depth)]
    for peer in peers:
        pl.semaphore_signal(barrier, inc=1, device_id=peer, device_id_type=pl.DeviceIdType.MESH)
    pl.semaphore_wait(barrier, len(peers))


def spread_units(piece, target_ref, depth):
    ring, _, columns = piece.shape
    own = columns // (2 * depth)
    for k in range(2 * depth):
        block = jnp.concatenate([piece[s, :, k * own : (k + 1) * own] for s in range(ring)], 1)
        target_ref[:, k * ring * own : (k + 1) * ring * own] = block.astype(target_ref.dtype)


def exchange_copies(cut_ref, land, send_sems, recv_sems, start):
    ring = cut_ref.shape[0]
    me = lax.axis_index("seq")
    copies = []
    for k in range(1, ring):
        peer = lax.rem(me + k, ring)
        copy = send_to(
            peer, cut_ref.at[peer], land, send_sems.at[start + k - 1], recv_sems.at[start + k - 1]
        )
        copy.start()
        copies.append(copy)
    return copies


def rank_head(rank, j, heads):
    return rank // 2 + lax.axis_size("seq") // 2 * (heads * (rank % 2) + j)


def plane_open_kernel(
    heads,
    first_ref,
    weight_hbm,
    pair_hbm,
    lanes_hbm,
    first_all_hbm,
    weight_all_hbm,
    pair_all_ref,
    mixed_ref,
    gate_ref,
    logit_ref,
    first_all_ref,
    weight_all_ref,
    pair_ref,
    cut_ref,
    lanes_ref,
    total_ref,
    send_sems,
    recv_sems,
    local_sems,
    *chain_sems,
):
    place, me = lax.axis_index("dp"), lax.axis_index("seq")
    depth, rows = weight_all_ref.shape[0], weight_hbm.shape[0]
    ring, units = cut_ref.shape[0], cut_ref.shape[2] // 2
    width = weight_all_ref.shape[2] // 4
    load = pltpu.make_async_copy(pair_hbm, pair_ref, local_sems.at[0])
    load.start()
    lanes_load = pltpu.make_async_copy(lanes_hbm, lanes_ref, local_sems.at[3])
    lanes_load.start()
    greet_all(ring, depth)
    keeps, early = [], []
    own_rows = pl.ds(pl.multiple_of(me * rows, rows), rows)
    size = width // heads
    for part in range(4 * heads):
        block, j = part // heads, part % heads
        target = weight_all_ref.at[place, own_rows, pl.ds(part * size, size)]

        def source(peer, block=block, j=j):
            start = (block * ring * heads + rank_head(peer, j, heads)) * size
            return weight_hbm.at[:, pl.ds(pl.multiple_of(start, size), size)]

        keep = pltpu.make_async_copy(source(me), target, local_sems.at[4 + part])
        keep.start()
        keeps.append(keep)
        for k in range(1, ring):
            peer = lax.rem(me + k, ring)
            spot = part * (ring - 1) + k - 1
            copy = send_to(peer, source(peer), target, send_sems.at[spot], recv_sems.at[spot])
            copy.start()
            early.append(copy)
    base = 4 * heads * (ring - 1)
    chains = [chain_hops(weight_all_ref, g, *chain_sems) for g in range(2)]
    for g, chain in enumerate(chains):
        for copy in early[g * base // 2 : (g + 1) * base // 2]:
            copy.wait_recv()
        for keep in keeps[2 * g * heads : 2 * (g + 1) * heads]:
            keep.wait()
        hop_start(chain[0])
    first = gather_phases(first_ref, first_all_ref, send_sems, recv_sems, local_sems.at[1], base)
    next(first)
    load.wait()
    own = units // depth
    half = pair_ref.shape[1] // 2
    for s in range(ring):
        pieces = []
        for g in range(2):
            for z in range(depth):
                start = g * half + (z * ring + s) * own
                pieces.append(pair_ref[:, start : start + own])
        cut_ref[s] = jnp.concatenate(pieces, 1)
    pair_keep = pltpu.make_async_copy(cut_ref.at[me], pair_all_ref.at[me], local_sems.at[2])
    pair_keep.start()
    later = exchange_copies(cut_ref, pair_all_ref.at[me], send_sems, recv_sems, base + 9)
    for t in range(depth - 2):
        for chain in chains:
            hop_arrive(chain[t])
            hop_start(chain[t + 1])
        if t == 0:
            next(first)
    next(first)
    next(first)
    lanes_load.wait()
    deep = weight_all_ref.shape[1]

    def spread_slot(slot, fresh=False):
        def run():
            at = pl.ds(pl.multiple_of(slot * deep, deep), deep)

            @pl.loop(0, ring)
            def _(r):
                term = low_dot(first_all_ref[r, :, at], weight_all_ref[slot], NN)
                total_ref[r] = term if fresh else total_ref[r] + term

        return run

    @pl.loop(0, ring)
    def _(r):
        logit_ref[r] = low_dot(first_all_ref[r], lanes_ref[...], NN)

    saves = [pltpu.make_async_copy(first_all_ref, first_all_hbm, local_sems.at[0])]
    saves[0].start()
    spread_slot(place, True)()
    for hop in chains[0][:-1]:
        for _, _, arrives, slot in hop:
            pl.when(arrives)(spread_slot(slot))
    def close(g, slot=None):
        def run():
            columns = slice(2 * g * width, 2 * (g + 1) * width)

            @pl.loop(0, ring)
            def _(r):
                total = total_ref[r, :, columns]
                if slot is not None:
                    at = pl.ds(pl.multiple_of(slot * deep, deep), deep)
                    total = total + low_dot(
                        first_all_ref[r, :, at], weight_all_ref[slot, :, columns], NN
                    )
                if g == 0:
                    mixed_ref[r, :, : 2 * width] = total.astype(BF16)
                else:
                    mixed_ref[r, :, 2 * width :] = total[:, :width].astype(BF16)
                    gate_ref[r] = total[:, width:]

        return run

    for g, chain in enumerate(chains):
        hop_arrive(chain[-1])
        if g == len(chains) - 1:
            saves.append(pltpu.make_async_copy(weight_all_ref, weight_all_hbm, local_sems.at[1]))
            saves[1].start()
        (_, _, from_below, low_slot), (_, _, from_above, high_slot) = chain[-1]
        pl.when(from_below)(close(g, low_slot))
        pl.when(from_above)(close(g, high_slot))
        pl.when(jnp.logical_not(from_below | from_above))(close(g))

    for copy in later:
        copy.wait_recv()
    for chain in chains:
        hop_finish(chain)
    for copy in early + later:
        copy.wait_send()
    pair_keep.wait()
    for save in saves:
        save.wait()


def plane_open(first, weight, pair, lanes, heads, collective_id):
    ring, depth = lax.axis_size("seq"), lax.axis_size("dp")
    rows, columns = first.shape
    weight_rows = weight.shape[0]
    width = weight.shape[1] // (4 * ring)
    total = (4 * heads + 1) * (ring - 1) + 9
    cut = jax.ShapeDtypeStruct((ring, weight_rows, pair.shape[1] // ring), pair.dtype)
    first_shape, weight_shape = (ring, rows, columns), (depth, ring * weight_rows, 4 * width)
    vmem, anywhere = pl.BlockSpec(memory_space=pltpu.VMEM), pl.BlockSpec(memory_space=pl.ANY)
    return pl.pallas_call(
        functools.partial(plane_open_kernel, heads),
        out_shape=[
            jax.ShapeDtypeStruct(first_shape, BF16),
            jax.ShapeDtypeStruct(weight_shape, BF16),
            cut,
            jax.ShapeDtypeStruct((ring, rows, 3 * width), BF16),
            jax.ShapeDtypeStruct((ring, rows, width), F32),
            jax.ShapeDtypeStruct((ring, rows, lanes.shape[1]), F32),
        ],
        in_specs=[anywhere] * 4,
        out_specs=[anywhere] * 3 + [vmem] * 3,
        scratch_shapes=[
            pltpu.VMEM(first_shape, BF16),
            pltpu.VMEM(weight_shape, BF16),
            pltpu.VMEM(pair.shape, BF16),
            pltpu.VMEM(cut.shape, BF16),
            pltpu.VMEM(lanes.shape, BF16),
            pltpu.VMEM((ring, rows, 4 * width), F32),
            pltpu.SemaphoreType.DMA((total,)),
            pltpu.SemaphoreType.DMA((total,)),
            pltpu.SemaphoreType.DMA((4 + 4 * heads,)),
        ]
        + [pltpu.SemaphoreType.DMA((2 * (depth - 1),))] * 4,
        compiler_params=pltpu.CompilerParams(
            collective_id=collective_id, has_side_effects=True, vmem_limit_bytes=VMEM_LIMIT
        ),
        cost_estimate=lasting(150),
        name="plane_open",
    )(first, weight, pair, lanes)


def trade_in_steps(rows_ref, rows_out_ref, send_sems, recv_sems, local_sems, heads):
    me = lax.axis_index("seq")
    core = lax.rem(me, 2)
    sibling = me + 1 - 2 * core
    rows = rows_out_ref.shape[0] // (2 * heads)

    def rows_of(ref, spot):
        return ref.at[pl.ds(pl.multiple_of(spot * rows, rows), rows)]

    copies, keeps = [], []
    for j in range(heads):
        target = rows_of(rows_out_ref, 2 * j + core)
        theirs = rows_of(rows_ref, heads * (1 - core) + j)
        copies.append(send_to(sibling, theirs, target, send_sems.at[9 + j], recv_sems.at[9 + j]))
        keeps.append(
            pltpu.make_async_copy(rows_of(rows_ref, heads * core + j), target, local_sems.at[1 + j])
        )
    step, steps = pl.program_id(0), pl.num_programs(0)

    @pl.when(step == 0)
    def _():
        for copy in copies + keeps:
            copy.start()

    @pl.when(step == steps - 1)
    def _():
        for copy in copies:
            copy.wait_recv()
            copy.wait_send()
        for keep in keeps:
            keep.wait()


def gather_in_steps(own_ref, all_ref, send_sems, recv_sems, local_sem):
    me, sibling, across, along = plane_peers()
    far = along + across - me
    half = own_ref.shape[0] // 2
    upper, lower = pl.ds(0, half), pl.ds(half, half)
    keep = pltpu.make_async_copy(own_ref, all_ref.at[me], local_sem)
    plan = [
        (across, own_ref, all_ref.at[me]),
        (along, own_ref, all_ref.at[me]),
        (sibling, own_ref, all_ref.at[me]),
        (along, all_ref.at[across, upper], all_ref.at[across, upper]),
        (across, all_ref.at[along, lower], all_ref.at[along, lower]),
        (sibling, all_ref.at[across], all_ref.at[across]),
        (sibling, all_ref.at[along], all_ref.at[along]),
        (sibling, all_ref.at[far, upper], all_ref.at[far, upper]),
        (sibling, all_ref.at[far, lower], all_ref.at[far, lower]),
    ]
    copies = [
        send_to(peer, source, target, send_sems.at[k], recv_sems.at[k])
        for k, (peer, source, target) in enumerate(plan)
    ]
    step, steps = pl.program_id(0), pl.num_programs(0)

    @pl.when(step == 0)
    def _():
        greet((sibling, across, along))
        keep.start()
        for k in (0, 1, 2):
            copies[k].start()

    @pl.when(step == 3)
    def _():
        copies[0].wait_recv()
        copies[1].wait_recv()
        for k in (3, 4, 5, 6):
            copies[k].start()

    @pl.when(step == 5)
    def _():
        copies[3].wait_recv()
        copies[4].wait_recv()
        for k in (7, 8):
            copies[k].start()

    @pl.when(step == steps - 1)
    def _():
        for k in (2, 5, 6, 7, 8):
            copies[k].wait_recv()
        for copy in copies:
            copy.wait_send()
        keep.wait()


def scatter_in_steps(
    part_ref,
    sum_ref,
    own_ref,
    near_ref,
    far_in_ref,
    side_in_ref,
    send_sems,
    recv_sems,
    load_sems,
):
    me, sibling, across, along = plane_peers()
    far = along + across - me
    flip = sibling - me
    rows = sum_ref.shape[0]
    half = rows // 2
    upper, lower = pl.ds(0, half), pl.ds(half, half)
    slabs = (far, across, along, me)
    loads = [
        pltpu.make_async_copy(part_ref.at[slab], own_ref.at[k], load_sems.at[k])
        for k, slab in enumerate(slabs)
    ]
    plan = [(sibling, part_ref.at[slab + flip], near_ref.at[k]) for k, slab in enumerate(slabs)]
    plan += [
        (across, own_ref.at[0, upper], far_in_ref.at[upper]),
        (along, own_ref.at[0, lower], far_in_ref.at[lower]),
        (across, own_ref.at[1, upper], side_in_ref.at[0, upper]),
        (along, own_ref.at[2, lower], side_in_ref.at[1, lower]),
        (along, own_ref.at[2, upper], side_in_ref.at[1, upper]),
        (across, own_ref.at[1, lower], side_in_ref.at[0, lower]),
    ]
    copies = [
        send_to(peer, source, target, send_sems.at[k], recv_sems.at[k])
        for k, (peer, source, target) in enumerate(plan)
    ]
    step, steps = pl.program_id(0), pl.num_programs(0)
    tall = 32

    def fold(target, other, start, size):
        @pl.loop(0, size // tall)
        def _(i):
            at = pl.ds(pl.multiple_of(start + i * tall, tall), tall)
            target[at] = (target[at].astype(F32) + other[at].astype(F32)).astype(BF16)

    def join(k):
        loads[k].wait()
        copies[k].wait_recv()
        fold(own_ref.at[k], near_ref.at[k], 0, rows)

    @pl.when(step == 0)
    def _():
        greet((sibling, across, along))
        for k in range(4):
            loads[k].start()
            copies[k].start()

    @pl.when(step == 1)
    def _():
        join(0)
        copies[4].start()
        copies[5].start()
        join(1)
        copies[6].start()
        join(2)
        copies[7].start()

    @pl.when(step == 3)
    def _():
        copies[4].wait_recv()
        fold(own_ref.at[2], far_in_ref, 0, half)
        copies[8].start()
        copies[5].wait_recv()
        fold(own_ref.at[1], far_in_ref, half, half)
        copies[9].start()

    @pl.when(step == steps - 1)
    def _():
        loads[3].wait()
        copies[3].wait_recv()
        for copy in copies[6:]:
            copy.wait_recv()

        @pl.loop(0, rows // tall)
        def _(i):
            at = pl.ds(pl.multiple_of(i * tall, tall), tall)
            sum_ref[at] = (
                own_ref[3, at].astype(F32)
                + near_ref[3, at].astype(F32)
                + side_in_ref[0, at].astype(F32)
                + side_in_ref[1, at].astype(F32)
            )

        for copy in copies:
            copy.wait_send()


def sum_phases(
    term_ref, share_ref, held_ref, land_ref, up_sems, down_sems, load_sems, trade_sems
):
    depth, rows, _ = held_ref.shape
    place = lax.axis_index("dp")
    above, below = lax.rem(place + 1, depth), lax.rem(place + depth - 1, depth)
    last = depth - 1
    mesh_ids = pl.DeviceIdType.MESH
    me = lax.axis_index("seq")
    core = lax.rem(me, 2)
    heads = depth // 2
    loads, trades = [], []
    for j in range(heads):
        target = held_ref.at[heads * core + j]

        def rows_of(spot):
            return term_ref.at[pl.ds(pl.multiple_of(spot * rows, rows), rows)]

        loads.append(pltpu.make_async_copy(rows_of(2 * j + core), target, load_sems.at[j]))
        trades.append(
            send_to(
                me + 1 - 2 * core,
                rows_of(2 * j + 1 - core),
                target,
                trade_sems.at[0, j],
                trade_sems.at[1, j],
            )
        )
    hops = []
    for r in range(last):
        hop = []
        for k, (peer, sems, block, leaves, mine, arrives) in enumerate(
            (
                (above, up_sems, place + last - r, place < r + 1, place + last - 1 - r, place > 0),
                (below, down_sems, place - last + r, place > last - 1 - r, place - last + 1 + r, place < last),
            )
        ):
            inside = (mine >= 0) & (mine <= last)
            spot = lax.rem(block + depth, depth)
            copy = pltpu.make_async_remote_copy(
                src_ref=held_ref.at[spot],
                dst_ref=land_ref.at[r, k],
                send_sem=sems.at[0, r],
                recv_sem=sems.at[1, r],
                device_id={"dp": peer},
                device_id_type=mesh_ids,
            )
            hop.append((copy, leaves, arrives & inside, lax.rem(mine + depth, depth)))
        hops.append(hop)
    def start(r, from_end):
        for end, (copy, leaves, _, _) in zip((0, last), hops[r]):
            pl.when(leaves & ((place == end) == from_end))(copy.start)

    def arrive(r):
        for k, (copy, _, arrives, block) in enumerate(hops[r]):

            @pl.when(arrives)
            def _(copy=copy, block=block, k=k):
                copy.wait_recv()
                total = held_ref[block].astype(F32) + land_ref[r, k].astype(F32)
                held_ref[block] = total.astype(BF16)

    for copy in loads + trades:
        copy.start()
    yield
    for load in loads:
        load.wait()
    for trade in trades:
        trade.wait_recv()
    for r in range(last):
        start(r, True)
    for r in range(last):
        start(r, False)
        yield
        arrive(r)
    share_ref[...] = held_ref[place].astype(F32)
    for trade in trades:
        trade.wait_send()
    for hop in hops:
        for copy, leaves, _, _ in hop:
            pl.when(leaves)(copy.wait_send)
    yield


def small_sum_kernel(
    heads,
    own_ref,
    cut_ref,
    term_ref,
    first_ref,
    second_ref,
    third_ref,
    decay_ref,
    taps_ref,
    param_ref,
    joined_ref,
    share_ref,
    all_ref,
    swapped_ref,
    stage_ref,
    total_ref,
    send_sems,
    recv_sems,
    local_sem,
    *sum_refs,
):
    depth, ring = stage_ref.shape[0], cut_ref.shape[0]
    place, me = lax.axis_index("dp"), lax.axis_index("seq")
    mesh_ids = pl.DeviceIdType.MESH
    columns = [lax.rem(place + k, depth) for k in range(1, depth)]
    plane = [lax.rem(me + k, ring) for k in range(1, ring)]
    greet_all(ring, depth)
    sums = sum_phases(term_ref, share_ref, *sum_refs)
    next(sums)
    keep = pltpu.make_async_copy(cut_ref.at[me], swapped_ref.at[me], local_sem)
    keep.start()
    first = []
    for k, peer in enumerate(columns):
        copy = pltpu.make_async_remote_copy(
            src_ref=own_ref,
            dst_ref=stage_ref.at[place],
            send_sem=send_sems.at[k],
            recv_sem=recv_sems.at[k],
            device_id={"dp": peer},
            device_id_type=mesh_ids,
        )
        copy.start()
        first.append(copy)
    stage_ref[place] = own_ref[...]
    next(sums)
    for copy in first:
        copy.wait_recv()
    total = stage_ref[0]
    for k in range(1, depth):
        total = total + stage_ref[k]
    total_ref[...] = total
    second = []
    for k, peer in enumerate(plane):
        copy = pltpu.make_async_remote_copy(
            src_ref=total_ref,
            dst_ref=all_ref.at[me],
            send_sem=send_sems.at[depth - 1 + k],
            recv_sem=recv_sems.at[depth - 1 + k],
            device_id={"seq": peer},
            device_id_type=mesh_ids,
        )
        copy.start()
        second.append(copy)
    swaps = exchange_copies(
        cut_ref, swapped_ref.at[me], send_sems, recv_sems, depth + ring - 2
    )
    all_ref[me] = total
    next(sums)
    next(sums)
    for copy in second:
        copy.wait_recv()
    start = 0
    for target in (first_ref, second_ref, third_ref):
        rows = target.shape[0]
        shared = all_ref[0, start : start + rows]
        for s in range(1, ring):
            shared = shared + all_ref[s, start : start + rows]
        target[...] = shared
        start += rows
    for target in (decay_ref, taps_ref, param_ref):
        rows = target.shape[1]
        target[...] = all_ref[:, start : start + rows]
        start += rows
    for copy in swaps:
        copy.wait_recv()
    keep.wait()
    size = cut_ref.shape[2] // (4 * heads)
    for part in range(4 * heads):
        block, j = part // heads, part % heads
        for s in range(ring):
            start = (block * ring * heads + rank_head(s, j, heads)) * size
            joined_ref[:, start : start + size] = swapped_ref[
                s, :, part * size : (part + 1) * size
            ]
    next(sums)
    for copy in first + second + swaps:
        copy.wait_send()


def small_sum(own, shared_counts, own_counts, cut, term, heads, collective_id):
    depth, ring = lax.axis_size("dp"), lax.axis_size("seq")
    count = depth + 2 * ring - 3
    term_rows, columns = term.shape[0] // depth, term.shape[1]
    vmem, anywhere = pl.BlockSpec(memory_space=pltpu.VMEM), pl.BlockSpec(memory_space=pl.ANY)
    return pl.pallas_call(
        functools.partial(small_sum_kernel, heads),
        out_shape=[
            *[jax.ShapeDtypeStruct((count, own.shape[1]), F32) for count in shared_counts],
            *[jax.ShapeDtypeStruct((ring, count, own.shape[1]), F32) for count in own_counts],
            jax.ShapeDtypeStruct((cut.shape[1], ring * cut.shape[2]), cut.dtype),
            jax.ShapeDtypeStruct((term_rows, columns), F32),
        ],
        in_specs=[vmem, anywhere, anywhere],
        out_specs=[vmem] * 8,
        scratch_shapes=[
            pltpu.VMEM((ring,) + own.shape, F32),
            pltpu.VMEM(cut.shape, cut.dtype),
            pltpu.VMEM((depth,) + own.shape, F32),
            pltpu.VMEM(own.shape, F32),
            pltpu.SemaphoreType.DMA((count,)),
            pltpu.SemaphoreType.DMA((count,)),
            pltpu.SemaphoreType.DMA,
            pltpu.VMEM((depth, term_rows, columns), BF16),
            pltpu.VMEM((depth - 1, 2, term_rows, columns), BF16),
            pltpu.SemaphoreType.DMA((2, depth - 1)),
            pltpu.SemaphoreType.DMA((2, depth - 1)),
            pltpu.SemaphoreType.DMA((depth // 2,)),
            pltpu.SemaphoreType.DMA((2, depth // 2)),
        ],
        compiler_params=pltpu.CompilerParams(collective_id=collective_id, has_side_effects=True),
        cost_estimate=lasting(20),
        name="small_sum",
    )(own, cut, term)


def greet_plane(ring):
    me = lax.axis_index("seq")
    greet([lax.rem(me + k, ring) for k in range(1, ring)])


def plane_scatter_dot_kernel(count, dims, fill, swaps, back, ends, low, *refs):
    refs = list(refs)

    def take(size):
        taken = refs[:size]
        del refs[:size]
        return taken

    left_hbm, right_hbm, fill_hbm = take(count), take(count), take(int(len(fill) > 0))
    cut_refs, back_hbm, end_hbm = take(swaps), take(2 * back), take(3 * ends)
    (sum_ref,) = take(1)
    terms, spread_refs = take(len(fill)), take(swaps)
    gain_grads, low_refs = take(ends), take(int(low))
    swapped_refs = take(swaps)
    lefts, rights, fill_refs = take(count), take(count), take(int(len(fill) > 0))
    out_ref, own_ref, near_ref, far_in_ref, side_in_ref = take(5)
    send_sems, recv_sems, load_sems, slab_sems = take(4)
    me, sibling, across, along = plane_peers()
    far = along + across - me
    flip = sibling - me
    slab_order = [far + flip, far, across + flip, across, along + flip, along, sibling, me]
    loads, slab_loads = [], []
    for k in range(count):
        load = pltpu.make_async_copy(right_hbm[k], rights[k], load_sems.at[k])
        load.start()
        loads.append(load)
    for n, slab in enumerate(slab_order):
        for k in range(count):
            load = pltpu.make_async_copy(
                left_hbm[k].at[slab], lefts[k].at[slab], slab_sems.at[k * len(slab_order) + n]
            )
            load.start()
            slab_loads.append(load)
    if ends:
        base_ref, up_ref, end_sems = take(3)
        end_loads = [
            pltpu.make_async_copy(end_hbm[0], base_ref, end_sems.at[0]),
            pltpu.make_async_copy(end_hbm[1], up_ref, end_sems.at[1]),
        ]
        gain_grads[0][...] = jnp.zeros_like(gain_grads[0])
    if back:
        error_ref, down_ref, error_sems, down_sem = refs
        down_load = pltpu.make_async_copy(back_hbm[1], down_ref, down_sem)
        down_load.start()
        error_loads = [
            pltpu.make_async_copy(back_hbm[0].at[slab], error_ref.at[k % 2], error_sems.at[k % 2])
            for k, slab in enumerate(slab_order)
        ]
        error_loads[0].start()
        error_loads[1].start()
    if fill:
        fill_load = pltpu.make_async_copy(fill_hbm[0], fill_refs[0], load_sems.at[count])
    rows, columns = sum_ref.shape
    half = rows // 2
    upper, lower = pl.ds(0, half), pl.ds(half, half)
    swapped = []
    if swaps:
        greet_plane(lefts[0].shape[0])
        keep = pltpu.make_async_copy(
            cut_refs[0].at[me], swapped_refs[0].at[me], load_sems.at[count + 1]
        )
        keep.start()
        swapped = exchange_copies(
            cut_refs[0], swapped_refs[0].at[me], send_sems, recv_sems, 10
        )
    else:
        greet((sibling, across, along))
    for load in loads:
        load.wait()
    if ends:
        for load in end_loads:
            load.start()
    if back:
        down_load.wait()
    wide = 512
    turns = iter(range(8))

    def feed_back(slab):
        k = next(turns)
        error_loads[k].wait()
        units = down_ref.shape[0]
        grad = low_dot(error_ref[k % 2], down_ref[...], NT)
        gate = lefts[0][slab, :, :units].astype(F32)
        up = lefts[0][slab, :, units:].astype(F32)
        opening = sigmoid(gate)
        gate_err = grad * up * (opening * (1.0 + gate * (1.0 - opening)))
        up_err = grad * (gate * opening)
        lefts[0][slab] = jnp.concatenate([gate_err, up_err], 1).astype(BF16)
        if k + 2 < len(error_loads):
            error_loads[k + 2].start()

    def slab_dot(slab, target):
        for _ in range(count):
            slab_loads.pop(0).wait()
        if back:
            feed_back(slab)

        @pl.loop(0, columns // wide)
        def _(i):
            at = pl.ds(pl.multiple_of(i * wide, wide), wide)
            total = None
            for k in range(count):
                right = rights[k][:, at] if dims[1] == (0,) else rights[k][at, :]
                term = low_dot(lefts[k][slab], right, dims)
                total = term if total is None else total + term
            target[:, at] = total.astype(BF16)

    def send(k, peer, source, target):
        copy = send_to(peer, source, target, send_sems.at[k], recv_sems.at[k])
        copy.start()
        return copy

    step = 32

    def fold(target, other, start, size):
        @pl.loop(0, size // step)
        def _(i):
            at = pl.ds(pl.multiple_of(start + i * step, step), step)
            target[at] = (target[at].astype(F32) + other[at].astype(F32)).astype(BF16)

    nears = []

    def near_slab(k, slab):
        slab_dot(slab + flip, out_ref.at[k])
        nears.append(send(k, sibling, out_ref.at[k], near_ref.at[k]))

    near_slab(0, far)
    if fill:
        fill_load.start()
    slab_dot(far, own_ref.at[0])
    near_slab(1, across)
    nears[0].wait_recv()
    fold(own_ref.at[0], near_ref.at[0], 0, rows)
    copies = [
        send(4, across, own_ref.at[0, upper], far_in_ref.at[upper]),
        send(5, along, own_ref.at[0, lower], far_in_ref.at[lower]),
    ]
    slab_dot(across, own_ref.at[1])
    near_slab(2, along)
    nears[1].wait_recv()
    fold(own_ref.at[1], near_ref.at[1], 0, rows)
    copies.append(send(6, across, own_ref.at[1, upper], side_in_ref.at[0, upper]))
    slab_dot(along, own_ref.at[2])
    near_slab(3, me)
    nears[2].wait_recv()
    fold(own_ref.at[2], near_ref.at[2], 0, rows)
    copies.append(send(7, along, own_ref.at[2, lower], side_in_ref.at[1, lower]))
    slab_dot(me, own_ref.at[3])
    copies[0].wait_recv()
    fold(own_ref.at[2], far_in_ref, 0, half)
    copies.append(send(8, along, own_ref.at[2, upper], side_in_ref.at[1, upper]))
    copies[1].wait_recv()
    fold(own_ref.at[1], far_in_ref, half, half)
    copies.append(send(9, across, own_ref.at[1, lower], side_in_ref.at[0, lower]))
    if swaps:
        for copy in swapped:
            copy.wait_recv()
        keep.wait()
        spread_units(swapped_refs[0], spread_refs[0], lax.axis_size("dp"))
    if fill:
        fill_load.wait()
        tall = 256

        @pl.loop(0, terms[0].shape[0] // tall)
        def _(i):
            at = pl.ds(pl.multiple_of(i * tall, tall), tall)
            turned = fill_refs[0][:, at]
            for term, k in zip(terms, fill):
                wide_left = lefts[k][...].reshape(-1, lefts[k].shape[2])
                term[at, :] = low_dot(turned, wide_left, TN).astype(term.dtype)

    nears[3].wait_recv()

    def finish(a, start):
        @pl.loop(0, half // step)
        def _(i):
            at = pl.ds(pl.multiple_of(start + i * step, step), step)
            total = (
                own_ref[3, at].astype(F32)
                + near_ref[3, at].astype(F32)
                + side_in_ref[0, at].astype(F32)
                + side_in_ref[1, at].astype(F32)
            )
            if ends:
                base = base_ref[at].astype(F32)
                scale = lax.rsqrt(jnp.mean(base * base, -1, keepdims=True) + 1e-05)
                normal = base * scale
                weighted = total * end_hbm[2][...]
                inner = jnp.mean(weighted * normal, -1, keepdims=True)
                gain_grads[0][0:1, :] += jnp.sum(total * normal, 0, keepdims=True)
                total = up_ref[at].astype(F32) + scale * (weighted - normal * inner)
            sum_ref[at] = total
            if low:
                low_refs[0][at] = total.astype(BF16)

    for copy in copies[2:]:
        copy.wait_recv()
    if ends:
        for load in end_loads:
            load.wait()
    finish(0, 0)
    finish(1, half)
    for copy in nears + copies + swapped:
        copy.wait_send()


def plane_scatter_dot(lefts, rights, dims, collective_id, fill=None, fill_lefts=(0,), term_type=BF16, cut=None, back=(), ends=(), low=False):
    count = len(lefts)
    ring, rows, _ = lefts[0].shape
    columns = rights[0].shape[1 - dims[1][0]]
    filled = fill is not None
    fills = [fill] if filled else []
    vmem, anywhere = pl.BlockSpec(memory_space=pltpu.VMEM), pl.BlockSpec(memory_space=pl.ANY)
    back_scratch = []
    if back:
        back_scratch = [
            pltpu.VMEM((2,) + back[0].shape[1:], BF16),
            pltpu.VMEM(back[1].shape, BF16),
            pltpu.SemaphoreType.DMA((2,)),
            pltpu.SemaphoreType.DMA,
        ]
    cuts = [] if cut is None else [cut]
    total = 10 + len(cuts) * (ring - 1)
    fill_lefts = fill_lefts if filled else ()
    term_shapes = [
        jax.ShapeDtypeStruct((fill.shape[1], lefts[k].shape[2]), term_type) for k in fill_lefts
    ]
    end_shapes = [jax.ShapeDtypeStruct((8, columns), F32)] if ends else []
    end_shapes += [jax.ShapeDtypeStruct((rows, columns), BF16)] if low else []
    end_scratch = []
    if ends:
        end_scratch = [
            pltpu.VMEM(ends[0].shape, ends[0].dtype),
            pltpu.VMEM(ends[1].shape, ends[1].dtype),
            pltpu.SemaphoreType.DMA((2,)),
        ]
    return pl.pallas_call(
        functools.partial(
            plane_scatter_dot_kernel,
            count,
            dims,
            fill_lefts,
            len(cuts),
            len(back) // 2,
            len(ends) // 3,
            low,
        ),
        out_shape=[jax.ShapeDtypeStruct((rows, columns), F32)]
        + term_shapes
        + [jax.ShapeDtypeStruct((cut.shape[1], ring * cut.shape[2]), BF16) for cut in cuts]
        + end_shapes,
        in_specs=[anywhere] * (2 * count + len(fills) + len(cuts) + len(back) + len(ends[:2]))
        + [vmem] * len(ends[2:]),
        out_specs=[vmem] * (1 + len(term_shapes) + len(cuts) + len(end_shapes)),
        scratch_shapes=[pltpu.VMEM(cut.shape, BF16) for cut in cuts]
        + [pltpu.VMEM(left.shape, BF16) for left in lefts]
        + [pltpu.VMEM(right.shape, BF16) for right in rights]
        + [pltpu.VMEM(value.shape, BF16) for value in fills]
        + [
            pltpu.VMEM((4, rows, columns), BF16),
            pltpu.VMEM((4, rows, columns), BF16),
            pltpu.VMEM((4, rows, columns), BF16),
            pltpu.VMEM((rows, columns), BF16),
            pltpu.VMEM((2, rows, columns), BF16),
            pltpu.SemaphoreType.DMA((total,)),
            pltpu.SemaphoreType.DMA((total,)),
            pltpu.SemaphoreType.DMA((count + 2,)),
            pltpu.SemaphoreType.DMA((8 * count,)),
        ]
        + end_scratch
        + back_scratch,
        compiler_params=pltpu.CompilerParams(
            collective_id=collective_id, has_side_effects=True, vmem_limit_bytes=VMEM_LIMIT
        ),
        cost_estimate=lasting(45),
        name="plane_scatter_dot",
    )(*lefts, *rights, *fills, *cuts, *back, *ends)


def gather_in_turn(own_ref, all_ref, send_sems, recv_sems, use):
    me, sibling, across, along = plane_peers()
    far = along + across - me
    flip = sibling - me
    half = own_ref.shape[0] // 2
    upper, lower = pl.ds(0, half), pl.ds(half, half)
    copies = []

    def send(peer, source, target):
        k = len(copies)
        copy = send_to(peer, source, target, send_sems.at[k], recv_sems.at[k])
        copy.start()
        copies.append(copy)

    send(across, own_ref, all_ref.at[me])
    send(along, own_ref, all_ref.at[me])
    send(sibling, own_ref, all_ref.at[me])
    all_ref[me] = own_ref[...]
    use(me)
    copies[2].wait_recv()
    use(sibling)
    copies[0].wait_recv()
    send(along, all_ref.at[across, upper], all_ref.at[across, upper])
    copies[1].wait_recv()
    send(across, all_ref.at[along, lower], all_ref.at[along, lower])
    send(sibling, all_ref.at[across], all_ref.at[across])
    send(sibling, all_ref.at[along], all_ref.at[along])
    use(across)
    use(along)
    copies[5].wait_recv()
    use(across + flip)
    copies[6].wait_recv()
    use(along + flip)
    copies[3].wait_recv()
    send(sibling, all_ref.at[far, upper], all_ref.at[far, upper])
    copies[4].wait_recv()
    send(sibling, all_ref.at[far, lower], all_ref.at[far, lower])
    use(far)
    copies[7].wait_recv()
    copies[8].wait_recv()
    use(far + flip)
    for copy in copies:
        copy.wait_send()


def gather_feed_kernel(
    own_hbm,
    pair_hbm,
    error_hbm,
    all_hbm,
    activated_hbm,
    pair_part_hbm,
    down_term_ref,
    own_ref,
    pair_ref,
    error_ref,
    all_ref,
    activated_out,
    pair_out,
    total_ref,
    send_sems,
    recv_sems,
    load_sems,
    save_sems,
):
    loads = []
    for source, target in (
        (own_hbm, own_ref),
        (pair_hbm, pair_ref),
        (error_hbm, error_ref),
    ):
        load = pltpu.make_async_copy(source, target, load_sems.at[len(loads)])
        load.start()
        loads.append(load)
    greet(plane_peers()[1:])
    loads[0].wait()
    waiting = loads[1:]
    saves = []
    tall = 256
    wide = 512
    rows, columns = own_ref.shape
    units = pair_ref.shape[1] // 2


    def use(slab):
        first = bool(waiting)
        while waiting:
            waiting.pop().wait()
        turn = len(saves) % 2
        if len(saves) > 1:
            for save in saves[-2]:
                save.wait()

        @pl.loop(0, rows // tall)
        def _(i):
            at = pl.ds(pl.multiple_of(i * tall, tall), tall)
            values = all_ref[slab, at, :]
            pair = low_dot(values, pair_ref[...], NN)
            gate, up = pair[:, :units], pair[:, units:]
            activated_out[turn, at, :] = (gate * sigmoid(gate) * up).astype(BF16)
            pair_out[turn, at, :] = pair.astype(BF16)

        batch = []
        for k, (source, target) in enumerate(
            (
                (activated_out.at[turn], activated_hbm.at[slab]),
                (pair_out.at[turn], pair_part_hbm.at[slab]),
                (all_ref.at[slab], all_hbm.at[slab]),
            )
        ):
            save = pltpu.make_async_copy(source, target, save_sems.at[turn, k])
            save.start()
            batch.append(save)
        saves.append(batch)

        @pl.loop(0, columns // wide)
        def _(i):
            at = pl.ds(pl.multiple_of(i * wide, wide), wide)
            term = low_dot(activated_out[turn], error_ref[slab, :, at], TN)
            if first:
                total_ref[:, at] = term
            else:
                total_ref[:, at] += term

    gather_in_turn(own_ref, all_ref, send_sems, recv_sems, use)
    down_term_ref[...] = total_ref[...].astype(BF16)
    for batch in saves[-2:]:
        for save in batch:
            save.wait()


def gather_feed(own, pair_own, error_all, collective_id):
    ring = lax.axis_size("seq")
    rows, columns = own.shape
    units = pair_own.shape[1] // 2
    anywhere = pl.BlockSpec(memory_space=pl.ANY)
    return pl.pallas_call(
        gather_feed_kernel,
        out_shape=[
            jax.ShapeDtypeStruct((ring, rows, columns), BF16),
            jax.ShapeDtypeStruct((ring, rows, units), BF16),
            jax.ShapeDtypeStruct((ring, rows, 2 * units), BF16),
            jax.ShapeDtypeStruct((units, columns), BF16),
        ],
        in_specs=[anywhere] * 3,
        out_specs=[anywhere] * 3 + [pl.BlockSpec(memory_space=pltpu.VMEM)],
        scratch_shapes=[
            pltpu.VMEM((rows, columns), BF16),
            pltpu.VMEM(pair_own.shape, BF16),
            pltpu.VMEM((ring, rows, columns), BF16),
            pltpu.VMEM((ring, rows, columns), BF16),
            pltpu.VMEM((2, rows, units), BF16),
            pltpu.VMEM((2, rows, 2 * units), BF16),
            pltpu.VMEM((units, columns), F32),
            pltpu.SemaphoreType.DMA((9,)),
            pltpu.SemaphoreType.DMA((9,)),
            pltpu.SemaphoreType.DMA((3,)),
            pltpu.SemaphoreType.DMA((2, 3)),
        ],
        compiler_params=pltpu.CompilerParams(
            collective_id=collective_id, has_side_effects=True, vmem_limit_bytes=VMEM_LIMIT
        ),
        cost_estimate=lasting(46),
        name="gather_feed",
    )(own, pair_own, error_all)


def gather_branch_kernel(
    own_hbm,
    gated_hbm,
    weight_hbm,
    activated_hbm,
    down_hbm,
    grad_ref,
    term_ref,
    part_hbm,
    own_ref,
    gated_ref,
    weight_ref,
    activated_ref,
    down_ref,
    all_ref,
    total_ref,
    part_out,
    send_sems,
    recv_sems,
    load_sems,
    save_sems,
):
    loads = []
    for source, target in (
        (own_hbm, own_ref),
        (gated_hbm, gated_ref),
        (weight_hbm, weight_ref),
        (activated_hbm, activated_ref),
        (down_hbm, down_ref),
    ):
        load = pltpu.make_async_copy(source, target, load_sems.at[len(loads)])
        load.start()
        loads.append(load)
    greet(plane_peers()[1:])
    loads[0].wait()
    waiting = loads[1:]
    total_ref[...] = jnp.zeros_like(total_ref)
    wide = 512
    saves = []

    def use(slab):
        while waiting:
            waiting.pop().wait()
        turn = len(saves) % 2
        if len(saves) > 1:
            saves[-2].wait()
        grad_ref[slab] = low_dot(all_ref[slab], weight_ref[...], NT).astype(BF16)

        @pl.loop(0, total_ref.shape[1] // wide)
        def _(i):
            at = pl.ds(pl.multiple_of(i * wide, wide), wide)
            total_ref[:, at] += low_dot(gated_ref[slab], all_ref[slab, :, at], TN)
            part_out[turn, :, at] = low_dot(activated_ref[slab], down_ref[:, at], NN).astype(BF16)

        save = pltpu.make_async_copy(part_out.at[turn], part_hbm.at[slab], save_sems.at[turn])
        save.start()
        saves.append(save)

    gather_in_turn(own_ref, all_ref, send_sems, recv_sems, use)
    term_ref[...] = total_ref[...].astype(BF16)
    for save in saves[-2:]:
        save.wait()


def gather_branch(own, gated, weight, activated, down_own, collective_id):
    ring, rows, width = gated.shape
    columns = own.shape[1]
    vmem = pl.BlockSpec(memory_space=pltpu.VMEM)
    anywhere = pl.BlockSpec(memory_space=pl.ANY)
    return pl.pallas_call(
        gather_branch_kernel,
        out_shape=[
            jax.ShapeDtypeStruct((ring, rows, width), BF16),
            jax.ShapeDtypeStruct((width, columns), BF16),
            jax.ShapeDtypeStruct((ring, rows, columns), BF16),
        ],
        in_specs=[anywhere] * 5,
        out_specs=[vmem, vmem, anywhere],
        scratch_shapes=[
            pltpu.VMEM(own.shape, BF16),
            pltpu.VMEM(gated.shape, BF16),
            pltpu.VMEM(weight.shape, BF16),
            pltpu.VMEM(activated.shape, BF16),
            pltpu.VMEM(down_own.shape, BF16),
            pltpu.VMEM((ring, rows, columns), BF16),
            pltpu.VMEM((width, columns), F32),
            pltpu.VMEM((2, rows, columns), BF16),
            pltpu.SemaphoreType.DMA((9,)),
            pltpu.SemaphoreType.DMA((9,)),
            pltpu.SemaphoreType.DMA((5,)),
            pltpu.SemaphoreType.DMA((2,)),
        ],
        compiler_params=pltpu.CompilerParams(
            collective_id=collective_id, has_side_effects=True, vmem_limit_bytes=VMEM_LIMIT
        ),
        cost_estimate=lasting(45),
        name="gather_branch",
    )(own, gated, weight, activated, down_own)


def low_dot(left, right, dims):
    return lax.dot_general(left, right, (dims, ((), ())), preferred_element_type=F32)


NN = ((1,), (0,))
NT = ((1,), (1,))
TN = ((0,), (0,))


def split_heads_device(
    inputs,
    lengths,
    first_gain,
    input_weight,
    decay_weight,
    conv_weight,
    decay_log,
    decay_bias,
    head_gain,
    output_weight,
    second_gain,
    gate_up_weight,
    down_weight,
    cotangent,
):
    micro_count, seq_local, span, model_width = inputs.shape
    ring = lax.axis_size("seq")
    depth = lax.axis_size("dp")
    rank = lax.axis_index("seq")
    seqs = micro_count * seq_local
    row_count = seqs * span
    all_rows = ring * row_count
    head_count = decay_log.shape[0]
    heads = head_count // ring
    head_size = head_gain.shape[0]
    key_width = head_count * head_size
    width = heads * head_size
    own_units = down_weight.shape[0]
    units = depth * own_units
    weight_rows = input_weight.shape[0]
    tap_count = conv_weight.shape[0]

    tokens = inputs.reshape(row_count, model_width).astype(F32)
    positions = rank * span + lax.broadcasted_iota(jnp.int32, (micro_count, seq_local, span), 2)
    valid_rows = (positions < lengths[:, :, None]).astype(F32).reshape(row_count, 1)
    normed_low = rms_norm(tokens, first_gain).astype(BF16)

    upstream = valid_rows * cotangent.reshape(row_count, model_width).astype(F32)
    out_err = upstream.astype(BF16)
    out_rows = gather_rows(output_weight, "dp")
    own_heads = [rank_head(rank, j, heads) for j in range(heads)]

    def own_lanes(pair):
        rows = pair.shape[0]
        lanes = [
            lax.dynamic_slice(pair, (0, start + head), (rows, 1))
            for start in range(0, pair.shape[1], head_count)
            for head in own_heads
        ]
        return jnp.pad(jnp.concatenate(lanes, 1), ((0, 0), (0, 128 - len(lanes))))

    decay_own = own_lanes(decay_weight)
    params = jnp.pad(own_lanes(jnp.stack([decay_log, decay_bias])), ((0, 6), (0, 0)))
    taps = jnp.concatenate(
        [
            lax.dynamic_slice(
                conv_weight, (0, block * key_width + head * head_size), (tap_count, head_size)
            )
            for block in range(3)
            for head in own_heads
        ],
        1,
    )
    gain = head_gain.reshape(1, head_size)

    def chunks(value):
        return value.reshape(ring, seqs, span, value.shape[-1])

    normed_all, in_own, pair_cut, mixed, gate_raw, logits = plane_open(
        normed_low, input_weight, gate_up_weight, decay_own, heads, 1
    )
    normed_all = normed_all.reshape(all_rows, model_width)
    in_own = in_own.reshape(model_width, 4 * width)
    pair_own = gather_rows(pair_cut.reshape(ring * weight_rows, 2 * units), "dp")
    mixed, out_rows, down_weight = lax.optimization_barrier((mixed, out_rows, down_weight))
    down_own = gather_rows(down_weight, "dp")
    mixed, gate_raw, logits = chunks(mixed), chunks(gate_raw), chunks(logits)
    gated, memory, inverse, fresh, mixer_out, out_err_all, out_own = run_forward(
        mixed, gate_raw, logits, taps, params, gain, heads, out_err, out_rows, 5
    )
    gated = gated.reshape(ring, row_count, width)
    hidden = tokens + plane_scatter_dot([gated], [out_own], NN, 2)[0]
    second_low = rms_norm(hidden, second_gain).astype(BF16)
    second_all, activated, pair_part, down_term = gather_feed(
        second_low, pair_own, out_err_all, 3
    )
    down_share = scatter_rows(down_term, "dp").astype(F32)
    hidden_grad, pair_term, second_gain_grad, branch_err = plane_scatter_dot(
        [pair_part],
        [pair_own],
        NT,
        4,
        second_all.reshape(all_rows, model_width),
        back=(out_err_all, down_own),
        ends=(hidden, out_err, second_gain.reshape(1, model_width)),
        low=True,
    )
    pair_share = scatter_rows(pair_term, "dp")
    gated_grad, output_term, down_part = gather_branch(
        branch_err, gated, out_own, activated, down_own, 11
    )
    in_err, logit_grad, taps_grad, param_grad, gain_grad, final_part = run_backward(
        mixed,
        gate_raw,
        logits,
        taps,
        params,
        gain,
        memory,
        inverse,
        fresh,
        mixer_out,
        gated_grad.reshape(ring, seqs, span, width),
        down_part,
        12,
    )
    result = valid_rows * (hidden + final_part)
    input_term = low_dot(normed_all, in_err.reshape(all_rows, 4 * width), TN).astype(BF16)
    input_term, in_err, logit_grad, down_share, pair_share = lax.optimization_barrier(
        (input_term, in_err, logit_grad, down_share, pair_share)
    )
    lanes = logit_grad.shape[-1]
    input_cut = scatter_rows(input_term, "dp")
    decay_twice = decay_own + jnp.roll(decay_own, lanes // 2, 1)
    inputs_grad, decay_term, gate_up_share, first_gain_grad = plane_scatter_dot(
        [
            in_err.reshape(ring, row_count, 4 * width),
            logit_grad.reshape(ring, row_count, lanes),
        ],
        [in_own, decay_twice],
        NT,
        6,
        normed_all,
        (1,),
        F32,
        cut=pair_share.reshape(ring, weight_rows, 2 * units),
        ends=(
            inputs.reshape(row_count, model_width),
            hidden_grad,
            first_gain.reshape(1, model_width),
        ),
    )
    decay_term = decay_term[:, : 2 * heads] + decay_term[:, lanes // 2 : lanes // 2 + 2 * heads]
    pieces = [
        first_gain_grad[0],
        second_gain_grad[0],
        gain_grad[0],
        jnp.transpose(decay_term),
        taps_grad[:tap_count],
        param_grad[:2],
    ]
    counts = [piece.size // 128 for piece in pieces]
    packed = jnp.concatenate([piece.reshape(-1) for piece in pieces])
    packed = jnp.pad(packed, (0, -packed.size % 1024)).reshape(-1, 128)
    gate_up_share = gate_up_share.astype(F32)
    packed, input_cut, gate_up_share, result = lax.optimization_barrier(
        (packed, input_cut, gate_up_share, result)
    )
    (
        first_gain_grad,
        second_gain_grad,
        gain_grad,
        decay_sum,
        taps_sum,
        param_sum,
        input_share,
        output_share,
    ) = small_sum(
        packed,
        counts[:3],
        counts[3:],
        input_cut.reshape(ring, weight_rows, 4 * width),
        output_term,
        heads,
        7,
    )
    input_share = input_share.astype(F32)
    first_gain_grad, second_gain_grad, gain_grad = [
        total.reshape(-1) for total in (first_gain_grad, second_gain_grad, gain_grad)
    ]
    chips = ring // 2
    decay_sum = decay_sum.reshape(chips, 2, 2, heads, model_width)
    decay_weight_grad = jnp.transpose(decay_sum, (4, 2, 1, 3, 0)).reshape(model_width, -1)
    taps_sum = taps_sum.reshape(chips, 2, tap_count, 3, heads, head_size)
    taps_sum = jnp.transpose(taps_sum, (2, 3, 1, 4, 0, 5))
    param_sum = param_sum[:, :, :heads].reshape(chips, 2, 2, heads)
    param_sum = jnp.transpose(param_sum, (2, 1, 3, 0)).reshape(2, head_count)
    return (
        result.reshape(inputs.shape),
        inputs_grad.reshape(inputs.shape),
        first_gain_grad,
        input_share,
        decay_weight_grad,
        taps_sum.reshape(tap_count, 3 * key_width),
        param_sum[0],
        param_sum[1],
        gain_grad,
        output_share,
        second_gain_grad,
        gate_up_share,
        down_share,
    )


def solution(mesh):
    in_specs = (
        P(None, "dp", "seq", None),
        P(None, "dp"),
        P(),
        P(("dp", "seq"), None),
        P(),
        P(),
        P(),
        P(),
        P(),
        P(("dp", "seq"), None),
        P(),
        P(("dp", "seq"), None),
        P(("dp", "seq"), None),
        P(None, "dp", "seq", None),
    )
    out_specs = (
        P(None, "dp", "seq", None),
        P(None, "dp", "seq", None),
        P(),
        P(("dp", "seq"), None),
        P(),
        P(),
        P(),
        P(),
        P(),
        P(("dp", "seq"), None),
        P(),
        P(("dp", "seq"), None),
        P(("dp", "seq"), None),
    )
    ring = mesh.shape["seq"]

    def whole_device(*arrays):
        heads_divide = ring == 8 and 2 * arrays[6].shape[0] == ring * mesh.shape["dp"]
        return (split_heads_device if heads_divide else per_device)(*arrays)

    return jax.shard_map(
        whole_device, mesh=mesh, in_specs=in_specs, out_specs=out_specs, check_vma=False
    )
```
